32 devices in a mesh: kv: 4 (over y, x), blk: 8 (over z, core).
Axes of the slice: x: 2, y: 2, z: 4, core: 2. Of those that a mesh axis runs over, the one named last changes fastest.
Arguments:
- queries: bfloat16 [32, 4096], P('blk', 'kv'), may hold values from -120 to 120
- cache_keys: bfloat16 [32, 4096, 4, 128], P('blk', None, 'kv'), may hold values from -5 to 5
- cache_values: bfloat16 [32, 4096, 4, 128], P('blk', None, 'kv'), may hold values from -6 to 6
- lengths: int32 [32], replicated, may hold values from 1 to 32768, as said below
- sinks: float32 [32], P('kv'), may hold values from 5 to 11
- out_proj: bfloat16 [4096, 2048], P('kv'), may hold values from -0.09375 to 0.09375
- decode_resid: bfloat16 [32, 2048], P(('blk', 'kv')), may hold values from -4 to 4
- prefill_hidden: bfloat16 [32, 111, 2048], P(('blk', 'kv')), may hold values from -6 to 6
- norm_gain: float32 [2048], replicated, may hold values from 0.1 to 1.9
- router: bfloat16 [2048, 32], replicated, may hold values from -80 to 80
- routes: int32 [32, 112, 8], P(('blk', 'kv')), may hold values from 0 to 31, all different within a row; in each aligned block of 112 rows (0 to 111, 112 to 223, ..., all dimensions but the last counted through in order) at most 56 rows name the same one
- expert_gate: bfloat16 [32, 2048, 768], P(('kv', 'blk')), may hold values from -0.125 to 0.125
- expert_up: bfloat16 [32, 2048, 768], P(('kv', 'blk')), may hold values from -0.125 to 0.125
- expert_down: bfloat16 [32, 768, 2048], P(('kv', 'blk')), may hold values from -0.21875 to 0.21875
Outputs:
- layer_out: bfloat16 [32, 112, 2048], P(('blk', 'kv'))
The draws below stay inside these ranges and needn't reach their ends.
Inputs may be any that keep to these rules, and one draw needn't show every extreme that they name: `lengths`: at least one request has exactly 32768 cached positions. `routes`: within the rows of one device (112 rows, aligned blocks) no expert is named by more than 56 rows, and in every draw some expert reaches 56 in some block.
All inputs are finite; a program needn't handle non-finite values.
Results may differ from the reference program's by a relative error of at most 0.0094.
Values may be sent and summed in bfloat16 or wider, within the bound.
No kernel may reach another device: no remote copies, remote signals or barrier semaphores. Data moves between devices by JAX's collectives and lax.ppermute only.
A program may use at most 128 MiB of HBM per device.

```python
import math
import jax
import jax.numpy as jnp
import numpy as np
from jax import lax

D = 2048
FF = 768
HQ = 32
KVH = 4
HD = 128
TOP = 8
WIN = 4096
CONTEXT = 32768
PREF_DEV = 111
EXPERTS = 32
REQ = 32
TOK_DEV = 112
CAP = 56
N_KV = 4
N_BLK = 8


def shared_keys(key):
    base = jax.random.fold_in(key, 7)
    raw = jnp.clip(jax.random.normal(base, (REQ, WIN, KVH, HD), jnp.float32), -5.0, 5.0)
    return raw


def draw_cache_keys(key, part):
    return shared_keys(key).astype(jnp.bfloat16)


def draw_queries(key, part):
    own_key = jax.random.fold_in(key, 11)
    raw = jnp.clip(2.5 * jax.random.normal(own_key, (REQ, HQ * HD), jnp.float32), -12.5, 12.5)
    return raw.astype(jnp.bfloat16)


def draw_router(key, part):
    base_key = jax.random.fold_in(key, 13)
    raw = jnp.clip(jax.random.normal(base_key, (D, EXPERTS), jnp.float32), -4.0, 4.0) / math.sqrt(D)
    return raw.astype(jnp.bfloat16)


def draw_lengths(key, part):
    first_key, second_key, third_key, fourth_key = jax.random.split(key, 4)
    short_len = jax.random.randint(first_key, (REQ,), 1, WIN + 1)
    long_len = jax.random.randint(second_key, (REQ,), WIN, CONTEXT + 1)
    picker = jax.random.randint(third_key, (REQ,), 0, 2)
    chosen_len = jnp.where(picker == 0, short_len, long_len)
    position = jax.random.randint(fourth_key, (), 0, REQ)
    return chosen_len.at[position].set(CONTEXT).astype(jnp.int32)


def block_levels(key, extent, cuts, low, largest):
    loudness = 1.0
    for axis_at, shards_of in cuts:
        heights = jax.random.uniform(jax.random.fold_in(jax.random.fold_in(key, 6), axis_at), (shards_of,), jnp.float32, low / len(cuts), largest / len(cuts))
        loudness = loudness * jnp.repeat(jnp.exp(heights), extent[axis_at] // shards_of).reshape((-1,) + (1,) * (len(extent) - 1 - axis_at))
    return loudness


def assign_block(stream_key, own, number, rows, amount, top, bound, skew):
    order = jax.random.permutation(stream_key, amount)
    crowded, usual = load_shares(amount, rows * top, bound, skew, True), load_shares(amount, rows * top, bound, skew, False)
    places = jnp.arange(amount)

    def named(tallies, offset_by):
        used = int((tallies > 0).sum())
        fixed = max(1, used // 4)
        moved = fixed + (places - fixed + offset_by * (used - fixed)) % max(1, amount - fixed)
        return jnp.zeros((amount,), jnp.int32).at[order[jnp.where(places < fixed, places, moved)]].set(jnp.asarray(tallies, jnp.int32))

    tallies = jnp.where(number % 4 == 0, named(crowded, number // 4), named(usual, number - number // 4 - 1))
    mixed = jax.random.permutation(jax.random.fold_in(own, 3), amount)
    source_of, receiver = mixed[0:amount // 2 * 2:2], mixed[1:amount // 2 * 2:2]
    margin = jnp.minimum(tallies[source_of] - 1, bound - tallies[receiver]) // 2
    margin = jnp.where((source_of == order[0]) | (receiver == order[0]) | (tallies[receiver] == 0), 0, jnp.maximum(margin, 0))
    moved = jax.random.randint(jax.random.fold_in(own, 4), (amount // 2,), 0, 1 << 20) % (margin + 1)
    tallies = tallies.at[source_of].add(-moved).at[receiver].add(moved)
    items = jnp.searchsorted(jnp.cumsum(tallies), jnp.arange(rows * top), side="right").astype(jnp.int32)
    table = items.reshape(top, rows).T
    table = table[jax.random.permutation(jax.random.fold_in(own, 1), rows)]
    offset_by = jax.random.randint(jax.random.fold_in(own, 2), (rows, 1), 0, top)
    return jnp.take_along_axis(table, (jnp.arange(top)[None, :] + offset_by) % top, axis=1)


def load_shares(count, total, most, lean, full):
    weights = [(1 << 20) // math.isqrt(standing ** lean) + 1 for standing in range(1, count + 1)]
    largest = most if full else min(most, max(-(-total // count), total * weights[0] // sum(weights)))
    least = 1 if total - largest >= count - 1 else 0
    counts, rest = [largest] + [least] * (count - 1), total - largest - least * (count - 1)
    while rest > 0:
        candidates = [i for i in range(1, count) if counts[i] < largest] or [i for i in range(1, count) if counts[i] < most]
        pool, left = sum([weights[i] for i in candidates]), rest
        for i in candidates:
            addition = min(most - counts[i], max(1, left * weights[i] // pool), rest)
            counts[i] = counts[i] + addition
            rest = rest - addition
    return np.array(counts)


def gaussian(stream_key, extent, spread, bound, cuts=(), kind=jnp.bfloat16):
    array = jax.random.normal(stream_key, extent, jnp.float32) * spread
    if len(cuts) > 0:
        array = block_levels(stream_key, extent, cuts, -0.22, 0.18) * array
    return jnp.clip(array, min=-bound, max=bound).astype(kind)


def setup_inputs(seed: int = 0) -> dict:
    key_list = jax.random.split(jax.random.key(seed), 15)
    queries = draw_queries(jax.random.fold_in(key_list[14], 71), 0)
    cache_keys = draw_cache_keys(jax.random.fold_in(key_list[14], 71), 0)
    cache_values = gaussian(key_list[2], (REQ, WIN, KVH, HD), 1.0, 6.0, ((0, 8), (2, 4)))
    lengths = draw_lengths(jax.random.fold_in(key_list[14], 71), 0)
    sinks = jnp.clip(5.0 + 6.0 * jax.random.uniform(key_list[4], (HQ,), jnp.float32) ** block_levels(key_list[4], (HQ,), ((0, 4),), -0.2, 0.2), 5.0, 11.0)
    out_proj = gaussian(key_list[5], (HQ * HD, D), (HQ * HD) ** -0.5, 0.09375, ((0, 4),))
    decode_resid = gaussian(key_list[6], (REQ, D), 0.5, 4.0, ((0, 32),))
    prefill_hidden = gaussian(key_list[7], (REQ, PREF_DEV, D), 1.0, 6.0, ((0, 32),))
    norm_gain = jnp.clip(1.0 + 0.18 * jax.random.normal(key_list[8], (D,), jnp.float32), 0.1, 1.9)
    router = draw_router(jax.random.fold_in(key_list[14], 71), 0)
    routes_keys = jax.random.split(jax.random.fold_in(key_list[10], 1), REQ * TOK_DEV // TOK_DEV)
    routes_turns = jax.random.permutation(jax.random.fold_in(key_list[10], 3), REQ * TOK_DEV // TOK_DEV)
    routes = jax.vmap(lambda own, number: assign_block(jax.random.fold_in(key_list[10], 2), own, number, TOK_DEV, EXPERTS, TOP, CAP, 1))(routes_keys, routes_turns).reshape((REQ, TOK_DEV, TOP))
    expert_gate = gaussian(key_list[11], (EXPERTS, D, FF), D ** -0.5, 0.125, ((0, 32),))
    expert_up = gaussian(key_list[12], (EXPERTS, D, FF), D ** -0.5, 0.125, ((0, 32),))
    expert_down = gaussian(key_list[13], (EXPERTS, FF, D), FF ** -0.5, 0.21875, ((0, 32),))
    return dict(queries=queries, cache_keys=cache_keys, cache_values=cache_values, lengths=lengths, sinks=sinks, out_proj=out_proj, decode_resid=decode_resid, prefill_hidden=prefill_hidden, norm_gain=norm_gain, router=router, routes=routes, expert_gate=expert_gate, expert_up=expert_up, expert_down=expert_down)


NEG_FILL = -1e+30
EPSILON = 1e-06

def reference(queries, cache_keys, cache_values, lengths, sinks, out_proj, decode_resid, prefill_hidden, norm_gain, router, routes, expert_gate, expert_up, expert_down):
    per_group = HQ // KVH
    sink_grid = sinks.reshape(KVH, per_group)

    def attend(packed):
        one_query, key_rows, value_rows, length = packed
        grouped_q = one_query.reshape(KVH, per_group, HD).astype(jnp.float32)
        scores = jnp.einsum('gqd,jgd->gqj', grouped_q, key_rows.astype(jnp.float32)) * (1.0 / math.sqrt(HD))
        first_valid = WIN - jnp.minimum(length, WIN)
        is_valid = (jnp.arange(WIN, dtype=jnp.int32) >= first_valid)[None, None, :]
        masked = jnp.where(is_valid, scores, NEG_FILL)
        top_limit = jnp.maximum(lax.optimization_barrier(jnp.max(masked, axis=2)), sink_grid)
        weights = jnp.where(is_valid, jnp.exp(masked - top_limit[..., None]), 0.0)
        denominator = lax.optimization_barrier(jnp.sum(weights, axis=2)) + jnp.exp(sink_grid - top_limit)
        rounded = lax.optimization_barrier(weights.astype(jnp.bfloat16))
        numerator = jnp.einsum('gqj,jgd->gqd', rounded.astype(jnp.float32), value_rows.astype(jnp.float32))
        return (numerator / denominator[..., None]).astype(jnp.bfloat16).reshape(HQ * HD)
    attended = lax.map(attend, (queries, cache_keys, cache_values, lengths))
    projected = jnp.dot(attended, out_proj, preferred_element_type=jnp.float32)
    decoded = (decode_resid.astype(jnp.float32) + projected).astype(jnp.bfloat16)
    hidden = jnp.concatenate([decoded[:, None, :], prefill_hidden], axis=1).reshape(-1, D)
    hidden_f = hidden.astype(jnp.float32)
    mean_sq = lax.optimization_barrier(jnp.mean(hidden_f * hidden_f, axis=1, keepdims=True))
    normed = (hidden_f * lax.rsqrt(mean_sq + EPSILON) * norm_gain).astype(jnp.bfloat16)
    logits = jnp.dot(normed, router, preferred_element_type=jnp.float32)
    flat_routes = routes.reshape(-1, TOP)
    chosen = jnp.take_along_axis(logits, flat_routes, axis=1)
    gate_probs = jax.nn.softmax(chosen, axis=1).reshape(-1)
    flat_ids = flat_routes.reshape(-1)
    max_rows = N_KV * N_BLK * CAP

    def one_expert(running, expert):
        row_order = jnp.argsort((flat_ids != expert).astype(jnp.int32), stable=True)[:max_rows].astype(jnp.int32)
        is_hit = flat_ids[row_order] == expert
        token_rows = row_order // TOP
        picked = normed[token_rows]
        gate_act = jnp.dot(picked, expert_gate[expert], preferred_element_type=jnp.float32)
        up_act = jnp.dot(picked, expert_up[expert], preferred_element_type=jnp.float32)
        inner_act = (jax.nn.silu(gate_act) * up_act).astype(jnp.bfloat16)
        output = jnp.dot(inner_act, expert_down[expert], preferred_element_type=jnp.float32)
        output = lax.optimization_barrier(output.astype(jnp.bfloat16)).astype(jnp.float32)
        weighted = jnp.where(is_hit, gate_probs[row_order], 0.0)[:, None] * output
        return (running.at[token_rows].add(weighted), None)
    running, ignored = lax.scan(one_expert, jnp.zeros((hidden.shape[0], D), jnp.float32), jnp.arange(EXPERTS, dtype=jnp.int32))
    return (hidden_f + running).astype(jnp.bfloat16).reshape(REQ, TOK_DEV, D)
```

```python
import math

import jax
import jax.numpy as jnp
from jax import lax
from jax.experimental import pallas as pl
from jax.experimental.pallas import tpu as pltpu
from jax.sharding import PartitionSpec as P

NEG_FILL = -1e30
EPSILON = 1e-06
AXES = ("blk", "kv")


def attend(queries, cache_keys, cache_values, lengths, sinks):
    my_block = lax.axis_index("blk")
    per_block = queries.shape[0]
    head_count = sinks.shape[0]
    head_dim = cache_keys.shape[3]
    window = cache_keys.shape[1]
    grouped_q = queries.reshape(per_block, head_count, head_dim)
    key_rows = cache_keys[:, :, 0, :]
    value_rows = cache_values[:, :, 0, :]
    my_lengths = lax.dynamic_slice_in_dim(lengths, my_block * per_block, per_block)
    scores = jnp.einsum("rgd,rjd->rgj", grouped_q, key_rows, preferred_element_type=jnp.float32) * (
        1.0 / math.sqrt(head_dim)
    )
    first_valid = window - jnp.minimum(my_lengths, window)
    is_valid = (jnp.arange(window, dtype=jnp.int32)[None, :] >= first_valid[:, None])[:, None, :]
    masked = jnp.where(is_valid, scores, NEG_FILL)
    top_limit = jnp.maximum(jnp.max(masked, axis=2), sinks[None, :])
    weights = jnp.where(is_valid, jnp.exp(masked - top_limit[..., None]), 0.0)
    denominator = jnp.sum(weights, axis=2) + jnp.exp(sinks[None, :] - top_limit)
    numerator = jnp.einsum(
        "rgj,rjd->rgd", weights.astype(jnp.bfloat16), value_rows, preferred_element_type=jnp.float32
    )
    return (
        (numerator / denominator[..., None])
        .astype(jnp.bfloat16)
        .reshape(per_block, head_count * head_dim)
    )


def prepare_kernel(hidden_ref, gain_ref, router_ref, routes_ref, out_ref):
    width = hidden_ref.shape[1]
    experts = router_ref.shape[1]
    hidden = hidden_ref[...].astype(jnp.float32)
    mean_sq = jnp.mean(hidden * hidden, axis=1, keepdims=True)
    normed = (hidden * lax.rsqrt(mean_sq + EPSILON) * gain_ref[...]).astype(jnp.bfloat16)
    out_ref[:, :width] = normed
    logits = jnp.dot(normed, router_ref[...], preferred_element_type=jnp.float32)
    lane = lax.broadcasted_iota(jnp.int32, logits.shape, 1)
    routes = routes_ref[...]
    chosen = jnp.zeros(logits.shape, jnp.bool_)
    for k in range(routes.shape[1]):
        chosen = chosen | (lane == routes[:, k : k + 1])
    top = jnp.max(jnp.where(chosen, logits, NEG_FILL), axis=1, keepdims=True)
    raised = jnp.where(chosen, jnp.exp(jnp.minimum(logits - top, 0.0)), 0.0)
    gates = raised / jnp.sum(raised, axis=1, keepdims=True)
    high = gates.astype(jnp.bfloat16).astype(jnp.float32)
    low = gates - high
    rest = out_ref.shape[1] - width - 2 * experts
    parts = [high, low]
    if rest:
        parts.append(jnp.zeros((high.shape[0], rest), jnp.float32))
    out_ref[:, width:] = jnp.concatenate(parts, axis=1).astype(jnp.bfloat16)


def prepare(hidden, norm_gain, router, routes):
    rows, width = hidden.shape
    extra = -(-2 * router.shape[1] // 128) * 128
    return pl.pallas_call(
        prepare_kernel,
        out_shape=jax.ShapeDtypeStruct((rows, width + extra), jnp.bfloat16),
        compiler_params=pltpu.CompilerParams(vmem_limit_bytes=32 << 20),
        name="prepare",
    )(hidden, norm_gain.reshape(1, width), router, routes)


def expert_kernel(expert_ref, rows_ref, gate_ref, up_ref, down_ref, out_ref):
    width = gate_ref.shape[0]
    payload = rows_ref[...]
    rows = payload[:, :width]
    tail = payload[:, width:].astype(jnp.float32)
    lane = lax.broadcasted_iota(jnp.int32, tail.shape, 1)
    expert = expert_ref[0]
    experts = expert_ref[1]
    mine = (lane == expert) | (lane == expert + experts)
    weight = jnp.sum(jnp.where(mine, tail, 0.0), axis=1, keepdims=True)
    gate_act = jnp.dot(rows, gate_ref[...], preferred_element_type=jnp.float32)
    up_act = jnp.dot(rows, up_ref[...], preferred_element_type=jnp.float32)
    inner = (gate_act / (1.0 + jnp.exp(-gate_act)) * up_act).astype(jnp.bfloat16)
    result = jnp.dot(inner, down_ref[...], preferred_element_type=jnp.float32)
    out_ref[...] = (weight * result).astype(jnp.bfloat16)


def run_expert(expert, rows, gate_weights, up_weights, down_weights):
    total, padded = rows.shape
    width, hidden_units = gate_weights.shape
    tile = 256
    return pl.pallas_call(
        expert_kernel,
        grid_spec=pltpu.PrefetchScalarGridSpec(
            num_scalar_prefetch=1,
            grid=(total // tile,),
            in_specs=[
                pl.BlockSpec((tile, padded), lambda i, e: (i, 0)),
                pl.BlockSpec((width, hidden_units), lambda i, e: (0, 0), pipeline_mode=pl.Buffered(1)),
                pl.BlockSpec((width, hidden_units), lambda i, e: (0, 0), pipeline_mode=pl.Buffered(1)),
                pl.BlockSpec((hidden_units, width), lambda i, e: (0, 0), pipeline_mode=pl.Buffered(1)),
            ],
            out_specs=pl.BlockSpec((tile, width), lambda i, e: (i, 0)),
        ),
        out_shape=jax.ShapeDtypeStruct((total, width), jnp.bfloat16),
        compiler_params=pltpu.CompilerParams(vmem_limit_bytes=48 << 20),
        name="expert",
    )(expert, rows, gate_weights, up_weights, down_weights)


def chunk_cuts(tokens, devices):
    step = (tokens // 2 + 15) // 16 * 16 if devices <= 32 else 32
    return [(start, min(start + step, tokens)) for start in range(0, tokens, step)]


def body(
    queries,
    cache_keys,
    cache_values,
    lengths,
    sinks,
    out_proj,
    decode_resid,
    prefill_hidden,
    norm_gain,
    router,
    routes,
    expert_gate,
    expert_up,
    expert_down,
):
    experts = router.shape[1]
    ids = routes[0]
    tokens = ids.shape[0]
    prefill = prefill_hidden[0]
    devices = lax.axis_size(AXES)
    cuts = chunk_cuts(tokens, devices)
    my_expert = lax.axis_index("kv") * lax.axis_size("blk") + lax.axis_index("blk")
    expert = jnp.stack([my_expert, jnp.int32(experts)]).astype(jnp.int32)
    weights = (expert_gate[0], expert_up[0], expert_down[0])

    attended = attend(queries, cache_keys, cache_values, lengths, sinks)
    partial_proj = jnp.dot(attended, out_proj, preferred_element_type=jnp.float32)
    projected = lax.psum_scatter(partial_proj, "kv", scatter_dimension=0, tiled=True)
    decoded = (decode_resid.astype(jnp.float32) + projected).astype(jnp.bfloat16)
    hidden = jnp.concatenate([prefill, decoded], axis=0)
    ids = jnp.concatenate([ids[1:], ids[:1]], axis=0)
    gathered = []
    for start, stop in cuts:
        source = prefill[start:stop] if stop < tokens else hidden[start:stop]
        sent = prepare(source, norm_gain, router, ids[start:stop])
        gathered.append(lax.all_gather(sent, AXES, axis=0, tiled=True))
    returned = []
    for rows in gathered:
        sums = run_expert(expert, rows, *weights)
        returned.append(lax.psum_scatter(sums, AXES, scatter_dimension=0, tiled=True))
    combined = jnp.concatenate(returned, axis=0)
    layer_sum = (hidden.astype(jnp.float32) + combined.astype(jnp.float32)).astype(jnp.bfloat16)
    layer_sum = jnp.concatenate([layer_sum[-1:], layer_sum[:-1]], axis=0)
    return layer_sum[None]


def solution(mesh):
    return jax.shard_map(
        body,
        mesh=mesh,
        in_specs=(
            P("blk", "kv"),
            P("blk", None, "kv", None),
            P("blk", None, "kv", None),
            P(),
            P("kv"),
            P("kv", None),
            P(("blk", "kv"), None),
            P(("blk", "kv"), None, None),
            P(),
            P(),
            P(("blk", "kv"), None, None),
            P(("kv", "blk"), None, None),
            P(("kv", "blk"), None, None),
            P(("kv", "blk"), None, None),
        ),
        out_specs=P(("blk", "kv"), None, None),
        check_vma=False,
    )
```

```python
import math

import jax
import jax.numpy as jnp
from jax import lax
from jax.experimental import pallas as pl
from jax.experimental.pallas import tpu as pltpu
from jax.sharding import PartitionSpec as P

NEG_FILL = -1e30
EPSILON = 1e-06
AXES = ("blk", "kv")


def attend(queries, cache_keys, cache_values, lengths, sinks):
    my_block = lax.axis_index("blk")
    per_block = queries.shape[0]
    head_count = sinks.shape[0]
    head_dim = cache_keys.shape[3]
    window = cache_keys.shape[1]
    grouped_q = queries.reshape(per_block, head_count, head_dim)
    key_rows = cache_keys[:, :, 0, :]
    value_rows = cache_values[:, :, 0, :]
    my_lengths = lax.dynamic_slice_in_dim(lengths, my_block * per_block, per_block)
    scores = jnp.einsum("rgd,rjd->rgj", grouped_q, key_rows, preferred_element_type=jnp.float32) * (
        1.0 / math.sqrt(head_dim)
    )
    first_valid = window - jnp.minimum(my_lengths, window)
    is_valid = (jnp.arange(window, dtype=jnp.int32)[None, :] >= first_valid[:, None])[:, None, :]
    masked = jnp.where(is_valid, scores, NEG_FILL)
    top_limit = jnp.maximum(jnp.max(masked, axis=2), sinks[None, :])
    weights = jnp.where(is_valid, jnp.exp(masked - top_limit[..., None]), 0.0)
    denominator = jnp.sum(weights, axis=2) + jnp.exp(sinks[None, :] - top_limit)
    numerator = jnp.einsum(
        "rgj,rjd->rgd", weights.astype(jnp.bfloat16), value_rows, preferred_element_type=jnp.float32
    )
    return (
        (numerator / denominator[..., None])
        .astype(jnp.bfloat16)
        .reshape(per_block, head_count * head_dim)
    )


def prepare_kernel(hidden_ref, gain_ref, router_ref, routes_ref, out_ref):
    width = hidden_ref.shape[1]
    experts = router_ref.shape[1]
    hidden = hidden_ref[...].astype(jnp.float32)
    mean_sq = jnp.mean(hidden * hidden, axis=1, keepdims=True)
    normed = (hidden * lax.rsqrt(mean_sq + EPSILON) * gain_ref[...]).astype(jnp.bfloat16)
    out_ref[:, :width] = normed
    logits = jnp.dot(normed, router_ref[...], preferred_element_type=jnp.float32)
    lane = lax.broadcasted_iota(jnp.int32, logits.shape, 1)
    routes = routes_ref[...]
    chosen = jnp.zeros(logits.shape, jnp.bool_)
    for k in range(routes.shape[1]):
        chosen = chosen | (lane == routes[:, k : k + 1])
    top = jnp.max(jnp.where(chosen, logits, NEG_FILL), axis=1, keepdims=True)
    raised = jnp.where(chosen, jnp.exp(jnp.minimum(logits - top, 0.0)), 0.0)
    gates = raised / jnp.sum(raised, axis=1, keepdims=True)
    high = gates.astype(jnp.bfloat16).astype(jnp.float32)
    low = gates - high
    rest = out_ref.shape[1] - width - 2 * experts
    parts = [high, low]
    if rest:
        parts.append(jnp.zeros((high.shape[0], rest), jnp.float32))
    out_ref[:, width:] = jnp.concatenate(parts, axis=1).astype(jnp.bfloat16)


def prepare(hidden, norm_gain, router, routes):
    rows, width = hidden.shape
    extra = -(-2 * router.shape[1] // 128) * 128
    return pl.pallas_call(
        prepare_kernel,
        out_shape=jax.ShapeDtypeStruct((rows, width + extra), jnp.bfloat16),
        compiler_params=pltpu.CompilerParams(vmem_limit_bytes=32 << 20),
        name="prepare",
    )(hidden, norm_gain.reshape(1, width), router, routes)


def expert_kernel(expert_ref, rows_ref, gate_ref, up_ref, down_ref, out_ref):
    width = gate_ref.shape[0]
    payload = rows_ref[...]
    rows = payload[:, :width]
    tail = payload[:, width:].astype(jnp.float32)
    lane = lax.broadcasted_iota(jnp.int32, tail.shape, 1)
    expert = expert_ref[0]
    experts = expert_ref[1]
    mine = (lane == expert) | (lane == expert + experts)
    weight = jnp.sum(jnp.where(mine, tail, 0.0), axis=1, keepdims=True)
    gate_act = jnp.dot(rows, gate_ref[...], preferred_element_type=jnp.float32)
    up_act = jnp.dot(rows, up_ref[...], preferred_element_type=jnp.float32)
    inner = (gate_act / (1.0 + jnp.exp(-gate_act)) * up_act).astype(jnp.bfloat16)
    result = jnp.dot(inner, down_ref[...], preferred_element_type=jnp.float32)
    out_ref[...] = (weight * result).astype(jnp.bfloat16)


def run_expert(expert, rows, gate_weights, up_weights, down_weights):
    total, padded = rows.shape
    width, hidden_units = gate_weights.shape
    tile = 256
    return pl.pallas_call(
        expert_kernel,
        grid_spec=pltpu.PrefetchScalarGridSpec(
            num_scalar_prefetch=1,
            grid=(total // tile,),
            in_specs=[
                pl.BlockSpec((tile, padded), lambda i, e: (i, 0)),
                pl.BlockSpec((width, hidden_units), lambda i, e: (0, 0), pipeline_mode=pl.Buffered(1)),
                pl.BlockSpec((width, hidden_units), lambda i, e: (0, 0), pipeline_mode=pl.Buffered(1)),
                pl.BlockSpec((hidden_units, width), lambda i, e: (0, 0), pipeline_mode=pl.Buffered(1)),
            ],
            out_specs=pl.BlockSpec((tile, width), lambda i, e: (i, 0)),
        ),
        out_shape=jax.ShapeDtypeStruct((total, width), jnp.bfloat16),
        compiler_params=pltpu.CompilerParams(vmem_limit_bytes=48 << 20),
        name="expert",
    )(expert, rows, gate_weights, up_weights, down_weights)


def plane_kernel(
    ids_ref,
    own_ref,
    x_ref,
    y_ref,
    d0_ref,
    d1_ref,
    gate0_ref,
    up0_ref,
    down0_ref,
    gate1_ref,
    up1_ref,
    down1_ref,
    own_out,
    x_out,
    y_out,
    d0_out,
    d1_out,
    rows,
    gates,
    ups,
    downs,
    inner,
    sums,
    row_sem,
    weight_sem,
    out_sem,
):
    width = sums.shape[1]
    units = gates.shape[2]
    tile = 256
    out_tile = 512
    sources = (own_ref, x_ref, y_ref, d0_ref, d1_ref)
    targets = (own_out, x_out, y_out, d0_out, d1_out)
    starts = []
    at = 0
    for ref in sources:
        starts.append(at)
        at += ref.shape[0]
    row_copies = [
        pltpu.make_async_copy(ref, rows.at[pl.ds(start, ref.shape[0])], row_sem.at[i])
        for i, (ref, start) in enumerate(zip(sources, starts))
    ]
    weight_copies = []
    for e, (gate, up) in enumerate(((gate0_ref, up0_ref), (gate1_ref, up1_ref))):
        for j in range(units // tile):
            part = pl.ds(j * tile, tile)
            for source, target in ((gate, gates), (up, ups)):
                weight_copies.append(
                    pltpu.make_async_copy(
                        source.at[:, part], target.at[e, :, part], weight_sem.at[len(weight_copies)]
                    )
                )
    first_down = len(weight_copies)
    for j in range(width // out_tile):
        part = pl.ds(j * out_tile, out_tile)
        for e, down in enumerate((down0_ref, down1_ref)):
            weight_copies.append(
                pltpu.make_async_copy(
                    down.at[:, part], downs.at[e, :, part], weight_sem.at[len(weight_copies)]
                )
            )
    for copy in row_copies + weight_copies:
        copy.start()
    for copy in row_copies:
        copy.wait()
    tail = rows[:, width:].astype(jnp.float32)
    lane = lax.broadcasted_iota(jnp.int32, tail.shape, 1)
    experts = ids_ref[2]
    at = 0
    for e in range(2):
        mine = (lane == ids_ref[e]) | (lane == ids_ref[e] + experts)
        weight = jnp.sum(jnp.where(mine, tail, 0.0), axis=1, keepdims=True)
        for j in range(units // tile):
            weight_copies[at].wait()
            weight_copies[at + 1].wait()
            at += 2
            part = pl.ds(j * tile, tile)
            gate_act = jnp.dot(
                rows[:, :width], gates[e, :, part], preferred_element_type=jnp.float32
            )
            up_act = jnp.dot(rows[:, :width], ups[e, :, part], preferred_element_type=jnp.float32)
            act = gate_act / (1.0 + jnp.exp(-gate_act)) * up_act * weight
            inner[:, pl.ds(e * units + j * tile, tile)] = act.astype(jnp.bfloat16)
    out_copies = []
    for j in range(width // out_tile):
        weight_copies[first_down + 2 * j].wait()
        weight_copies[first_down + 2 * j + 1].wait()
        part = pl.ds(j * out_tile, out_tile)
        result = jnp.dot(inner[:, :units], downs[0, :, part], preferred_element_type=jnp.float32)
        result += jnp.dot(inner[:, units:], downs[1, :, part], preferred_element_type=jnp.float32)
        sums[:, part] = result.astype(jnp.bfloat16)
        for ref, start in zip(targets, starts):
            copy = pltpu.make_async_copy(
                sums.at[pl.ds(start, ref.shape[0]), part],
                ref.at[:, part],
                out_sem.at[len(out_copies)],
            )
            copy.start()
            out_copies.append(copy)
    for copy in out_copies:
        copy.wait()


def run_plane(ids, blocks, own_weights, other_weights):
    width, units = own_weights[0].shape
    padded = blocks[0].shape[1]
    total = sum(block.shape[0] for block in blocks)
    kept = jnp.bfloat16
    return pl.pallas_call(
        plane_kernel,
        in_specs=[pl.BlockSpec(memory_space=pltpu.SMEM)] + [pl.BlockSpec(memory_space=pl.ANY)] * 11,
        out_specs=[pl.BlockSpec(memory_space=pl.ANY)] * 5,
        out_shape=[jax.ShapeDtypeStruct((block.shape[0], width), kept) for block in blocks],
        scratch_shapes=[
            pltpu.VMEM((total, padded), kept),
            pltpu.VMEM((2, width, units), kept),
            pltpu.VMEM((2, width, units), kept),
            pltpu.VMEM((2, units, width), kept),
            pltpu.VMEM((total, 2 * units), kept),
            pltpu.VMEM((total, width), kept),
            pltpu.SemaphoreType.DMA((5,)),
            pltpu.SemaphoreType.DMA((4 * (units // 256) + 2 * (width // 512),)),
            pltpu.SemaphoreType.DMA((5 * (width // 512),)),
        ],
        compiler_params=pltpu.CompilerParams(vmem_limit_bytes=48 << 20),
        name="plane",
    )(ids, *blocks, *own_weights, *other_weights)


def along_x(value):
    return lax.ppermute(value, "kv", [(i, i ^ 1) for i in range(4)])


def along_y(value):
    return lax.ppermute(value, "kv", [(i, i ^ 2) for i in range(4)])


def along_diagonal(value):
    return lax.ppermute(value, "kv", [(i, i ^ 3) for i in range(4)])


def around_z(value):
    return lax.ppermute(value, "blk", [(i, (i + 2) % 8) for i in range(8)])


def across_chip(value):
    return lax.ppermute(value, "blk", [(i, i ^ 1) for i in range(8)])


def added(*parts):
    total = parts[0].astype(jnp.float32)
    for part in parts[1:]:
        total = total + part.astype(jnp.float32)
    return total


def permuted_plan(
    queries,
    cache_keys,
    cache_values,
    lengths,
    sinks,
    out_proj,
    decode_resid,
    prefill_hidden,
    norm_gain,
    router,
    routes,
    expert_gate,
    expert_up,
    expert_down,
):
    experts = router.shape[1]
    ids = routes[0]
    tokens = ids.shape[0]
    own_weights = (expert_gate[0], expert_up[0], expert_down[0])
    other_weights = tuple(across_chip(w) for w in own_weights)
    my_kv = lax.axis_index("kv")
    my_blk = lax.axis_index("blk")
    first_expert = my_kv * 8
    expert_ids = jnp.stack(
        [first_expert + my_blk, first_expert + (my_blk ^ 1), jnp.int32(experts)]
    ).astype(jnp.int32)

    attended = attend(queries, cache_keys, cache_values, lengths, sinks)
    partial_proj = jnp.dot(attended, out_proj, preferred_element_type=jnp.float32)

    def row_of(index):
        return lax.dynamic_slice_in_dim(partial_proj, index, 1)

    projected = (
        row_of(my_kv)
        + along_x(row_of(my_kv ^ 1))
        + along_y(row_of(my_kv ^ 2))
        + along_diagonal(row_of(my_kv ^ 3))
    )
    decoded = (decode_resid.astype(jnp.float32) + projected).astype(jnp.bfloat16)
    hidden = jnp.concatenate([decoded, prefill_hidden[0]], axis=0)
    block = prepare(hidden, norm_gain, router, ids)
    layer_sum = hidden.astype(jnp.float32)
    carried = None
    long = (tokens // 2 + 15) // 16 * 16
    for step in range(4):
        cut = long if step % 2 == 0 else tokens - long
        from_x = along_x(block)
        from_y = along_y(block)
        diagonal_0 = along_y(from_x[:cut])
        diagonal_1 = along_x(from_y[cut:])
        following = around_z(block) if step < 3 else None
        own, to_x, to_y, far_0, far_1 = run_plane(
            expert_ids, (block, from_x, from_y, diagonal_0, diagonal_1), own_weights, other_weights
        )
        passed_0 = along_y(far_0)
        passed_1 = along_x(far_1)
        to_x = jnp.concatenate([added(to_x[:cut], passed_0), to_x[cut:].astype(jnp.float32)], axis=0)
        to_y = jnp.concatenate([to_y[:cut].astype(jnp.float32), added(to_y[cut:], passed_1)], axis=0)
        back_x = along_x(to_x.astype(jnp.bfloat16))
        back_y = along_y(to_y.astype(jnp.bfloat16))
        if step == 0:
            layer_sum = added(layer_sum, own, back_x, back_y)
        else:
            parts = (own, back_x, back_y) + ((carried,) if step > 1 else ())
            carried = around_z(added(*parts).astype(jnp.bfloat16))
        block = following
    return added(layer_sum, carried).astype(jnp.bfloat16)[None]


def chunk_cuts(tokens, devices):
    step = (tokens // 2 + 15) // 16 * 16 if devices < 128 else 32
    return [(start, min(start + step, tokens)) for start in range(0, tokens, step)]


def gathered_plan(
    queries,
    cache_keys,
    cache_values,
    lengths,
    sinks,
    out_proj,
    decode_resid,
    prefill_hidden,
    norm_gain,
    router,
    routes,
    expert_gate,
    expert_up,
    expert_down,
):
    experts = router.shape[1]
    ids = routes[0]
    tokens = ids.shape[0]
    prefill = prefill_hidden[0]
    devices = lax.axis_size(AXES)
    cuts = chunk_cuts(tokens, devices)
    my_expert = lax.axis_index("kv") * lax.axis_size("blk") + lax.axis_index("blk")
    expert = jnp.stack([my_expert, jnp.int32(experts)]).astype(jnp.int32)
    weights = (expert_gate[0], expert_up[0], expert_down[0])

    attended = attend(queries, cache_keys, cache_values, lengths, sinks)
    partial_proj = jnp.dot(attended, out_proj, preferred_element_type=jnp.float32)
    projected = lax.psum_scatter(partial_proj, "kv", scatter_dimension=0, tiled=True)
    decoded = (decode_resid.astype(jnp.float32) + projected).astype(jnp.bfloat16)
    hidden = jnp.concatenate([prefill, decoded], axis=0)
    ids = jnp.concatenate([ids[1:], ids[:1]], axis=0)
    gathered = []
    for start, stop in cuts:
        source = prefill[start:stop] if stop < tokens else hidden[start:stop]
        sent = prepare(source, norm_gain, router, ids[start:stop])
        gathered.append(lax.all_gather(sent, AXES, axis=0, tiled=True))
    returned = []
    for rows in gathered:
        sums = run_expert(expert, rows, *weights)
        returned.append(lax.psum_scatter(sums, AXES, scatter_dimension=0, tiled=True))
    combined = jnp.concatenate(returned, axis=0)
    layer_sum = (hidden.astype(jnp.float32) + combined.astype(jnp.float32)).astype(jnp.bfloat16)
    layer_sum = jnp.concatenate([layer_sum[-1:], layer_sum[:-1]], axis=0)
    return layer_sum[None]


def solution(mesh):
    plan = permuted_plan if (mesh.shape["kv"], mesh.shape["blk"]) == (4, 8) else gathered_plan
    return jax.shard_map(
        plan,
        mesh=mesh,
        in_specs=(
            P("blk", "kv"),
            P("blk", None, "kv", None),
            P("blk", None, "kv", None),
            P(),
            P("kv"),
            P("kv", None),
            P(("blk", "kv"), None),
            P(("blk", "kv"), None, None),
            P(),
            P(),
            P(("blk", "kv"), None, None),
            P(("kv", "blk"), None, None),
            P(("kv", "blk"), None, None),
            P(("kv", "blk"), None, None),
        ),
        out_specs=P(("blk", "kv"), None, None),
        check_vma=False,
    )
```

```python
import functools
import math

import jax
import jax.numpy as jnp
from jax import lax
from jax.experimental import pallas as pl
from jax.experimental.pallas import tpu as pltpu
from jax.sharding import PartitionSpec as P

NEG_FILL = -1e30
EPSILON = 1e-06
AXES = ("blk", "kv")


def attend(queries, cache_keys, cache_values, lengths, sinks):
    my_block = lax.axis_index("blk")
    per_block = queries.shape[0]
    head_count = sinks.shape[0]
    head_dim = cache_keys.shape[3]
    window = cache_keys.shape[1]
    grouped_q = queries.reshape(per_block, head_count, head_dim)
    key_rows = cache_keys[:, :, 0, :]
    value_rows = cache_values[:, :, 0, :]
    my_lengths = lax.dynamic_slice_in_dim(lengths, my_block * per_block, per_block)
    scores = jnp.einsum("rgd,rjd->rgj", grouped_q, key_rows, preferred_element_type=jnp.float32) * (
        1.0 / math.sqrt(head_dim)
    )
    first_valid = window - jnp.minimum(my_lengths, window)
    is_valid = (jnp.arange(window, dtype=jnp.int32)[None, :] >= first_valid[:, None])[:, None, :]
    masked = jnp.where(is_valid, scores, NEG_FILL)
    top_limit = jnp.maximum(jnp.max(masked, axis=2), sinks[None, :])
    weights = jnp.where(is_valid, jnp.exp(masked - top_limit[..., None]), 0.0)
    denominator = jnp.sum(weights, axis=2) + jnp.exp(sinks[None, :] - top_limit)
    numerator = jnp.einsum(
        "rgj,rjd->rgd", weights.astype(jnp.bfloat16), value_rows, preferred_element_type=jnp.float32
    )
    return (
        (numerator / denominator[..., None])
        .astype(jnp.bfloat16)
        .reshape(per_block, head_count * head_dim)
    )


def prepare_kernel(hidden_ref, gain_ref, router_ref, routes_ref, out_ref):
    width = hidden_ref.shape[1]
    experts = router_ref.shape[1]
    hidden = hidden_ref[...].astype(jnp.float32)
    mean_sq = jnp.mean(hidden * hidden, axis=1, keepdims=True)
    normed = (hidden * lax.rsqrt(mean_sq + EPSILON) * gain_ref[...]).astype(jnp.bfloat16)
    out_ref[:, :width] = normed
    logits = jnp.dot(normed, router_ref[...], preferred_element_type=jnp.float32)
    lane = lax.broadcasted_iota(jnp.int32, logits.shape, 1)
    routes = routes_ref[...]
    chosen = jnp.zeros(logits.shape, jnp.bool_)
    for k in range(routes.shape[1]):
        chosen = chosen | (lane == routes[:, k : k + 1])
    top = jnp.max(jnp.where(chosen, logits, NEG_FILL), axis=1, keepdims=True)
    raised = jnp.where(chosen, jnp.exp(jnp.minimum(logits - top, 0.0)), 0.0)
    gates = raised / jnp.sum(raised, axis=1, keepdims=True)
    high = gates.astype(jnp.bfloat16).astype(jnp.float32)
    low = gates - high
    rest = out_ref.shape[1] - width - 2 * experts
    parts = [high, low]
    if rest:
        parts.append(jnp.zeros((high.shape[0], rest), jnp.float32))
    out_ref[:, width:] = jnp.concatenate(parts, axis=1).astype(jnp.bfloat16)


def prepare(hidden, norm_gain, router, routes):
    rows, width = hidden.shape
    extra = -(-2 * router.shape[1] // 128) * 128
    return pl.pallas_call(
        prepare_kernel,
        out_shape=jax.ShapeDtypeStruct((rows, width + extra), jnp.bfloat16),
        compiler_params=pltpu.CompilerParams(vmem_limit_bytes=32 << 20),
        name="prepare",
    )(hidden, norm_gain.reshape(1, width), router, routes)


def expert_kernel(expert_ref, rows_ref, gate_ref, up_ref, down_ref, out_ref):
    width = gate_ref.shape[0]
    payload = rows_ref[...]
    rows = payload[:, :width]
    tail = payload[:, width:].astype(jnp.float32)
    lane = lax.broadcasted_iota(jnp.int32, tail.shape, 1)
    expert = expert_ref[0]
    experts = expert_ref[1]
    mine = (lane == expert) | (lane == expert + experts)
    weight = jnp.sum(jnp.where(mine, tail, 0.0), axis=1, keepdims=True)
    gate_act = jnp.dot(rows, gate_ref[...], preferred_element_type=jnp.float32)
    up_act = jnp.dot(rows, up_ref[...], preferred_element_type=jnp.float32)
    inner = (gate_act / (1.0 + jnp.exp(-gate_act)) * up_act).astype(jnp.bfloat16)
    result = jnp.dot(inner, down_ref[...], preferred_element_type=jnp.float32)
    out_ref[...] = (weight * result).astype(jnp.bfloat16)


def run_expert(expert, rows, gate_weights, up_weights, down_weights):
    total, padded = rows.shape
    width, hidden_units = gate_weights.shape
    tile = 256
    return pl.pallas_call(
        expert_kernel,
        grid_spec=pltpu.PrefetchScalarGridSpec(
            num_scalar_prefetch=1,
            grid=(total // tile,),
            in_specs=[
                pl.BlockSpec((tile, padded), lambda i, e: (i, 0)),
                pl.BlockSpec((width, hidden_units), lambda i, e: (0, 0), pipeline_mode=pl.Buffered(1)),
                pl.BlockSpec((width, hidden_units), lambda i, e: (0, 0), pipeline_mode=pl.Buffered(1)),
                pl.BlockSpec((hidden_units, width), lambda i, e: (0, 0), pipeline_mode=pl.Buffered(1)),
            ],
            out_specs=pl.BlockSpec((tile, width), lambda i, e: (i, 0)),
        ),
        out_shape=jax.ShapeDtypeStruct((total, width), jnp.bfloat16),
        compiler_params=pltpu.CompilerParams(vmem_limit_bytes=48 << 20),
        name="expert",
    )(expert, rows, gate_weights, up_weights, down_weights)


def plane_kernel(piece_rows, block_rows, *refs):
    refs = list(refs)
    ids_ref = refs.pop(0)
    sources = [refs.pop(0) for _ in piece_rows]
    gate_ref, up_ref, down_ref = [refs.pop(0) for _ in range(3)]
    targets = [refs.pop(0) for _ in block_rows]
    rows, gates, ups, downs, inner, sums, row_sem, weight_sem, out_sem = refs
    width = sums.shape[1]
    units = gates.shape[2]
    tile = 256
    out_tile = 512
    row_copies = []
    at = 0
    for ref, count in zip(sources, piece_rows):
        copy = pltpu.make_async_copy(ref, rows.at[pl.ds(at, count)], row_sem.at[len(row_copies)])
        row_copies.append(copy)
        at += count
    weight_copies = []
    for e in range(2):
        for j in range(units // tile):
            part = pl.ds(j * tile, tile)
            for source, target in ((gate_ref, gates), (up_ref, ups)):
                weight_copies.append(
                    pltpu.make_async_copy(
                        source.at[e, :, part], target.at[e, :, part], weight_sem.at[len(weight_copies)]
                    )
                )
    first_down = len(weight_copies)
    for j in range(width // out_tile):
        part = pl.ds(j * out_tile, out_tile)
        for e in range(2):
            weight_copies.append(
                pltpu.make_async_copy(
                    down_ref.at[e, :, part],
                    downs.at[e, :, part],
                    weight_sem.at[len(weight_copies)],
                )
            )
    for copy in row_copies + weight_copies:
        copy.start()
    for copy in row_copies:
        copy.wait()
    tail = rows[:, width:].astype(jnp.float32)
    lane = lax.broadcasted_iota(jnp.int32, tail.shape, 1)
    experts = ids_ref[2]
    at = 0
    for e in range(2):
        mine = (lane == ids_ref[e]) | (lane == ids_ref[e] + experts)
        weight = jnp.sum(jnp.where(mine, tail, 0.0), axis=1, keepdims=True)
        for j in range(units // tile):
            weight_copies[at].wait()
            weight_copies[at + 1].wait()
            at += 2
            part = pl.ds(j * tile, tile)
            gate_act = jnp.dot(
                rows[:, :width], gates[e, :, part], preferred_element_type=jnp.float32
            )
            up_act = jnp.dot(rows[:, :width], ups[e, :, part], preferred_element_type=jnp.float32)
            act = gate_act / (1.0 + jnp.exp(-gate_act)) * up_act * weight
            inner[:, pl.ds(e * units + j * tile, tile)] = act.astype(jnp.bfloat16)
    out_copies = []
    for j in range(width // out_tile):
        weight_copies[first_down + 2 * j].wait()
        weight_copies[first_down + 2 * j + 1].wait()
        part = pl.ds(j * out_tile, out_tile)
        result = jnp.dot(inner[:, :units], downs[0, :, part], preferred_element_type=jnp.float32)
        result += jnp.dot(inner[:, units:], downs[1, :, part], preferred_element_type=jnp.float32)
        sums[:, part] = result.astype(jnp.bfloat16)
        at = 0
        for ref, count in zip(targets, block_rows):
            copy = pltpu.make_async_copy(
                sums.at[pl.ds(at, count), part], ref.at[:, part], out_sem.at[len(out_copies)]
            )
            copy.start()
            out_copies.append(copy)
            at += count
    for copy in out_copies:
        copy.wait()


def run_plane(ids, pieces, block_rows, weights):
    _, width, units = weights[0].shape
    padded = pieces[0].shape[1]
    piece_rows = tuple(piece.shape[0] for piece in pieces)
    total = sum(piece_rows)
    kept = jnp.bfloat16
    anywhere = pl.BlockSpec(memory_space=pl.ANY)
    return pl.pallas_call(
        functools.partial(plane_kernel, piece_rows, block_rows),
        in_specs=[pl.BlockSpec(memory_space=pltpu.SMEM)] + [anywhere] * (len(pieces) + 3),
        out_specs=[anywhere] * len(block_rows),
        out_shape=[jax.ShapeDtypeStruct((count, width), kept) for count in block_rows],
        scratch_shapes=[
            pltpu.VMEM((total, padded), kept),
            pltpu.VMEM((2, width, units), kept),
            pltpu.VMEM((2, width, units), kept),
            pltpu.VMEM((2, units, width), kept),
            pltpu.VMEM((total, 2 * units), kept),
            pltpu.VMEM((total, width), kept),
            pltpu.SemaphoreType.DMA((len(pieces),)),
            pltpu.SemaphoreType.DMA((4 * (units // 256) + 2 * (width // 512),)),
            pltpu.SemaphoreType.DMA((len(block_rows) * (width // 512),)),
        ],
        compiler_params=pltpu.CompilerParams(vmem_limit_bytes=48 << 20),
        cost_estimate=pl.CostEstimate(
            flops=12 * total * width * units, bytes_accessed=24 << 20, transcendentals=total * units
        ),
        name="plane",
    )(ids, *pieces, *weights)


def merge_kernel(cut, x_ref, y_ref, passed_0_ref, passed_1_ref, x_out, y_out):
    def sum_of(one, other):
        return (one.astype(jnp.float32) + other.astype(jnp.float32)).astype(jnp.bfloat16)

    x_out[:cut, :] = sum_of(x_ref[:cut, :], passed_0_ref[...])
    x_out[cut:, :] = x_ref[cut:, :]
    y_out[:cut, :] = y_ref[:cut, :]
    y_out[cut:, :] = sum_of(y_ref[cut:, :], passed_1_ref[...])


def merge_passed(cut, to_x, to_y, passed_0, passed_1):
    return pl.pallas_call(
        functools.partial(merge_kernel, cut),
        out_shape=[jax.ShapeDtypeStruct(to_x.shape, to_x.dtype)] * 2,
        compiler_params=pltpu.CompilerParams(vmem_limit_bytes=16 << 20),
        name="merge",
    )(to_x, to_y, passed_0, passed_1)


def along_x(value):
    return lax.ppermute(value, "kv", [(i, i ^ 1) for i in range(4)])


def along_y(value):
    return lax.ppermute(value, "kv", [(i, i ^ 2) for i in range(4)])


def around_z(value):
    return lax.ppermute(value, "blk", [(i, (i + 2) % 8) for i in range(8)])


def both_cores(value):
    pairs = [[i, i + 1] for i in range(0, 8, 2)]
    return lax.all_gather(value, "blk", axis_index_groups=pairs, axis=0, tiled=True)


def fence(*values):
    return lax.optimization_barrier(values)


def added(*parts):
    total = parts[0].astype(jnp.float32)
    for part in parts[1:]:
        total = total + part.astype(jnp.float32)
    return total


def permuted_plan(
    queries,
    cache_keys,
    cache_values,
    lengths,
    sinks,
    out_proj,
    decode_resid,
    prefill_hidden,
    norm_gain,
    router,
    routes,
    expert_gate,
    expert_up,
    expert_down,
):
    experts = router.shape[1]
    ids = routes[0]
    tokens = ids.shape[0]
    weights = tuple(both_cores(w) for w in (expert_gate, expert_up, expert_down))
    my_kv = lax.axis_index("kv")
    my_blk = lax.axis_index("blk")
    first_expert = my_kv * 8 + my_blk // 2 * 2
    expert_ids = jnp.stack([first_expert, first_expert + 1, jnp.int32(experts)]).astype(jnp.int32)

    late = 16
    prefill = prefill_hidden[0]
    body = prepare(prefill[late - 1 :], norm_gain, router, ids[late:])
    body, queries = fence(body, queries)
    body_sides = along_x(body), along_y(body)
    body_next = around_z(body)

    attended = attend(queries, cache_keys, cache_values, lengths, sinks)
    partial_proj = jnp.dot(attended, out_proj, preferred_element_type=jnp.float32)
    partial_proj = jnp.concatenate(
        [lax.dynamic_slice_in_dim(partial_proj, my_kv ^ other, 1) for other in (0, 2, 1, 3)], axis=0
    )
    pair = partial_proj[:2] + along_x(partial_proj[2:])
    projected = pair[:1] + along_y(pair[1:])
    decoded = (decode_resid.astype(jnp.float32) + projected).astype(jnp.bfloat16)
    decoded, body_sides, body_next = fence(decoded, body_sides, body_next)
    hidden = jnp.concatenate([decoded, prefill], axis=0)
    head = prepare(
        jnp.concatenate([decoded, prefill[: late - 1]], axis=0), norm_gain, router, ids[:late]
    )
    head_sides = along_x(head), along_y(head)
    head_next = around_z(head)
    head_sides, head_next = fence(head_sides, head_next)

    long = (tokens // 2 + 15) // 16 * 16
    cuts = [long, tokens - long, long, tokens - long]
    blocks = [None, jnp.concatenate([head_next, body_next], axis=0), None, None]
    sides = [None] * 4
    corners = [None] * 4
    sums = [None] * 4
    passed = [None] * 4
    back = [None] * 4

    def spread(step):
        sides[step] = along_x(blocks[step]), along_y(blocks[step])
        if step < 3:
            blocks[step + 1] = around_z(blocks[step])

    def spread_corners(step):
        cut = cuts[step]
        if step == 0:
            by_y = jnp.concatenate([head_sides[0], body_sides[0][: cut - late]], axis=0)
            by_x = body_sides[1][cut - late :]
        else:
            by_y, by_x = sides[step][0][:cut], sides[step][1][cut:]
        corners[step] = along_y(by_y), along_x(by_x)

    def apply(step):
        if step == 0:
            pieces = (head, body, head_sides[0], body_sides[0], head_sides[1], body_sides[1])
        else:
            pieces = (blocks[step],) + sides[step]
        counts = (tokens, tokens, tokens, cuts[step], tokens - cuts[step])
        sums[step] = run_plane(expert_ids, pieces + corners[step], counts, weights)

    def return_corners(step):
        passed[step] = along_y(sums[step][3]), along_x(sums[step][4])

    def return_sides(step):
        to_x, to_y = merge_passed(cuts[step], sums[step][1], sums[step][2], *passed[step])
        back[step] = along_x(to_x), along_y(to_y)

    spread_corners(0)
    spread(1)
    corners[0], sides[1], blocks[2] = fence(corners[0], sides[1], blocks[2])

    spread_corners(1)
    spread(2)
    apply(0)
    corners[1], sides[2], blocks[3], sums[0] = fence(corners[1], sides[2], blocks[3], sums[0])

    spread_corners(2)
    spread(3)
    far_0 = along_y(sums[0][3])
    apply(1)
    corners[2], sides[3], far_0, sums[0], sums[1] = fence(
        corners[2], sides[3], far_0, sums[0], sums[1]
    )

    spread_corners(3)
    passed[0] = far_0, along_x(sums[0][4])
    return_corners(1)
    apply(2)
    corners[3], passed[0], passed[1], sums[0], sums[1], sums[2] = fence(
        corners[3], passed[0], passed[1], sums[0], sums[1], sums[2]
    )

    return_sides(0)
    return_corners(2)
    apply(3)
    back[0], passed[2], sums[1], sums[2], sums[3] = fence(
        back[0], passed[2], sums[1], sums[2], sums[3]
    )

    return_corners(3)
    return_sides(1)
    layer_sum = added(hidden, sums[0][0], *back[0])
    passed[3], back[1], sums[2], sums[3] = fence(passed[3], back[1], sums[2], sums[3])

    return_sides(2)
    return_sides(3)
    carried = None
    for step in range(1, 4):
        parts = (sums[step][0],) + back[step] + ((carried,) if step > 1 else ())
        carried = around_z(added(*parts).astype(jnp.bfloat16))
    return added(layer_sum, carried).astype(jnp.bfloat16)[None]


def chunk_cuts(tokens, devices):
    step = (tokens // 2 + 15) // 16 * 16 if devices < 128 else 32
    return [(start, min(start + step, tokens)) for start in range(0, tokens, step)]


def gathered_plan(
    queries,
    cache_keys,
    cache_values,
    lengths,
    sinks,
    out_proj,
    decode_resid,
    prefill_hidden,
    norm_gain,
    router,
    routes,
    expert_gate,
    expert_up,
    expert_down,
):
    experts = router.shape[1]
    ids = routes[0]
    tokens = ids.shape[0]
    prefill = prefill_hidden[0]
    devices = lax.axis_size(AXES)
    cuts = chunk_cuts(tokens, devices)
    my_expert = lax.axis_index("kv") * lax.axis_size("blk") + lax.axis_index("blk")
    expert = jnp.stack([my_expert, jnp.int32(experts)]).astype(jnp.int32)
    weights = (expert_gate[0], expert_up[0], expert_down[0])

    attended = attend(queries, cache_keys, cache_values, lengths, sinks)
    partial_proj = jnp.dot(attended, out_proj, preferred_element_type=jnp.float32)
    projected = lax.psum_scatter(partial_proj, "kv", scatter_dimension=0, tiled=True)
    decoded = (decode_resid.astype(jnp.float32) + projected).astype(jnp.bfloat16)
    hidden = jnp.concatenate([prefill, decoded], axis=0)
    ids = jnp.concatenate([ids[1:], ids[:1]], axis=0)
    gathered = []
    for start, stop in cuts:
        source = prefill[start:stop] if stop < tokens else hidden[start:stop]
        sent = prepare(source, norm_gain, router, ids[start:stop])
        gathered.append(lax.all_gather(sent, AXES, axis=0, tiled=True))
    returned = []
    for rows in gathered:
        sums = run_expert(expert, rows, *weights)
        returned.append(lax.psum_scatter(sums, AXES, scatter_dimension=0, tiled=True))
    combined = jnp.concatenate(returned, axis=0)
    layer_sum = (hidden.astype(jnp.float32) + combined.astype(jnp.float32)).astype(jnp.bfloat16)
    layer_sum = jnp.concatenate([layer_sum[-1:], layer_sum[:-1]], axis=0)
    return layer_sum[None]


def solution(mesh):
    plan = permuted_plan if (mesh.shape["kv"], mesh.shape["blk"]) == (4, 8) else gathered_plan
    return jax.shard_map(
        plan,
        mesh=mesh,
        in_specs=(
            P("blk", "kv"),
            P("blk", None, "kv", None),
            P("blk", None, "kv", None),
            P(),
            P("kv"),
            P("kv", None),
            P(("blk", "kv"), None),
            P(("blk", "kv"), None, None),
            P(),
            P(),
            P(("blk", "kv"), None, None),
            P(("kv", "blk"), None, None),
            P(("kv", "blk"), None, None),
            P(("kv", "blk"), None, None),
        ),
        out_specs=P(("blk", "kv"), None, None),
        check_vma=False,
    )
```

```python
import functools
import math

import jax
import jax.numpy as jnp
from jax import lax
from jax.experimental import pallas as pl
from jax.experimental.pallas import tpu as pltpu
from jax.sharding import PartitionSpec as P

NEG_FILL = -1e30
EPSILON = 1e-06
NOT_CHOSEN = -256.0
AXES = ("blk", "kv")


def attend(queries, cache_keys, cache_values, lengths, sinks):
    my_block = lax.axis_index("blk")
    per_block = queries.shape[0]
    head_count = sinks.shape[0]
    head_dim = cache_keys.shape[3]
    window = cache_keys.shape[1]
    grouped_q = queries.reshape(per_block, head_count, head_dim)
    key_rows = cache_keys[:, :, 0, :]
    value_rows = cache_values[:, :, 0, :]
    my_lengths = lax.dynamic_slice_in_dim(lengths, my_block * per_block, per_block)
    scores = jnp.einsum("rgd,rjd->rgj", grouped_q, key_rows, preferred_element_type=jnp.float32) * (
        1.0 / math.sqrt(head_dim)
    )
    first_valid = window - jnp.minimum(my_lengths, window)
    is_valid = (jnp.arange(window, dtype=jnp.int32)[None, :] >= first_valid[:, None])[:, None, :]
    masked = jnp.where(is_valid, scores, NEG_FILL)
    top_limit = jnp.maximum(jnp.max(masked, axis=2), sinks[None, :])
    weights = jnp.where(is_valid, jnp.exp(masked - top_limit[..., None]), 0.0)
    denominator = jnp.sum(weights, axis=2) + jnp.exp(sinks[None, :] - top_limit)
    numerator = jnp.einsum(
        "rgj,rjd->rgd", weights.astype(jnp.bfloat16), value_rows, preferred_element_type=jnp.float32
    )
    return (
        (numerator / denominator[..., None])
        .astype(jnp.bfloat16)
        .reshape(per_block, head_count * head_dim)
    )


def prepare_kernel(ranking, hidden_ref, gain_ref, router_ref, routes_ref, out_ref):
    width = hidden_ref.shape[1]
    experts = router_ref.shape[1]
    hidden = hidden_ref[...].astype(jnp.float32)
    mean_sq = jnp.mean(hidden * hidden, axis=1, keepdims=True)
    normed = (hidden * lax.rsqrt(mean_sq + EPSILON) * gain_ref[...]).astype(jnp.bfloat16)
    out_ref[:, :width] = normed
    logits = jnp.dot(normed, router_ref[...], preferred_element_type=jnp.float32)
    lane = lax.broadcasted_iota(jnp.int32, logits.shape, 1)
    routes = routes_ref[...]
    chosen = jnp.zeros(logits.shape, jnp.bool_)
    for k in range(routes.shape[1]):
        chosen = chosen | (lane == routes[:, k : k + 1])
    top = jnp.max(jnp.where(chosen, logits, NEG_FILL), axis=1, keepdims=True)
    raised = jnp.where(chosen, jnp.exp(jnp.minimum(logits - top, 0.0)), 0.0)
    gates = raised / jnp.sum(raised, axis=1, keepdims=True)
    high = gates.astype(jnp.bfloat16).astype(jnp.float32)
    parts = [high, gates - high]
    if ranking == "block":
        rows = logits.shape[0]
        row = lax.broadcasted_iota(jnp.int32, (rows, rows), 0)
        earlier = lax.broadcasted_iota(jnp.int32, (rows, rows), 1) < row
        ranks = jnp.dot(
            jnp.where(earlier, 1.0, 0.0).astype(jnp.bfloat16),
            jnp.where(chosen, 1.0, 0.0).astype(jnp.bfloat16),
            preferred_element_type=jnp.float32,
        )
        parts.append(jnp.where(chosen, ranks, NOT_CHOSEN))
    elif ranking == "first":
        parts.append(jnp.where(chosen, 0.0, NOT_CHOSEN))
    rest = out_ref.shape[1] - width - len(parts) * experts
    if rest:
        parts.append(jnp.zeros((high.shape[0], rest), jnp.float32))
    out_ref[:, width:] = jnp.concatenate(parts, axis=1).astype(jnp.bfloat16)


def prepare(hidden, norm_gain, router, routes, ranking=None):
    rows, width = hidden.shape
    extra = -(-(3 if ranking else 2) * router.shape[1] // 128) * 128
    return pl.pallas_call(
        functools.partial(prepare_kernel, ranking),
        out_shape=jax.ShapeDtypeStruct((rows, width + extra), jnp.bfloat16),
        compiler_params=pltpu.CompilerParams(vmem_limit_bytes=32 << 20),
        name="prepare",
    )(hidden, norm_gain.reshape(1, width), router, routes)


def expert_kernel(expert_ref, rows_ref, gate_ref, up_ref, down_ref, out_ref):
    width = gate_ref.shape[0]
    payload = rows_ref[...]
    rows = payload[:, :width]
    tail = payload[:, width:].astype(jnp.float32)
    lane = lax.broadcasted_iota(jnp.int32, tail.shape, 1)
    expert = expert_ref[0]
    experts = expert_ref[1]
    mine = (lane == expert) | (lane == expert + experts)
    weight = jnp.sum(jnp.where(mine, tail, 0.0), axis=1, keepdims=True)
    gate_act = jnp.dot(rows, gate_ref[...], preferred_element_type=jnp.float32)
    up_act = jnp.dot(rows, up_ref[...], preferred_element_type=jnp.float32)
    inner = (gate_act / (1.0 + jnp.exp(-gate_act)) * up_act).astype(jnp.bfloat16)
    result = jnp.dot(inner, down_ref[...], preferred_element_type=jnp.float32)
    out_ref[...] = (weight * result).astype(jnp.bfloat16)


def run_expert(expert, rows, gate_weights, up_weights, down_weights):
    total, padded = rows.shape
    width, hidden_units = gate_weights.shape
    tile = 256
    return pl.pallas_call(
        expert_kernel,
        grid_spec=pltpu.PrefetchScalarGridSpec(
            num_scalar_prefetch=1,
            grid=(total // tile,),
            in_specs=[
                pl.BlockSpec((tile, padded), lambda i, e: (i, 0)),
                pl.BlockSpec((width, hidden_units), lambda i, e: (0, 0), pipeline_mode=pl.Buffered(1)),
                pl.BlockSpec((width, hidden_units), lambda i, e: (0, 0), pipeline_mode=pl.Buffered(1)),
                pl.BlockSpec((hidden_units, width), lambda i, e: (0, 0), pipeline_mode=pl.Buffered(1)),
            ],
            out_specs=pl.BlockSpec((tile, width), lambda i, e: (i, 0)),
        ),
        out_shape=jax.ShapeDtypeStruct((total, width), jnp.bfloat16),
        compiler_params=pltpu.CompilerParams(vmem_limit_bytes=48 << 20),
        name="expert",
    )(expert, rows, gate_weights, up_weights, down_weights)


def plane_kernel(cap, piece_rows, block_rows, *refs):
    refs = list(refs)
    ids_ref = refs.pop(0)
    decode_ref = refs.pop(0)
    sources = [refs.pop(0) for _ in piece_rows]
    weight_refs = [refs.pop(0) for _ in range(6)]
    targets = [refs.pop(0) for _ in block_rows]
    decodes, rows, weights, downs, slots, inner, results, spread, sums, row_sem, weight_sem, out_sem = refs
    width = sums.shape[1]
    tokens = block_rows[0]
    pair_rows = 2 * tokens
    pair_slots = 2 * cap
    row_copies = [pltpu.make_async_copy(decode_ref, decodes, row_sem.at[len(sources)])]
    at = 0
    for i, (ref, count) in enumerate(zip(sources, piece_rows)):
        copy = pltpu.make_async_copy(ref, rows.at[pl.ds(at, count)], row_sem.at[i])
        row_copies.append(copy)
        at += count
    up_copies = [
        pltpu.make_async_copy(weight_refs[3 * e + i], weights.at[2 * e + i], weight_sem.at[2 * e + i])
        for e in range(2)
        for i in range(2)
    ]
    down_copies = [
        pltpu.make_async_copy(weight_refs[3 * e + 2], downs.at[e], weight_sem.at[4 + e])
        for e in range(2)
    ]
    for copy in row_copies + up_copies + down_copies:
        copy.start()
    for copy in row_copies:
        copy.wait()
    few = decodes.shape[0]
    is_first = lax.broadcasted_iota(jnp.int32, (few, 1), 0) == 0
    for j in range(4):
        part = pl.ds(j * tokens, few)
        decode_row = decodes[...].astype(jnp.float32)[j : j + 1]
        kept = rows[part, :].astype(jnp.float32)
        rows[part, :] = jnp.where(is_first, decode_row, kept).astype(jnp.bfloat16)

    experts = ids_ref[2]
    extra = rows.shape[1] - width
    lanes = lax.broadcasted_iota(jnp.int32, (8, extra), 1)
    line = lax.broadcasted_iota(jnp.int32, (8, extra), 0)
    wanted = ((line == 0) & (lanes == ids_ref[0] + 2 * experts)) | (
        (line == 1) & (lanes == ids_ref[1] + 2 * experts)
    )
    wanted = jnp.where(wanted, 1.0, 0.0).astype(jnp.bfloat16)
    for p in range(2):
        part = pl.ds(p * pair_rows, pair_rows)
        tail = rows[part, width:]
        ranks = lax.dot_general(
            wanted, tail, (((1,), (1,)), ((), ())), preferred_element_type=jnp.float32
        )
        second = lax.broadcasted_iota(jnp.int32, (1, pair_rows), 1) >= tokens
        shift = jnp.where(second, float(cap), 0.0)
        slot = lax.broadcasted_iota(jnp.int32, (2 * pair_slots, pair_rows), 0).astype(jnp.float32)
        taken = (slot == ranks[0:1] + shift) | (slot == ranks[1:2] + shift + float(pair_slots))
        taken = jnp.where(taken, 1.0, 0.0).astype(jnp.bfloat16)
        picked = jnp.dot(taken, rows[part, :], preferred_element_type=jnp.float32)
        picked = picked.astype(jnp.bfloat16)
        for e in range(2):
            slots[e, pl.ds(p * pair_slots, pair_slots), :] = picked[e * pair_slots : (e + 1) * pair_slots]
        tail = tail.astype(jnp.float32)
        lane = lax.broadcasted_iota(jnp.int32, tail.shape, 1)
        second = lax.broadcasted_iota(jnp.int32, (pair_rows, 1), 0) >= tokens
        shift = jnp.where(second, float(cap), 0.0)
        slot = lax.broadcasted_iota(jnp.int32, (pair_rows, 2 * pair_slots), 1).astype(jnp.float32)
        back = jnp.zeros(slot.shape, jnp.bool_)
        for e in range(2):
            mine = lane == ids_ref[e] + 2 * experts
            rank = jnp.sum(jnp.where(mine, tail, 0.0), axis=1, keepdims=True)
            back = back | (slot == rank + shift + float(e * pair_slots))
        spread[p] = jnp.where(back, 1.0, 0.0).astype(jnp.bfloat16)

    for e in range(2):
        tail = slots[e, :, width:].astype(jnp.float32)
        lane = lax.broadcasted_iota(jnp.int32, tail.shape, 1)
        mine = (lane == ids_ref[e]) | (lane == ids_ref[e] + experts)
        weight = jnp.sum(jnp.where(mine, tail, 0.0), axis=1, keepdims=True)
        up_copies[2 * e].wait()
        gate_act = jnp.dot(
            slots[e, :, :width], weights[2 * e], preferred_element_type=jnp.float32
        )
        up_copies[2 * e + 1].wait()
        up_act = jnp.dot(
            slots[e, :, :width], weights[2 * e + 1], preferred_element_type=jnp.float32
        )
        act = gate_act / (1.0 + jnp.exp(-gate_act)) * up_act * weight
        inner[e] = act.astype(jnp.bfloat16)
    for e in range(2):
        down_copies[e].wait()
        result = jnp.dot(inner[e], downs[e], preferred_element_type=jnp.float32)
        result = result.astype(jnp.bfloat16)
        for p in range(2):
            results[p, pl.ds(e * pair_slots, pair_slots), :] = result[p * pair_slots : (p + 1) * pair_slots]
    out_copies = []
    at = 0
    for p in range(2):
        part = pl.ds(p * pair_rows, pair_rows)
        total = jnp.dot(spread[p], results[p], preferred_element_type=jnp.float32)
        sums[part, :] = total.astype(jnp.bfloat16)
        while len(out_copies) < len(targets) and at < (p + 1) * pair_rows:
            count = block_rows[len(out_copies)]
            copy = pltpu.make_async_copy(
                sums.at[pl.ds(at, count)], targets[len(out_copies)], out_sem.at[len(out_copies)]
            )
            copy.start()
            out_copies.append(copy)
            at += count
    for copy in out_copies:
        copy.wait()


def run_plane(ids, cap, decodes, pieces, block_rows, weights):
    width, units = weights[0].shape
    padded = pieces[0].shape[1]
    piece_rows = tuple(piece.shape[0] for piece in pieces)
    total = sum(piece_rows)
    kept = jnp.bfloat16
    anywhere = pl.BlockSpec(memory_space=pl.ANY)
    return pl.pallas_call(
        functools.partial(plane_kernel, cap, piece_rows, block_rows),
        in_specs=[pl.BlockSpec(memory_space=pltpu.SMEM)] + [anywhere] * (len(pieces) + 7),
        out_specs=[anywhere] * len(block_rows),
        out_shape=[jax.ShapeDtypeStruct((count, width), kept) for count in block_rows],
        scratch_shapes=[
            pltpu.VMEM(decodes.shape, kept),
            pltpu.VMEM((total, padded), kept),
            pltpu.VMEM((4, width, units), kept),
            pltpu.VMEM((2, units, width), kept),
            pltpu.VMEM((2, 4 * cap, padded), kept),
            pltpu.VMEM((2, 4 * cap, units), kept),
            pltpu.VMEM((2, 4 * cap, width), kept),
            pltpu.VMEM((2, total // 2, 4 * cap), kept),
            pltpu.VMEM((total, width), kept),
            pltpu.SemaphoreType.DMA((len(pieces) + 1,)),
            pltpu.SemaphoreType.DMA((6,)),
            pltpu.SemaphoreType.DMA((len(block_rows),)),
        ],
        compiler_params=pltpu.CompilerParams(vmem_limit_bytes=48 << 20),
        cost_estimate=pl.CostEstimate(
            flops=12 * total * width * units, bytes_accessed=24 << 20, transcendentals=total * units
        ),
        name="plane",
    )(ids, decodes, *pieces, *weights)


def merge_kernel(cut, x_ref, y_ref, passed_0_ref, passed_1_ref, x_out, y_out):
    def sum_of(one, other):
        return (one.astype(jnp.float32) + other.astype(jnp.float32)).astype(jnp.bfloat16)

    x_out[:cut, :] = sum_of(x_ref[:cut, :], passed_0_ref[...])
    x_out[cut:, :] = x_ref[cut:, :]
    y_out[:cut, :] = y_ref[:cut, :]
    y_out[cut:, :] = sum_of(y_ref[cut:, :], passed_1_ref[...])


def merge_passed(cut, to_x, to_y, passed_0, passed_1):
    return pl.pallas_call(
        functools.partial(merge_kernel, cut),
        out_shape=[jax.ShapeDtypeStruct(to_x.shape, to_x.dtype)] * 2,
        compiler_params=pltpu.CompilerParams(vmem_limit_bytes=16 << 20),
        name="merge",
    )(to_x, to_y, passed_0, passed_1)


def along_x(value):
    return lax.ppermute(value, "kv", [(i, i ^ 1) for i in range(4)])


def along_y(value):
    return lax.ppermute(value, "kv", [(i, i ^ 2) for i in range(4)])


def around_z(value):
    return lax.ppermute(value, "blk", [(i, (i + 2) % 8) for i in range(8)])


def across_chip(value):
    return lax.ppermute(value, "blk", [(i, i ^ 1) for i in range(8)])


def fence(*values):
    return lax.optimization_barrier(values)


def added(*parts):
    total = parts[0].astype(jnp.float32)
    for part in parts[1:]:
        total = total + part.astype(jnp.float32)
    return total


def permuted_plan(
    queries,
    cache_keys,
    cache_values,
    lengths,
    sinks,
    out_proj,
    decode_resid,
    prefill_hidden,
    norm_gain,
    router,
    routes,
    expert_gate,
    expert_up,
    expert_down,
):
    experts = router.shape[1]
    ids = routes[0]
    tokens = ids.shape[0]
    my_kv = lax.axis_index("kv")
    my_blk = lax.axis_index("blk")
    first_expert = my_kv * 8
    expert_ids = jnp.stack(
        [first_expert + my_blk, first_expert + (my_blk ^ 1), jnp.int32(experts)]
    ).astype(jnp.int32)
    cap = (2 * tokens * ids.shape[1] + experts - 1) // experts
    long = (tokens // 2 + 15) // 16 * 16
    cuts = [long, tokens - long, long, tokens - long]
    blocks = [None] * 4
    sides = [None] * 4
    corners = [None] * 4
    decodes = [None] * 4
    sums = [None] * 4
    passed = [None] * 4
    back = [None] * 4

    def spread_sides(step):
        sides[step] = along_x(blocks[step]), along_y(blocks[step])

    def spread_corners(step):
        cut = cuts[step]
        corners[step] = along_y(sides[step][0][:cut]), along_x(sides[step][1][cut:])

    def apply(step):
        counts = (tokens, tokens, tokens, cuts[step], tokens - cuts[step])
        pieces = (blocks[step],) + sides[step] + corners[step]
        sums[step] = run_plane(expert_ids, cap, decodes[step], pieces, counts, weights)

    def return_corners(step):
        passed[step] = along_y(sums[step][3]), along_x(sums[step][4])

    def return_sides(step):
        to_x, to_y = merge_passed(cuts[step], sums[step][1], sums[step][2], *passed[step])
        back[step] = along_x(to_x), along_y(to_y)

    prefill = prefill_hidden[0]
    nothing = jnp.zeros((1, prefill.shape[1]), prefill.dtype)
    blocks[0] = prepare(
        jnp.concatenate([nothing, prefill], axis=0), norm_gain, router, ids, "block"
    )
    blocks[0], queries, cache_keys, expert_gate, expert_up = fence(
        blocks[0], queries, cache_keys, expert_gate, expert_up
    )
    spread_sides(0)
    blocks[1] = around_z(blocks[0])
    other_gate = across_chip(expert_gate[0])
    other_up = across_chip(expert_up[0])

    attended = attend(queries, cache_keys, cache_values, lengths, sinks)
    partial_proj = jnp.dot(attended, out_proj, preferred_element_type=jnp.float32)
    is_mine = jnp.arange(4)[:, None] == my_kv
    partial_proj += jnp.where(is_mine, decode_resid.astype(jnp.float32), 0.0)
    width = partial_proj.shape[1]
    ids_row = jnp.pad(ids[:1].astype(jnp.float32), ((0, 0), (0, width - ids.shape[1])))
    shared = jnp.concatenate([partial_proj, jnp.where(is_mine, ids_row, 0.0)], axis=0)

    shared, other_gate = fence(shared, other_gate)
    shared = shared + along_x(shared)
    sides[0], blocks[1], shared, expert_down = fence(sides[0], blocks[1], shared, expert_down)

    spread_sides(1)
    blocks[2] = around_z(blocks[1])
    other_down = across_chip(expert_down[0])
    sides[1], sides[0], blocks[2], shared = fence(sides[1], sides[0], blocks[2], shared)

    spread_corners(0)
    shared = shared + along_y(shared)
    order = [my_kv ^ j for j in range(4)]
    decoded = jnp.concatenate(
        [lax.dynamic_slice_in_dim(shared, index, 1) for index in order], axis=0
    ).astype(jnp.bfloat16)
    decode_ids = jnp.concatenate(
        [lax.dynamic_slice_in_dim(shared, 4 + index, 1) for index in order], axis=0
    )[:, : ids.shape[1]].astype(jnp.int32)
    hidden = jnp.concatenate([decoded[:1], prefill], axis=0)
    decodes[0] = prepare(
        jnp.pad(decoded, ((0, 12), (0, 0))),
        norm_gain,
        router,
        jnp.pad(decode_ids, ((0, 12), (0, 0))),
        "first",
    )
    corners[0], sides[1], blocks[2], decodes[0], other_up, other_down = fence(
        corners[0], sides[1], blocks[2], decodes[0], other_up, other_down
    )
    weights = (expert_gate[0], expert_up[0], expert_down[0], other_gate, other_up, other_down)

    spread_corners(1)
    spread_sides(2)
    arrived = around_z(jnp.concatenate([blocks[2], decodes[0]], axis=0))
    apply(0)
    corners[1], sides[2], arrived, sums[0] = fence(corners[1], sides[2], arrived, sums[0])
    blocks[3], decodes[1] = arrived[:tokens], arrived[tokens:]

    spread_corners(2)
    spread_sides(3)
    decodes[2] = around_z(decodes[1])
    apply(1)
    corners[2], sides[3], decodes[2], sums[1] = fence(corners[2], sides[3], decodes[2], sums[1])

    spread_corners(3)
    decodes[3] = around_z(decodes[2])
    return_corners(1)
    apply(2)
    corners[3], decodes[3], passed[1], sums[1], sums[2] = fence(
        corners[3], decodes[3], passed[1], sums[1], sums[2]
    )

    return_sides(1)
    return_corners(2)
    apply(3)
    back[1], passed[2], sums[1], sums[2], sums[3] = fence(
        back[1], passed[2], sums[1], sums[2], sums[3]
    )

    return_sides(2)
    return_corners(3)
    carried = around_z(added(sums[1][0], *back[1]).astype(jnp.bfloat16))
    back[2], passed[3], carried, sums[2], sums[3], sums[0] = fence(
        back[2], passed[3], carried, sums[2], sums[3], sums[0]
    )

    return_sides(3)
    return_corners(0)
    carried = around_z(added(sums[2][0], *back[2], carried).astype(jnp.bfloat16))
    back[3], passed[0], carried, sums[3], sums[0] = fence(
        back[3], passed[0], carried, sums[3], sums[0]
    )

    return_sides(0)
    carried = around_z(added(sums[3][0], *back[3], carried).astype(jnp.bfloat16))
    return added(hidden, sums[0][0], *back[0], carried).astype(jnp.bfloat16)[None]


def chunk_cuts(tokens, devices):
    step = (tokens // 2 + 15) // 16 * 16 if devices < 128 else 32
    return [(start, min(start + step, tokens)) for start in range(0, tokens, step)]


def gathered_plan(
    queries,
    cache_keys,
    cache_values,
    lengths,
    sinks,
    out_proj,
    decode_resid,
    prefill_hidden,
    norm_gain,
    router,
    routes,
    expert_gate,
    expert_up,
    expert_down,
):
    experts = router.shape[1]
    ids = routes[0]
    tokens = ids.shape[0]
    prefill = prefill_hidden[0]
    devices = lax.axis_size(AXES)
    cuts = chunk_cuts(tokens, devices)
    my_expert = lax.axis_index("kv") * lax.axis_size("blk") + lax.axis_index("blk")
    expert = jnp.stack([my_expert, jnp.int32(experts)]).astype(jnp.int32)
    weights = (expert_gate[0], expert_up[0], expert_down[0])

    attended = attend(queries, cache_keys, cache_values, lengths, sinks)
    partial_proj = jnp.dot(attended, out_proj, preferred_element_type=jnp.float32)
    projected = lax.psum_scatter(partial_proj, "kv", scatter_dimension=0, tiled=True)
    decoded = (decode_resid.astype(jnp.float32) + projected).astype(jnp.bfloat16)
    hidden = jnp.concatenate([prefill, decoded], axis=0)
    ids = jnp.concatenate([ids[1:], ids[:1]], axis=0)
    gathered = []
    for start, stop in cuts:
        source = prefill[start:stop] if stop < tokens else hidden[start:stop]
        sent = prepare(source, norm_gain, router, ids[start:stop])
        gathered.append(lax.all_gather(sent, AXES, axis=0, tiled=True))
    returned = []
    for rows in gathered:
        sums = run_expert(expert, rows, *weights)
        returned.append(lax.psum_scatter(sums, AXES, scatter_dimension=0, tiled=True))
    combined = jnp.concatenate(returned, axis=0)
    layer_sum = (hidden.astype(jnp.float32) + combined.astype(jnp.float32)).astype(jnp.bfloat16)
    layer_sum = jnp.concatenate([layer_sum[-1:], layer_sum[:-1]], axis=0)
    return layer_sum[None]


def solution(mesh):
    plan = permuted_plan if (mesh.shape["kv"], mesh.shape["blk"]) == (4, 8) else gathered_plan
    return jax.shard_map(
        plan,
        mesh=mesh,
        in_specs=(
            P("blk", "kv"),
            P("blk", None, "kv", None),
            P("blk", None, "kv", None),
            P(),
            P("kv"),
            P("kv", None),
            P(("blk", "kv"), None),
            P(("blk", "kv"), None, None),
            P(),
            P(),
            P(("blk", "kv"), None, None),
            P(("kv", "blk"), None, None),
            P(("kv", "blk"), None, None),
            P(("kv", "blk"), None, None),
        ),
        out_specs=P(("blk", "kv"), None, None),
        check_vma=False,
    )
```

```python
import functools
import math

import jax
import jax.numpy as jnp
from jax import lax
from jax.experimental import pallas as pl
from jax.experimental.pallas import tpu as pltpu
from jax.sharding import PartitionSpec as P

NEG_FILL = -1e30
EPSILON = 1e-06
NOT_CHOSEN = -256.0
AXES = ("blk", "kv")


def attend(queries, cache_keys, cache_values, lengths, sinks):
    my_block = lax.axis_index("blk")
    per_block = queries.shape[0]
    head_count = sinks.shape[0]
    head_dim = cache_keys.shape[3]
    window = cache_keys.shape[1]
    grouped_q = queries.reshape(per_block, head_count, head_dim)
    key_rows = cache_keys[:, :, 0, :]
    value_rows = cache_values[:, :, 0, :]
    my_lengths = lax.dynamic_slice_in_dim(lengths, my_block * per_block, per_block)
    scores = jnp.einsum("rgd,rjd->rgj", grouped_q, key_rows, preferred_element_type=jnp.float32) * (
        1.0 / math.sqrt(head_dim)
    )
    first_valid = window - jnp.minimum(my_lengths, window)
    is_valid = (jnp.arange(window, dtype=jnp.int32)[None, :] >= first_valid[:, None])[:, None, :]
    masked = jnp.where(is_valid, scores, NEG_FILL)
    top_limit = jnp.maximum(jnp.max(masked, axis=2), sinks[None, :])
    weights = jnp.where(is_valid, jnp.exp(masked - top_limit[..., None]), 0.0)
    denominator = jnp.sum(weights, axis=2) + jnp.exp(sinks[None, :] - top_limit)
    numerator = jnp.einsum(
        "rgj,rjd->rgd", weights.astype(jnp.bfloat16), value_rows, preferred_element_type=jnp.float32
    )
    return (
        (numerator / denominator[..., None])
        .astype(jnp.bfloat16)
        .reshape(per_block, head_count * head_dim)
    )


def prepare_kernel(ranking, hidden_ref, gain_ref, router_ref, routes_ref, out_ref, *scratch):
    experts, width = router_ref.shape
    if scratch:
        (shifted,) = scratch
        shifted[0:1, :] = jnp.zeros((1, width), jnp.float32)
        shifted[1:, :] = hidden_ref[...].astype(jnp.float32)
        hidden = shifted[...]
    else:
        hidden = hidden_ref[...].astype(jnp.float32)
    rows = hidden.shape[0]
    mean_sq = jnp.mean(hidden * hidden, axis=1, keepdims=True)
    normed = (hidden * lax.rsqrt(mean_sq + EPSILON) * gain_ref[...]).astype(jnp.bfloat16)
    out_ref[:, :width] = normed
    by_lanes = (((1,), (1,)), ((), ()))
    logits = lax.dot_general(normed, router_ref[...], by_lanes, preferred_element_type=jnp.float32)
    expert = lax.broadcasted_iota(jnp.int32, (experts, rows), 0)
    routes = routes_ref[...]
    chosen = jnp.zeros(expert.shape, jnp.bool_)
    for k in range(routes.shape[0]):
        chosen = chosen | (expert == routes[k : k + 1, :])
    chosen = jnp.where(chosen, 1.0, 0.0).astype(jnp.bfloat16)
    row = lax.broadcasted_iota(jnp.int32, (rows, rows), 0)
    other = lax.broadcasted_iota(jnp.int32, (rows, rows), 1)

    def of_rows(taken):
        taken = jnp.where(taken, 1.0, 0.0).astype(jnp.bfloat16)
        return lax.dot_general(taken, chosen, by_lanes, preferred_element_type=jnp.float32)

    mine = of_rows(row == other) > 0.5
    top = jnp.max(jnp.where(mine, logits, NEG_FILL), axis=1, keepdims=True)
    raised = jnp.where(mine, jnp.exp(jnp.minimum(logits - top, 0.0)), 0.0)
    gates = raised / jnp.sum(raised, axis=1, keepdims=True)
    high = gates.astype(jnp.bfloat16).astype(jnp.float32)
    parts = [high, gates - high]
    if ranking == "block":
        parts.append(jnp.where(mine, of_rows(other < row), NOT_CHOSEN))
    elif ranking == "first":
        parts.append(jnp.where(mine, 0.0, NOT_CHOSEN))
    rest = out_ref.shape[1] - width - len(parts) * experts
    if rest:
        parts.append(jnp.zeros((rows, rest), jnp.float32))
    out_ref[:, width:] = jnp.concatenate(parts, axis=1).astype(jnp.bfloat16)


def prepare(hidden, norm_gain, router, routes, ranking=None):
    width = hidden.shape[1]
    rows = routes.shape[0]
    extra = -(-(3 if ranking else 2) * router.shape[1] // 128) * 128
    shifted = rows > hidden.shape[0]
    return pl.pallas_call(
        functools.partial(prepare_kernel, ranking),
        out_shape=jax.ShapeDtypeStruct((rows, width + extra), jnp.bfloat16),
        scratch_shapes=[pltpu.VMEM((rows, width), jnp.float32)] if shifted else [],
        compiler_params=pltpu.CompilerParams(vmem_limit_bytes=32 << 20),
        name="prepare",
    )(hidden, norm_gain.reshape(1, width), router.T, routes.T)


def expert_kernel(expert_ref, rows_ref, gate_ref, up_ref, down_ref, out_ref):
    width = gate_ref.shape[0]
    payload = rows_ref[...]
    rows = payload[:, :width]
    tail = payload[:, width:].astype(jnp.float32)
    lane = lax.broadcasted_iota(jnp.int32, tail.shape, 1)
    expert = expert_ref[0]
    experts = expert_ref[1]
    mine = (lane == expert) | (lane == expert + experts)
    weight = jnp.sum(jnp.where(mine, tail, 0.0), axis=1, keepdims=True)
    gate_act = jnp.dot(rows, gate_ref[...], preferred_element_type=jnp.float32)
    up_act = jnp.dot(rows, up_ref[...], preferred_element_type=jnp.float32)
    inner = (gate_act / (1.0 + jnp.exp(-gate_act)) * up_act).astype(jnp.bfloat16)
    result = jnp.dot(inner, down_ref[...], preferred_element_type=jnp.float32)
    out_ref[...] = (weight * result).astype(jnp.bfloat16)


def run_expert(expert, rows, gate_weights, up_weights, down_weights):
    total, padded = rows.shape
    width, hidden_units = gate_weights.shape
    tile = 256
    return pl.pallas_call(
        expert_kernel,
        grid_spec=pltpu.PrefetchScalarGridSpec(
            num_scalar_prefetch=1,
            grid=(total // tile,),
            in_specs=[
                pl.BlockSpec((tile, padded), lambda i, e: (i, 0)),
                pl.BlockSpec((width, hidden_units), lambda i, e: (0, 0), pipeline_mode=pl.Buffered(1)),
                pl.BlockSpec((width, hidden_units), lambda i, e: (0, 0), pipeline_mode=pl.Buffered(1)),
                pl.BlockSpec((hidden_units, width), lambda i, e: (0, 0), pipeline_mode=pl.Buffered(1)),
            ],
            out_specs=pl.BlockSpec((tile, width), lambda i, e: (i, 0)),
        ),
        out_shape=jax.ShapeDtypeStruct((total, width), jnp.bfloat16),
        compiler_params=pltpu.CompilerParams(vmem_limit_bytes=48 << 20),
        name="expert",
    )(expert, rows, gate_weights, up_weights, down_weights)


def plane_kernel(cap, piece_rows, block_rows, *refs):
    refs = list(refs)
    ids_ref = refs.pop(0)
    decode_ref = refs.pop(0)
    sources = [refs.pop(0) for _ in piece_rows]
    weight_refs = [refs.pop(0) for _ in range(6)]
    targets = [refs.pop(0) for _ in block_rows]
    decodes, rows, weights, downs, slots, inner, results, spread, sums, row_sem, weight_sem, out_sem = refs
    width = sums.shape[1]
    tokens = block_rows[0]
    pair_rows = 2 * tokens
    pair_slots = 2 * cap
    row_copies = [pltpu.make_async_copy(decode_ref, decodes, row_sem.at[len(sources)])]
    at = 0
    for i, (ref, count) in enumerate(zip(sources, piece_rows)):
        copy = pltpu.make_async_copy(ref, rows.at[pl.ds(at, count)], row_sem.at[i])
        row_copies.append(copy)
        at += count
    up_copies = [
        pltpu.make_async_copy(weight_refs[3 * e + i], weights.at[2 * e + i], weight_sem.at[2 * e + i])
        for e in range(2)
        for i in range(2)
    ]
    down_copies = [
        pltpu.make_async_copy(weight_refs[3 * e + 2], downs.at[e], weight_sem.at[4 + e])
        for e in range(2)
    ]
    for copy in row_copies + up_copies + down_copies:
        copy.start()
    for copy in row_copies:
        copy.wait()
    few = decodes.shape[0]
    is_first = lax.broadcasted_iota(jnp.int32, (few, 1), 0) == 0
    for j in range(4):
        part = pl.ds(j * tokens, few)
        decode_row = decodes[...].astype(jnp.float32)[j : j + 1]
        kept = rows[part, :].astype(jnp.float32)
        rows[part, :] = jnp.where(is_first, decode_row, kept).astype(jnp.bfloat16)

    experts = ids_ref[2]
    extra = rows.shape[1] - width
    lanes = lax.broadcasted_iota(jnp.int32, (8, extra), 1)
    line = lax.broadcasted_iota(jnp.int32, (8, extra), 0)
    wanted = ((line == 0) & (lanes == ids_ref[0] + 2 * experts)) | (
        (line == 1) & (lanes == ids_ref[1] + 2 * experts)
    )
    wanted = jnp.where(wanted, 1.0, 0.0).astype(jnp.bfloat16)
    pairs = [pl.ds(p * pair_rows, pair_rows) for p in range(2)]

    def shift_of(shape, axis):
        second = lax.broadcasted_iota(jnp.int32, shape, axis) >= tokens
        return jnp.where(second, float(cap), 0.0)

    for p in range(2):
        ranks = lax.dot_general(
            wanted, rows[pairs[p], width:], (((1,), (1,)), ((), ())), preferred_element_type=jnp.float32
        )
        ranks += shift_of(ranks.shape, 1)
        slot = lax.broadcasted_iota(jnp.int32, (2 * pair_slots, pair_rows), 0).astype(jnp.float32)
        taken = (slot == ranks[0:1]) | (slot == ranks[1:2] + float(pair_slots))
        taken = jnp.where(taken, 1.0, 0.0).astype(jnp.bfloat16)
        picked = jnp.dot(taken, rows[pairs[p], :], preferred_element_type=jnp.float32)
        picked = picked.astype(jnp.bfloat16)
        for e in range(2):
            slots[e, pl.ds(p * pair_slots, pair_slots), :] = picked[e * pair_slots : (e + 1) * pair_slots]

    def make_spread(p):
        tail = rows[pairs[p], width:].astype(jnp.float32)
        lane = lax.broadcasted_iota(jnp.int32, tail.shape, 1)
        slot = lax.broadcasted_iota(jnp.int32, (pair_rows, 2 * pair_slots), 1).astype(jnp.float32)
        back = jnp.zeros(slot.shape, jnp.bool_)
        for e in range(2):
            mine = lane == ids_ref[e] + 2 * experts
            rank = jnp.sum(jnp.where(mine, tail, 0.0), axis=1, keepdims=True)
            back = back | (slot == rank + shift_of(rank.shape, 0) + float(e * pair_slots))
        spread[p] = jnp.where(back, 1.0, 0.0).astype(jnp.bfloat16)

    def weight_of(e):
        tail = slots[e, :, width:].astype(jnp.float32)
        lane = lax.broadcasted_iota(jnp.int32, tail.shape, 1)
        mine = (lane == ids_ref[e]) | (lane == ids_ref[e] + experts)
        return jnp.sum(jnp.where(mine, tail, 0.0), axis=1, keepdims=True)

    def product(e, i):
        return jnp.dot(slots[e, :, :width], weights[2 * e + i], preferred_element_type=jnp.float32)

    def activate(e, gate_act, up_act):
        act = gate_act / (1.0 + jnp.exp(-gate_act)) * up_act * weight_of(e)
        inner[e] = act.astype(jnp.bfloat16)

    def finish(e):
        result = jnp.dot(inner[e], downs[e], preferred_element_type=jnp.float32)
        result = result.astype(jnp.bfloat16)
        for p in range(2):
            results[p, pl.ds(e * pair_slots, pair_slots), :] = result[p * pair_slots : (p + 1) * pair_slots]

    up_copies[0].wait()
    gate_0 = product(0, 0)
    make_spread(0)
    up_copies[1].wait()
    up_0 = product(0, 1)
    make_spread(1)
    up_copies[2].wait()
    activate(0, gate_0, up_0)
    gate_1 = product(1, 0)
    up_copies[3].wait()
    up_1 = product(1, 1)
    down_copies[0].wait()
    finish(0)
    activate(1, gate_1, up_1)
    down_copies[1].wait()
    finish(1)
    out_copies = []
    at = 0
    for p in range(2):
        total = jnp.dot(spread[p], results[p], preferred_element_type=jnp.float32)
        sums[pairs[p], :] = total.astype(jnp.bfloat16)
        while len(out_copies) < len(targets) and at < (p + 1) * pair_rows:
            count = block_rows[len(out_copies)]
            copy = pltpu.make_async_copy(
                sums.at[pl.ds(at, count)], targets[len(out_copies)], out_sem.at[len(out_copies)]
            )
            copy.start()
            out_copies.append(copy)
            at += count
    for copy in out_copies:
        copy.wait()


def run_plane(ids, cap, decodes, pieces, block_rows, weights):
    width, units = weights[0].shape
    padded = pieces[0].shape[1]
    piece_rows = tuple(piece.shape[0] for piece in pieces)
    total = sum(piece_rows)
    kept = jnp.bfloat16
    anywhere = pl.BlockSpec(memory_space=pl.ANY)
    return pl.pallas_call(
        functools.partial(plane_kernel, cap, piece_rows, block_rows),
        in_specs=[pl.BlockSpec(memory_space=pltpu.SMEM)] + [anywhere] * (len(pieces) + 7),
        out_specs=[anywhere] * len(block_rows),
        out_shape=[jax.ShapeDtypeStruct((count, width), kept) for count in block_rows],
        scratch_shapes=[
            pltpu.VMEM(decodes.shape, kept),
            pltpu.VMEM((total, padded), kept),
            pltpu.VMEM((4, width, units), kept),
            pltpu.VMEM((2, units, width), kept),
            pltpu.VMEM((2, 4 * cap, padded), kept),
            pltpu.VMEM((2, 4 * cap, units), kept),
            pltpu.VMEM((2, 4 * cap, width), kept),
            pltpu.VMEM((2, total // 2, 4 * cap), kept),
            pltpu.VMEM((total, width), kept),
            pltpu.SemaphoreType.DMA((len(pieces) + 1,)),
            pltpu.SemaphoreType.DMA((6,)),
            pltpu.SemaphoreType.DMA((len(block_rows),)),
        ],
        compiler_params=pltpu.CompilerParams(vmem_limit_bytes=48 << 20),
        cost_estimate=pl.CostEstimate(
            flops=12 * total * width * units, bytes_accessed=24 << 20, transcendentals=total * units
        ),
        name="plane",
    )(ids, decodes, *pieces, *weights)


def merge_kernel(cut, x_ref, y_ref, passed_0_ref, passed_1_ref, x_out, y_out):
    def sum_of(one, other):
        return (one.astype(jnp.float32) + other.astype(jnp.float32)).astype(jnp.bfloat16)

    x_out[:cut, :] = sum_of(x_ref[:cut, :], passed_0_ref[...])
    x_out[cut:, :] = x_ref[cut:, :]
    y_out[:cut, :] = y_ref[:cut, :]
    y_out[cut:, :] = sum_of(y_ref[cut:, :], passed_1_ref[...])


def merge_passed(cut, to_x, to_y, passed_0, passed_1):
    return pl.pallas_call(
        functools.partial(merge_kernel, cut),
        out_shape=[jax.ShapeDtypeStruct(to_x.shape, to_x.dtype)] * 2,
        compiler_params=pltpu.CompilerParams(vmem_limit_bytes=16 << 20),
        name="merge",
    )(to_x, to_y, passed_0, passed_1)


def along_x(value):
    return lax.ppermute(value, "kv", [(i, i ^ 1) for i in range(4)])


def along_y(value):
    return lax.ppermute(value, "kv", [(i, i ^ 2) for i in range(4)])


def along_diagonal(value):
    return lax.ppermute(value, "kv", [(i, i ^ 3) for i in range(4)])


def around_z(value):
    return lax.ppermute(value, "blk", [(i, (i + 2) % 8) for i in range(8)])


def across_chip(value):
    return lax.ppermute(value, "blk", [(i, i ^ 1) for i in range(8)])


def fence(*values):
    return lax.optimization_barrier(values)


def added(*parts):
    total = parts[0].astype(jnp.float32)
    for part in parts[1:]:
        total = total + part.astype(jnp.float32)
    return total


def permuted_plan(
    queries,
    cache_keys,
    cache_values,
    lengths,
    sinks,
    out_proj,
    decode_resid,
    prefill_hidden,
    norm_gain,
    router,
    routes,
    expert_gate,
    expert_up,
    expert_down,
):
    experts = router.shape[1]
    ids = routes[0]
    tokens = ids.shape[0]
    my_kv = lax.axis_index("kv")
    my_blk = lax.axis_index("blk")
    first_expert = my_kv * 8
    expert_ids = jnp.stack(
        [first_expert + my_blk, first_expert + (my_blk ^ 1), jnp.int32(experts)]
    ).astype(jnp.int32)
    cap = (2 * tokens * ids.shape[1] + experts - 1) // experts
    long = (tokens // 2 + 15) // 16 * 16
    cuts = [long, tokens - long, long, tokens - long]
    blocks = [None] * 4
    sides = [None] * 4
    corners = [None] * 4
    decodes = [None] * 4
    sums = [None] * 4
    passed = [None] * 4
    back = [None] * 4

    def spread_sides(step):
        sides[step] = along_x(blocks[step]), along_y(blocks[step])

    def spread_corners(step):
        cut = cuts[step]
        corners[step] = along_y(sides[step][0][:cut]), along_x(sides[step][1][cut:])

    def apply(step):
        counts = (tokens, tokens, tokens, cuts[step], tokens - cuts[step])
        pieces = (blocks[step],) + sides[step] + corners[step]
        sums[step] = run_plane(expert_ids, cap, decodes[step], pieces, counts, weights)

    def return_corners(step):
        passed[step] = along_y(sums[step][3]), along_x(sums[step][4])

    def return_sides(step):
        to_x, to_y = merge_passed(cuts[step], sums[step][1], sums[step][2], *passed[step])
        back[step] = along_x(to_x), along_y(to_y)

    prefill = prefill_hidden[0]
    blocks[0] = prepare(prefill, norm_gain, router, ids, "block")
    blocks[0], queries, cache_keys, expert_gate, expert_up = fence(
        blocks[0], queries, cache_keys, expert_gate, expert_up
    )
    spread_sides(0)
    corners[0] = (along_diagonal(blocks[0]),)
    blocks[1] = around_z(blocks[0])
    other_gate = across_chip(expert_gate[0])
    other_up = across_chip(expert_up[0])

    attended = attend(queries, cache_keys, cache_values, lengths, sinks)
    partial_proj = jnp.dot(attended, out_proj, preferred_element_type=jnp.float32)
    is_mine = jnp.arange(4)[:, None] == my_kv
    partial_proj += jnp.where(is_mine, decode_resid.astype(jnp.float32), 0.0)
    width = partial_proj.shape[1]
    ids_row = jnp.pad(ids[:1].astype(jnp.float32), ((0, 0), (0, width - ids.shape[1])))
    shared = jnp.concatenate([partial_proj, jnp.where(is_mine, ids_row, 0.0)], axis=0)

    shared, other_gate = fence(shared, other_gate)
    shared = shared + along_x(shared)
    sides[0], corners[0], blocks[1], shared, expert_down = fence(
        sides[0], corners[0], blocks[1], shared, expert_down
    )

    spread_sides(1)
    blocks[2] = around_z(blocks[1])
    other_down = across_chip(expert_down[0])
    shared = shared + along_y(shared)
    order = [my_kv ^ j for j in range(4)]
    decoded = jnp.concatenate(
        [lax.dynamic_slice_in_dim(shared, index, 1) for index in order], axis=0
    ).astype(jnp.bfloat16)
    decode_ids = jnp.concatenate(
        [lax.dynamic_slice_in_dim(shared, 4 + index, 1) for index in order], axis=0
    )[:, : ids.shape[1]].astype(jnp.int32)
    hidden = jnp.concatenate([decoded[:1], prefill], axis=0)
    decodes[0] = prepare(
        jnp.pad(decoded, ((0, 12), (0, 0))),
        norm_gain,
        router,
        jnp.pad(decode_ids, ((0, 12), (0, 0))),
        "first",
    )
    sides[1], blocks[2], decodes[0], other_up = fence(sides[1], blocks[2], decodes[0], other_up)
    weights = (expert_gate[0], expert_up[0], expert_down[0], other_gate, other_up, other_down)

    spread_corners(1)
    spread_sides(2)
    arrived = around_z(jnp.concatenate([blocks[2], decodes[0]], axis=0))
    apply(0)
    corners[1], sides[2], arrived, sums[0] = fence(corners[1], sides[2], arrived, sums[0])
    blocks[3], decodes[1] = arrived[:tokens], arrived[tokens:]

    spread_corners(2)
    spread_sides(3)
    decodes[2] = around_z(decodes[1])
    apply(1)
    corners[2], sides[3], decodes[2], sums[1] = fence(corners[2], sides[3], decodes[2], sums[1])

    spread_corners(3)
    decodes[3] = around_z(decodes[2])
    return_corners(1)
    apply(2)
    corners[3], decodes[3], passed[1], sums[1], sums[2] = fence(
        corners[3], decodes[3], passed[1], sums[1], sums[2]
    )

    return_sides(1)
    return_corners(2)
    apply(3)
    back[1], passed[2], sums[1], sums[2], sums[3] = fence(
        back[1], passed[2], sums[1], sums[2], sums[3]
    )

    return_sides(2)
    return_corners(3)
    carried = around_z(added(sums[1][0], *back[1]).astype(jnp.bfloat16))
    back[2], passed[3], carried, sums[2], sums[3], sums[0] = fence(
        back[2], passed[3], carried, sums[2], sums[3], sums[0]
    )

    return_sides(3)
    return_corners(0)
    carried = around_z(added(sums[2][0], *back[2], carried).astype(jnp.bfloat16))
    back[3], passed[0], carried, sums[3], sums[0] = fence(
        back[3], passed[0], carried, sums[3], sums[0]
    )

    return_sides(0)
    carried = around_z(added(sums[3][0], *back[3], carried).astype(jnp.bfloat16))
    return added(hidden, sums[0][0], *back[0], carried).astype(jnp.bfloat16)[None]


def chunk_cuts(tokens, devices):
    step = (tokens // 2 + 15) // 16 * 16 if devices < 128 else 32
    return [(start, min(start + step, tokens)) for start in range(0, tokens, step)]


def gathered_plan(
    queries,
    cache_keys,
    cache_values,
    lengths,
    sinks,
    out_proj,
    decode_resid,
    prefill_hidden,
    norm_gain,
    router,
    routes,
    expert_gate,
    expert_up,
    expert_down,
):
    experts = router.shape[1]
    ids = routes[0]
    tokens = ids.shape[0]
    prefill = prefill_hidden[0]
    devices = lax.axis_size(AXES)
    cuts = chunk_cuts(tokens, devices)
    my_expert = lax.axis_index("kv") * lax.axis_size("blk") + lax.axis_index("blk")
    expert = jnp.stack([my_expert, jnp.int32(experts)]).astype(jnp.int32)
    weights = (expert_gate[0], expert_up[0], expert_down[0])

    attended = attend(queries, cache_keys, cache_values, lengths, sinks)
    partial_proj = jnp.dot(attended, out_proj, preferred_element_type=jnp.float32)
    projected = lax.psum_scatter(partial_proj, "kv", scatter_dimension=0, tiled=True)
    decoded = (decode_resid.astype(jnp.float32) + projected).astype(jnp.bfloat16)
    hidden = jnp.concatenate([prefill, decoded], axis=0)
    ids = jnp.concatenate([ids[1:], ids[:1]], axis=0)
    gathered = []
    for start, stop in cuts:
        source = prefill[start:stop] if stop < tokens else hidden[start:stop]
        sent = prepare(source, norm_gain, router, ids[start:stop])
        gathered.append(lax.all_gather(sent, AXES, axis=0, tiled=True))
    returned = []
    for rows in gathered:
        sums = run_expert(expert, rows, *weights)
        returned.append(lax.psum_scatter(sums, AXES, scatter_dimension=0, tiled=True))
    combined = jnp.concatenate(returned, axis=0)
    layer_sum = (hidden.astype(jnp.float32) + combined.astype(jnp.float32)).astype(jnp.bfloat16)
    layer_sum = jnp.concatenate([layer_sum[-1:], layer_sum[:-1]], axis=0)
    return layer_sum[None]


def solution(mesh):
    plan = permuted_plan if (mesh.shape["kv"], mesh.shape["blk"]) == (4, 8) else gathered_plan
    return jax.shard_map(
        plan,
        mesh=mesh,
        in_specs=(
            P("blk", "kv"),
            P("blk", None, "kv", None),
            P("blk", None, "kv", None),
            P(),
            P("kv"),
            P("kv", None),
            P(("blk", "kv"), None),
            P(("blk", "kv"), None, None),
            P(),
            P(),
            P(("blk", "kv"), None, None),
            P(("kv", "blk"), None, None),
            P(("kv", "blk"), None, None),
            P(("kv", "blk"), None, None),
        ),
        out_specs=P(("blk", "kv"), None, None),
        check_vma=False,
    )
```

```python
import functools
import math

import jax
import jax.numpy as jnp
from jax import lax
from jax.experimental import pallas as pl
from jax.experimental.pallas import tpu as pltpu
from jax.sharding import PartitionSpec as P

NEG_FILL = -1e30
EPSILON = 1e-06
NOT_CHOSEN = -256.0
AXES = ("blk", "kv")


def attend(queries, cache_keys, cache_values, lengths, sinks):
    my_block = lax.axis_index("blk")
    per_block = queries.shape[0]
    head_count = sinks.shape[0]
    head_dim = cache_keys.shape[3]
    window = cache_keys.shape[1]
    grouped_q = queries.reshape(per_block, head_count, head_dim)
    key_rows = cache_keys[:, :, 0, :]
    value_rows = cache_values[:, :, 0, :]
    my_lengths = lax.dynamic_slice_in_dim(lengths, my_block * per_block, per_block)
    scores = jnp.einsum("rgd,rjd->rgj", grouped_q, key_rows, preferred_element_type=jnp.float32) * (
        1.0 / math.sqrt(head_dim)
    )
    first_valid = window - jnp.minimum(my_lengths, window)
    is_valid = (jnp.arange(window, dtype=jnp.int32)[None, :] >= first_valid[:, None])[:, None, :]
    masked = jnp.where(is_valid, scores, NEG_FILL)
    top_limit = jnp.maximum(jnp.max(masked, axis=2), sinks[None, :])
    weights = jnp.where(is_valid, jnp.exp(masked - top_limit[..., None]), 0.0)
    denominator = jnp.sum(weights, axis=2) + jnp.exp(sinks[None, :] - top_limit)
    numerator = jnp.einsum(
        "rgj,rjd->rgd", weights.astype(jnp.bfloat16), value_rows, preferred_element_type=jnp.float32
    )
    return (
        (numerator / denominator[..., None])
        .astype(jnp.bfloat16)
        .reshape(per_block, head_count * head_dim)
    )


def prepare_kernel(ranking, hidden_ref, gain_ref, router_ref, routes_ref, out_ref, *scratch):
    experts, width = router_ref.shape
    if scratch:
        (shifted,) = scratch
        shifted[0:1, :] = jnp.zeros((1, width), jnp.float32)
        shifted[1:, :] = hidden_ref[...].astype(jnp.float32)
        hidden = shifted[...]
    else:
        hidden = hidden_ref[...].astype(jnp.float32)
    rows = hidden.shape[0]
    mean_sq = jnp.mean(hidden * hidden, axis=1, keepdims=True)
    normed = (hidden * lax.rsqrt(mean_sq + EPSILON) * gain_ref[...]).astype(jnp.bfloat16)
    out_ref[:, :width] = normed
    by_lanes = (((1,), (1,)), ((), ()))
    logits = lax.dot_general(normed, router_ref[...], by_lanes, preferred_element_type=jnp.float32)
    expert = lax.broadcasted_iota(jnp.int32, (experts, rows), 0)
    routes = routes_ref[...]
    chosen = jnp.zeros(expert.shape, jnp.bool_)
    for k in range(routes.shape[0]):
        chosen = chosen | (expert == routes[k : k + 1, :])
    chosen = jnp.where(chosen, 1.0, 0.0).astype(jnp.bfloat16)
    row = lax.broadcasted_iota(jnp.int32, (rows, rows), 0)
    other = lax.broadcasted_iota(jnp.int32, (rows, rows), 1)

    def of_rows(taken):
        taken = jnp.where(taken, 1.0, 0.0).astype(jnp.bfloat16)
        return lax.dot_general(taken, chosen, by_lanes, preferred_element_type=jnp.float32)

    mine = of_rows(row == other) > 0.5
    top = jnp.max(jnp.where(mine, logits, NEG_FILL), axis=1, keepdims=True)
    raised = jnp.where(mine, jnp.exp(jnp.minimum(logits - top, 0.0)), 0.0)
    gates = raised / jnp.sum(raised, axis=1, keepdims=True)
    high = gates.astype(jnp.bfloat16).astype(jnp.float32)
    parts = [high, gates - high]
    if ranking == "block":
        parts.append(jnp.where(mine, of_rows(other < row), NOT_CHOSEN))
    elif ranking == "first":
        parts.append(jnp.where(mine, 0.0, NOT_CHOSEN))
    rest = out_ref.shape[1] - width - len(parts) * experts
    if rest:
        parts.append(jnp.zeros((rows, rest), jnp.float32))
    out_ref[:, width:] = jnp.concatenate(parts, axis=1).astype(jnp.bfloat16)


def prepare(hidden, norm_gain, router, routes, ranking=None):
    width = hidden.shape[1]
    rows = routes.shape[0]
    extra = -(-(3 if ranking else 2) * router.shape[1] // 128) * 128
    shifted = rows > hidden.shape[0]
    return pl.pallas_call(
        functools.partial(prepare_kernel, ranking),
        out_shape=jax.ShapeDtypeStruct((rows, width + extra), jnp.bfloat16),
        scratch_shapes=[pltpu.VMEM((rows, width), jnp.float32)] if shifted else [],
        compiler_params=pltpu.CompilerParams(vmem_limit_bytes=32 << 20),
        name="prepare",
    )(hidden, norm_gain.reshape(1, width), router.T, routes.T)


def expert_kernel(expert_ref, rows_ref, gate_ref, up_ref, down_ref, out_ref):
    width = gate_ref.shape[0]
    payload = rows_ref[...]
    rows = payload[:, :width]
    tail = payload[:, width:].astype(jnp.float32)
    lane = lax.broadcasted_iota(jnp.int32, tail.shape, 1)
    expert = expert_ref[0]
    experts = expert_ref[1]
    mine = (lane == expert) | (lane == expert + experts)
    weight = jnp.sum(jnp.where(mine, tail, 0.0), axis=1, keepdims=True)
    gate_act = jnp.dot(rows, gate_ref[...], preferred_element_type=jnp.float32)
    up_act = jnp.dot(rows, up_ref[...], preferred_element_type=jnp.float32)
    inner = (gate_act / (1.0 + jnp.exp(-gate_act)) * up_act).astype(jnp.bfloat16)
    result = jnp.dot(inner, down_ref[...], preferred_element_type=jnp.float32)
    out_ref[...] = (weight * result).astype(jnp.bfloat16)


def run_expert(expert, rows, gate_weights, up_weights, down_weights):
    total, padded = rows.shape
    width, hidden_units = gate_weights.shape
    tile = 256
    return pl.pallas_call(
        expert_kernel,
        grid_spec=pltpu.PrefetchScalarGridSpec(
            num_scalar_prefetch=1,
            grid=(total // tile,),
            in_specs=[
                pl.BlockSpec((tile, padded), lambda i, e: (i, 0)),
                pl.BlockSpec((width, hidden_units), lambda i, e: (0, 0), pipeline_mode=pl.Buffered(1)),
                pl.BlockSpec((width, hidden_units), lambda i, e: (0, 0), pipeline_mode=pl.Buffered(1)),
                pl.BlockSpec((hidden_units, width), lambda i, e: (0, 0), pipeline_mode=pl.Buffered(1)),
            ],
            out_specs=pl.BlockSpec((tile, width), lambda i, e: (i, 0)),
        ),
        out_shape=jax.ShapeDtypeStruct((total, width), jnp.bfloat16),
        compiler_params=pltpu.CompilerParams(vmem_limit_bytes=48 << 20),
        name="expert",
    )(expert, rows, gate_weights, up_weights, down_weights)


def plane_kernel(cap, piece_rows, block_rows, *refs):
    refs = list(refs)
    ids_ref = refs.pop(0)
    decode_ref = refs.pop(0)
    sources = [refs.pop(0) for _ in piece_rows]
    weight_refs = [refs.pop(0) for _ in range(6)]
    targets = [refs.pop(0) for _ in block_rows]
    decodes, rows, slots, inner, results, spread, sums, row_sem, out_sem = refs
    width = sums.shape[1]
    tokens = block_rows[0]
    pair_rows = 2 * tokens
    pair_slots = 2 * cap
    row_copies = [pltpu.make_async_copy(decode_ref, decodes, row_sem.at[len(sources)])]
    at = 0
    for i, (ref, count) in enumerate(zip(sources, piece_rows)):
        copy = pltpu.make_async_copy(ref, rows.at[pl.ds(at, count)], row_sem.at[i])
        row_copies.append(copy)
        at += count
    for copy in row_copies:
        copy.start()
    for copy in row_copies:
        copy.wait()
    few = decodes.shape[0]
    is_first = lax.broadcasted_iota(jnp.int32, (few, 1), 0) == 0
    for j in range(4):
        part = pl.ds(j * tokens, few)
        decode_row = decodes[...].astype(jnp.float32)[j : j + 1]
        kept = rows[part, :].astype(jnp.float32)
        rows[part, :] = jnp.where(is_first, decode_row, kept).astype(jnp.bfloat16)

    experts = ids_ref[2]
    extra = rows.shape[1] - width
    lanes = lax.broadcasted_iota(jnp.int32, (8, extra), 1)
    line = lax.broadcasted_iota(jnp.int32, (8, extra), 0)
    wanted = ((line == 0) & (lanes == ids_ref[0] + 2 * experts)) | (
        (line == 1) & (lanes == ids_ref[1] + 2 * experts)
    )
    wanted = jnp.where(wanted, 1.0, 0.0).astype(jnp.bfloat16)
    pairs = [pl.ds(p * pair_rows, pair_rows) for p in range(2)]

    def shift_of(shape, axis):
        second = lax.broadcasted_iota(jnp.int32, shape, axis) >= tokens
        return jnp.where(second, float(cap), 0.0)

    for p in range(2):
        ranks = lax.dot_general(
            wanted, rows[pairs[p], width:], (((1,), (1,)), ((), ())), preferred_element_type=jnp.float32
        )
        ranks += shift_of(ranks.shape, 1)
        slot = lax.broadcasted_iota(jnp.int32, (2 * pair_slots, pair_rows), 0).astype(jnp.float32)
        taken = (slot == ranks[0:1]) | (slot == ranks[1:2] + float(pair_slots))
        taken = jnp.where(taken, 1.0, 0.0).astype(jnp.bfloat16)
        picked = jnp.dot(taken, rows[pairs[p], :], preferred_element_type=jnp.float32)
        picked = picked.astype(jnp.bfloat16)
        for e in range(2):
            slots[e, pl.ds(p * pair_slots, pair_slots), :] = picked[e * pair_slots : (e + 1) * pair_slots]

    def make_spread(p):
        tail = rows[pairs[p], width:].astype(jnp.float32)
        lane = lax.broadcasted_iota(jnp.int32, tail.shape, 1)
        slot = lax.broadcasted_iota(jnp.int32, (pair_rows, 2 * pair_slots), 1).astype(jnp.float32)
        back = jnp.zeros(slot.shape, jnp.bool_)
        for e in range(2):
            mine = lane == ids_ref[e] + 2 * experts
            rank = jnp.sum(jnp.where(mine, tail, 0.0), axis=1, keepdims=True)
            back = back | (slot == rank + shift_of(rank.shape, 0) + float(e * pair_slots))
        spread[p] = jnp.where(back, 1.0, 0.0).astype(jnp.bfloat16)

    def weight_of(e):
        tail = slots[e, :, width:].astype(jnp.float32)
        lane = lax.broadcasted_iota(jnp.int32, tail.shape, 1)
        mine = (lane == ids_ref[e]) | (lane == ids_ref[e] + experts)
        return jnp.sum(jnp.where(mine, tail, 0.0), axis=1, keepdims=True)

    def product(e, i):
        return jnp.dot(slots[e, :, :width], weight_refs[3 * e + i][...], preferred_element_type=jnp.float32)

    def activate(e, gate_act, up_act):
        act = gate_act / (1.0 + jnp.exp(-gate_act)) * up_act * weight_of(e)
        inner[e] = act.astype(jnp.bfloat16)

    def finish(e):
        result = jnp.dot(inner[e], weight_refs[3 * e + 2][...], preferred_element_type=jnp.float32)
        result = result.astype(jnp.bfloat16)
        for p in range(2):
            results[p, pl.ds(e * pair_slots, pair_slots), :] = result[p * pair_slots : (p + 1) * pair_slots]

    gate_0 = product(0, 0)
    make_spread(0)
    up_0 = product(0, 1)
    make_spread(1)
    activate(0, gate_0, up_0)
    gate_1 = product(1, 0)
    up_1 = product(1, 1)
    finish(0)
    activate(1, gate_1, up_1)
    finish(1)
    out_copies = []
    at = 0
    for p in range(2):
        total = jnp.dot(spread[p], results[p], preferred_element_type=jnp.float32)
        sums[pairs[p], :] = total.astype(jnp.bfloat16)
        while len(out_copies) < len(targets) and at < (p + 1) * pair_rows:
            count = block_rows[len(out_copies)]
            copy = pltpu.make_async_copy(
                sums.at[pl.ds(at, count)], targets[len(out_copies)], out_sem.at[len(out_copies)]
            )
            copy.start()
            out_copies.append(copy)
            at += count
    for copy in out_copies:
        copy.wait()


def run_plane(ids, cap, decodes, pieces, block_rows, weights):
    width, units = weights[0].shape
    padded = pieces[0].shape[1]
    piece_rows = tuple(piece.shape[0] for piece in pieces)
    total = sum(piece_rows)
    kept = jnp.bfloat16
    anywhere = pl.BlockSpec(memory_space=pl.ANY)
    return pl.pallas_call(
        functools.partial(plane_kernel, cap, piece_rows, block_rows),
        in_specs=[pl.BlockSpec(memory_space=pltpu.SMEM)]
        + [anywhere] * (len(pieces) + 1)
        + [pl.BlockSpec(memory_space=pltpu.VMEM)] * 6,
        out_specs=[anywhere] * len(block_rows),
        out_shape=[jax.ShapeDtypeStruct((count, width), kept) for count in block_rows],
        scratch_shapes=[
            pltpu.VMEM(decodes.shape, kept),
            pltpu.VMEM((total, padded), kept),
            pltpu.VMEM((2, 4 * cap, padded), kept),
            pltpu.VMEM((2, 4 * cap, units), kept),
            pltpu.VMEM((2, 4 * cap, width), kept),
            pltpu.VMEM((2, total // 2, 4 * cap), kept),
            pltpu.VMEM((total, width), kept),
            pltpu.SemaphoreType.DMA((len(pieces) + 1,)),
            pltpu.SemaphoreType.DMA((len(block_rows),)),
        ],
        compiler_params=pltpu.CompilerParams(vmem_limit_bytes=24 << 20),
        cost_estimate=pl.CostEstimate(
            flops=12 * total * width * units, bytes_accessed=24 << 20, transcendentals=total * units
        ),
        name="plane",
    )(ids, decodes, *pieces, *weights)


def merge_kernel(cut, x_ref, y_ref, passed_0_ref, passed_1_ref, x_out, y_out):
    def sum_of(one, other):
        return (one.astype(jnp.float32) + other.astype(jnp.float32)).astype(jnp.bfloat16)

    x_out[:cut, :] = sum_of(x_ref[:cut, :], passed_0_ref[...])
    x_out[cut:, :] = x_ref[cut:, :]
    y_out[:cut, :] = y_ref[:cut, :]
    y_out[cut:, :] = sum_of(y_ref[cut:, :], passed_1_ref[...])


def merge_passed(cut, to_x, to_y, passed_0, passed_1):
    return pl.pallas_call(
        functools.partial(merge_kernel, cut),
        out_shape=[jax.ShapeDtypeStruct(to_x.shape, to_x.dtype)] * 2,
        compiler_params=pltpu.CompilerParams(vmem_limit_bytes=16 << 20),
        name="merge",
    )(to_x, to_y, passed_0, passed_1)


def along_x(value):
    return lax.ppermute(value, "kv", [(i, i ^ 1) for i in range(4)])


def along_y(value):
    return lax.ppermute(value, "kv", [(i, i ^ 2) for i in range(4)])


def around_z(value):
    return lax.ppermute(value, "blk", [(i, (i + 2) % 8) for i in range(8)])


def across_chip(value):
    return lax.ppermute(value, "blk", [(i, i ^ 1) for i in range(8)])


def fence(*values):
    return lax.optimization_barrier(values)


def added(*parts):
    total = parts[0].astype(jnp.float32)
    for part in parts[1:]:
        total = total + part.astype(jnp.float32)
    return total


def permuted_plan(
    queries,
    cache_keys,
    cache_values,
    lengths,
    sinks,
    out_proj,
    decode_resid,
    prefill_hidden,
    norm_gain,
    router,
    routes,
    expert_gate,
    expert_up,
    expert_down,
):
    experts = router.shape[1]
    ids = routes[0]
    tokens = ids.shape[0]
    my_kv = lax.axis_index("kv")
    my_blk = lax.axis_index("blk")
    first_expert = my_kv * 8
    expert_ids = jnp.stack(
        [first_expert + my_blk, first_expert + (my_blk ^ 1), jnp.int32(experts)]
    ).astype(jnp.int32)
    cap = (2 * tokens * ids.shape[1] + experts - 1) // experts
    long = (tokens // 2 + 15) // 16 * 16
    cuts = [long, tokens - long, long, tokens - long]
    blocks = [None] * 4
    sides = [None] * 4
    corners = [None] * 4
    decodes = [None] * 4
    sums = [None] * 4
    passed = [None] * 4
    back = [None] * 4

    def spread_sides(step):
        sides[step] = along_x(blocks[step]), along_y(blocks[step])

    def spread_corners(step):
        cut = cuts[step]
        corners[step] = along_y(sides[step][0][:cut]), along_x(sides[step][1][cut:])

    def apply(step):
        counts = (tokens, tokens, tokens, cuts[step], tokens - cuts[step])
        pieces = (blocks[step],) + sides[step] + corners[step]
        sums[step] = run_plane(expert_ids, cap, decodes[step], pieces, counts, weights)

    def return_corners(step):
        passed[step] = along_y(sums[step][3]), along_x(sums[step][4])

    def return_sides(step):
        to_x, to_y = merge_passed(cuts[step], sums[step][1], sums[step][2], *passed[step])
        back[step] = along_x(to_x), along_y(to_y)

    prefill = prefill_hidden[0]
    blocks[0] = prepare(prefill, norm_gain, router, ids, "block")
    blocks[0], queries, cache_keys, expert_gate, expert_up = fence(
        blocks[0], queries, cache_keys, expert_gate, expert_up
    )
    spread_sides(0)
    blocks[1] = around_z(blocks[0])
    other_gate = across_chip(expert_gate[0])
    other_up = across_chip(expert_up[0])

    attended = attend(queries, cache_keys, cache_values, lengths, sinks)
    partial_proj = jnp.dot(attended, out_proj, preferred_element_type=jnp.float32)
    is_mine = jnp.arange(4)[:, None] == my_kv
    partial_proj += jnp.where(is_mine, decode_resid.astype(jnp.float32), 0.0)
    width = partial_proj.shape[1]
    ids_row = jnp.pad(ids[:1].astype(jnp.float32), ((0, 0), (0, width - ids.shape[1])))
    shared = jnp.concatenate([partial_proj, jnp.where(is_mine, ids_row, 0.0)], axis=0)

    shared, other_gate = fence(shared, other_gate)
    shared = shared + along_x(shared)
    sides[0], blocks[1], shared, expert_down = fence(sides[0], blocks[1], shared, expert_down)

    spread_sides(1)
    blocks[2] = around_z(blocks[1])
    other_down = across_chip(expert_down[0])
    sides[1], sides[0], blocks[2], shared = fence(sides[1], sides[0], blocks[2], shared)

    spread_corners(0)
    shared = shared + along_y(shared)
    order = [my_kv ^ j for j in range(4)]
    decoded = jnp.concatenate(
        [lax.dynamic_slice_in_dim(shared, index, 1) for index in order], axis=0
    ).astype(jnp.bfloat16)
    decode_ids = jnp.concatenate(
        [lax.dynamic_slice_in_dim(shared, 4 + index, 1) for index in order], axis=0
    )[:, : ids.shape[1]].astype(jnp.int32)
    hidden = jnp.concatenate([decoded[:1], prefill], axis=0)
    decodes[0] = prepare(
        jnp.pad(decoded, ((0, 12), (0, 0))),
        norm_gain,
        router,
        jnp.pad(decode_ids, ((0, 12), (0, 0))),
        "first",
    )
    corners[0], sides[1], blocks[2], decodes[0], other_up, other_down = fence(
        corners[0], sides[1], blocks[2], decodes[0], other_up, other_down
    )
    weights = (expert_gate[0], expert_up[0], expert_down[0], other_gate, other_up, other_down)

    spread_corners(1)
    spread_sides(2)
    arrived = around_z(jnp.concatenate([blocks[2], decodes[0]], axis=0))
    apply(0)
    corners[1], sides[2], arrived, sums[0] = fence(corners[1], sides[2], arrived, sums[0])
    blocks[3], decodes[1] = arrived[:tokens], arrived[tokens:]

    spread_corners(2)
    spread_sides(3)
    decodes[2] = around_z(decodes[1])
    apply(1)
    corners[2], sides[3], decodes[2], sums[1] = fence(corners[2], sides[3], decodes[2], sums[1])

    spread_corners(3)
    decodes[3] = around_z(decodes[2])
    return_corners(1)
    apply(2)
    corners[3], decodes[3], passed[1], sums[1], sums[2] = fence(
        corners[3], decodes[3], passed[1], sums[1], sums[2]
    )

    return_sides(1)
    return_corners(2)
    apply(3)
    back[1], passed[2], sums[1], sums[2], sums[3] = fence(
        back[1], passed[2], sums[1], sums[2], sums[3]
    )

    return_sides(2)
    return_corners(3)
    carried = around_z(added(sums[1][0], *back[1]).astype(jnp.bfloat16))
    back[2], passed[3], carried, sums[2], sums[3], sums[0] = fence(
        back[2], passed[3], carried, sums[2], sums[3], sums[0]
    )

    return_sides(3)
    return_corners(0)
    carried = around_z(added(sums[2][0], *back[2], carried).astype(jnp.bfloat16))
    back[3], passed[0], carried, sums[3], sums[0] = fence(
        back[3], passed[0], carried, sums[3], sums[0]
    )

    return_sides(0)
    carried = around_z(added(sums[3][0], *back[3], carried).astype(jnp.bfloat16))
    return added(hidden, sums[0][0], *back[0], carried).astype(jnp.bfloat16)[None]


def chunk_cuts(tokens, devices):
    step = (tokens // 2 + 15) // 16 * 16 if devices < 128 else 32
    return [(start, min(start + step, tokens)) for start in range(0, tokens, step)]


def gathered_plan(
    queries,
    cache_keys,
    cache_values,
    lengths,
    sinks,
    out_proj,
    decode_resid,
    prefill_hidden,
    norm_gain,
    router,
    routes,
    expert_gate,
    expert_up,
    expert_down,
):
    experts = router.shape[1]
    ids = routes[0]
    tokens = ids.shape[0]
    prefill = prefill_hidden[0]
    devices = lax.axis_size(AXES)
    cuts = chunk_cuts(tokens, devices)
    my_expert = lax.axis_index("kv") * lax.axis_size("blk") + lax.axis_index("blk")
    expert = jnp.stack([my_expert, jnp.int32(experts)]).astype(jnp.int32)
    weights = (expert_gate[0], expert_up[0], expert_down[0])

    attended = attend(queries, cache_keys, cache_values, lengths, sinks)
    partial_proj = jnp.dot(attended, out_proj, preferred_element_type=jnp.float32)
    projected = lax.psum_scatter(partial_proj, "kv", scatter_dimension=0, tiled=True)
    decoded = (decode_resid.astype(jnp.float32) + projected).astype(jnp.bfloat16)
    hidden = jnp.concatenate([prefill, decoded], axis=0)
    ids = jnp.concatenate([ids[1:], ids[:1]], axis=0)
    gathered = []
    for start, stop in cuts:
        source = prefill[start:stop] if stop < tokens else hidden[start:stop]
        sent = prepare(source, norm_gain, router, ids[start:stop])
        gathered.append(lax.all_gather(sent, AXES, axis=0, tiled=True))
    returned = []
    for rows in gathered:
        sums = run_expert(expert, rows, *weights)
        returned.append(lax.psum_scatter(sums, AXES, scatter_dimension=0, tiled=True))
    combined = jnp.concatenate(returned, axis=0)
    layer_sum = (hidden.astype(jnp.float32) + combined.astype(jnp.float32)).astype(jnp.bfloat16)
    layer_sum = jnp.concatenate([layer_sum[-1:], layer_sum[:-1]], axis=0)
    return layer_sum[None]


def solution(mesh):
    plan = permuted_plan if (mesh.shape["kv"], mesh.shape["blk"]) == (4, 8) else gathered_plan
    return jax.shard_map(
        plan,
        mesh=mesh,
        in_specs=(
            P("blk", "kv"),
            P("blk", None, "kv", None),
            P("blk", None, "kv", None),
            P(),
            P("kv"),
            P("kv", None),
            P(("blk", "kv"), None),
            P(("blk", "kv"), None, None),
            P(),
            P(),
            P(("blk", "kv"), None, None),
            P(("kv", "blk"), None, None),
            P(("kv", "blk"), None, None),
            P(("kv", "blk"), None, None),
        ),
        out_specs=P(("blk", "kv"), None, None),
        check_vma=False,
    )
```

```python
import functools
import math

import jax
import jax.numpy as jnp
from jax import lax
from jax.experimental import pallas as pl
from jax.experimental.pallas import tpu as pltpu
from jax.sharding import PartitionSpec as P

NEG_FILL = -1e30
EPSILON = 1e-06
NOT_CHOSEN = -256.0
AXES = ("blk", "kv")


def attend(queries, cache_keys, cache_values, lengths, sinks):
    my_block = lax.axis_index("blk")
    per_block = queries.shape[0]
    head_count = sinks.shape[0]
    head_dim = cache_keys.shape[3]
    window = cache_keys.shape[1]
    grouped_q = queries.reshape(per_block, head_count, head_dim)
    key_rows = cache_keys[:, :, 0, :]
    value_rows = cache_values[:, :, 0, :]
    my_lengths = lax.dynamic_slice_in_dim(lengths, my_block * per_block, per_block)
    scores = jnp.einsum("rgd,rjd->rgj", grouped_q, key_rows, preferred_element_type=jnp.float32) * (
        1.0 / math.sqrt(head_dim)
    )
    first_valid = window - jnp.minimum(my_lengths, window)
    is_valid = (jnp.arange(window, dtype=jnp.int32)[None, :] >= first_valid[:, None])[:, None, :]
    masked = jnp.where(is_valid, scores, NEG_FILL)
    top_limit = jnp.maximum(jnp.max(masked, axis=2), sinks[None, :])
    weights = jnp.where(is_valid, jnp.exp(masked - top_limit[..., None]), 0.0)
    denominator = jnp.sum(weights, axis=2) + jnp.exp(sinks[None, :] - top_limit)
    numerator = jnp.einsum(
        "rgj,rjd->rgd", weights.astype(jnp.bfloat16), value_rows, preferred_element_type=jnp.float32
    )
    return (
        (numerator / denominator[..., None])
        .astype(jnp.bfloat16)
        .reshape(per_block, head_count * head_dim)
    )


def prepare_kernel(ranking, hidden_ref, gain_ref, router_ref, routes_ref, out_ref, *scratch):
    experts, width = router_ref.shape
    if scratch:
        (shifted,) = scratch
        shifted[0:1, :] = jnp.zeros((1, width), jnp.float32)
        shifted[1:, :] = hidden_ref[...].astype(jnp.float32)
        hidden = shifted[...]
    else:
        hidden = hidden_ref[...].astype(jnp.float32)
    rows = hidden.shape[0]
    mean_sq = jnp.mean(hidden * hidden, axis=1, keepdims=True)
    normed = (hidden * lax.rsqrt(mean_sq + EPSILON) * gain_ref[...]).astype(jnp.bfloat16)
    out_ref[:, :width] = normed
    by_lanes = (((1,), (1,)), ((), ()))
    logits = lax.dot_general(normed, router_ref[...], by_lanes, preferred_element_type=jnp.float32)
    expert = lax.broadcasted_iota(jnp.int32, (experts, rows), 0)
    routes = routes_ref[...]
    chosen = jnp.zeros(expert.shape, jnp.bool_)
    for k in range(routes.shape[0]):
        chosen = chosen | (expert == routes[k : k + 1, :])
    chosen = jnp.where(chosen, 1.0, 0.0).astype(jnp.bfloat16)
    row = lax.broadcasted_iota(jnp.int32, (rows, rows), 0)
    other = lax.broadcasted_iota(jnp.int32, (rows, rows), 1)

    def of_rows(taken):
        taken = jnp.where(taken, 1.0, 0.0).astype(jnp.bfloat16)
        return lax.dot_general(taken, chosen, by_lanes, preferred_element_type=jnp.float32)

    mine = of_rows(row == other) > 0.5
    top = jnp.max(jnp.where(mine, logits, NEG_FILL), axis=1, keepdims=True)
    raised = jnp.where(mine, jnp.exp(jnp.minimum(logits - top, 0.0)), 0.0)
    gates = raised / jnp.sum(raised, axis=1, keepdims=True)
    high = gates.astype(jnp.bfloat16).astype(jnp.float32)
    parts = [high, gates - high]
    if ranking == "block":
        parts.append(jnp.where(mine, of_rows(other < row), NOT_CHOSEN))
    elif ranking == "first":
        parts.append(jnp.where(mine, 0.0, NOT_CHOSEN))
    rest = out_ref.shape[1] - width - len(parts) * experts
    if rest:
        parts.append(jnp.zeros((rows, rest), jnp.float32))
    out_ref[:, width:] = jnp.concatenate(parts, axis=1).astype(jnp.bfloat16)


def prepare(hidden, norm_gain, router, routes, ranking=None):
    width = hidden.shape[1]
    rows = routes.shape[0]
    extra = -(-(3 if ranking else 2) * router.shape[1] // 128) * 128
    shifted = rows > hidden.shape[0]
    return pl.pallas_call(
        functools.partial(prepare_kernel, ranking),
        out_shape=jax.ShapeDtypeStruct((rows, width + extra), jnp.bfloat16),
        scratch_shapes=[pltpu.VMEM((rows, width), jnp.float32)] if shifted else [],
        compiler_params=pltpu.CompilerParams(vmem_limit_bytes=32 << 20),
        name="prepare",
    )(hidden, norm_gain.reshape(1, width), router.T, routes.T)


def expert_kernel(expert_ref, rows_ref, gate_ref, up_ref, down_ref, out_ref):
    width = gate_ref.shape[0]
    payload = rows_ref[...]
    rows = payload[:, :width]
    tail = payload[:, width:].astype(jnp.float32)
    lane = lax.broadcasted_iota(jnp.int32, tail.shape, 1)
    expert = expert_ref[0]
    experts = expert_ref[1]
    mine = (lane == expert) | (lane == expert + experts)
    weight = jnp.sum(jnp.where(mine, tail, 0.0), axis=1, keepdims=True)
    gate_act = jnp.dot(rows, gate_ref[...], preferred_element_type=jnp.float32)
    up_act = jnp.dot(rows, up_ref[...], preferred_element_type=jnp.float32)
    inner = (gate_act / (1.0 + jnp.exp(-gate_act)) * up_act).astype(jnp.bfloat16)
    result = jnp.dot(inner, down_ref[...], preferred_element_type=jnp.float32)
    out_ref[...] = (weight * result).astype(jnp.bfloat16)


def run_expert(expert, rows, gate_weights, up_weights, down_weights):
    total, padded = rows.shape
    width, hidden_units = gate_weights.shape
    tile = 256
    return pl.pallas_call(
        expert_kernel,
        grid_spec=pltpu.PrefetchScalarGridSpec(
            num_scalar_prefetch=1,
            grid=(total // tile,),
            in_specs=[
                pl.BlockSpec((tile, padded), lambda i, e: (i, 0)),
                pl.BlockSpec((width, hidden_units), lambda i, e: (0, 0), pipeline_mode=pl.Buffered(1)),
                pl.BlockSpec((width, hidden_units), lambda i, e: (0, 0), pipeline_mode=pl.Buffered(1)),
                pl.BlockSpec((hidden_units, width), lambda i, e: (0, 0), pipeline_mode=pl.Buffered(1)),
            ],
            out_specs=pl.BlockSpec((tile, width), lambda i, e: (i, 0)),
        ),
        out_shape=jax.ShapeDtypeStruct((total, width), jnp.bfloat16),
        compiler_params=pltpu.CompilerParams(vmem_limit_bytes=48 << 20),
        name="expert",
    )(expert, rows, gate_weights, up_weights, down_weights)


def plane_kernel(cap, piece_rows, block_rows, *refs):
    refs = list(refs)
    ids_ref = refs.pop(0)
    decode_ref = refs.pop(0)
    sources = [refs.pop(0) for _ in piece_rows]
    weight_refs = [refs.pop(0) for _ in range(6)]
    targets = [refs.pop(0) for _ in block_rows]
    decodes, rows, weights, downs, slots, inner, results, spread, sums, row_sem, weight_sem, out_sem = refs
    width = sums.shape[1]
    tokens = block_rows[0]
    pair_rows = 2 * tokens
    pair_slots = 2 * cap
    row_copies = [pltpu.make_async_copy(decode_ref, decodes, row_sem.at[len(sources)])]
    at = 0
    for i, (ref, count) in enumerate(zip(sources, piece_rows)):
        copy = pltpu.make_async_copy(ref, rows.at[pl.ds(at, count)], row_sem.at[i])
        row_copies.append(copy)
        at += count
    up_copies = [
        pltpu.make_async_copy(weight_refs[3 * e + i], weights.at[2 * e + i], weight_sem.at[2 * e + i])
        for e in range(2)
        for i in range(2)
    ]
    down_copies = [
        pltpu.make_async_copy(weight_refs[3 * e + 2], downs.at[e], weight_sem.at[4 + e])
        for e in range(2)
    ]
    for copy in row_copies + up_copies + down_copies:
        copy.start()
    for copy in row_copies:
        copy.wait()
    few = decodes.shape[0]
    is_first = lax.broadcasted_iota(jnp.int32, (few, 1), 0) == 0
    for j in range(4):
        part = pl.ds(j * tokens, few)
        decode_row = decodes[...].astype(jnp.float32)[j : j + 1]
        kept = rows[part, :].astype(jnp.float32)
        rows[part, :] = jnp.where(is_first, decode_row, kept).astype(jnp.bfloat16)

    experts = ids_ref[2]
    extra = rows.shape[1] - width
    lanes = lax.broadcasted_iota(jnp.int32, (8, extra), 1)
    line = lax.broadcasted_iota(jnp.int32, (8, extra), 0)
    wanted = ((line == 0) & (lanes == ids_ref[0] + 2 * experts)) | (
        (line == 1) & (lanes == ids_ref[1] + 2 * experts)
    )
    wanted = jnp.where(wanted, 1.0, 0.0).astype(jnp.bfloat16)
    pairs = [pl.ds(p * pair_rows, pair_rows) for p in range(2)]

    def shift_of(shape, axis):
        second = lax.broadcasted_iota(jnp.int32, shape, axis) >= tokens
        return jnp.where(second, float(cap), 0.0)

    for p in range(2):
        ranks = lax.dot_general(
            wanted, rows[pairs[p], width:], (((1,), (1,)), ((), ())), preferred_element_type=jnp.float32
        )
        ranks += shift_of(ranks.shape, 1)
        slot = lax.broadcasted_iota(jnp.int32, (2 * pair_slots, pair_rows), 0).astype(jnp.float32)
        taken = (slot == ranks[0:1]) | (slot == ranks[1:2] + float(pair_slots))
        taken = jnp.where(taken, 1.0, 0.0).astype(jnp.bfloat16)
        picked = jnp.dot(taken, rows[pairs[p], :], preferred_element_type=jnp.float32)
        picked = picked.astype(jnp.bfloat16)
        for e in range(2):
            slots[e, pl.ds(p * pair_slots, pair_slots), :] = picked[e * pair_slots : (e + 1) * pair_slots]

    def make_spread(p):
        tail = rows[pairs[p], width:].astype(jnp.float32)
        lane = lax.broadcasted_iota(jnp.int32, tail.shape, 1)
        slot = lax.broadcasted_iota(jnp.int32, (pair_rows, 2 * pair_slots), 1).astype(jnp.float32)
        back = jnp.zeros(slot.shape, jnp.bool_)
        for e in range(2):
            mine = lane == ids_ref[e] + 2 * experts
            rank = jnp.sum(jnp.where(mine, tail, 0.0), axis=1, keepdims=True)
            back = back | (slot == rank + shift_of(rank.shape, 0) + float(e * pair_slots))
        spread[p] = jnp.where(back, 1.0, 0.0).astype(jnp.bfloat16)

    def weight_of(e):
        tail = slots[e, :, width:].astype(jnp.float32)
        lane = lax.broadcasted_iota(jnp.int32, tail.shape, 1)
        mine = (lane == ids_ref[e]) | (lane == ids_ref[e] + experts)
        return jnp.sum(jnp.where(mine, tail, 0.0), axis=1, keepdims=True)

    def product(e, i):
        return jnp.dot(slots[e, :, :width], weights[2 * e + i], preferred_element_type=jnp.float32)

    def activate(e, gate_act, up_act):
        act = gate_act / (1.0 + jnp.exp(-gate_act)) * up_act * weight_of(e)
        inner[e] = act.astype(jnp.bfloat16)

    def finish(e):
        result = jnp.dot(inner[e], downs[e], preferred_element_type=jnp.float32)
        result = result.astype(jnp.bfloat16)
        for p in range(2):
            results[p, pl.ds(e * pair_slots, pair_slots), :] = result[p * pair_slots : (p + 1) * pair_slots]

    up_copies[0].wait()
    gate_0 = product(0, 0)
    make_spread(0)
    up_copies[1].wait()
    up_0 = product(0, 1)
    make_spread(1)
    up_copies[2].wait()
    activate(0, gate_0, up_0)
    gate_1 = product(1, 0)
    up_copies[3].wait()
    up_1 = product(1, 1)
    down_copies[0].wait()
    finish(0)
    activate(1, gate_1, up_1)
    down_copies[1].wait()
    finish(1)
    out_copies = []
    at = 0
    for p in range(2):
        total = jnp.dot(spread[p], results[p], preferred_element_type=jnp.float32)
        sums[pairs[p], :] = total.astype(jnp.bfloat16)
        while len(out_copies) < len(targets) and at < (p + 1) * pair_rows:
            count = block_rows[len(out_copies)]
            copy = pltpu.make_async_copy(
                sums.at[pl.ds(at, count)], targets[len(out_copies)], out_sem.at[len(out_copies)]
            )
            copy.start()
            out_copies.append(copy)
            at += count
    for copy in out_copies:
        copy.wait()


def run_plane(ids, cap, decodes, pieces, block_rows, weights):
    width, units = weights[0].shape
    padded = pieces[0].shape[1]
    piece_rows = tuple(piece.shape[0] for piece in pieces)
    total = sum(piece_rows)
    kept = jnp.bfloat16
    anywhere = pl.BlockSpec(memory_space=pl.ANY)
    return pl.pallas_call(
        functools.partial(plane_kernel, cap, piece_rows, block_rows),
        in_specs=[pl.BlockSpec(memory_space=pltpu.SMEM)] + [anywhere] * (len(pieces) + 7),
        out_specs=[anywhere] * len(block_rows),
        out_shape=[jax.ShapeDtypeStruct((count, width), kept) for count in block_rows],
        scratch_shapes=[
            pltpu.VMEM(decodes.shape, kept),
            pltpu.VMEM((total, padded), kept),
            pltpu.VMEM((4, width, units), kept),
            pltpu.VMEM((2, units, width), kept),
            pltpu.VMEM((2, 4 * cap, padded), kept),
            pltpu.VMEM((2, 4 * cap, units), kept),
            pltpu.VMEM((2, 4 * cap, width), kept),
            pltpu.VMEM((2, total // 2, 4 * cap), kept),
            pltpu.VMEM((total, width), kept),
            pltpu.SemaphoreType.DMA((len(pieces) + 1,)),
            pltpu.SemaphoreType.DMA((6,)),
            pltpu.SemaphoreType.DMA((len(block_rows),)),
        ],
        compiler_params=pltpu.CompilerParams(vmem_limit_bytes=48 << 20),
        cost_estimate=pl.CostEstimate(
            flops=12 * total * width * units, bytes_accessed=24 << 20, transcendentals=total * units
        ),
        name="plane",
    )(ids, decodes, *pieces, *weights)


def merge_kernel(cut, at_0, at_1, x_ref, y_ref, passed_0_ref, passed_1_ref, x_out, y_out):
    def sum_of(one, other):
        return (one.astype(jnp.float32) + other.astype(jnp.float32)).astype(jnp.bfloat16)

    rest = x_ref.shape[0] - cut
    x_out[:cut, :] = sum_of(x_ref[:cut, :], passed_0_ref[at_0 : at_0 + cut, :])
    x_out[cut:, :] = x_ref[cut:, :]
    y_out[:cut, :] = y_ref[:cut, :]
    y_out[cut:, :] = sum_of(y_ref[cut:, :], passed_1_ref[at_1 : at_1 + rest, :])


def merge_passed(cut, to_x, to_y, passed_0, passed_1, at_0=0, at_1=0):
    return pl.pallas_call(
        functools.partial(merge_kernel, cut, at_0, at_1),
        out_shape=[jax.ShapeDtypeStruct(to_x.shape, to_x.dtype)] * 2,
        compiler_params=pltpu.CompilerParams(vmem_limit_bytes=16 << 20),
        name="merge",
    )(to_x, to_y, passed_0, passed_1)


def along_x(value):
    return lax.ppermute(value, "kv", [(i, i ^ 1) for i in range(4)])


def along_y(value):
    return lax.ppermute(value, "kv", [(i, i ^ 2) for i in range(4)])


def around_z(value):
    return lax.ppermute(value, "blk", [(i, (i + 2) % 8) for i in range(8)])


def across_chip(value):
    return lax.ppermute(value, "blk", [(i, i ^ 1) for i in range(8)])


def fence(*values):
    return lax.optimization_barrier(values)


def added(*parts):
    total = parts[0].astype(jnp.float32)
    for part in parts[1:]:
        total = total + part.astype(jnp.float32)
    return total


def permuted_plan(
    queries,
    cache_keys,
    cache_values,
    lengths,
    sinks,
    out_proj,
    decode_resid,
    prefill_hidden,
    norm_gain,
    router,
    routes,
    expert_gate,
    expert_up,
    expert_down,
):
    experts = router.shape[1]
    ids = routes[0]
    tokens = ids.shape[0]
    my_kv = lax.axis_index("kv")
    my_blk = lax.axis_index("blk")
    first_expert = my_kv * 8
    expert_ids = jnp.stack(
        [first_expert + my_blk, first_expert + (my_blk ^ 1), jnp.int32(experts)]
    ).astype(jnp.int32)
    cap = (2 * tokens * ids.shape[1] + experts - 1) // experts
    long = (tokens // 2 + 15) // 16 * 16
    cuts = [long, tokens - long, long, tokens - long]
    blocks = [None] * 4
    sides = [None] * 4
    corners = [None] * 4
    decodes = [None] * 4
    sums = [None] * 4
    passed = [None] * 4
    back = [None] * 4

    def spread_sides(step):
        sides[step] = along_x(blocks[step]), along_y(blocks[step])

    def spread_corners(step):
        cut = cuts[step]
        corners[step] = along_y(sides[step][0][:cut]), along_x(sides[step][1][cut:])

    def apply(step):
        counts = (tokens, tokens, tokens, cuts[step], tokens - cuts[step])
        pieces = (blocks[step],) + sides[step] + corners[step]
        sums[step] = run_plane(expert_ids, cap, decodes[step], pieces, counts, weights)

    def return_corners(step):
        passed[step] = along_y(sums[step][3]), along_x(sums[step][4])

    def return_sides(step):
        to_x, to_y = merge_passed(cuts[step], sums[step][1], sums[step][2], *passed[step])
        back[step] = along_x(to_x), along_y(to_y)

    other_gate = across_chip(expert_gate[0])
    other_up = across_chip(expert_up[0])

    attended = attend(queries, cache_keys, cache_values, lengths, sinks)
    partial_proj = jnp.dot(attended, out_proj, preferred_element_type=jnp.float32)
    is_mine = jnp.arange(4)[:, None] == my_kv
    partial_proj += jnp.where(is_mine, decode_resid.astype(jnp.float32), 0.0)
    width = partial_proj.shape[1]
    ids_row = jnp.pad(ids[:1].astype(jnp.float32), ((0, 0), (0, width - ids.shape[1])))
    shared = jnp.concatenate([partial_proj, jnp.where(is_mine, ids_row, 0.0)], axis=0)

    prefill = prefill_hidden[0]
    blocks[0] = prepare(prefill, norm_gain, router, ids, "block")
    blocks[0], shared, other_gate = fence(blocks[0], shared, other_gate)
    shared = shared + along_x(shared)
    spread_sides(0)
    blocks[1] = around_z(blocks[0])
    shared = shared + along_y(shared)
    sides[0], blocks[1], shared, other_gate, other_up, expert_down = fence(
        sides[0], blocks[1], shared, other_gate, other_up, expert_down
    )

    other_down = across_chip(expert_down[0])
    spread_sides(1)
    blocks[2] = around_z(blocks[1])
    by_y, by_x = sides[0][0][: cuts[0]], sides[0][1][cuts[0] :]
    by_y, other_down = fence(by_y, other_down)
    corners[0] = along_y(by_y), along_x(by_x)
    order = [my_kv ^ j for j in range(4)]
    decoded = jnp.concatenate(
        [lax.dynamic_slice_in_dim(shared, index, 1) for index in order], axis=0
    ).astype(jnp.bfloat16)
    decode_ids = jnp.concatenate(
        [lax.dynamic_slice_in_dim(shared, 4 + index, 1) for index in order], axis=0
    )[:, : ids.shape[1]].astype(jnp.int32)
    hidden = jnp.concatenate([decoded[:1], prefill], axis=0)
    decodes[0] = prepare(
        jnp.pad(decoded, ((0, 12), (0, 0))),
        norm_gain,
        router,
        jnp.pad(decode_ids, ((0, 12), (0, 0))),
        "first",
    )
    corners[0], sides[1], blocks[2], decodes[0], other_down = fence(
        corners[0], sides[1], blocks[2], decodes[0], other_down
    )
    weights = (expert_gate[0], expert_up[0], expert_down[0], other_gate, other_up, other_down)

    spread_corners(1)
    spread_sides(2)
    arrived = around_z(jnp.concatenate([blocks[2], decodes[0]], axis=0))
    apply(0)
    corners[1], sides[2], arrived, sums[0] = fence(corners[1], sides[2], arrived, sums[0])
    blocks[3], decodes[1] = arrived[:tokens], arrived[tokens:]

    spread_corners(2)
    spread_sides(3)
    decodes[2] = around_z(decodes[1])
    apply(1)
    corners[2], sides[3], decodes[2], sums[0], sums[1] = fence(
        corners[2], sides[3], decodes[2], sums[0], sums[1]
    )

    spread_corners(3)
    decodes[3] = around_z(decodes[2])
    by_y = along_y(jnp.concatenate([sums[0][3], sums[1][3]], axis=0))
    by_x = along_x(jnp.concatenate([sums[0][4], sums[1][4]], axis=0))
    passed[0] = by_y, by_x
    apply(2)
    corners[3], decodes[3], passed[0], sums[1], sums[2] = fence(
        corners[3], decodes[3], passed[0], sums[1], sums[2]
    )
    passed[1] = passed[0] + (cuts[0], tokens - cuts[0])

    return_sides(1)
    return_corners(2)
    apply(3)
    back[1], passed[2], sums[1], sums[2], sums[3] = fence(
        back[1], passed[2], sums[1], sums[2], sums[3]
    )

    return_corners(3)
    return_sides(2)
    carried = around_z(added(sums[1][0], *back[1]).astype(jnp.bfloat16))
    return_sides(3)
    carried = around_z(added(sums[2][0], *back[2], carried).astype(jnp.bfloat16))
    back[3], passed[0], sums[0] = fence(back[3], passed[0], sums[0])
    return_sides(0)
    carried = around_z(added(sums[3][0], *back[3], carried).astype(jnp.bfloat16))
    return added(hidden, sums[0][0], *back[0], carried).astype(jnp.bfloat16)[None]


def chunk_cuts(tokens, devices):
    step = (tokens // 2 + 15) // 16 * 16 if devices < 128 else 32
    return [(start, min(start + step, tokens)) for start in range(0, tokens, step)]


def gathered_plan(
    queries,
    cache_keys,
    cache_values,
    lengths,
    sinks,
    out_proj,
    decode_resid,
    prefill_hidden,
    norm_gain,
    router,
    routes,
    expert_gate,
    expert_up,
    expert_down,
):
    experts = router.shape[1]
    ids = routes[0]
    tokens = ids.shape[0]
    prefill = prefill_hidden[0]
    devices = lax.axis_size(AXES)
    cuts = chunk_cuts(tokens, devices)
    my_expert = lax.axis_index("kv") * lax.axis_size("blk") + lax.axis_index("blk")
    expert = jnp.stack([my_expert, jnp.int32(experts)]).astype(jnp.int32)
    weights = (expert_gate[0], expert_up[0], expert_down[0])

    attended = attend(queries, cache_keys, cache_values, lengths, sinks)
    partial_proj = jnp.dot(attended, out_proj, preferred_element_type=jnp.float32)
    projected = lax.psum_scatter(partial_proj, "kv", scatter_dimension=0, tiled=True)
    decoded = (decode_resid.astype(jnp.float32) + projected).astype(jnp.bfloat16)
    hidden = jnp.concatenate([prefill, decoded], axis=0)
    ids = jnp.concatenate([ids[1:], ids[:1]], axis=0)
    gathered = []
    for start, stop in cuts:
        source = prefill[start:stop] if stop < tokens else hidden[start:stop]
        sent = prepare(source, norm_gain, router, ids[start:stop])
        gathered.append(lax.all_gather(sent, AXES, axis=0, tiled=True))
    returned = []
    for rows in gathered:
        sums = run_expert(expert, rows, *weights)
        returned.append(lax.psum_scatter(sums, AXES, scatter_dimension=0, tiled=True))
    combined = jnp.concatenate(returned, axis=0)
    layer_sum = (hidden.astype(jnp.float32) + combined.astype(jnp.float32)).astype(jnp.bfloat16)
    layer_sum = jnp.concatenate([layer_sum[-1:], layer_sum[:-1]], axis=0)
    return layer_sum[None]


def solution(mesh):
    plan = permuted_plan if (mesh.shape["kv"], mesh.shape["blk"]) == (4, 8) else gathered_plan
    return jax.shard_map(
        plan,
        mesh=mesh,
        in_specs=(
            P("blk", "kv"),
            P("blk", None, "kv", None),
            P("blk", None, "kv", None),
            P(),
            P("kv"),
            P("kv", None),
            P(("blk", "kv"), None),
            P(("blk", "kv"), None, None),
            P(),
            P(),
            P(("blk", "kv"), None, None),
            P(("kv", "blk"), None, None),
            P(("kv", "blk"), None, None),
            P(("kv", "blk"), None, None),
        ),
        out_specs=P(("blk", "kv"), None, None),
        check_vma=False,
    )
```

```python
import functools
import math

import jax
import jax.numpy as jnp
from jax import lax
from jax.experimental import pallas as pl
from jax.experimental.pallas import tpu as pltpu
from jax.sharding import PartitionSpec as P

NEG_FILL = -1e30
EPSILON = 1e-06
NOT_CHOSEN = -256.0
AXES = ("blk", "kv")


def attend(queries, cache_keys, cache_values, lengths, sinks):
    my_block = lax.axis_index("blk")
    per_block = queries.shape[0]
    head_count = sinks.shape[0]
    head_dim = cache_keys.shape[3]
    window = cache_keys.shape[1]
    grouped_q = queries.reshape(per_block, head_count, head_dim)
    key_rows = cache_keys[:, :, 0, :]
    value_rows = cache_values[:, :, 0, :]
    my_lengths = lax.dynamic_slice_in_dim(lengths, my_block * per_block, per_block)
    scores = jnp.einsum("rgd,rjd->rgj", grouped_q, key_rows, preferred_element_type=jnp.float32) * (
        1.0 / math.sqrt(head_dim)
    )
    first_valid = window - jnp.minimum(my_lengths, window)
    is_valid = (jnp.arange(window, dtype=jnp.int32)[None, :] >= first_valid[:, None])[:, None, :]
    masked = jnp.where(is_valid, scores, NEG_FILL)
    top_limit = jnp.maximum(jnp.max(masked, axis=2), sinks[None, :])
    weights = jnp.where(is_valid, jnp.exp(masked - top_limit[..., None]), 0.0)
    denominator = jnp.sum(weights, axis=2) + jnp.exp(sinks[None, :] - top_limit)
    numerator = jnp.einsum(
        "rgj,rjd->rgd", weights.astype(jnp.bfloat16), value_rows, preferred_element_type=jnp.float32
    )
    return (
        (numerator / denominator[..., None])
        .astype(jnp.bfloat16)
        .reshape(per_block, head_count * head_dim)
    )


def fetched_prepare_kernel(ranking, hidden_in, gain_in, router_in, routes_in, out_ref, *scratch):
    shifted, hidden_ref, gain_ref, router_ref, routes_ref, sems = scratch
    sources = (hidden_in, gain_in, router_in, routes_in)
    targets = (hidden_ref, gain_ref, router_ref, routes_ref)
    copies = [
        pltpu.make_async_copy(source, target, sems.at[i])
        for i, (source, target) in enumerate(zip(sources, targets))
    ]
    for copy in copies:
        copy.start()
    for copy in copies:
        copy.wait()
    prepare_kernel(ranking, *targets, out_ref, shifted)


def prepare_kernel(ranking, hidden_ref, gain_ref, router_ref, routes_ref, out_ref, *scratch):
    experts, width = router_ref.shape
    if scratch:
        (shifted,) = scratch
        shifted[0:1, :] = jnp.zeros((1, width), jnp.float32)
        shifted[1:, :] = hidden_ref[...].astype(jnp.float32)
        hidden = shifted[...]
    else:
        hidden = hidden_ref[...].astype(jnp.float32)
    rows = hidden.shape[0]
    mean_sq = jnp.mean(hidden * hidden, axis=1, keepdims=True)
    normed = (hidden * lax.rsqrt(mean_sq + EPSILON) * gain_ref[...]).astype(jnp.bfloat16)
    out_ref[:, :width] = normed
    by_lanes = (((1,), (1,)), ((), ()))
    logits = lax.dot_general(normed, router_ref[...], by_lanes, preferred_element_type=jnp.float32)
    expert = lax.broadcasted_iota(jnp.int32, (experts, rows), 0)
    routes = routes_ref[...]
    chosen = jnp.zeros(expert.shape, jnp.bool_)
    for k in range(routes.shape[0]):
        chosen = chosen | (expert == routes[k : k + 1, :])
    chosen = jnp.where(chosen, 1.0, 0.0).astype(jnp.bfloat16)
    row = lax.broadcasted_iota(jnp.int32, (rows, rows), 0)
    other = lax.broadcasted_iota(jnp.int32, (rows, rows), 1)

    def of_rows(taken):
        taken = jnp.where(taken, 1.0, 0.0).astype(jnp.bfloat16)
        return lax.dot_general(taken, chosen, by_lanes, preferred_element_type=jnp.float32)

    mine = of_rows(row == other) > 0.5
    top = jnp.max(jnp.where(mine, logits, NEG_FILL), axis=1, keepdims=True)
    raised = jnp.where(mine, jnp.exp(jnp.minimum(logits - top, 0.0)), 0.0)
    gates = raised / jnp.sum(raised, axis=1, keepdims=True)
    high = gates.astype(jnp.bfloat16).astype(jnp.float32)
    parts = [high, gates - high]
    if ranking == "block":
        parts.append(jnp.where(mine, of_rows(other < row), NOT_CHOSEN))
    elif ranking == "first":
        parts.append(jnp.where(mine, 0.0, NOT_CHOSEN))
    rest = out_ref.shape[1] - width - len(parts) * experts
    if rest:
        parts.append(jnp.zeros((rows, rest), jnp.float32))
    out_ref[:, width:] = jnp.concatenate(parts, axis=1).astype(jnp.bfloat16)


def prepare(hidden, norm_gain, router, routes, ranking=None):
    width = hidden.shape[1]
    rows = routes.shape[0]
    extra = -(-(3 if ranking else 2) * router.shape[1] // 128) * 128
    operands = (hidden, norm_gain.reshape(1, width), router.T, routes.T)
    fetched = rows > hidden.shape[0]
    kernel, options = prepare_kernel, {}
    if fetched:
        kernel = fetched_prepare_kernel
        options = dict(
            in_specs=[pl.BlockSpec(memory_space=pltpu.HBM)] * 4,
            scratch_shapes=[pltpu.VMEM((rows, width), jnp.float32)]
            + [pltpu.VMEM(operand.shape, operand.dtype) for operand in operands]
            + [pltpu.SemaphoreType.DMA((4,))],
        )
    return pl.pallas_call(
        functools.partial(kernel, ranking),
        out_shape=jax.ShapeDtypeStruct((rows, width + extra), jnp.bfloat16),
        compiler_params=pltpu.CompilerParams(vmem_limit_bytes=32 << 20),
        name="prepare",
        **options,
    )(*operands)


def expert_kernel(expert_ref, rows_ref, gate_ref, up_ref, down_ref, out_ref):
    width = gate_ref.shape[0]
    payload = rows_ref[...]
    rows = payload[:, :width]
    tail = payload[:, width:].astype(jnp.float32)
    lane = lax.broadcasted_iota(jnp.int32, tail.shape, 1)
    expert = expert_ref[0]
    experts = expert_ref[1]
    mine = (lane == expert) | (lane == expert + experts)
    weight = jnp.sum(jnp.where(mine, tail, 0.0), axis=1, keepdims=True)
    gate_act = jnp.dot(rows, gate_ref[...], preferred_element_type=jnp.float32)
    up_act = jnp.dot(rows, up_ref[...], preferred_element_type=jnp.float32)
    inner = (gate_act / (1.0 + jnp.exp(-gate_act)) * up_act).astype(jnp.bfloat16)
    result = jnp.dot(inner, down_ref[...], preferred_element_type=jnp.float32)
    out_ref[...] = (weight * result).astype(jnp.bfloat16)


def run_expert(expert, rows, gate_weights, up_weights, down_weights):
    total, padded = rows.shape
    width, hidden_units = gate_weights.shape
    tile = 256
    return pl.pallas_call(
        expert_kernel,
        grid_spec=pltpu.PrefetchScalarGridSpec(
            num_scalar_prefetch=1,
            grid=(total // tile,),
            in_specs=[
                pl.BlockSpec((tile, padded), lambda i, e: (i, 0)),
                pl.BlockSpec((width, hidden_units), lambda i, e: (0, 0), pipeline_mode=pl.Buffered(1)),
                pl.BlockSpec((width, hidden_units), lambda i, e: (0, 0), pipeline_mode=pl.Buffered(1)),
                pl.BlockSpec((hidden_units, width), lambda i, e: (0, 0), pipeline_mode=pl.Buffered(1)),
            ],
            out_specs=pl.BlockSpec((tile, width), lambda i, e: (i, 0)),
        ),
        out_shape=jax.ShapeDtypeStruct((total, width), jnp.bfloat16),
        compiler_params=pltpu.CompilerParams(vmem_limit_bytes=48 << 20),
        name="expert",
    )(expert, rows, gate_weights, up_weights, down_weights)


def plane_kernel(cap, piece_rows, block_rows, *refs):
    refs = list(refs)
    ids_ref = refs.pop(0)
    sources = [refs.pop(0) for _ in piece_rows]
    weight_refs = [refs.pop(0) for _ in range(6)]
    targets = [refs.pop(0) for _ in block_rows]
    decodes, rows, weights, downs, slots, inner, results, spread, sums, row_sem, weight_sem, out_sem = refs
    width = sums.shape[1]
    tokens = block_rows[0]
    pair_rows = 2 * tokens
    pair_slots = 2 * cap
    few = decodes.shape[0]
    row_copies = []
    at = 0
    for ref, count in zip(sources, piece_rows):
        if ref is sources[-1]:
            count -= few
            copy = pltpu.make_async_copy(
                ref.at[pl.ds(count, few)], decodes, row_sem.at[len(row_copies)]
            )
            row_copies.append(copy)
        if count:
            copy = pltpu.make_async_copy(
                ref.at[pl.ds(0, count)], rows.at[pl.ds(at, count)], row_sem.at[len(row_copies)]
            )
            row_copies.append(copy)
        at += count
    up_copies = [
        pltpu.make_async_copy(weight_refs[3 * e + i], weights.at[2 * e + i], weight_sem.at[2 * e + i])
        for e in range(2)
        for i in range(2)
    ]
    down_copies = [
        pltpu.make_async_copy(weight_refs[3 * e + 2], downs.at[e], weight_sem.at[4 + e])
        for e in range(2)
    ]
    for copy in row_copies + up_copies + down_copies:
        copy.start()
    for copy in row_copies:
        copy.wait()
    is_first = lax.broadcasted_iota(jnp.int32, (few, 1), 0) == 0
    for j in range(4):
        part = pl.ds(j * tokens, few)
        decode_row = decodes[...].astype(jnp.float32)[j : j + 1]
        kept = rows[part, :].astype(jnp.float32)
        rows[part, :] = jnp.where(is_first, decode_row, kept).astype(jnp.bfloat16)

    experts = ids_ref[2]
    extra = rows.shape[1] - width
    lanes = lax.broadcasted_iota(jnp.int32, (8, extra), 1)
    line = lax.broadcasted_iota(jnp.int32, (8, extra), 0)
    wanted = ((line == 0) & (lanes == ids_ref[0] + 2 * experts)) | (
        (line == 1) & (lanes == ids_ref[1] + 2 * experts)
    )
    wanted = jnp.where(wanted, 1.0, 0.0).astype(jnp.bfloat16)
    pairs = [pl.ds(p * pair_rows, pair_rows) for p in range(2)]

    def shift_of(shape, axis):
        second = lax.broadcasted_iota(jnp.int32, shape, axis) >= tokens
        return jnp.where(second, float(cap), 0.0)

    for p in range(2):
        ranks = lax.dot_general(
            wanted, rows[pairs[p], width:], (((1,), (1,)), ((), ())), preferred_element_type=jnp.float32
        )
        ranks += shift_of(ranks.shape, 1)
        slot = lax.broadcasted_iota(jnp.int32, (2 * pair_slots, pair_rows), 0).astype(jnp.float32)
        taken = (slot == ranks[0:1]) | (slot == ranks[1:2] + float(pair_slots))
        taken = jnp.where(taken, 1.0, 0.0).astype(jnp.bfloat16)
        picked = jnp.dot(taken, rows[pairs[p], :], preferred_element_type=jnp.float32)
        picked = picked.astype(jnp.bfloat16)
        for e in range(2):
            slots[e, pl.ds(p * pair_slots, pair_slots), :] = picked[e * pair_slots : (e + 1) * pair_slots]

    def make_spread(p):
        tail = rows[pairs[p], width:].astype(jnp.float32)
        lane = lax.broadcasted_iota(jnp.int32, tail.shape, 1)
        slot = lax.broadcasted_iota(jnp.int32, (pair_rows, 2 * pair_slots), 1).astype(jnp.float32)
        back = jnp.zeros(slot.shape, jnp.bool_)
        for e in range(2):
            mine = lane == ids_ref[e] + 2 * experts
            rank = jnp.sum(jnp.where(mine, tail, 0.0), axis=1, keepdims=True)
            back = back | (slot == rank + shift_of(rank.shape, 0) + float(e * pair_slots))
        spread[p] = jnp.where(back, 1.0, 0.0).astype(jnp.bfloat16)

    def weight_of(e):
        tail = slots[e, :, width:].astype(jnp.float32)
        lane = lax.broadcasted_iota(jnp.int32, tail.shape, 1)
        mine = (lane == ids_ref[e]) | (lane == ids_ref[e] + experts)
        return jnp.sum(jnp.where(mine, tail, 0.0), axis=1, keepdims=True)

    def product(e, i):
        return jnp.dot(slots[e, :, :width], weights[2 * e + i], preferred_element_type=jnp.float32)

    def activate(e, gate_act, up_act):
        act = gate_act / (1.0 + jnp.exp(-gate_act)) * up_act * weight_of(e)
        inner[e] = act.astype(jnp.bfloat16)

    def finish(e):
        result = jnp.dot(inner[e], downs[e], preferred_element_type=jnp.float32)
        result = result.astype(jnp.bfloat16)
        for p in range(2):
            results[p, pl.ds(e * pair_slots, pair_slots), :] = result[p * pair_slots : (p + 1) * pair_slots]

    up_copies[0].wait()
    gate_0 = product(0, 0)
    make_spread(0)
    up_copies[1].wait()
    up_0 = product(0, 1)
    make_spread(1)
    up_copies[2].wait()
    activate(0, gate_0, up_0)
    gate_1 = product(1, 0)
    up_copies[3].wait()
    up_1 = product(1, 1)
    down_copies[0].wait()
    finish(0)
    activate(1, gate_1, up_1)
    down_copies[1].wait()
    finish(1)
    out_copies = []
    at = 0
    for p in range(2):
        total = jnp.dot(spread[p], results[p], preferred_element_type=jnp.float32)
        sums[pairs[p], :] = total.astype(jnp.bfloat16)
        while len(out_copies) < len(targets) and at < (p + 1) * pair_rows:
            count = block_rows[len(out_copies)]
            copy = pltpu.make_async_copy(
                sums.at[pl.ds(at, count)], targets[len(out_copies)], out_sem.at[len(out_copies)]
            )
            copy.start()
            out_copies.append(copy)
            at += count
    for copy in out_copies:
        copy.wait()


def run_plane(ids, cap, few, pieces, block_rows, weights):
    width, units = weights[0].shape
    padded = pieces[0].shape[1]
    piece_rows = tuple(piece.shape[0] for piece in pieces)
    total = sum(piece_rows) - few
    kept = jnp.bfloat16
    anywhere = pl.BlockSpec(memory_space=pl.ANY)
    return pl.pallas_call(
        functools.partial(plane_kernel, cap, piece_rows, block_rows),
        in_specs=[pl.BlockSpec(memory_space=pltpu.SMEM)] + [anywhere] * (len(pieces) + 6),
        out_specs=[anywhere] * len(block_rows),
        out_shape=[jax.ShapeDtypeStruct((count, width), kept) for count in block_rows],
        scratch_shapes=[
            pltpu.VMEM((few, padded), kept),
            pltpu.VMEM((total, padded), kept),
            pltpu.VMEM((4, width, units), kept),
            pltpu.VMEM((2, units, width), kept),
            pltpu.VMEM((2, 4 * cap, padded), kept),
            pltpu.VMEM((2, 4 * cap, units), kept),
            pltpu.VMEM((2, 4 * cap, width), kept),
            pltpu.VMEM((2, total // 2, 4 * cap), kept),
            pltpu.VMEM((total, width), kept),
            pltpu.SemaphoreType.DMA((len(pieces) + 1,)),
            pltpu.SemaphoreType.DMA((6,)),
            pltpu.SemaphoreType.DMA((len(block_rows),)),
        ],
        compiler_params=pltpu.CompilerParams(vmem_limit_bytes=48 << 20),
        cost_estimate=pl.CostEstimate(
            flops=12 * total * width * units, bytes_accessed=24 << 20, transcendentals=total * units
        ),
        name="plane",
    )(ids, *pieces, *weights)


def merge_kernel(cut, x_ref, y_ref, passed_0_ref, passed_1_ref, x_out, y_out):
    def sum_of(one, other):
        return (one.astype(jnp.float32) + other.astype(jnp.float32)).astype(jnp.bfloat16)

    x_out[:cut, :] = sum_of(x_ref[:cut, :], passed_0_ref[...])
    x_out[cut:, :] = x_ref[cut:, :]
    y_out[:cut, :] = y_ref[:cut, :]
    y_out[cut:, :] = sum_of(y_ref[cut:, :], passed_1_ref[...])


def merge_passed(cut, to_x, to_y, passed_0, passed_1):
    return pl.pallas_call(
        functools.partial(merge_kernel, cut),
        out_shape=[jax.ShapeDtypeStruct(to_x.shape, to_x.dtype)] * 2,
        compiler_params=pltpu.CompilerParams(vmem_limit_bytes=16 << 20),
        name="merge",
    )(to_x, to_y, passed_0, passed_1)


def along_x(value):
    return lax.ppermute(value, "kv", [(i, i ^ 1) for i in range(4)])


def along_y(value):
    return lax.ppermute(value, "kv", [(i, i ^ 2) for i in range(4)])


def around_z(value):
    return lax.ppermute(value, "blk", [(i, (i + 2) % 8) for i in range(8)])


def across_chip(value):
    return lax.ppermute(value, "blk", [(i, i ^ 1) for i in range(8)])


def fence(*values):
    return lax.optimization_barrier(values)


def added(*parts):
    total = parts[0].astype(jnp.float32)
    for part in parts[1:]:
        total = total + part.astype(jnp.float32)
    return total


def permuted_plan(
    queries,
    cache_keys,
    cache_values,
    lengths,
    sinks,
    out_proj,
    decode_resid,
    prefill_hidden,
    norm_gain,
    router,
    routes,
    expert_gate,
    expert_up,
    expert_down,
):
    experts = router.shape[1]
    ids = routes[0]
    tokens = ids.shape[0]
    my_kv = lax.axis_index("kv")
    my_blk = lax.axis_index("blk")
    first_expert = my_kv * 8
    expert_ids = jnp.stack(
        [first_expert + my_blk, first_expert + (my_blk ^ 1), jnp.int32(experts)]
    ).astype(jnp.int32)
    cap = (2 * tokens * ids.shape[1] + experts - 1) // experts
    cut = (tokens // 2 + 15) // 16 * 16
    few = 16

    def spread_sides(block):
        return along_x(block), along_y(block)

    def spread_corner(sides):
        return along_y(sides[0][:cut]), along_x(sides[1][cut:])

    def apply(pieces, counts):
        return run_plane(expert_ids, cap, few, pieces, counts, weights)

    def return_corner(sums):
        return along_y(sums[3]), along_x(sums[4])

    def return_sides(sums, passed=None):
        to_x, to_y = sums[1:3] if passed is None else merge_passed(cut, *sums[1:3], *passed)
        return along_x(to_x), along_y(to_y)

    prefill = prefill_hidden[0]
    block_0 = prepare(prefill, norm_gain, router, ids, "block")
    block_0, queries, cache_keys, expert_gate, expert_up = fence(
        block_0, queries, cache_keys, expert_gate, expert_up
    )
    sides_0 = spread_sides(block_0)
    block_1 = around_z(block_0)
    other_gate = across_chip(expert_gate[0])
    other_up = across_chip(expert_up[0])
    attended = attend(queries, cache_keys, cache_values, lengths, sinks)
    partial_proj = jnp.dot(attended, out_proj, preferred_element_type=jnp.float32)
    is_mine = jnp.arange(4)[:, None] == my_kv
    partial_proj += jnp.where(is_mine, decode_resid.astype(jnp.float32), 0.0)
    width = partial_proj.shape[1]
    ids_row = jnp.pad(ids[:1].astype(jnp.float32), ((0, 0), (0, width - ids.shape[1])))
    shared = jnp.concatenate([partial_proj, jnp.where(is_mine, ids_row, 0.0)], axis=0)
    sides_0, other_gate, shared = fence(sides_0, other_gate, shared)

    shared = shared + along_x(shared)
    corner_0 = spread_corner(sides_0)
    corner_0, block_1, shared, expert_down = fence(corner_0, block_1, shared, expert_down)

    shared = shared + along_y(shared)
    sides_1 = spread_sides(block_1)
    block_2 = around_z(block_1)
    other_down = across_chip(expert_down[0])
    order = [my_kv ^ j for j in range(4)]
    decoded = jnp.concatenate(
        [lax.dynamic_slice_in_dim(shared, index, 1) for index in order], axis=0
    ).astype(jnp.bfloat16)
    decode_ids = jnp.concatenate(
        [lax.dynamic_slice_in_dim(shared, 4 + index, 1) for index in order], axis=0
    )[:, : ids.shape[1]].astype(jnp.int32)
    hidden = jnp.concatenate([decoded[:1], prefill], axis=0)
    decodes_0 = prepare(
        jnp.pad(decoded, ((0, few - 4), (0, 0))),
        norm_gain,
        router,
        jnp.pad(decode_ids, ((0, few - 4), (0, 0))),
        "first",
    )
    sides_1, block_2, decodes_0, other_up, other_down = fence(
        sides_1, block_2, decodes_0, other_up, other_down
    )
    weights = (expert_gate[0], expert_up[0], expert_down[0], other_gate, other_up, other_down)
    halves = (tokens, tokens, tokens, cut, tokens - cut)

    corner_1 = spread_corner(sides_1)
    sides_2 = spread_sides(block_2)
    arrived = around_z(jnp.concatenate([block_2, decodes_0], axis=0))
    sums_0 = apply((block_0,) + sides_0 + corner_0 + (decodes_0,), halves)
    corner_1, sides_2, arrived, sums_0 = fence(corner_1, sides_2, arrived, sums_0)
    block_3, decodes_1 = arrived[:tokens], arrived[tokens:]

    sides_3 = spread_sides(block_3)
    risen_2 = around_z(jnp.concatenate(corner_1 + (decodes_1,), axis=0))
    passed_0 = return_corner(sums_0)
    sums_1 = apply((block_1,) + sides_1 + corner_1 + (decodes_1,), halves)
    sides_3, risen_2, passed_0, sums_0, sums_1 = fence(sides_3, risen_2, passed_0, sums_0, sums_1)

    risen_3 = around_z(risen_2)
    passed_1 = return_corner(sums_1)
    back_0 = return_sides(sums_0, passed_0)
    sums_2 = apply((block_2,) + sides_2 + (risen_2,), (tokens,) * 4)
    risen_3, passed_1, back_0, sums_0, sums_1, sums_2 = fence(
        risen_3, passed_1, back_0, sums_0, sums_1, sums_2
    )

    back_1 = return_sides(sums_1, passed_1)
    risen_sums = around_z(sums_2[3])
    back_2 = return_sides(sums_2)
    layer_sum = added(hidden, sums_0[0], *back_0)
    sums_3 = apply((block_3,) + sides_3 + (risen_3,), (tokens,) * 4)
    back_1, risen_sums, sums_1, sums_2, sums_3 = fence(back_1, risen_sums, sums_1, sums_2, sums_3)

    far = added(sums_3[3], risen_sums).astype(jnp.bfloat16)
    passed_3 = return_corner(tuple(sums_3[:3]) + (far[:cut], far[cut:]))
    carried = around_z(added(sums_1[0], *back_1).astype(jnp.bfloat16))
    back_3 = return_sides(sums_3, passed_3)
    carried = around_z(added(sums_2[0], *back_2, carried).astype(jnp.bfloat16))
    carried = around_z(added(sums_3[0], *back_3, carried).astype(jnp.bfloat16))
    return added(layer_sum, carried).astype(jnp.bfloat16)[None]


def chunk_cuts(tokens, devices):
    step = (tokens // 2 + 15) // 16 * 16 if devices < 128 else 32
    return [(start, min(start + step, tokens)) for start in range(0, tokens, step)]


def gathered_plan(
    queries,
    cache_keys,
    cache_values,
    lengths,
    sinks,
    out_proj,
    decode_resid,
    prefill_hidden,
    norm_gain,
    router,
    routes,
    expert_gate,
    expert_up,
    expert_down,
):
    experts = router.shape[1]
    ids = routes[0]
    tokens = ids.shape[0]
    prefill = prefill_hidden[0]
    devices = lax.axis_size(AXES)
    cuts = chunk_cuts(tokens, devices)
    my_expert = lax.axis_index("kv") * lax.axis_size("blk") + lax.axis_index("blk")
    expert = jnp.stack([my_expert, jnp.int32(experts)]).astype(jnp.int32)
    weights = (expert_gate[0], expert_up[0], expert_down[0])

    attended = attend(queries, cache_keys, cache_values, lengths, sinks)
    partial_proj = jnp.dot(attended, out_proj, preferred_element_type=jnp.float32)
    projected = lax.psum_scatter(partial_proj, "kv", scatter_dimension=0, tiled=True)
    decoded = (decode_resid.astype(jnp.float32) + projected).astype(jnp.bfloat16)
    hidden = jnp.concatenate([prefill, decoded], axis=0)
    ids = jnp.concatenate([ids[1:], ids[:1]], axis=0)
    gathered = []
    for start, stop in cuts:
        source = prefill[start:stop] if stop < tokens else hidden[start:stop]
        sent = prepare(source, norm_gain, router, ids[start:stop])
        gathered.append(lax.all_gather(sent, AXES, axis=0, tiled=True))
    returned = []
    for rows in gathered:
        sums = run_expert(expert, rows, *weights)
        returned.append(lax.psum_scatter(sums, AXES, scatter_dimension=0, tiled=True))
    combined = jnp.concatenate(returned, axis=0)
    layer_sum = (hidden.astype(jnp.float32) + combined.astype(jnp.float32)).astype(jnp.bfloat16)
    layer_sum = jnp.concatenate([layer_sum[-1:], layer_sum[:-1]], axis=0)
    return layer_sum[None]


def solution(mesh):
    plan = permuted_plan if (mesh.shape["kv"], mesh.shape["blk"]) == (4, 8) else gathered_plan
    return jax.shard_map(
        plan,
        mesh=mesh,
        in_specs=(
            P("blk", "kv"),
            P("blk", None, "kv", None),
            P("blk", None, "kv", None),
            P(),
            P("kv"),
            P("kv", None),
            P(("blk", "kv"), None),
            P(("blk", "kv"), None, None),
            P(),
            P(),
            P(("blk", "kv"), None, None),
            P(("kv", "blk"), None, None),
            P(("kv", "blk"), None, None),
            P(("kv", "blk"), None, None),
        ),
        out_specs=P(("blk", "kv"), None, None),
        check_vma=False,
    )
```

```python
import functools
import math

import jax
import jax.numpy as jnp
from jax import lax
from jax.experimental import pallas as pl
from jax.experimental.pallas import tpu as pltpu
from jax.sharding import PartitionSpec as P

NEG_FILL = -1e30
EPSILON = 1e-06
NOT_CHOSEN = -256.0
AXES = ("blk", "kv")


def attend(queries, cache_keys, cache_values, lengths, sinks):
    my_block = lax.axis_index("blk")
    per_block = queries.shape[0]
    head_count = sinks.shape[0]
    head_dim = cache_keys.shape[3]
    window = cache_keys.shape[1]
    grouped_q = queries.reshape(per_block, head_count, head_dim)
    key_rows = cache_keys[:, :, 0, :]
    value_rows = cache_values[:, :, 0, :]
    my_lengths = lax.dynamic_slice_in_dim(lengths, my_block * per_block, per_block)
    scores = jnp.einsum("rgd,rjd->rgj", grouped_q, key_rows, preferred_element_type=jnp.float32) * (
        1.0 / math.sqrt(head_dim)
    )
    first_valid = window - jnp.minimum(my_lengths, window)
    is_valid = (jnp.arange(window, dtype=jnp.int32)[None, :] >= first_valid[:, None])[:, None, :]
    masked = jnp.where(is_valid, scores, NEG_FILL)
    top_limit = jnp.maximum(jnp.max(masked, axis=2), sinks[None, :])
    weights = jnp.where(is_valid, jnp.exp(masked - top_limit[..., None]), 0.0)
    denominator = jnp.sum(weights, axis=2) + jnp.exp(sinks[None, :] - top_limit)
    numerator = jnp.einsum(
        "rgj,rjd->rgd", weights.astype(jnp.bfloat16), value_rows, preferred_element_type=jnp.float32
    )
    return (
        (numerator / denominator[..., None])
        .astype(jnp.bfloat16)
        .reshape(per_block, head_count * head_dim)
    )


def fetched_prepare_kernel(ranking, hidden_in, gain_in, router_in, routes_in, out_ref, *scratch):
    shifted, hidden_ref, gain_ref, router_ref, routes_ref, sems = scratch
    sources = (hidden_in, gain_in, router_in, routes_in)
    targets = (hidden_ref, gain_ref, router_ref, routes_ref)
    copies = [
        pltpu.make_async_copy(source, target, sems.at[i])
        for i, (source, target) in enumerate(zip(sources, targets))
    ]
    for copy in copies:
        copy.start()
    for copy in copies:
        copy.wait()
    prepare_kernel(ranking, *targets, out_ref, shifted)


def prepare_kernel(ranking, hidden_ref, gain_ref, router_ref, routes_ref, out_ref, *scratch):
    experts, width = router_ref.shape
    if scratch:
        (shifted,) = scratch
        shifted[0:1, :] = jnp.zeros((1, width), jnp.float32)
        shifted[1:, :] = hidden_ref[...].astype(jnp.float32)
        hidden = shifted[...]
    else:
        hidden = hidden_ref[...].astype(jnp.float32)
    rows = hidden.shape[0]
    mean_sq = jnp.mean(hidden * hidden, axis=1, keepdims=True)
    normed = (hidden * lax.rsqrt(mean_sq + EPSILON) * gain_ref[...]).astype(jnp.bfloat16)
    out_ref[:, :width] = normed
    by_lanes = (((1,), (1,)), ((), ()))
    logits = lax.dot_general(normed, router_ref[...], by_lanes, preferred_element_type=jnp.float32)
    expert = lax.broadcasted_iota(jnp.int32, (experts, rows), 0)
    routes = routes_ref[...]
    chosen = jnp.zeros(expert.shape, jnp.bool_)
    for k in range(routes.shape[0]):
        chosen = chosen | (expert == routes[k : k + 1, :])
    chosen = jnp.where(chosen, 1.0, 0.0).astype(jnp.bfloat16)
    row = lax.broadcasted_iota(jnp.int32, (rows, rows), 0)
    other = lax.broadcasted_iota(jnp.int32, (rows, rows), 1)

    def of_rows(taken):
        taken = jnp.where(taken, 1.0, 0.0).astype(jnp.bfloat16)
        return lax.dot_general(taken, chosen, by_lanes, preferred_element_type=jnp.float32)

    mine = of_rows(row == other) > 0.5
    top = jnp.max(jnp.where(mine, logits, NEG_FILL), axis=1, keepdims=True)
    raised = jnp.where(mine, jnp.exp(jnp.minimum(logits - top, 0.0)), 0.0)
    gates = raised / jnp.sum(raised, axis=1, keepdims=True)
    high = gates.astype(jnp.bfloat16).astype(jnp.float32)
    parts = [high, gates - high]
    if ranking == "block":
        parts.append(jnp.where(mine, of_rows(other < row), NOT_CHOSEN))
    elif ranking == "first":
        parts.append(jnp.where(mine, 0.0, NOT_CHOSEN))
    rest = out_ref.shape[1] - width - len(parts) * experts
    if rest:
        parts.append(jnp.zeros((rows, rest), jnp.float32))
    out_ref[:, width:] = jnp.concatenate(parts, axis=1).astype(jnp.bfloat16)


def prepare(hidden, norm_gain, router, routes, ranking=None):
    width = hidden.shape[1]
    rows = routes.shape[0]
    extra = -(-(3 if ranking else 2) * router.shape[1] // 128) * 128
    operands = (hidden, norm_gain.reshape(1, width), router.T, routes.T)
    fetched = rows > hidden.shape[0]
    kernel, options = prepare_kernel, {}
    if fetched:
        kernel = fetched_prepare_kernel
        options = dict(
            in_specs=[pl.BlockSpec(memory_space=pltpu.HBM)] * 4,
            scratch_shapes=[pltpu.VMEM((rows, width), jnp.float32)]
            + [pltpu.VMEM(operand.shape, operand.dtype) for operand in operands]
            + [pltpu.SemaphoreType.DMA((4,))],
        )
    return pl.pallas_call(
        functools.partial(kernel, ranking),
        out_shape=jax.ShapeDtypeStruct((rows, width + extra), jnp.bfloat16),
        compiler_params=pltpu.CompilerParams(vmem_limit_bytes=32 << 20),
        name="prepare",
        **options,
    )(*operands)


def expert_kernel(expert_ref, rows_ref, gate_ref, up_ref, down_ref, out_ref):
    width = gate_ref.shape[0]
    payload = rows_ref[...]
    rows = payload[:, :width]
    tail = payload[:, width:].astype(jnp.float32)
    lane = lax.broadcasted_iota(jnp.int32, tail.shape, 1)
    expert = expert_ref[0]
    experts = expert_ref[1]
    mine = (lane == expert) | (lane == expert + experts)
    weight = jnp.sum(jnp.where(mine, tail, 0.0), axis=1, keepdims=True)
    gate_act = jnp.dot(rows, gate_ref[...], preferred_element_type=jnp.float32)
    up_act = jnp.dot(rows, up_ref[...], preferred_element_type=jnp.float32)
    inner = (gate_act / (1.0 + jnp.exp(-gate_act)) * up_act).astype(jnp.bfloat16)
    result = jnp.dot(inner, down_ref[...], preferred_element_type=jnp.float32)
    out_ref[...] = (weight * result).astype(jnp.bfloat16)


def run_expert(expert, rows, gate_weights, up_weights, down_weights):
    total, padded = rows.shape
    width, hidden_units = gate_weights.shape
    tile = 256
    return pl.pallas_call(
        expert_kernel,
        grid_spec=pltpu.PrefetchScalarGridSpec(
            num_scalar_prefetch=1,
            grid=(total // tile,),
            in_specs=[
                pl.BlockSpec((tile, padded), lambda i, e: (i, 0)),
                pl.BlockSpec((width, hidden_units), lambda i, e: (0, 0), pipeline_mode=pl.Buffered(1)),
                pl.BlockSpec((width, hidden_units), lambda i, e: (0, 0), pipeline_mode=pl.Buffered(1)),
                pl.BlockSpec((hidden_units, width), lambda i, e: (0, 0), pipeline_mode=pl.Buffered(1)),
            ],
            out_specs=pl.BlockSpec((tile, width), lambda i, e: (i, 0)),
        ),
        out_shape=jax.ShapeDtypeStruct((total, width), jnp.bfloat16),
        compiler_params=pltpu.CompilerParams(vmem_limit_bytes=48 << 20),
        name="expert",
    )(expert, rows, gate_weights, up_weights, down_weights)


def plane_kernel(cap, piece_rows, block_rows, *refs):
    refs = list(refs)
    ids_ref = refs.pop(0)
    sources = [refs.pop(0) for _ in piece_rows]
    weight_refs = [refs.pop(0) for _ in range(6)]
    targets = [refs.pop(0) for _ in block_rows]
    decodes, rows, weights, downs, slots, inner, results, spread, sums, row_sem, weight_sem, out_sem = refs
    width = sums.shape[1]
    tokens = block_rows[0]
    pair_rows = 2 * tokens
    pair_slots = 2 * cap
    few = decodes.shape[0]
    row_copies = []
    at = 0
    for ref, count in zip(sources, piece_rows):
        if ref is sources[-1]:
            count -= few
            copy = pltpu.make_async_copy(
                ref.at[pl.ds(count, few)], decodes, row_sem.at[len(row_copies)]
            )
            row_copies.append(copy)
        if count:
            copy = pltpu.make_async_copy(
                ref.at[pl.ds(0, count)], rows.at[pl.ds(at, count)], row_sem.at[len(row_copies)]
            )
            row_copies.append(copy)
        at += count
    up_copies = [
        pltpu.make_async_copy(weight_refs[3 * e + i], weights.at[2 * e + i], weight_sem.at[2 * e + i])
        for e in range(2)
        for i in range(2)
    ]
    down_copies = [
        pltpu.make_async_copy(weight_refs[3 * e + 2], downs.at[e], weight_sem.at[4 + e])
        for e in range(2)
    ]
    for copy in row_copies + up_copies + down_copies:
        copy.start()
    for copy in row_copies:
        copy.wait()
    is_first = lax.broadcasted_iota(jnp.int32, (few, 1), 0) == 0
    for j in range(4):
        part = pl.ds(j * tokens, few)
        decode_row = decodes[...].astype(jnp.float32)[j : j + 1]
        kept = rows[part, :].astype(jnp.float32)
        rows[part, :] = jnp.where(is_first, decode_row, kept).astype(jnp.bfloat16)

    experts = ids_ref[2]
    extra = rows.shape[1] - width
    lanes = lax.broadcasted_iota(jnp.int32, (8, extra), 1)
    line = lax.broadcasted_iota(jnp.int32, (8, extra), 0)
    wanted = ((line == 0) & (lanes == ids_ref[0] + 2 * experts)) | (
        (line == 1) & (lanes == ids_ref[1] + 2 * experts)
    )
    wanted = jnp.where(wanted, 1.0, 0.0).astype(jnp.bfloat16)
    pairs = [pl.ds(p * pair_rows, pair_rows) for p in range(2)]

    def shift_of(shape, axis):
        second = lax.broadcasted_iota(jnp.int32, shape, axis) >= tokens
        return jnp.where(second, float(cap), 0.0)

    for p in range(2):
        ranks = lax.dot_general(
            wanted, rows[pairs[p], width:], (((1,), (1,)), ((), ())), preferred_element_type=jnp.float32
        )
        ranks += shift_of(ranks.shape, 1)
        slot = lax.broadcasted_iota(jnp.int32, (2 * pair_slots, pair_rows), 0).astype(jnp.float32)
        taken = (slot == ranks[0:1]) | (slot == ranks[1:2] + float(pair_slots))
        taken = jnp.where(taken, 1.0, 0.0).astype(jnp.bfloat16)
        picked = jnp.dot(taken, rows[pairs[p], :], preferred_element_type=jnp.float32)
        picked = picked.astype(jnp.bfloat16)
        for e in range(2):
            slots[e, pl.ds(p * pair_slots, pair_slots), :] = picked[e * pair_slots : (e + 1) * pair_slots]

    def make_spread(p):
        tail = rows[pairs[p], width:].astype(jnp.float32)
        lane = lax.broadcasted_iota(jnp.int32, tail.shape, 1)
        slot = lax.broadcasted_iota(jnp.int32, (pair_rows, 2 * pair_slots), 1).astype(jnp.float32)
        back = jnp.zeros(slot.shape, jnp.bool_)
        for e in range(2):
            mine = lane == ids_ref[e] + 2 * experts
            rank = jnp.sum(jnp.where(mine, tail, 0.0), axis=1, keepdims=True)
            back = back | (slot == rank + shift_of(rank.shape, 0) + float(e * pair_slots))
        spread[p] = jnp.where(back, 1.0, 0.0).astype(jnp.bfloat16)

    def weight_of(e):
        tail = slots[e, :, width:].astype(jnp.float32)
        lane = lax.broadcasted_iota(jnp.int32, tail.shape, 1)
        mine = (lane == ids_ref[e]) | (lane == ids_ref[e] + experts)
        return jnp.sum(jnp.where(mine, tail, 0.0), axis=1, keepdims=True)

    def product(e, i):
        return jnp.dot(slots[e, :, :width], weights[2 * e + i], preferred_element_type=jnp.float32)

    def activate(e, gate_act, up_act):
        act = gate_act / (1.0 + jnp.exp(-gate_act)) * up_act * weight_of(e)
        inner[e] = act.astype(jnp.bfloat16)

    def finish(e):
        result = jnp.dot(inner[e], downs[e], preferred_element_type=jnp.float32)
        result = result.astype(jnp.bfloat16)
        for p in range(2):
            results[p, pl.ds(e * pair_slots, pair_slots), :] = result[p * pair_slots : (p + 1) * pair_slots]

    up_copies[0].wait()
    gate_0 = product(0, 0)
    make_spread(0)
    up_copies[1].wait()
    up_0 = product(0, 1)
    make_spread(1)
    up_copies[2].wait()
    activate(0, gate_0, up_0)
    gate_1 = product(1, 0)
    up_copies[3].wait()
    up_1 = product(1, 1)
    down_copies[0].wait()
    finish(0)
    activate(1, gate_1, up_1)
    down_copies[1].wait()
    finish(1)
    out_copies = []
    at = 0
    for p in range(2):
        total = jnp.dot(spread[p], results[p], preferred_element_type=jnp.float32)
        sums[pairs[p], :] = total.astype(jnp.bfloat16)
        while len(out_copies) < len(targets) and at < (p + 1) * pair_rows:
            count = block_rows[len(out_copies)]
            copy = pltpu.make_async_copy(
                sums.at[pl.ds(at, count)], targets[len(out_copies)], out_sem.at[len(out_copies)]
            )
            copy.start()
            out_copies.append(copy)
            at += count
    for copy in out_copies:
        copy.wait()


def run_plane(ids, cap, few, pieces, block_rows, weights):
    width, units = weights[0].shape
    padded = pieces[0].shape[1]
    piece_rows = tuple(piece.shape[0] for piece in pieces)
    total = sum(piece_rows) - few
    kept = jnp.bfloat16
    anywhere = pl.BlockSpec(memory_space=pl.ANY)
    return pl.pallas_call(
        functools.partial(plane_kernel, cap, piece_rows, block_rows),
        in_specs=[pl.BlockSpec(memory_space=pltpu.SMEM)] + [anywhere] * (len(pieces) + 6),
        out_specs=[anywhere] * len(block_rows),
        out_shape=[jax.ShapeDtypeStruct((count, width), kept) for count in block_rows],
        scratch_shapes=[
            pltpu.VMEM((few, padded), kept),
            pltpu.VMEM((total, padded), kept),
            pltpu.VMEM((4, width, units), kept),
            pltpu.VMEM((2, units, width), kept),
            pltpu.VMEM((2, 4 * cap, padded), kept),
            pltpu.VMEM((2, 4 * cap, units), kept),
            pltpu.VMEM((2, 4 * cap, width), kept),
            pltpu.VMEM((2, total // 2, 4 * cap), kept),
            pltpu.VMEM((total, width), kept),
            pltpu.SemaphoreType.DMA((len(pieces) + 1,)),
            pltpu.SemaphoreType.DMA((6,)),
            pltpu.SemaphoreType.DMA((len(block_rows),)),
        ],
        compiler_params=pltpu.CompilerParams(vmem_limit_bytes=48 << 20),
        cost_estimate=pl.CostEstimate(
            flops=12 * total * width * units, bytes_accessed=24 << 20, transcendentals=total * units
        ),
        name="plane",
    )(ids, *pieces, *weights)


def merge_kernel(cut, x_ref, y_ref, passed_0_ref, passed_1_ref, x_out, y_out):
    def sum_of(one, other):
        return (one.astype(jnp.float32) + other.astype(jnp.float32)).astype(jnp.bfloat16)

    x_out[:cut, :] = sum_of(x_ref[:cut, :], passed_0_ref[...])
    x_out[cut:, :] = x_ref[cut:, :]
    y_out[:cut, :] = y_ref[:cut, :]
    y_out[cut:, :] = sum_of(y_ref[cut:, :], passed_1_ref[...])


def merge_passed(cut, to_x, to_y, passed_0, passed_1):
    return pl.pallas_call(
        functools.partial(merge_kernel, cut),
        out_shape=[jax.ShapeDtypeStruct(to_x.shape, to_x.dtype)] * 2,
        compiler_params=pltpu.CompilerParams(vmem_limit_bytes=16 << 20),
        name="merge",
    )(to_x, to_y, passed_0, passed_1)


def join_kernel(far_ref, risen_ref, own_ref, x_ref, y_ref, far_out, own_out):
    far_out[...] = (far_ref[...].astype(jnp.float32) + risen_ref[...].astype(jnp.float32)).astype(jnp.bfloat16)
    total = own_ref[...].astype(jnp.float32) + x_ref[...].astype(jnp.float32) + y_ref[...].astype(jnp.float32)
    own_out[...] = total.astype(jnp.bfloat16)


def join(far, risen, own, from_x, from_y):
    return pl.pallas_call(
        join_kernel,
        out_shape=[jax.ShapeDtypeStruct(own.shape, own.dtype)] * 2,
        compiler_params=pltpu.CompilerParams(vmem_limit_bytes=16 << 20),
        name="join",
    )(far, risen, own, from_x, from_y)


def along_x(value):
    return lax.ppermute(value, "kv", [(i, i ^ 1) for i in range(4)])


def along_y(value):
    return lax.ppermute(value, "kv", [(i, i ^ 2) for i in range(4)])


def around_z(value):
    return lax.ppermute(value, "blk", [(i, (i + 2) % 8) for i in range(8)])


def across_chip(value):
    return lax.ppermute(value, "blk", [(i, i ^ 1) for i in range(8)])


def fence(*values):
    return lax.optimization_barrier(values)


def added(*parts):
    total = parts[0].astype(jnp.float32)
    for part in parts[1:]:
        total = total + part.astype(jnp.float32)
    return total


def permuted_plan(
    queries,
    cache_keys,
    cache_values,
    lengths,
    sinks,
    out_proj,
    decode_resid,
    prefill_hidden,
    norm_gain,
    router,
    routes,
    expert_gate,
    expert_up,
    expert_down,
):
    experts = router.shape[1]
    ids = routes[0]
    tokens = ids.shape[0]
    my_kv = lax.axis_index("kv")
    my_blk = lax.axis_index("blk")
    first_expert = my_kv * 8
    expert_ids = jnp.stack(
        [first_expert + my_blk, first_expert + (my_blk ^ 1), jnp.int32(experts)]
    ).astype(jnp.int32)
    cap = (2 * tokens * ids.shape[1] + experts - 1) // experts
    cut = (tokens // 2 + 15) // 16 * 16
    few = 16

    def spread_sides(block):
        return along_x(block), along_y(block)

    def spread_corner(sides):
        return along_y(sides[0][:cut]), along_x(sides[1][cut:])

    def apply(pieces, counts):
        return run_plane(expert_ids, cap, few, pieces, counts, weights)

    def return_corner(sums):
        return along_y(sums[3]), along_x(sums[4])

    def return_sides(sums, passed=None):
        to_x, to_y = sums[1:3] if passed is None else merge_passed(cut, *sums[1:3], *passed)
        return along_x(to_x), along_y(to_y)

    prefill = prefill_hidden[0]
    block_0 = prepare(prefill, norm_gain, router, ids, "block")
    block_0, queries, cache_keys, expert_gate, expert_up = fence(
        block_0, queries, cache_keys, expert_gate, expert_up
    )
    sides_0 = spread_sides(block_0)
    block_1 = around_z(block_0)
    other_gate = across_chip(expert_gate[0])
    other_up = across_chip(expert_up[0])
    attended = attend(queries, cache_keys, cache_values, lengths, sinks)
    partial_proj = jnp.dot(attended, out_proj, preferred_element_type=jnp.float32)
    is_mine = jnp.arange(4)[:, None] == my_kv
    partial_proj += jnp.where(is_mine, decode_resid.astype(jnp.float32), 0.0)
    width = partial_proj.shape[1]
    ids_row = jnp.pad(ids[:1].astype(jnp.float32), ((0, 0), (0, width - ids.shape[1])))
    shared = jnp.concatenate([partial_proj, jnp.where(is_mine, ids_row, 0.0)], axis=0)
    shared = shared + along_x(shared)
    sides_0, block_1, other_gate = fence(sides_0, block_1, other_gate)

    corner_0 = spread_corner(sides_0)
    corner_0, shared = fence(corner_0, shared)

    shared = shared + along_y(shared)
    shared, expert_down = fence(shared, expert_down)
    sides_1 = spread_sides(block_1)
    block_2 = around_z(block_1)
    other_down = across_chip(expert_down[0])
    order = [my_kv ^ j for j in range(4)]
    decoded = jnp.concatenate(
        [lax.dynamic_slice_in_dim(shared, index, 1) for index in order], axis=0
    ).astype(jnp.bfloat16)
    decode_ids = jnp.concatenate(
        [lax.dynamic_slice_in_dim(shared, 4 + index, 1) for index in order], axis=0
    )[:, : ids.shape[1]].astype(jnp.int32)
    hidden = jnp.concatenate([decoded[:1], prefill], axis=0)
    decodes_0 = prepare(
        jnp.pad(decoded, ((0, few - 4), (0, 0))),
        norm_gain,
        router,
        jnp.pad(decode_ids, ((0, few - 4), (0, 0))),
        "first",
    )
    sides_1, block_2, decodes_0, other_up, other_down = fence(
        sides_1, block_2, decodes_0, other_up, other_down
    )
    weights = (expert_gate[0], expert_up[0], expert_down[0], other_gate, other_up, other_down)
    halves = (tokens, tokens, tokens, cut, tokens - cut)

    corner_1 = spread_corner(sides_1)
    sides_2 = spread_sides(block_2)
    arrived = around_z(jnp.concatenate([block_2, decodes_0], axis=0))
    sums_0 = apply((block_0,) + sides_0 + corner_0 + (decodes_0,), halves)
    corner_1, sides_2, arrived, sums_0 = fence(corner_1, sides_2, arrived, sums_0)
    block_3, decodes_1 = arrived[:tokens], arrived[tokens:]

    sides_3 = spread_sides(block_3)
    risen = around_z(jnp.concatenate(corner_1 + (decodes_1,), axis=0))
    passed_0 = return_corner(sums_0)
    sums_1 = apply((block_1,) + sides_1 + corner_1 + (decodes_1,), (tokens,) * 4)
    sides_3, risen, passed_0, sums_0, sums_1 = fence(sides_3, risen, passed_0, sums_0, sums_1)

    decodes_3 = around_z(risen[tokens:])
    decodes_3, far = fence(decodes_3, sums_1[3])
    far = around_z(far)
    corner_3 = spread_corner(sides_3)
    back_1 = return_sides(sums_1)
    sums_2 = apply((block_2,) + sides_2 + (risen,), (tokens,) * 4)
    decodes_3, far, corner_3, back_1, sums_1, sums_2 = fence(
        decodes_3, far, corner_3, back_1, sums_1, sums_2
    )

    far, first = join(sums_2[3], far, sums_1[0], *back_1)
    far = around_z(far)
    back_2 = return_sides(sums_2)
    carried = around_z(first)
    sums_3 = apply((block_3,) + sides_3 + corner_3 + (decodes_3,), (tokens,) * 4)
    far, sums_2, sums_3 = fence(far, sums_2, sums_3)

    far = added(sums_3[3], far).astype(jnp.bfloat16)
    passed_3 = return_corner(tuple(sums_3[:3]) + (far[:cut], far[cut:]))
    back_3 = return_sides(sums_3, passed_3)
    carried = around_z(added(sums_2[0], *back_2, carried).astype(jnp.bfloat16))
    back_3, passed_0, sums_0 = fence(back_3, passed_0, sums_0)
    carried = around_z(added(sums_3[0], *back_3, carried).astype(jnp.bfloat16))
    back_0 = return_sides(sums_0, passed_0)
    return added(hidden, sums_0[0], *back_0, carried).astype(jnp.bfloat16)[None]


def chunk_cuts(tokens, devices):
    step = (tokens // 2 + 15) // 16 * 16 if devices < 128 else 32
    return [(start, min(start + step, tokens)) for start in range(0, tokens, step)]


def gathered_plan(
    queries,
    cache_keys,
    cache_values,
    lengths,
    sinks,
    out_proj,
    decode_resid,
    prefill_hidden,
    norm_gain,
    router,
    routes,
    expert_gate,
    expert_up,
    expert_down,
):
    experts = router.shape[1]
    ids = routes[0]
    tokens = ids.shape[0]
    prefill = prefill_hidden[0]
    devices = lax.axis_size(AXES)
    cuts = chunk_cuts(tokens, devices)
    my_expert = lax.axis_index("kv") * lax.axis_size("blk") + lax.axis_index("blk")
    expert = jnp.stack([my_expert, jnp.int32(experts)]).astype(jnp.int32)
    weights = (expert_gate[0], expert_up[0], expert_down[0])

    attended = attend(queries, cache_keys, cache_values, lengths, sinks)
    partial_proj = jnp.dot(attended, out_proj, preferred_element_type=jnp.float32)
    projected = lax.psum_scatter(partial_proj, "kv", scatter_dimension=0, tiled=True)
    decoded = (decode_resid.astype(jnp.float32) + projected).astype(jnp.bfloat16)
    hidden = jnp.concatenate([prefill, decoded], axis=0)
    ids = jnp.concatenate([ids[1:], ids[:1]], axis=0)
    gathered = []
    for start, stop in cuts:
        source = prefill[start:stop] if stop < tokens else hidden[start:stop]
        sent = prepare(source, norm_gain, router, ids[start:stop])
        gathered.append(lax.all_gather(sent, AXES, axis=0, tiled=True))
    returned = []
    for rows in gathered:
        sums = run_expert(expert, rows, *weights)
        returned.append(lax.psum_scatter(sums, AXES, scatter_dimension=0, tiled=True))
    combined = jnp.concatenate(returned, axis=0)
    layer_sum = (hidden.astype(jnp.float32) + combined.astype(jnp.float32)).astype(jnp.bfloat16)
    layer_sum = jnp.concatenate([layer_sum[-1:], layer_sum[:-1]], axis=0)
    return layer_sum[None]


def solution(mesh):
    plan = permuted_plan if (mesh.shape["kv"], mesh.shape["blk"]) == (4, 8) else gathered_plan
    return jax.shard_map(
        plan,
        mesh=mesh,
        in_specs=(
            P("blk", "kv"),
            P("blk", None, "kv", None),
            P("blk", None, "kv", None),
            P(),
            P("kv"),
            P("kv", None),
            P(("blk", "kv"), None),
            P(("blk", "kv"), None, None),
            P(),
            P(),
            P(("blk", "kv"), None, None),
            P(("kv", "blk"), None, None),
            P(("kv", "blk"), None, None),
            P(("kv", "blk"), None, None),
        ),
        out_specs=P(("blk", "kv"), None, None),
        check_vma=False,
    )
```

```python
import functools
import math

import jax
import jax.numpy as jnp
from jax import lax
from jax.experimental import pallas as pl
from jax.experimental.pallas import tpu as pltpu
from jax.sharding import PartitionSpec as P

NEG_FILL = -1e30
EPSILON = 1e-06
NOT_CHOSEN = -256.0
AXES = ("blk", "kv")


def attend(queries, cache_keys, cache_values, lengths, sinks):
    my_block = lax.axis_index("blk")
    per_block = queries.shape[0]
    head_count = sinks.shape[0]
    head_dim = cache_keys.shape[3]
    window = cache_keys.shape[1]
    grouped_q = queries.reshape(per_block, head_count, head_dim)
    key_rows = cache_keys[:, :, 0, :]
    value_rows = cache_values[:, :, 0, :]
    my_lengths = lax.dynamic_slice_in_dim(lengths, my_block * per_block, per_block)
    scores = jnp.einsum("rgd,rjd->rgj", grouped_q, key_rows, preferred_element_type=jnp.float32) * (
        1.0 / math.sqrt(head_dim)
    )
    first_valid = window - jnp.minimum(my_lengths, window)
    is_valid = (jnp.arange(window, dtype=jnp.int32)[None, :] >= first_valid[:, None])[:, None, :]
    masked = jnp.where(is_valid, scores, NEG_FILL)
    top_limit = jnp.maximum(jnp.max(masked, axis=2), sinks[None, :])
    weights = jnp.where(is_valid, jnp.exp(masked - top_limit[..., None]), 0.0)
    denominator = jnp.sum(weights, axis=2) + jnp.exp(sinks[None, :] - top_limit)
    numerator = jnp.einsum(
        "rgj,rjd->rgd", weights.astype(jnp.bfloat16), value_rows, preferred_element_type=jnp.float32
    )
    return (
        (numerator / denominator[..., None])
        .astype(jnp.bfloat16)
        .reshape(per_block, head_count * head_dim)
    )


def fetched_prepare_kernel(ranking, hidden_in, gain_in, router_in, routes_in, out_ref, *scratch):
    shifted, hidden_ref, gain_ref, router_ref, routes_ref, sems = scratch
    sources = (hidden_in, gain_in, router_in, routes_in)
    targets = (hidden_ref, gain_ref, router_ref, routes_ref)
    copies = [
        pltpu.make_async_copy(source, target, sems.at[i])
        for i, (source, target) in enumerate(zip(sources, targets))
    ]
    for copy in copies:
        copy.start()
    for copy in copies:
        copy.wait()
    prepare_kernel(ranking, *targets, out_ref, shifted)


def prepare_kernel(ranking, hidden_ref, gain_ref, router_ref, routes_ref, out_ref, *scratch):
    experts, width = router_ref.shape
    if scratch:
        (shifted,) = scratch
        shifted[0:1, :] = jnp.zeros((1, width), jnp.float32)
        shifted[1:, :] = hidden_ref[...].astype(jnp.float32)
        hidden = shifted[...]
    else:
        hidden = hidden_ref[...].astype(jnp.float32)
    rows = hidden.shape[0]
    mean_sq = jnp.mean(hidden * hidden, axis=1, keepdims=True)
    normed = (hidden * lax.rsqrt(mean_sq + EPSILON) * gain_ref[...]).astype(jnp.bfloat16)
    out_ref[:, :width] = normed
    by_lanes = (((1,), (1,)), ((), ()))
    logits = lax.dot_general(normed, router_ref[...], by_lanes, preferred_element_type=jnp.float32)
    expert = lax.broadcasted_iota(jnp.int32, (experts, rows), 0)
    routes = routes_ref[...]
    chosen = jnp.zeros(expert.shape, jnp.bool_)
    for k in range(routes.shape[0]):
        chosen = chosen | (expert == routes[k : k + 1, :])
    chosen = jnp.where(chosen, 1.0, 0.0).astype(jnp.bfloat16)
    row = lax.broadcasted_iota(jnp.int32, (rows, rows), 0)
    other = lax.broadcasted_iota(jnp.int32, (rows, rows), 1)

    def of_rows(taken):
        taken = jnp.where(taken, 1.0, 0.0).astype(jnp.bfloat16)
        return lax.dot_general(taken, chosen, by_lanes, preferred_element_type=jnp.float32)

    mine = of_rows(row == other) > 0.5
    top = jnp.max(jnp.where(mine, logits, NEG_FILL), axis=1, keepdims=True)
    raised = jnp.where(mine, jnp.exp(jnp.minimum(logits - top, 0.0)), 0.0)
    gates = raised / jnp.sum(raised, axis=1, keepdims=True)
    high = gates.astype(jnp.bfloat16).astype(jnp.float32)
    parts = [high, gates - high]
    if ranking == "block":
        parts.append(jnp.where(mine, of_rows(other < row), NOT_CHOSEN))
    elif ranking == "first":
        parts.append(jnp.where(mine, 0.0, NOT_CHOSEN))
    rest = out_ref.shape[1] - width - len(parts) * experts
    if rest:
        parts.append(jnp.zeros((rows, rest), jnp.float32))
    out_ref[:, width:] = jnp.concatenate(parts, axis=1).astype(jnp.bfloat16)


def prepare(hidden, norm_gain, router, routes, ranking=None):
    width = hidden.shape[1]
    rows = routes.shape[0]
    extra = -(-(3 if ranking else 2) * router.shape[1] // 128) * 128
    operands = (hidden, norm_gain.reshape(1, width), router.T, routes.T)
    fetched = rows > hidden.shape[0]
    kernel, options = prepare_kernel, {}
    if fetched:
        kernel = fetched_prepare_kernel
        options = dict(
            in_specs=[pl.BlockSpec(memory_space=pltpu.HBM)] * 4,
            scratch_shapes=[pltpu.VMEM((rows, width), jnp.float32)]
            + [pltpu.VMEM(operand.shape, operand.dtype) for operand in operands]
            + [pltpu.SemaphoreType.DMA((4,))],
        )
    return pl.pallas_call(
        functools.partial(kernel, ranking),
        out_shape=jax.ShapeDtypeStruct((rows, width + extra), jnp.bfloat16),
        compiler_params=pltpu.CompilerParams(vmem_limit_bytes=32 << 20),
        name="prepare",
        **options,
    )(*operands)


def expert_kernel(expert_ref, rows_ref, gate_ref, up_ref, down_ref, out_ref):
    width = gate_ref.shape[0]
    payload = rows_ref[...]
    rows = payload[:, :width]
    tail = payload[:, width:].astype(jnp.float32)
    lane = lax.broadcasted_iota(jnp.int32, tail.shape, 1)
    expert = expert_ref[0]
    experts = expert_ref[1]
    mine = (lane == expert) | (lane == expert + experts)
    weight = jnp.sum(jnp.where(mine, tail, 0.0), axis=1, keepdims=True)
    gate_act = jnp.dot(rows, gate_ref[...], preferred_element_type=jnp.float32)
    up_act = jnp.dot(rows, up_ref[...], preferred_element_type=jnp.float32)
    inner = (gate_act / (1.0 + jnp.exp(-gate_act)) * up_act).astype(jnp.bfloat16)
    result = jnp.dot(inner, down_ref[...], preferred_element_type=jnp.float32)
    out_ref[...] = (weight * result).astype(jnp.bfloat16)


def run_expert(expert, rows, gate_weights, up_weights, down_weights):
    total, padded = rows.shape
    width, hidden_units = gate_weights.shape
    tile = 256
    return pl.pallas_call(
        expert_kernel,
        grid_spec=pltpu.PrefetchScalarGridSpec(
            num_scalar_prefetch=1,
            grid=(total // tile,),
            in_specs=[
                pl.BlockSpec((tile, padded), lambda i, e: (i, 0)),
                pl.BlockSpec((width, hidden_units), lambda i, e: (0, 0), pipeline_mode=pl.Buffered(1)),
                pl.BlockSpec((width, hidden_units), lambda i, e: (0, 0), pipeline_mode=pl.Buffered(1)),
                pl.BlockSpec((hidden_units, width), lambda i, e: (0, 0), pipeline_mode=pl.Buffered(1)),
            ],
            out_specs=pl.BlockSpec((tile, width), lambda i, e: (i, 0)),
        ),
        out_shape=jax.ShapeDtypeStruct((total, width), jnp.bfloat16),
        compiler_params=pltpu.CompilerParams(vmem_limit_bytes=48 << 20),
        name="expert",
    )(expert, rows, gate_weights, up_weights, down_weights)


def plane_kernel(cap, piece_rows, block_rows, *refs):
    refs = list(refs)
    ids_ref = refs.pop(0)
    sources = [refs.pop(0) for _ in piece_rows]
    weight_refs = [refs.pop(0) for _ in range(6)]
    targets = [refs.pop(0) for _ in block_rows]
    decodes, rows, weights, downs, slots, inner, results, spread, sums, row_sem, weight_sem, out_sem = refs
    width = sums.shape[1]
    tokens = block_rows[0]
    pair_rows = 2 * tokens
    pair_slots = 2 * cap
    few = decodes.shape[0]
    row_copies = []
    at = 0
    for ref, count in zip(sources, piece_rows):
        if ref is sources[-1]:
            count -= few
            copy = pltpu.make_async_copy(
                ref.at[pl.ds(count, few)], decodes, row_sem.at[len(row_copies)]
            )
            row_copies.append(copy)
        if count:
            copy = pltpu.make_async_copy(
                ref.at[pl.ds(0, count)], rows.at[pl.ds(at, count)], row_sem.at[len(row_copies)]
            )
            row_copies.append(copy)
        at += count
    up_copies = [
        pltpu.make_async_copy(weight_refs[3 * e + i], weights.at[2 * e + i], weight_sem.at[2 * e + i])
        for e in range(2)
        for i in range(2)
    ]
    down_copies = [
        pltpu.make_async_copy(weight_refs[3 * e + 2], downs.at[e], weight_sem.at[4 + e])
        for e in range(2)
    ]
    for copy in row_copies + up_copies + down_copies:
        copy.start()
    for copy in row_copies:
        copy.wait()
    is_first = lax.broadcasted_iota(jnp.int32, (few, 1), 0) == 0
    for j in range(4):
        part = pl.ds(j * tokens, few)
        decode_row = decodes[...].astype(jnp.float32)[j : j + 1]
        kept = rows[part, :].astype(jnp.float32)
        rows[part, :] = jnp.where(is_first, decode_row, kept).astype(jnp.bfloat16)

    experts = ids_ref[2]
    extra = rows.shape[1] - width
    lanes = lax.broadcasted_iota(jnp.int32, (8, extra), 1)
    line = lax.broadcasted_iota(jnp.int32, (8, extra), 0)
    wanted = ((line == 0) & (lanes == ids_ref[0] + 2 * experts)) | (
        (line == 1) & (lanes == ids_ref[1] + 2 * experts)
    )
    wanted = jnp.where(wanted, 1.0, 0.0).astype(jnp.bfloat16)
    pairs = [pl.ds(p * pair_rows, pair_rows) for p in range(2)]

    def shift_of(shape, axis):
        second = lax.broadcasted_iota(jnp.int32, shape, axis) >= tokens
        return jnp.where(second, float(cap), 0.0)

    for p in range(2):
        ranks = lax.dot_general(
            wanted, rows[pairs[p], width:], (((1,), (1,)), ((), ())), preferred_element_type=jnp.float32
        )
        ranks += shift_of(ranks.shape, 1)
        slot = lax.broadcasted_iota(jnp.int32, (2 * pair_slots, pair_rows), 0).astype(jnp.float32)
        taken = (slot == ranks[0:1]) | (slot == ranks[1:2] + float(pair_slots))
        taken = jnp.where(taken, 1.0, 0.0).astype(jnp.bfloat16)
        picked = jnp.dot(taken, rows[pairs[p], :], preferred_element_type=jnp.float32)
        picked = picked.astype(jnp.bfloat16)
        for e in range(2):
            slots[e, pl.ds(p * pair_slots, pair_slots), :] = picked[e * pair_slots : (e + 1) * pair_slots]

    def make_spread(p):
        tail = rows[pairs[p], width:].astype(jnp.float32)
        lane = lax.broadcasted_iota(jnp.int32, tail.shape, 1)
        slot = lax.broadcasted_iota(jnp.int32, (pair_rows, 2 * pair_slots), 1).astype(jnp.float32)
        back = jnp.zeros(slot.shape, jnp.bool_)
        for e in range(2):
            mine = lane == ids_ref[e] + 2 * experts
            rank = jnp.sum(jnp.where(mine, tail, 0.0), axis=1, keepdims=True)
            back = back | (slot == rank + shift_of(rank.shape, 0) + float(e * pair_slots))
        spread[p] = jnp.where(back, 1.0, 0.0).astype(jnp.bfloat16)

    def weight_of(e):
        tail = slots[e, :, width:].astype(jnp.float32)
        lane = lax.broadcasted_iota(jnp.int32, tail.shape, 1)
        mine = (lane == ids_ref[e]) | (lane == ids_ref[e] + experts)
        return jnp.sum(jnp.where(mine, tail, 0.0), axis=1, keepdims=True)

    def product(e, i):
        return jnp.dot(slots[e, :, :width], weights[2 * e + i], preferred_element_type=jnp.float32)

    def activate(e, gate_act, up_act):
        act = gate_act / (1.0 + jnp.exp(-gate_act)) * up_act * weight_of(e)
        inner[e] = act.astype(jnp.bfloat16)

    def finish(e):
        result = jnp.dot(inner[e], downs[e], preferred_element_type=jnp.float32)
        result = result.astype(jnp.bfloat16)
        for p in range(2):
            results[p, pl.ds(e * pair_slots, pair_slots), :] = result[p * pair_slots : (p + 1) * pair_slots]

    up_copies[0].wait()
    gate_0 = product(0, 0)
    make_spread(0)
    up_copies[1].wait()
    up_0 = product(0, 1)
    make_spread(1)
    up_copies[2].wait()
    activate(0, gate_0, up_0)
    gate_1 = product(1, 0)
    up_copies[3].wait()
    up_1 = product(1, 1)
    down_copies[0].wait()
    finish(0)
    activate(1, gate_1, up_1)
    down_copies[1].wait()
    finish(1)
    out_copies = []
    at = 0
    for p in range(2):
        total = jnp.dot(spread[p], results[p], preferred_element_type=jnp.float32)
        sums[pairs[p], :] = total.astype(jnp.bfloat16)
        while len(out_copies) < len(targets) and at < (p + 1) * pair_rows:
            count = block_rows[len(out_copies)]
            copy = pltpu.make_async_copy(
                sums.at[pl.ds(at, count)], targets[len(out_copies)], out_sem.at[len(out_copies)]
            )
            copy.start()
            out_copies.append(copy)
            at += count
    for copy in out_copies:
        copy.wait()


def run_plane(ids, cap, few, pieces, block_rows, weights):
    width, units = weights[0].shape
    padded = pieces[0].shape[1]
    piece_rows = tuple(piece.shape[0] for piece in pieces)
    total = sum(piece_rows) - few
    kept = jnp.bfloat16
    anywhere = pl.BlockSpec(memory_space=pl.ANY)
    return pl.pallas_call(
        functools.partial(plane_kernel, cap, piece_rows, block_rows),
        in_specs=[pl.BlockSpec(memory_space=pltpu.SMEM)] + [anywhere] * (len(pieces) + 6),
        out_specs=[anywhere] * len(block_rows),
        out_shape=[jax.ShapeDtypeStruct((count, width), kept) for count in block_rows],
        scratch_shapes=[
            pltpu.VMEM((few, padded), kept),
            pltpu.VMEM((total, padded), kept),
            pltpu.VMEM((4, width, units), kept),
            pltpu.VMEM((2, units, width), kept),
            pltpu.VMEM((2, 4 * cap, padded), kept),
            pltpu.VMEM((2, 4 * cap, units), kept),
            pltpu.VMEM((2, 4 * cap, width), kept),
            pltpu.VMEM((2, total // 2, 4 * cap), kept),
            pltpu.VMEM((total, width), kept),
            pltpu.SemaphoreType.DMA((len(pieces) + 1,)),
            pltpu.SemaphoreType.DMA((6,)),
            pltpu.SemaphoreType.DMA((len(block_rows),)),
        ],
        compiler_params=pltpu.CompilerParams(vmem_limit_bytes=48 << 20),
        cost_estimate=pl.CostEstimate(
            flops=12 * total * width * units, bytes_accessed=24 << 20, transcendentals=total * units
        ),
        name="plane",
    )(ids, *pieces, *weights)


def merge_kernel(cut, x_ref, y_ref, passed_0_ref, passed_1_ref, x_out, y_out):
    def sum_of(one, other):
        return (one.astype(jnp.float32) + other.astype(jnp.float32)).astype(jnp.bfloat16)

    x_out[:cut, :] = sum_of(x_ref[:cut, :], passed_0_ref[...])
    x_out[cut:, :] = x_ref[cut:, :]
    y_out[:cut, :] = y_ref[:cut, :]
    y_out[cut:, :] = sum_of(y_ref[cut:, :], passed_1_ref[...])


def merge_passed(cut, to_x, to_y, passed_0, passed_1):
    return pl.pallas_call(
        functools.partial(merge_kernel, cut),
        out_shape=[jax.ShapeDtypeStruct(to_x.shape, to_x.dtype)] * 2,
        compiler_params=pltpu.CompilerParams(vmem_limit_bytes=16 << 20),
        name="merge",
    )(to_x, to_y, passed_0, passed_1)


def join_kernel(far_ref, risen_ref, own_ref, x_ref, y_ref, far_out, own_out):
    far_out[...] = (far_ref[...].astype(jnp.float32) + risen_ref[...].astype(jnp.float32)).astype(jnp.bfloat16)
    total = own_ref[...].astype(jnp.float32) + x_ref[...].astype(jnp.float32) + y_ref[...].astype(jnp.float32)
    own_out[...] = total.astype(jnp.bfloat16)


def join(far, risen, own, from_x, from_y):
    return pl.pallas_call(
        join_kernel,
        out_shape=[jax.ShapeDtypeStruct(own.shape, own.dtype)] * 2,
        compiler_params=pltpu.CompilerParams(vmem_limit_bytes=16 << 20),
        name="join",
    )(far, risen, own, from_x, from_y)


def along_x(value):
    return lax.ppermute(value, "kv", [(i, i ^ 1) for i in range(4)])


def along_y(value):
    return lax.ppermute(value, "kv", [(i, i ^ 2) for i in range(4)])


def around_z(value, hops=1):
    return lax.ppermute(value, "blk", [(i, (i + 2 * hops) % 8) for i in range(8)])


def across_chip(value):
    return lax.ppermute(value, "blk", [(i, i ^ 1) for i in range(8)])


def fence(*values):
    return lax.optimization_barrier(values)


def added(*parts):
    total = parts[0].astype(jnp.float32)
    for part in parts[1:]:
        total = total + part.astype(jnp.float32)
    return total


def permuted_plan(
    queries,
    cache_keys,
    cache_values,
    lengths,
    sinks,
    out_proj,
    decode_resid,
    prefill_hidden,
    norm_gain,
    router,
    routes,
    expert_gate,
    expert_up,
    expert_down,
):
    experts = router.shape[1]
    ids = routes[0]
    tokens = ids.shape[0]
    my_kv = lax.axis_index("kv")
    my_blk = lax.axis_index("blk")
    first_expert = my_kv * 8
    expert_ids = jnp.stack(
        [first_expert + my_blk, first_expert + (my_blk ^ 1), jnp.int32(experts)]
    ).astype(jnp.int32)
    cap = (2 * tokens * ids.shape[1] + experts - 1) // experts
    cut = (tokens // 2 + 15) // 16 * 16
    few = 16

    def spread_sides(block):
        return along_x(block), along_y(block)

    def spread_corner(sides):
        return along_y(sides[0][:cut]), along_x(sides[1][cut:])

    def apply(pieces, counts):
        return run_plane(expert_ids, cap, few, pieces, counts, weights)

    def return_corner(sums):
        return along_y(sums[3]), along_x(sums[4])

    def return_sides(sums, passed=None):
        to_x, to_y = sums[1:3] if passed is None else merge_passed(cut, *sums[1:3], *passed)
        return along_x(to_x), along_y(to_y)

    prefill = prefill_hidden[0]
    block_0 = prepare(prefill, norm_gain, router, ids, "block")
    block_0, queries, cache_keys, expert_gate = fence(block_0, queries, cache_keys, expert_gate)
    sides_0 = spread_sides(block_0)
    block_1 = around_z(block_0)
    other_gate = across_chip(expert_gate[0])
    attended = attend(queries, cache_keys, cache_values, lengths, sinks)
    partial_proj = jnp.dot(attended, out_proj, preferred_element_type=jnp.float32)
    is_mine = jnp.arange(4)[:, None] == my_kv
    partial_proj += jnp.where(is_mine, decode_resid.astype(jnp.float32), 0.0)
    width = partial_proj.shape[1]
    ids_row = jnp.pad(ids[:1].astype(jnp.float32), ((0, 0), (0, width - ids.shape[1])))
    shared = jnp.concatenate([partial_proj, jnp.where(is_mine, ids_row, 0.0)], axis=0)
    sides_0, block_1, other_gate, expert_up, shared = fence(
        sides_0, block_1, other_gate, expert_up, shared
    )

    shared = shared + along_x(shared)
    corner_0 = spread_corner(sides_0)
    other_up = across_chip(expert_up[0])
    corner_0, shared, block_1, other_up, expert_down = fence(
        corner_0, shared, block_1, other_up, expert_down
    )

    shared = shared + along_y(shared)
    sides_1 = spread_sides(block_1)
    block_2 = around_z(block_1)
    other_down = across_chip(expert_down[0])
    order = [my_kv ^ j for j in range(4)]
    decoded = jnp.concatenate(
        [lax.dynamic_slice_in_dim(shared, index, 1) for index in order], axis=0
    ).astype(jnp.bfloat16)
    decode_ids = jnp.concatenate(
        [lax.dynamic_slice_in_dim(shared, 4 + index, 1) for index in order], axis=0
    )[:, : ids.shape[1]].astype(jnp.int32)
    hidden = jnp.concatenate([decoded[:1], prefill], axis=0)
    decodes_0 = prepare(
        jnp.pad(decoded, ((0, few - 4), (0, 0))),
        norm_gain,
        router,
        jnp.pad(decode_ids, ((0, few - 4), (0, 0))),
        "first",
    )
    sides_1, block_2, decodes_0, other_down = fence(sides_1, block_2, decodes_0, other_down)
    weights = (expert_gate[0], expert_up[0], expert_down[0], other_gate, other_up, other_down)
    halves = (tokens, tokens, tokens, cut, tokens - cut)

    corner_1 = spread_corner(sides_1)
    sides_2 = spread_sides(block_2)
    arrived = around_z(jnp.concatenate([block_2, decodes_0], axis=0))
    sums_0 = apply((block_0,) + sides_0 + corner_0 + (decodes_0,), halves)
    corner_1, sides_2, arrived, sums_0 = fence(corner_1, sides_2, arrived, sums_0)
    block_3, decodes_1 = arrived[:tokens], arrived[tokens:]

    sides_3 = spread_sides(block_3)
    risen = around_z(jnp.concatenate(corner_1 + (decodes_1,), axis=0))
    passed_0 = return_corner(sums_0)
    sums_1 = apply((block_1,) + sides_1 + corner_1 + (decodes_1,), (tokens,) * 4)
    sides_3, risen, passed_0, sums_0, sums_1 = fence(sides_3, risen, passed_0, sums_0, sums_1)

    decodes_3 = around_z(risen[tokens:])
    decodes_3, far = fence(decodes_3, sums_1[3])
    far = around_z(far)
    corner_3 = spread_corner(sides_3)
    back_1 = return_sides(sums_1)
    sums_2 = apply((block_2,) + sides_2 + (risen,), (tokens,) * 4)
    decodes_3, far, corner_3, back_1, sums_1, sums_2 = fence(
        decodes_3, far, corner_3, back_1, sums_1, sums_2
    )

    far, first = join(sums_2[3], far, sums_1[0], *back_1)
    far = around_z(far)
    back_2 = return_sides(sums_2)
    carried_1 = around_z(first, -1)
    sums_3 = apply((block_3,) + sides_3 + corner_3 + (decodes_3,), (tokens,) * 4)
    far, sums_2, sums_3 = fence(far, sums_2, sums_3)

    far = added(sums_3[3], far).astype(jnp.bfloat16)
    passed_3 = return_corner(tuple(sums_3[:3]) + (far[:cut], far[cut:]))
    passed_3, passed_0, sums_0 = fence(passed_3, passed_0, sums_0)
    back_3 = return_sides(sums_3, passed_3)
    carried = around_z(added(sums_2[0], *back_2).astype(jnp.bfloat16))
    back_3, carried_1 = fence(back_3, carried_1)
    carried = around_z(added(sums_3[0], *back_3, carried).astype(jnp.bfloat16))
    back_0 = return_sides(sums_0, passed_0)
    return added(hidden, sums_0[0], carried_1, *back_0, carried).astype(jnp.bfloat16)[None]


def chunk_cuts(tokens, devices):
    step = (tokens // 2 + 15) // 16 * 16 if devices < 128 else 32
    return [(start, min(start + step, tokens)) for start in range(0, tokens, step)]


def gathered_plan(
    queries,
    cache_keys,
    cache_values,
    lengths,
    sinks,
    out_proj,
    decode_resid,
    prefill_hidden,
    norm_gain,
    router,
    routes,
    expert_gate,
    expert_up,
    expert_down,
):
    experts = router.shape[1]
    ids = routes[0]
    tokens = ids.shape[0]
    prefill = prefill_hidden[0]
    devices = lax.axis_size(AXES)
    cuts = chunk_cuts(tokens, devices)
    my_expert = lax.axis_index("kv") * lax.axis_size("blk") + lax.axis_index("blk")
    expert = jnp.stack([my_expert, jnp.int32(experts)]).astype(jnp.int32)
    weights = (expert_gate[0], expert_up[0], expert_down[0])

    attended = attend(queries, cache_keys, cache_values, lengths, sinks)
    partial_proj = jnp.dot(attended, out_proj, preferred_element_type=jnp.float32)
    projected = lax.psum_scatter(partial_proj, "kv", scatter_dimension=0, tiled=True)
    decoded = (decode_resid.astype(jnp.float32) + projected).astype(jnp.bfloat16)
    hidden = jnp.concatenate([prefill, decoded], axis=0)
    ids = jnp.concatenate([ids[1:], ids[:1]], axis=0)
    gathered = []
    for start, stop in cuts:
        source = prefill[start:stop] if stop < tokens else hidden[start:stop]
        sent = prepare(source, norm_gain, router, ids[start:stop])
        gathered.append(lax.all_gather(sent, AXES, axis=0, tiled=True))
    returned = []
    for rows in gathered:
        sums = run_expert(expert, rows, *weights)
        returned.append(lax.psum_scatter(sums, AXES, scatter_dimension=0, tiled=True))
    combined = jnp.concatenate(returned, axis=0)
    layer_sum = (hidden.astype(jnp.float32) + combined.astype(jnp.float32)).astype(jnp.bfloat16)
    layer_sum = jnp.concatenate([layer_sum[-1:], layer_sum[:-1]], axis=0)
    return layer_sum[None]


def solution(mesh):
    plan = permuted_plan if (mesh.shape["kv"], mesh.shape["blk"]) == (4, 8) else gathered_plan
    return jax.shard_map(
        plan,
        mesh=mesh,
        in_specs=(
            P("blk", "kv"),
            P("blk", None, "kv", None),
            P("blk", None, "kv", None),
            P(),
            P("kv"),
            P("kv", None),
            P(("blk", "kv"), None),
            P(("blk", "kv"), None, None),
            P(),
            P(),
            P(("blk", "kv"), None, None),
            P(("kv", "blk"), None, None),
            P(("kv", "blk"), None, None),
            P(("kv", "blk"), None, None),
        ),
        out_specs=P(("blk", "kv"), None, None),
        check_vma=False,
    )
```

```python
import functools
import math

import jax
import jax.numpy as jnp
from jax import lax
from jax.experimental import pallas as pl
from jax.experimental.pallas import tpu as pltpu
from jax.sharding import PartitionSpec as P

NEG_FILL = -1e30
EPSILON = 1e-06
NOT_CHOSEN = -256.0
AXES = ("blk", "kv")


def attend(queries, cache_keys, cache_values, lengths, sinks):
    my_block = lax.axis_index("blk")
    per_block = queries.shape[0]
    head_count = sinks.shape[0]
    head_dim = cache_keys.shape[3]
    window = cache_keys.shape[1]
    grouped_q = queries.reshape(per_block, head_count, head_dim)
    key_rows = cache_keys[:, :, 0, :]
    value_rows = cache_values[:, :, 0, :]
    my_lengths = lax.dynamic_slice_in_dim(lengths, my_block * per_block, per_block)
    scores = jnp.einsum("rgd,rjd->rgj", grouped_q, key_rows, preferred_element_type=jnp.float32) * (
        1.0 / math.sqrt(head_dim)
    )
    first_valid = window - jnp.minimum(my_lengths, window)
    is_valid = (jnp.arange(window, dtype=jnp.int32)[None, :] >= first_valid[:, None])[:, None, :]
    masked = jnp.where(is_valid, scores, NEG_FILL)
    top_limit = jnp.maximum(jnp.max(masked, axis=2), sinks[None, :])
    weights = jnp.where(is_valid, jnp.exp(masked - top_limit[..., None]), 0.0)
    denominator = jnp.sum(weights, axis=2) + jnp.exp(sinks[None, :] - top_limit)
    numerator = jnp.einsum(
        "rgj,rjd->rgd", weights.astype(jnp.bfloat16), value_rows, preferred_element_type=jnp.float32
    )
    return (
        (numerator / denominator[..., None])
        .astype(jnp.bfloat16)
        .reshape(per_block, head_count * head_dim)
    )


def fetched_prepare_kernel(ranking, hidden_in, gain_in, router_in, routes_in, out_ref, *scratch):
    shifted, hidden_ref, gain_ref, router_ref, routes_ref, sems = scratch
    sources = (hidden_in, gain_in, router_in, routes_in)
    targets = (hidden_ref, gain_ref, router_ref, routes_ref)
    copies = [
        pltpu.make_async_copy(source, target, sems.at[i])
        for i, (source, target) in enumerate(zip(sources, targets))
    ]
    for copy in copies:
        copy.start()
    for copy in copies:
        copy.wait()
    prepare_kernel(ranking, *targets, out_ref, shifted)


def prepare_kernel(ranking, hidden_ref, gain_ref, router_ref, routes_ref, out_ref, *scratch):
    experts, width = router_ref.shape
    if scratch:
        (shifted,) = scratch
        shifted[0:1, :] = jnp.zeros((1, width), jnp.float32)
        shifted[1:, :] = hidden_ref[...].astype(jnp.float32)
        hidden = shifted[...]
    else:
        hidden = hidden_ref[...].astype(jnp.float32)
    rows = hidden.shape[0]
    mean_sq = jnp.mean(hidden * hidden, axis=1, keepdims=True)
    normed = (hidden * lax.rsqrt(mean_sq + EPSILON) * gain_ref[...]).astype(jnp.bfloat16)
    out_ref[:, :width] = normed
    by_lanes = (((1,), (1,)), ((), ()))
    logits = lax.dot_general(normed, router_ref[...], by_lanes, preferred_element_type=jnp.float32)
    expert = lax.broadcasted_iota(jnp.int32, (experts, rows), 0)
    routes = routes_ref[...]
    chosen = jnp.zeros(expert.shape, jnp.bool_)
    for k in range(routes.shape[0]):
        chosen = chosen | (expert == routes[k : k + 1, :])
    chosen = jnp.where(chosen, 1.0, 0.0).astype(jnp.bfloat16)
    row = lax.broadcasted_iota(jnp.int32, (rows, rows), 0)
    other = lax.broadcasted_iota(jnp.int32, (rows, rows), 1)

    def of_rows(taken):
        taken = jnp.where(taken, 1.0, 0.0).astype(jnp.bfloat16)
        return lax.dot_general(taken, chosen, by_lanes, preferred_element_type=jnp.float32)

    mine = of_rows(row == other) > 0.5
    top = jnp.max(jnp.where(mine, logits, NEG_FILL), axis=1, keepdims=True)
    raised = jnp.where(mine, jnp.exp(jnp.minimum(logits - top, 0.0)), 0.0)
    gates = raised / jnp.sum(raised, axis=1, keepdims=True)
    high = gates.astype(jnp.bfloat16).astype(jnp.float32)
    parts = [high, gates - high]
    if ranking == "block":
        parts.append(jnp.where(mine, of_rows(other < row), NOT_CHOSEN))
    elif ranking == "first":
        parts.append(jnp.where(mine, 0.0, NOT_CHOSEN))
    rest = out_ref.shape[1] - width - len(parts) * experts
    if rest:
        parts.append(jnp.zeros((rows, rest), jnp.float32))
    out_ref[:, width:] = jnp.concatenate(parts, axis=1).astype(jnp.bfloat16)


def prepare(hidden, norm_gain, router, routes, ranking=None):
    width = hidden.shape[1]
    rows = routes.shape[0]
    extra = -(-(3 if ranking else 2) * router.shape[1] // 128) * 128
    operands = (hidden, norm_gain.reshape(1, width), router.T, routes.T)
    fetched = rows > hidden.shape[0]
    kernel, options = prepare_kernel, {}
    if fetched:
        kernel = fetched_prepare_kernel
        options = dict(
            in_specs=[pl.BlockSpec(memory_space=pltpu.HBM)] * 4,
            scratch_shapes=[pltpu.VMEM((rows, width), jnp.float32)]
            + [pltpu.VMEM(operand.shape, operand.dtype) for operand in operands]
            + [pltpu.SemaphoreType.DMA((4,))],
        )
    return pl.pallas_call(
        functools.partial(kernel, ranking),
        out_shape=jax.ShapeDtypeStruct((rows, width + extra), jnp.bfloat16),
        compiler_params=pltpu.CompilerParams(vmem_limit_bytes=32 << 20),
        name="prepare",
        **options,
    )(*operands)


def expert_kernel(expert_ref, rows_ref, gate_ref, up_ref, down_ref, out_ref):
    width = gate_ref.shape[0]
    payload = rows_ref[...]
    rows = payload[:, :width]
    tail = payload[:, width:].astype(jnp.float32)
    lane = lax.broadcasted_iota(jnp.int32, tail.shape, 1)
    expert = expert_ref[0]
    experts = expert_ref[1]
    mine = (lane == expert) | (lane == expert + experts)
    weight = jnp.sum(jnp.where(mine, tail, 0.0), axis=1, keepdims=True)
    gate_act = jnp.dot(rows, gate_ref[...], preferred_element_type=jnp.float32)
    up_act = jnp.dot(rows, up_ref[...], preferred_element_type=jnp.float32)
    inner = (gate_act / (1.0 + jnp.exp(-gate_act)) * up_act).astype(jnp.bfloat16)
    result = jnp.dot(inner, down_ref[...], preferred_element_type=jnp.float32)
    out_ref[...] = (weight * result).astype(jnp.bfloat16)


def run_expert(expert, rows, gate_weights, up_weights, down_weights):
    total, padded = rows.shape
    width, hidden_units = gate_weights.shape
    tile = 256
    return pl.pallas_call(
        expert_kernel,
        grid_spec=pltpu.PrefetchScalarGridSpec(
            num_scalar_prefetch=1,
            grid=(total // tile,),
            in_specs=[
                pl.BlockSpec((tile, padded), lambda i, e: (i, 0)),
                pl.BlockSpec((width, hidden_units), lambda i, e: (0, 0), pipeline_mode=pl.Buffered(1)),
                pl.BlockSpec((width, hidden_units), lambda i, e: (0, 0), pipeline_mode=pl.Buffered(1)),
                pl.BlockSpec((hidden_units, width), lambda i, e: (0, 0), pipeline_mode=pl.Buffered(1)),
            ],
            out_specs=pl.BlockSpec((tile, width), lambda i, e: (i, 0)),
        ),
        out_shape=jax.ShapeDtypeStruct((total, width), jnp.bfloat16),
        compiler_params=pltpu.CompilerParams(vmem_limit_bytes=48 << 20),
        name="expert",
    )(expert, rows, gate_weights, up_weights, down_weights)


def plane_kernel(cap, piece_rows, block_rows, *refs):
    refs = list(refs)
    ids_ref = refs.pop(0)
    sources = [refs.pop(0) for _ in piece_rows]
    weight_refs = [refs.pop(0) for _ in range(6)]
    targets = [refs.pop(0) for _ in block_rows]
    decodes, rows, weights, downs, slots, inner, results, spread, sums, row_sem, weight_sem, out_sem = refs
    width = sums.shape[1]
    tokens = block_rows[0]
    pair_rows = 2 * tokens
    pair_slots = 2 * cap
    few = decodes.shape[0]
    row_copies = []
    at = 0
    for ref, count in zip(sources, piece_rows):
        if ref is sources[-1]:
            count -= few
            copy = pltpu.make_async_copy(
                ref.at[pl.ds(count, few)], decodes, row_sem.at[len(row_copies)]
            )
            row_copies.append(copy)
        if count:
            copy = pltpu.make_async_copy(
                ref.at[pl.ds(0, count)], rows.at[pl.ds(at, count)], row_sem.at[len(row_copies)]
            )
            row_copies.append(copy)
        at += count
    up_copies = [
        pltpu.make_async_copy(weight_refs[3 * e + i], weights.at[2 * e + i], weight_sem.at[2 * e + i])
        for e in range(2)
        for i in range(2)
    ]
    down_copies = [
        pltpu.make_async_copy(weight_refs[3 * e + 2], downs.at[e], weight_sem.at[4 + e])
        for e in range(2)
    ]
    for copy in row_copies + up_copies + down_copies:
        copy.start()
    for copy in row_copies:
        copy.wait()
    is_first = lax.broadcasted_iota(jnp.int32, (few, 1), 0) == 0
    for j in range(4):
        part = pl.ds(j * tokens, few)
        decode_row = decodes[...].astype(jnp.float32)[j : j + 1]
        kept = rows[part, :].astype(jnp.float32)
        rows[part, :] = jnp.where(is_first, decode_row, kept).astype(jnp.bfloat16)

    experts = ids_ref[2]
    extra = rows.shape[1] - width
    lanes = lax.broadcasted_iota(jnp.int32, (8, extra), 1)
    line = lax.broadcasted_iota(jnp.int32, (8, extra), 0)
    wanted = ((line == 0) & (lanes == ids_ref[0] + 2 * experts)) | (
        (line == 1) & (lanes == ids_ref[1] + 2 * experts)
    )
    wanted = jnp.where(wanted, 1.0, 0.0).astype(jnp.bfloat16)
    pairs = [pl.ds(p * pair_rows, pair_rows) for p in range(2)]

    def shift_of(shape, axis):
        second = lax.broadcasted_iota(jnp.int32, shape, axis) >= tokens
        return jnp.where(second, float(cap), 0.0)

    for p in range(2):
        ranks = lax.dot_general(
            wanted, rows[pairs[p], width:], (((1,), (1,)), ((), ())), preferred_element_type=jnp.float32
        )
        ranks += shift_of(ranks.shape, 1)
        slot = lax.broadcasted_iota(jnp.int32, (2 * pair_slots, pair_rows), 0).astype(jnp.float32)
        taken = (slot == ranks[0:1]) | (slot == ranks[1:2] + float(pair_slots))
        taken = jnp.where(taken, 1.0, 0.0).astype(jnp.bfloat16)
        picked = jnp.dot(taken, rows[pairs[p], :], preferred_element_type=jnp.float32)
        picked = picked.astype(jnp.bfloat16)
        for e in range(2):
            slots[e, pl.ds(p * pair_slots, pair_slots), :] = picked[e * pair_slots : (e + 1) * pair_slots]

    def make_spread(p):
        tail = rows[pairs[p], width:].astype(jnp.float32)
        lane = lax.broadcasted_iota(jnp.int32, tail.shape, 1)
        slot = lax.broadcasted_iota(jnp.int32, (pair_rows, 2 * pair_slots), 1).astype(jnp.float32)
        back = jnp.zeros(slot.shape, jnp.bool_)
        for e in range(2):
            mine = lane == ids_ref[e] + 2 * experts
            rank = jnp.sum(jnp.where(mine, tail, 0.0), axis=1, keepdims=True)
            back = back | (slot == rank + shift_of(rank.shape, 0) + float(e * pair_slots))
        spread[p] = jnp.where(back, 1.0, 0.0).astype(jnp.bfloat16)

    def weight_of(e):
        tail = slots[e, :, width:].astype(jnp.float32)
        lane = lax.broadcasted_iota(jnp.int32, tail.shape, 1)
        mine = (lane == ids_ref[e]) | (lane == ids_ref[e] + experts)
        return jnp.sum(jnp.where(mine, tail, 0.0), axis=1, keepdims=True)

    def product(e, i):
        return jnp.dot(slots[e, :, :width], weights[2 * e + i], preferred_element_type=jnp.float32)

    def activate(e, gate_act, up_act):
        act = gate_act / (1.0 + jnp.exp(-gate_act)) * up_act * weight_of(e)
        inner[e] = act.astype(jnp.bfloat16)

    def finish(e):
        result = jnp.dot(inner[e], downs[e], preferred_element_type=jnp.float32)
        result = result.astype(jnp.bfloat16)
        for p in range(2):
            results[p, pl.ds(e * pair_slots, pair_slots), :] = result[p * pair_slots : (p + 1) * pair_slots]

    up_copies[0].wait()
    gate_0 = product(0, 0)
    make_spread(0)
    up_copies[1].wait()
    up_0 = product(0, 1)
    make_spread(1)
    up_copies[2].wait()
    activate(0, gate_0, up_0)
    gate_1 = product(1, 0)
    up_copies[3].wait()
    up_1 = product(1, 1)
    down_copies[0].wait()
    finish(0)
    activate(1, gate_1, up_1)
    down_copies[1].wait()
    finish(1)
    out_copies = []
    at = 0
    for p in range(2):
        total = jnp.dot(spread[p], results[p], preferred_element_type=jnp.float32)
        sums[pairs[p], :] = total.astype(jnp.bfloat16)
        while len(out_copies) < len(targets) and at < (p + 1) * pair_rows:
            count = block_rows[len(out_copies)]
            copy = pltpu.make_async_copy(
                sums.at[pl.ds(at, count)], targets[len(out_copies)], out_sem.at[len(out_copies)]
            )
            copy.start()
            out_copies.append(copy)
            at += count
    for copy in out_copies:
        copy.wait()


def run_plane(ids, cap, few, pieces, block_rows, weights):
    width, units = weights[0].shape
    padded = pieces[0].shape[1]
    piece_rows = tuple(piece.shape[0] for piece in pieces)
    total = sum(piece_rows) - few
    kept = jnp.bfloat16
    anywhere = pl.BlockSpec(memory_space=pl.ANY)
    return pl.pallas_call(
        functools.partial(plane_kernel, cap, piece_rows, block_rows),
        in_specs=[pl.BlockSpec(memory_space=pltpu.SMEM)] + [anywhere] * (len(pieces) + 6),
        out_specs=[anywhere] * len(block_rows),
        out_shape=[jax.ShapeDtypeStruct((count, width), kept) for count in block_rows],
        scratch_shapes=[
            pltpu.VMEM((few, padded), kept),
            pltpu.VMEM((total, padded), kept),
            pltpu.VMEM((4, width, units), kept),
            pltpu.VMEM((2, units, width), kept),
            pltpu.VMEM((2, 4 * cap, padded), kept),
            pltpu.VMEM((2, 4 * cap, units), kept),
            pltpu.VMEM((2, 4 * cap, width), kept),
            pltpu.VMEM((2, total // 2, 4 * cap), kept),
            pltpu.VMEM((total, width), kept),
            pltpu.SemaphoreType.DMA((len(pieces) + 1,)),
            pltpu.SemaphoreType.DMA((6,)),
            pltpu.SemaphoreType.DMA((len(block_rows),)),
        ],
        compiler_params=pltpu.CompilerParams(vmem_limit_bytes=48 << 20),
        cost_estimate=pl.CostEstimate(
            flops=12 * total * width * units, bytes_accessed=24 << 20, transcendentals=total * units
        ),
        name="plane",
    )(ids, *pieces, *weights)


def merge_kernel(cut, x_ref, y_ref, passed_0_ref, passed_1_ref, x_out, y_out):
    def sum_of(one, other):
        return (one.astype(jnp.float32) + other.astype(jnp.float32)).astype(jnp.bfloat16)

    x_out[:cut, :] = sum_of(x_ref[:cut, :], passed_0_ref[...])
    x_out[cut:, :] = x_ref[cut:, :]
    y_out[:cut, :] = y_ref[:cut, :]
    y_out[cut:, :] = sum_of(y_ref[cut:, :], passed_1_ref[...])


def merge_passed(cut, to_x, to_y, passed_0, passed_1):
    return pl.pallas_call(
        functools.partial(merge_kernel, cut),
        out_shape=[jax.ShapeDtypeStruct(to_x.shape, to_x.dtype)] * 2,
        compiler_params=pltpu.CompilerParams(vmem_limit_bytes=16 << 20),
        name="merge",
    )(to_x, to_y, passed_0, passed_1)


def join_kernel(far_ref, risen_ref, own_ref, x_ref, y_ref, far_out, own_out):
    far_out[...] = (far_ref[...].astype(jnp.float32) + risen_ref[...].astype(jnp.float32)).astype(jnp.bfloat16)
    total = own_ref[...].astype(jnp.float32) + x_ref[...].astype(jnp.float32) + y_ref[...].astype(jnp.float32)
    own_out[...] = total.astype(jnp.bfloat16)


def join(far, risen, own, from_x, from_y):
    return pl.pallas_call(
        join_kernel,
        out_shape=[jax.ShapeDtypeStruct(own.shape, own.dtype)] * 2,
        compiler_params=pltpu.CompilerParams(vmem_limit_bytes=16 << 20),
        name="join",
    )(far, risen, own, from_x, from_y)


def along_x(value):
    return lax.ppermute(value, "kv", [(i, i ^ 1) for i in range(4)])


def along_y(value):
    return lax.ppermute(value, "kv", [(i, i ^ 2) for i in range(4)])


def around_z(value, hops=1):
    return lax.ppermute(value, "blk", [(i, (i + 2 * hops) % 8) for i in range(8)])


def across_chip(value):
    return lax.ppermute(value, "blk", [(i, i ^ 1) for i in range(8)])


def fence(*values):
    return lax.optimization_barrier(values)


def added(*parts):
    total = parts[0].astype(jnp.float32)
    for part in parts[1:]:
        total = total + part.astype(jnp.float32)
    return total


def permuted_plan(
    queries,
    cache_keys,
    cache_values,
    lengths,
    sinks,
    out_proj,
    decode_resid,
    prefill_hidden,
    norm_gain,
    router,
    routes,
    expert_gate,
    expert_up,
    expert_down,
):
    experts = router.shape[1]
    ids = routes[0]
    tokens = ids.shape[0]
    my_kv = lax.axis_index("kv")
    my_blk = lax.axis_index("blk")
    first_expert = my_kv * 8
    expert_ids = jnp.stack(
        [first_expert + my_blk, first_expert + (my_blk ^ 1), jnp.int32(experts)]
    ).astype(jnp.int32)
    cap = (2 * tokens * ids.shape[1] + experts - 1) // experts
    cut = (tokens // 2 + 15) // 16 * 16
    few = 16

    def spread_sides(block):
        return along_x(block), along_y(block)

    def spread_corner(sides):
        return along_y(sides[0][:cut]), along_x(sides[1][cut:])

    def apply(pieces, counts):
        return run_plane(expert_ids, cap, few, pieces, counts, weights)

    def return_corner(sums):
        return along_y(sums[3]), along_x(sums[4])

    def return_sides(sums, passed=None):
        to_x, to_y = sums[1:3] if passed is None else merge_passed(cut, *sums[1:3], *passed)
        return along_x(to_x), along_y(to_y)

    prefill = prefill_hidden[0]
    block_0 = prepare(prefill, norm_gain, router, ids, "block")
    block_0, queries, cache_keys, expert_gate = fence(block_0, queries, cache_keys, expert_gate)
    sides_0 = spread_sides(block_0)
    block_1 = around_z(block_0)
    other_gate = across_chip(expert_gate[0])
    attended = attend(queries, cache_keys, cache_values, lengths, sinks)
    partial_proj = jnp.dot(attended, out_proj, preferred_element_type=jnp.float32)
    is_mine = jnp.arange(4)[:, None] == my_kv
    partial_proj += jnp.where(is_mine, decode_resid.astype(jnp.float32), 0.0)
    width = partial_proj.shape[1]
    ids_row = jnp.pad(ids[:1].astype(jnp.float32), ((0, 0), (0, width - ids.shape[1])))
    shared = jnp.concatenate([partial_proj, jnp.where(is_mine, ids_row, 0.0)], axis=0)
    shared = shared + along_x(shared)
    sides_0, block_1, other_gate = fence(sides_0, block_1, other_gate)

    corner_0 = spread_corner(sides_0)
    other_up = across_chip(expert_up[0])
    corner_0, shared, block_1, other_up, expert_down = fence(
        corner_0, shared, block_1, other_up, expert_down
    )

    shared = shared + along_y(shared)
    sides_1 = spread_sides(block_1)
    block_2 = around_z(block_1)
    other_down = across_chip(expert_down[0])
    order = [my_kv ^ j for j in range(4)]
    decoded = jnp.concatenate(
        [lax.dynamic_slice_in_dim(shared, index, 1) for index in order], axis=0
    ).astype(jnp.bfloat16)
    decode_ids = jnp.concatenate(
        [lax.dynamic_slice_in_dim(shared, 4 + index, 1) for index in order], axis=0
    )[:, : ids.shape[1]].astype(jnp.int32)
    hidden = jnp.concatenate([decoded[:1], prefill], axis=0)
    decodes_0 = prepare(
        jnp.pad(decoded, ((0, few - 4), (0, 0))),
        norm_gain,
        router,
        jnp.pad(decode_ids, ((0, few - 4), (0, 0))),
        "first",
    )
    sides_1, block_2, decodes_0, other_down = fence(sides_1, block_2, decodes_0, other_down)
    weights = (expert_gate[0], expert_up[0], expert_down[0], other_gate, other_up, other_down)
    halves = (tokens, tokens, tokens, cut, tokens - cut)

    corner_1 = spread_corner(sides_1)
    sides_2 = spread_sides(block_2)
    arrived = around_z(jnp.concatenate([block_2, decodes_0], axis=0))
    sums_0 = apply((block_0,) + sides_0 + corner_0 + (decodes_0,), halves)
    corner_1, sides_2, arrived, sums_0 = fence(corner_1, sides_2, arrived, sums_0)
    block_3, decodes_1 = arrived[:tokens], arrived[tokens:]

    sides_3 = spread_sides(block_3)
    risen = around_z(jnp.concatenate(corner_1 + (decodes_1,), axis=0))
    passed_0 = return_corner(sums_0)
    sums_1 = apply((block_1,) + sides_1 + corner_1 + (decodes_1,), (tokens,) * 4)
    sides_3, risen, passed_0, sums_0, sums_1 = fence(sides_3, risen, passed_0, sums_0, sums_1)

    decodes_3 = around_z(risen[tokens:])
    decodes_3, far = fence(decodes_3, sums_1[3])
    far = around_z(far)
    corner_3 = spread_corner(sides_3)
    back_1 = return_sides(sums_1)
    sums_2 = apply((block_2,) + sides_2 + (risen,), (tokens,) * 4)
    decodes_3, far, corner_3, back_1, sums_1, sums_2 = fence(
        decodes_3, far, corner_3, back_1, sums_1, sums_2
    )

    far, first = join(sums_2[3], far, sums_1[0], *back_1)
    far = around_z(far)
    back_2 = return_sides(sums_2)
    carried_1 = around_z(first, -1)
    sums_3 = apply((block_3,) + sides_3 + corner_3 + (decodes_3,), (tokens,) * 4)
    far, sums_2, sums_3 = fence(far, sums_2, sums_3)

    far = added(sums_3[3], far).astype(jnp.bfloat16)
    passed_3 = return_corner(tuple(sums_3[:3]) + (far[:cut], far[cut:]))
    passed_3, carried_1 = fence(passed_3, carried_1)
    back_3 = return_sides(sums_3, passed_3)
    carried = around_z(added(sums_2[0], *back_2).astype(jnp.bfloat16))
    carried, passed_0, sums_0 = fence(carried, passed_0, sums_0)
    back_0 = return_sides(sums_0, passed_0)
    carried = around_z(added(sums_3[0], *back_3, carried).astype(jnp.bfloat16))
    return added(hidden, sums_0[0], carried_1, *back_0, carried).astype(jnp.bfloat16)[None]


def chunk_cuts(tokens, devices):
    step = (tokens // 2 + 15) // 16 * 16 if devices < 128 else 32
    return [(start, min(start + step, tokens)) for start in range(0, tokens, step)]


def gathered_plan(
    queries,
    cache_keys,
    cache_values,
    lengths,
    sinks,
    out_proj,
    decode_resid,
    prefill_hidden,
    norm_gain,
    router,
    routes,
    expert_gate,
    expert_up,
    expert_down,
):
    experts = router.shape[1]
    ids = routes[0]
    tokens = ids.shape[0]
    prefill = prefill_hidden[0]
    devices = lax.axis_size(AXES)
    cuts = chunk_cuts(tokens, devices)
    my_expert = lax.axis_index("kv") * lax.axis_size("blk") + lax.axis_index("blk")
    expert = jnp.stack([my_expert, jnp.int32(experts)]).astype(jnp.int32)
    weights = (expert_gate[0], expert_up[0], expert_down[0])

    attended = attend(queries, cache_keys, cache_values, lengths, sinks)
    partial_proj = jnp.dot(attended, out_proj, preferred_element_type=jnp.float32)
    projected = lax.psum_scatter(partial_proj, "kv", scatter_dimension=0, tiled=True)
    decoded = (decode_resid.astype(jnp.float32) + projected).astype(jnp.bfloat16)
    hidden = jnp.concatenate([prefill, decoded], axis=0)
    ids = jnp.concatenate([ids[1:], ids[:1]], axis=0)
    gathered = []
    for start, stop in cuts:
        source = prefill[start:stop] if stop < tokens else hidden[start:stop]
        sent = prepare(source, norm_gain, router, ids[start:stop])
        gathered.append(lax.all_gather(sent, AXES, axis=0, tiled=True))
    returned = []
    for rows in gathered:
        sums = run_expert(expert, rows, *weights)
        returned.append(lax.psum_scatter(sums, AXES, scatter_dimension=0, tiled=True))
    combined = jnp.concatenate(returned, axis=0)
    layer_sum = (hidden.astype(jnp.float32) + combined.astype(jnp.float32)).astype(jnp.bfloat16)
    layer_sum = jnp.concatenate([layer_sum[-1:], layer_sum[:-1]], axis=0)
    return layer_sum[None]


def solution(mesh):
    plan = permuted_plan if (mesh.shape["kv"], mesh.shape["blk"]) == (4, 8) else gathered_plan
    return jax.shard_map(
        plan,
        mesh=mesh,
        in_specs=(
            P("blk", "kv"),
            P("blk", None, "kv", None),
            P("blk", None, "kv", None),
            P(),
            P("kv"),
            P("kv", None),
            P(("blk", "kv"), None),
            P(("blk", "kv"), None, None),
            P(),
            P(),
            P(("blk", "kv"), None, None),
            P(("kv", "blk"), None, None),
            P(("kv", "blk"), None, None),
            P(("kv", "blk"), None, None),
        ),
        out_specs=P(("blk", "kv"), None, None),
        check_vma=False,
    )
```

```python
import functools
import math

import jax
import jax.numpy as jnp
from jax import lax
from jax.experimental import pallas as pl
from jax.experimental.pallas import tpu as pltpu
from jax.sharding import PartitionSpec as P

NEG_FILL = -1e30
EPSILON = 1e-06
NOT_CHOSEN = -256.0
AXES = ("blk", "kv")


def attend(queries, cache_keys, cache_values, lengths, sinks):
    my_block = lax.axis_index("blk")
    per_block = queries.shape[0]
    head_count = sinks.shape[0]
    head_dim = cache_keys.shape[3]
    window = cache_keys.shape[1]
    grouped_q = queries.reshape(per_block, head_count, head_dim)
    key_rows = cache_keys[:, :, 0, :]
    value_rows = cache_values[:, :, 0, :]
    my_lengths = lax.dynamic_slice_in_dim(lengths, my_block * per_block, per_block)
    scores = jnp.einsum("rgd,rjd->rgj", grouped_q, key_rows, preferred_element_type=jnp.float32) * (
        1.0 / math.sqrt(head_dim)
    )
    first_valid = window - jnp.minimum(my_lengths, window)
    is_valid = (jnp.arange(window, dtype=jnp.int32)[None, :] >= first_valid[:, None])[:, None, :]
    masked = jnp.where(is_valid, scores, NEG_FILL)
    top_limit = jnp.maximum(jnp.max(masked, axis=2), sinks[None, :])
    weights = jnp.where(is_valid, jnp.exp(masked - top_limit[..., None]), 0.0)
    denominator = jnp.sum(weights, axis=2) + jnp.exp(sinks[None, :] - top_limit)
    numerator = jnp.einsum(
        "rgj,rjd->rgd", weights.astype(jnp.bfloat16), value_rows, preferred_element_type=jnp.float32
    )
    return (
        (numerator / denominator[..., None])
        .astype(jnp.bfloat16)
        .reshape(per_block, head_count * head_dim)
    )


def fetched_prepare_kernel(ranking, hidden_in, gain_in, router_in, routes_in, out_ref, *scratch):
    shifted, hidden_ref, gain_ref, router_ref, routes_ref, sems = scratch
    sources = (hidden_in, gain_in, router_in, routes_in)
    targets = (hidden_ref, gain_ref, router_ref, routes_ref)
    copies = [
        pltpu.make_async_copy(source, target, sems.at[i])
        for i, (source, target) in enumerate(zip(sources, targets))
    ]
    for copy in copies:
        copy.start()
    for copy in copies:
        copy.wait()
    prepare_kernel(ranking, *targets, out_ref, shifted)


def prepare_kernel(ranking, hidden_ref, gain_ref, router_ref, routes_ref, out_ref, *scratch):
    experts, width = router_ref.shape
    if scratch:
        (shifted,) = scratch
        shifted[0:1, :] = jnp.zeros((1, width), jnp.float32)
        shifted[1:, :] = hidden_ref[...].astype(jnp.float32)
        hidden = shifted[...]
    else:
        hidden = hidden_ref[...].astype(jnp.float32)
    rows = hidden.shape[0]
    mean_sq = jnp.mean(hidden * hidden, axis=1, keepdims=True)
    normed = (hidden * lax.rsqrt(mean_sq + EPSILON) * gain_ref[...]).astype(jnp.bfloat16)
    out_ref[:, :width] = normed
    by_lanes = (((1,), (1,)), ((), ()))
    logits = lax.dot_general(normed, router_ref[...], by_lanes, preferred_element_type=jnp.float32)
    expert = lax.broadcasted_iota(jnp.int32, (experts, rows), 0)
    routes = routes_ref[...]
    chosen = jnp.zeros(expert.shape, jnp.bool_)
    for k in range(routes.shape[0]):
        chosen = chosen | (expert == routes[k : k + 1, :])
    chosen = jnp.where(chosen, 1.0, 0.0).astype(jnp.bfloat16)
    row = lax.broadcasted_iota(jnp.int32, (rows, rows), 0)
    other = lax.broadcasted_iota(jnp.int32, (rows, rows), 1)

    def of_rows(taken):
        taken = jnp.where(taken, 1.0, 0.0).astype(jnp.bfloat16)
        return lax.dot_general(taken, chosen, by_lanes, preferred_element_type=jnp.float32)

    mine = of_rows(row == other) > 0.5
    top = jnp.max(jnp.where(mine, logits, NEG_FILL), axis=1, keepdims=True)
    raised = jnp.where(mine, jnp.exp(jnp.minimum(logits - top, 0.0)), 0.0)
    gates = raised / jnp.sum(raised, axis=1, keepdims=True)
    high = gates.astype(jnp.bfloat16).astype(jnp.float32)
    parts = [high, gates - high]
    if ranking == "block":
        parts.append(jnp.where(mine, of_rows(other < row), NOT_CHOSEN))
    elif ranking == "first":
        parts.append(jnp.where(mine, 0.0, NOT_CHOSEN))
    rest = out_ref.shape[1] - width - len(parts) * experts
    if rest:
        parts.append(jnp.zeros((rows, rest), jnp.float32))
    out_ref[:, width:] = jnp.concatenate(parts, axis=1).astype(jnp.bfloat16)


def prepare(hidden, norm_gain, router, routes, ranking=None):
    width = hidden.shape[1]
    rows = routes.shape[0]
    extra = -(-(3 if ranking else 2) * router.shape[1] // 128) * 128
    operands = (hidden, norm_gain.reshape(1, width), router.T, routes.T)
    fetched = rows > hidden.shape[0]
    kernel, options = prepare_kernel, {}
    if fetched:
        kernel = fetched_prepare_kernel
        options = dict(
            in_specs=[pl.BlockSpec(memory_space=pltpu.HBM)] * 4,
            scratch_shapes=[pltpu.VMEM((rows, width), jnp.float32)]
            + [pltpu.VMEM(operand.shape, operand.dtype) for operand in operands]
            + [pltpu.SemaphoreType.DMA((4,))],
        )
    return pl.pallas_call(
        functools.partial(kernel, ranking),
        out_shape=jax.ShapeDtypeStruct((rows, width + extra), jnp.bfloat16),
        compiler_params=pltpu.CompilerParams(vmem_limit_bytes=32 << 20),
        name="prepare",
        **options,
    )(*operands)


def expert_kernel(expert_ref, rows_ref, gate_ref, up_ref, down_ref, out_ref):
    width = gate_ref.shape[0]
    payload = rows_ref[...]
    rows = payload[:, :width]
    tail = payload[:, width:].astype(jnp.float32)
    lane = lax.broadcasted_iota(jnp.int32, tail.shape, 1)
    expert = expert_ref[0]
    experts = expert_ref[1]
    mine = (lane == expert) | (lane == expert + experts)
    weight = jnp.sum(jnp.where(mine, tail, 0.0), axis=1, keepdims=True)
    gate_act = jnp.dot(rows, gate_ref[...], preferred_element_type=jnp.float32)
    up_act = jnp.dot(rows, up_ref[...], preferred_element_type=jnp.float32)
    inner = (gate_act / (1.0 + jnp.exp(-gate_act)) * up_act).astype(jnp.bfloat16)
    result = jnp.dot(inner, down_ref[...], preferred_element_type=jnp.float32)
    out_ref[...] = (weight * result).astype(jnp.bfloat16)


def run_expert(expert, rows, gate_weights, up_weights, down_weights):
    total, padded = rows.shape
    width, hidden_units = gate_weights.shape
    tile = 256
    return pl.pallas_call(
        expert_kernel,
        grid_spec=pltpu.PrefetchScalarGridSpec(
            num_scalar_prefetch=1,
            grid=(total // tile,),
            in_specs=[
                pl.BlockSpec((tile, padded), lambda i, e: (i, 0)),
                pl.BlockSpec((width, hidden_units), lambda i, e: (0, 0), pipeline_mode=pl.Buffered(1)),
                pl.BlockSpec((width, hidden_units), lambda i, e: (0, 0), pipeline_mode=pl.Buffered(1)),
                pl.BlockSpec((hidden_units, width), lambda i, e: (0, 0), pipeline_mode=pl.Buffered(1)),
            ],
            out_specs=pl.BlockSpec((tile, width), lambda i, e: (i, 0)),
        ),
        out_shape=jax.ShapeDtypeStruct((total, width), jnp.bfloat16),
        compiler_params=pltpu.CompilerParams(vmem_limit_bytes=48 << 20),
        name="expert",
    )(expert, rows, gate_weights, up_weights, down_weights)


def plane_kernel(cap, piece_rows, block_rows, *refs):
    refs = list(refs)
    ids_ref = refs.pop(0)
    sources = [refs.pop(0) for _ in piece_rows]
    weight_refs = [refs.pop(0) for _ in range(6)]
    targets = [refs.pop(0) for _ in block_rows]
    decodes, rows, weights, downs, slots, inner, results, spread, sums, row_sem, weight_sem, out_sem = refs
    width = sums.shape[1]
    tokens = block_rows[0]
    pair_rows = 2 * tokens
    pair_slots = 2 * cap
    few = decodes.shape[0]
    row_copies = ([], [])
    at = 0
    for ref, count in zip(sources, piece_rows):
        if ref is sources[-1]:
            count -= few
            copy = pltpu.make_async_copy(ref.at[pl.ds(count, few)], decodes, row_sem.at[len(sources)])
            row_copies[0].append(copy)
        if count:
            p = 0 if at < pair_rows else 1
            index = len(row_copies[0]) + len(row_copies[1]) if ref is not sources[-1] else len(sources) - 1
            copy = pltpu.make_async_copy(
                ref.at[pl.ds(0, count)], rows.at[pl.ds(at, count)], row_sem.at[index]
            )
            row_copies[p].append(copy)
        at += count
    up_copies = [
        pltpu.make_async_copy(weight_refs[3 * e + i], weights.at[2 * e + i], weight_sem.at[2 * e + i])
        for e in range(2)
        for i in range(2)
    ]
    down_copies = [
        pltpu.make_async_copy(weight_refs[3 * e + 2], downs.at[e], weight_sem.at[4 + e])
        for e in range(2)
    ]
    for copy in row_copies[0] + row_copies[1] + up_copies + down_copies:
        copy.start()
    is_first = lax.broadcasted_iota(jnp.int32, (few, 1), 0) == 0

    def receive(p):
        for copy in row_copies[p]:
            copy.wait()
        for j in (2 * p, 2 * p + 1):
            part = pl.ds(j * tokens, few)
            decode_row = decodes[...].astype(jnp.float32)[j : j + 1]
            kept = rows[part, :].astype(jnp.float32)
            rows[part, :] = jnp.where(is_first, decode_row, kept).astype(jnp.bfloat16)

    experts = ids_ref[2]
    extra = rows.shape[1] - width
    lanes = lax.broadcasted_iota(jnp.int32, (8, extra), 1)
    line = lax.broadcasted_iota(jnp.int32, (8, extra), 0)
    wanted = ((line == 0) & (lanes == ids_ref[0] + 2 * experts)) | (
        (line == 1) & (lanes == ids_ref[1] + 2 * experts)
    )
    wanted = jnp.where(wanted, 1.0, 0.0).astype(jnp.bfloat16)
    pairs = [pl.ds(p * pair_rows, pair_rows) for p in range(2)]

    def shift_of(shape, axis):
        second = lax.broadcasted_iota(jnp.int32, shape, axis) >= tokens
        return jnp.where(second, float(cap), 0.0)

    for p in range(2):
        receive(p)
        ranks = lax.dot_general(
            wanted, rows[pairs[p], width:], (((1,), (1,)), ((), ())), preferred_element_type=jnp.float32
        )
        ranks += shift_of(ranks.shape, 1)
        slot = lax.broadcasted_iota(jnp.int32, (2 * pair_slots, pair_rows), 0).astype(jnp.float32)
        taken = (slot == ranks[0:1]) | (slot == ranks[1:2] + float(pair_slots))
        taken = jnp.where(taken, 1.0, 0.0).astype(jnp.bfloat16)
        picked = jnp.dot(taken, rows[pairs[p], :], preferred_element_type=jnp.float32)
        picked = picked.astype(jnp.bfloat16)
        for e in range(2):
            slots[e, pl.ds(p * pair_slots, pair_slots), :] = picked[e * pair_slots : (e + 1) * pair_slots]

    def make_spread(p):
        tail = rows[pairs[p], width:].astype(jnp.float32)
        lane = lax.broadcasted_iota(jnp.int32, tail.shape, 1)
        slot = lax.broadcasted_iota(jnp.int32, (pair_rows, 2 * pair_slots), 1).astype(jnp.float32)
        back = jnp.zeros(slot.shape, jnp.bool_)
        for e in range(2):
            mine = lane == ids_ref[e] + 2 * experts
            rank = jnp.sum(jnp.where(mine, tail, 0.0), axis=1, keepdims=True)
            back = back | (slot == rank + shift_of(rank.shape, 0) + float(e * pair_slots))
        spread[p] = jnp.where(back, 1.0, 0.0).astype(jnp.bfloat16)

    def weight_of(e):
        tail = slots[e, :, width:].astype(jnp.float32)
        lane = lax.broadcasted_iota(jnp.int32, tail.shape, 1)
        mine = (lane == ids_ref[e]) | (lane == ids_ref[e] + experts)
        return jnp.sum(jnp.where(mine, tail, 0.0), axis=1, keepdims=True)

    def product(e, i):
        return jnp.dot(slots[e, :, :width], weights[2 * e + i], preferred_element_type=jnp.float32)

    def activate(e, gate_act, up_act):
        act = gate_act / (1.0 + jnp.exp(-gate_act)) * up_act * weight_of(e)
        inner[e] = act.astype(jnp.bfloat16)

    def finish(e):
        result = jnp.dot(inner[e], downs[e], preferred_element_type=jnp.float32)
        result = result.astype(jnp.bfloat16)
        for p in range(2):
            results[p, pl.ds(e * pair_slots, pair_slots), :] = result[p * pair_slots : (p + 1) * pair_slots]

    up_copies[0].wait()
    gate_0 = product(0, 0)
    make_spread(0)
    up_copies[1].wait()
    up_0 = product(0, 1)
    make_spread(1)
    up_copies[2].wait()
    activate(0, gate_0, up_0)
    gate_1 = product(1, 0)
    up_copies[3].wait()
    up_1 = product(1, 1)
    down_copies[0].wait()
    finish(0)
    activate(1, gate_1, up_1)
    down_copies[1].wait()
    finish(1)
    out_copies = []
    at = 0
    for p in range(2):
        total = jnp.dot(spread[p], results[p], preferred_element_type=jnp.float32)
        sums[pairs[p], :] = total.astype(jnp.bfloat16)
        while len(out_copies) < len(targets) and at < (p + 1) * pair_rows:
            count = block_rows[len(out_copies)]
            copy = pltpu.make_async_copy(
                sums.at[pl.ds(at, count)], targets[len(out_copies)], out_sem.at[len(out_copies)]
            )
            copy.start()
            out_copies.append(copy)
            at += count
    for copy in out_copies:
        copy.wait()


def run_plane(ids, cap, few, pieces, block_rows, weights):
    width, units = weights[0].shape
    padded = pieces[0].shape[1]
    piece_rows = tuple(piece.shape[0] for piece in pieces)
    total = sum(piece_rows) - few
    kept = jnp.bfloat16
    anywhere = pl.BlockSpec(memory_space=pl.ANY)
    return pl.pallas_call(
        functools.partial(plane_kernel, cap, piece_rows, block_rows),
        in_specs=[pl.BlockSpec(memory_space=pltpu.SMEM)] + [anywhere] * (len(pieces) + 6),
        out_specs=[anywhere] * len(block_rows),
        out_shape=[jax.ShapeDtypeStruct((count, width), kept) for count in block_rows],
        scratch_shapes=[
            pltpu.VMEM((few, padded), kept),
            pltpu.VMEM((total, padded), kept),
            pltpu.VMEM((4, width, units), kept),
            pltpu.VMEM((2, units, width), kept),
            pltpu.VMEM((2, 4 * cap, padded), kept),
            pltpu.VMEM((2, 4 * cap, units), kept),
            pltpu.VMEM((2, 4 * cap, width), kept),
            pltpu.VMEM((2, total // 2, 4 * cap), kept),
            pltpu.VMEM((total, width), kept),
            pltpu.SemaphoreType.DMA((len(pieces) + 1,)),
            pltpu.SemaphoreType.DMA((6,)),
            pltpu.SemaphoreType.DMA((len(block_rows),)),
        ],
        compiler_params=pltpu.CompilerParams(vmem_limit_bytes=48 << 20),
        cost_estimate=pl.CostEstimate(
            flops=12 * total * width * units, bytes_accessed=24 << 20, transcendentals=total * units
        ),
        name="plane",
    )(ids, *pieces, *weights)


def merge_kernel(cut, x_ref, y_ref, passed_0_ref, passed_1_ref, x_out, y_out):
    def sum_of(one, other):
        return (one.astype(jnp.float32) + other.astype(jnp.float32)).astype(jnp.bfloat16)

    x_out[:cut, :] = sum_of(x_ref[:cut, :], passed_0_ref[...])
    x_out[cut:, :] = x_ref[cut:, :]
    y_out[:cut, :] = y_ref[:cut, :]
    y_out[cut:, :] = sum_of(y_ref[cut:, :], passed_1_ref[...])


def merge_passed(cut, to_x, to_y, passed_0, passed_1):
    return pl.pallas_call(
        functools.partial(merge_kernel, cut),
        out_shape=[jax.ShapeDtypeStruct(to_x.shape, to_x.dtype)] * 2,
        compiler_params=pltpu.CompilerParams(vmem_limit_bytes=16 << 20),
        name="merge",
    )(to_x, to_y, passed_0, passed_1)


def join_kernel(far_ref, risen_ref, own_ref, x_ref, y_ref, far_out, own_out):
    rows, width = far_ref.shape
    far = far_ref[...].astype(jnp.float32) + risen_ref[:rows, :width].astype(jnp.float32)
    far_out[...] = far.astype(jnp.bfloat16)
    total = own_ref[...].astype(jnp.float32) + x_ref[...].astype(jnp.float32) + y_ref[...].astype(jnp.float32)
    own_out[...] = total.astype(jnp.bfloat16)


def join(far, risen, own, from_x, from_y):
    return pl.pallas_call(
        join_kernel,
        out_shape=[jax.ShapeDtypeStruct(own.shape, own.dtype)] * 2,
        compiler_params=pltpu.CompilerParams(vmem_limit_bytes=16 << 20),
        name="join",
    )(far, risen, own, from_x, from_y)


def meet_kernel(far_0_ref, far_1_ref, risen_ref, x_ref, y_ref, out_0, out_1, x_out, y_out):
    x_out[...] = x_ref[...]
    y_out[...] = y_ref[...]
    cut = out_0.shape[0]
    risen = risen_ref[...].astype(jnp.float32)
    out_0[...] = (far_0_ref[...].astype(jnp.float32) + risen[:cut]).astype(jnp.bfloat16)
    out_1[...] = (far_1_ref[...].astype(jnp.float32) + risen[cut:]).astype(jnp.bfloat16)


def meet(far_0, far_1, risen, x_part, y_part):
    outputs = (far_0, far_1, x_part, y_part)
    return pl.pallas_call(
        meet_kernel,
        out_shape=[jax.ShapeDtypeStruct(output.shape, output.dtype) for output in outputs],
        compiler_params=pltpu.CompilerParams(vmem_limit_bytes=16 << 20),
        name="meet",
    )(far_0, far_1, risen, x_part, y_part)


def gather_kernel(own_ref, x_0_ref, x_1_ref, y_0_ref, y_1_ref, carried_ref, out_ref):
    cut = x_0_ref.shape[0]
    for part, x_ref, y_ref in ((slice(0, cut), x_0_ref, y_0_ref), (slice(cut, None), x_1_ref, y_1_ref)):
        total = own_ref[part, :].astype(jnp.float32) + carried_ref[part, :].astype(jnp.float32)
        total += x_ref[...].astype(jnp.float32) + y_ref[...].astype(jnp.float32)
        out_ref[part, :] = total.astype(jnp.bfloat16)


def gather_sums(own, x_0, x_1, y_0, y_1, carried):
    return pl.pallas_call(
        gather_kernel,
        out_shape=jax.ShapeDtypeStruct(own.shape, own.dtype),
        compiler_params=pltpu.CompilerParams(vmem_limit_bytes=16 << 20),
        name="gather",
    )(own, x_0, x_1, y_0, y_1, carried)


def along_x(value):
    return lax.ppermute(value, "kv", [(i, i ^ 1) for i in range(4)])


def along_y(value):
    return lax.ppermute(value, "kv", [(i, i ^ 2) for i in range(4)])


def around_z(value, hops=1):
    return lax.ppermute(value, "blk", [(i, (i + 2 * hops) % 8) for i in range(8)])


def across_chip(value):
    return lax.ppermute(value, "blk", [(i, i ^ 1) for i in range(8)])


def fence(*values):
    return lax.optimization_barrier(values)


def added(*parts):
    total = parts[0].astype(jnp.float32)
    for part in parts[1:]:
        total = total + part.astype(jnp.float32)
    return total


def permuted_plan(
    queries,
    cache_keys,
    cache_values,
    lengths,
    sinks,
    out_proj,
    decode_resid,
    prefill_hidden,
    norm_gain,
    router,
    routes,
    expert_gate,
    expert_up,
    expert_down,
):
    experts = router.shape[1]
    ids = routes[0]
    tokens = ids.shape[0]
    my_kv = lax.axis_index("kv")
    my_blk = lax.axis_index("blk")
    first_expert = my_kv * 8
    expert_ids = jnp.stack(
        [first_expert + my_blk, first_expert + (my_blk ^ 1), jnp.int32(experts)]
    ).astype(jnp.int32)
    cap = (2 * tokens * ids.shape[1] + experts - 1) // experts
    cut = (tokens // 2 + 15) // 16 * 16
    few = 16

    def spread_sides(block):
        return along_x(block), along_y(block)

    def spread_corner(sides):
        return along_y(sides[0][:cut]), along_x(sides[1][cut:])

    def apply(pieces, counts):
        return run_plane(expert_ids, cap, few, pieces, counts, weights)

    def return_corner(sums):
        return along_y(sums[3]), along_x(sums[4])

    def return_sides(sums, passed=None):
        to_x, to_y = sums[1:3] if passed is None else merge_passed(cut, *sums[1:3], *passed)
        return along_x(to_x), along_y(to_y)

    prefill = prefill_hidden[0]
    block_0 = prepare(prefill, norm_gain, router, ids, "block")
    block_0, queries, cache_keys, expert_gate = fence(block_0, queries, cache_keys, expert_gate)
    sides_0 = spread_sides(block_0)
    block_1 = around_z(block_0)
    other_gate = across_chip(expert_gate[0])
    attended = attend(queries, cache_keys, cache_values, lengths, sinks)
    partial_proj = jnp.dot(attended, out_proj, preferred_element_type=jnp.float32)
    is_mine = jnp.arange(4)[:, None] == my_kv
    partial_proj += jnp.where(is_mine, decode_resid.astype(jnp.float32), 0.0)
    width = partial_proj.shape[1]
    ids_row = jnp.pad(ids[:1].astype(jnp.float32), ((0, 0), (0, width - ids.shape[1])))
    shared = jnp.concatenate([partial_proj, jnp.where(is_mine, ids_row, 0.0)], axis=0)
    shared = shared + along_x(shared)
    sides_0, block_1, other_gate = fence(sides_0, block_1, other_gate)

    corner_0 = spread_corner(sides_0)
    other_up = across_chip(expert_up[0])
    corner_0, shared, block_1, other_up, expert_down = fence(
        corner_0, shared, block_1, other_up, expert_down
    )

    shared = shared + along_y(shared)
    sides_1 = spread_sides(block_1)
    block_2 = around_z(block_1)
    other_down = across_chip(expert_down[0])
    order = [my_kv ^ j for j in range(4)]
    decoded = jnp.concatenate(
        [lax.dynamic_slice_in_dim(shared, index, 1) for index in order], axis=0
    ).astype(jnp.bfloat16)
    decode_ids = jnp.concatenate(
        [lax.dynamic_slice_in_dim(shared, 4 + index, 1) for index in order], axis=0
    )[:, : ids.shape[1]].astype(jnp.int32)
    hidden = jnp.concatenate([decoded[:1], prefill], axis=0)
    decodes_0 = prepare(
        jnp.pad(decoded, ((0, few - 4), (0, 0))),
        norm_gain,
        router,
        jnp.pad(decode_ids, ((0, few - 4), (0, 0))),
        "first",
    )
    sides_1, block_2, decodes_0, other_down = fence(sides_1, block_2, decodes_0, other_down)
    weights = (expert_gate[0], expert_up[0], expert_down[0], other_gate, other_up, other_down)
    halves = (tokens, tokens, tokens, cut, tokens - cut)

    corner_1 = spread_corner(sides_1)
    sides_2 = spread_sides(block_2)
    arrived = around_z(jnp.concatenate([block_2, decodes_0], axis=0))
    sums_0 = apply((block_0,) + sides_0 + corner_0 + (decodes_0,), halves)
    corner_1, sides_2, arrived, sums_0 = fence(corner_1, sides_2, arrived, sums_0)
    block_3, decodes_1 = arrived[:tokens], arrived[tokens:]

    sides_3 = spread_sides(block_3)
    risen = around_z(jnp.concatenate(corner_1 + (decodes_1,), axis=0))
    passed_0 = return_corner(sums_0)
    sums_1 = apply((block_1,) + sides_1 + corner_1 + (decodes_1,), (tokens,) * 4)
    sides_3, risen, passed_0, sums_0, sums_1 = fence(sides_3, risen, passed_0, sums_0, sums_1)

    far = jnp.pad(sums_1[3], ((0, 0), (0, risen.shape[1] - sums_1[3].shape[1])))
    far = around_z(jnp.concatenate([far, risen[tokens:]], axis=0))
    corner_3 = spread_corner(sides_3)
    back_1 = return_sides(sums_1)
    sums_2 = apply((block_2,) + sides_2 + (risen,), (tokens,) * 4)
    far, corner_3, back_1, sums_1, sums_2 = fence(far, corner_3, back_1, sums_1, sums_2)
    decodes_3 = far[tokens:]

    far, first = join(sums_2[3], far, sums_1[0], *back_1)
    far = around_z(far)
    back_2 = return_sides(sums_2)
    carried_1 = around_z(first, -1)
    parts = (cut, tokens - cut)
    sums_3 = apply((block_3,) + sides_3 + corner_3 + (decodes_3,), (tokens,) + parts * 3)
    far, sums_2, sums_3 = fence(far, sums_2, sums_3)

    own, x_0, x_1, y_0, y_1, far_0, far_1 = sums_3
    far_0, far_1, x_1, y_0 = meet(far_0, far_1, far, x_1, y_0)
    passed_3 = along_y(far_0), along_x(far_1)
    back_x1, back_y0 = along_x(x_1), along_y(y_0)
    passed_3, carried_1 = fence(passed_3, carried_1)
    back_x0 = along_x(added(x_0, passed_3[0]).astype(jnp.bfloat16))
    back_y1 = along_y(added(y_1, passed_3[1]).astype(jnp.bfloat16))
    carried = around_z(added(sums_2[0], *back_2).astype(jnp.bfloat16))
    carried, passed_0, sums_0 = fence(carried, passed_0, sums_0)
    back_0 = return_sides(sums_0, passed_0)
    carried = around_z(gather_sums(own, back_x0, back_x1, back_y0, back_y1, carried))
    return added(hidden, sums_0[0], carried_1, *back_0, carried).astype(jnp.bfloat16)[None]


def chunk_cuts(tokens, devices):
    step = (tokens // 2 + 15) // 16 * 16 if devices < 128 else 32
    return [(start, min(start + step, tokens)) for start in range(0, tokens, step)]


def gathered_plan(
    queries,
    cache_keys,
    cache_values,
    lengths,
    sinks,
    out_proj,
    decode_resid,
    prefill_hidden,
    norm_gain,
    router,
    routes,
    expert_gate,
    expert_up,
    expert_down,
):
    experts = router.shape[1]
    ids = routes[0]
    tokens = ids.shape[0]
    prefill = prefill_hidden[0]
    devices = lax.axis_size(AXES)
    cuts = chunk_cuts(tokens, devices)
    my_expert = lax.axis_index("kv") * lax.axis_size("blk") + lax.axis_index("blk")
    expert = jnp.stack([my_expert, jnp.int32(experts)]).astype(jnp.int32)
    weights = (expert_gate[0], expert_up[0], expert_down[0])

    attended = attend(queries, cache_keys, cache_values, lengths, sinks)
    partial_proj = jnp.dot(attended, out_proj, preferred_element_type=jnp.float32)
    projected = lax.psum_scatter(partial_proj, "kv", scatter_dimension=0, tiled=True)
    decoded = (decode_resid.astype(jnp.float32) + projected).astype(jnp.bfloat16)
    hidden = jnp.concatenate([prefill, decoded], axis=0)
    ids = jnp.concatenate([ids[1:], ids[:1]], axis=0)
    gathered = []
    for start, stop in cuts:
        source = prefill[start:stop] if stop < tokens else hidden[start:stop]
        sent = prepare(source, norm_gain, router, ids[start:stop])
        gathered.append(lax.all_gather(sent, AXES, axis=0, tiled=True))
    returned = []
    for rows in gathered:
        sums = run_expert(expert, rows, *weights)
        returned.append(lax.psum_scatter(sums, AXES, scatter_dimension=0, tiled=True))
    combined = jnp.concatenate(returned, axis=0)
    layer_sum = (hidden.astype(jnp.float32) + combined.astype(jnp.float32)).astype(jnp.bfloat16)
    layer_sum = jnp.concatenate([layer_sum[-1:], layer_sum[:-1]], axis=0)
    return layer_sum[None]


def solution(mesh):
    plan = permuted_plan if (mesh.shape["kv"], mesh.shape["blk"]) == (4, 8) else gathered_plan
    return jax.shard_map(
        plan,
        mesh=mesh,
        in_specs=(
            P("blk", "kv"),
            P("blk", None, "kv", None),
            P("blk", None, "kv", None),
            P(),
            P("kv"),
            P("kv", None),
            P(("blk", "kv"), None),
            P(("blk", "kv"), None, None),
            P(),
            P(),
            P(("blk", "kv"), None, None),
            P(("kv", "blk"), None, None),
            P(("kv", "blk"), None, None),
            P(("kv", "blk"), None, None),
        ),
        out_specs=P(("blk", "kv"), None, None),
        check_vma=False,
    )
```

```python
import functools
import math

import jax
import jax.numpy as jnp
from jax import lax
from jax.experimental import pallas as pl
from jax.experimental.pallas import tpu as pltpu
from jax.sharding import PartitionSpec as P

NEG_FILL = -1e30
EPSILON = 1e-06
NOT_CHOSEN = -256.0
AXES = ("blk", "kv")


def attend(queries, cache_keys, cache_values, lengths, sinks):
    my_block = lax.axis_index("blk")
    per_block = queries.shape[0]
    head_count = sinks.shape[0]
    head_dim = cache_keys.shape[3]
    window = cache_keys.shape[1]
    grouped_q = queries.reshape(per_block, head_count, head_dim)
    key_rows = cache_keys[:, :, 0, :]
    value_rows = cache_values[:, :, 0, :]
    my_lengths = lax.dynamic_slice_in_dim(lengths, my_block * per_block, per_block)
    scores = jnp.einsum("rgd,rjd->rgj", grouped_q, key_rows, preferred_element_type=jnp.float32) * (
        1.0 / math.sqrt(head_dim)
    )
    first_valid = window - jnp.minimum(my_lengths, window)
    is_valid = (jnp.arange(window, dtype=jnp.int32)[None, :] >= first_valid[:, None])[:, None, :]
    masked = jnp.where(is_valid, scores, NEG_FILL)
    top_limit = jnp.maximum(jnp.max(masked, axis=2), sinks[None, :])
    weights = jnp.where(is_valid, jnp.exp(masked - top_limit[..., None]), 0.0)
    denominator = jnp.sum(weights, axis=2) + jnp.exp(sinks[None, :] - top_limit)
    numerator = jnp.einsum(
        "rgj,rjd->rgd", weights.astype(jnp.bfloat16), value_rows, preferred_element_type=jnp.float32
    )
    return (
        (numerator / denominator[..., None])
        .astype(jnp.bfloat16)
        .reshape(per_block, head_count * head_dim)
    )


def prepare_kernel(ranking, hidden_ref, gain_ref, router_ref, routes_ref, out_ref, *scratch):
    experts, width = router_ref.shape
    if scratch:
        (shifted,) = scratch
        shifted[0:1, :] = jnp.zeros((1, width), jnp.float32)
        shifted[1:, :] = hidden_ref[...].astype(jnp.float32)
        hidden = shifted[...]
    else:
        hidden = hidden_ref[...].astype(jnp.float32)
    rows = hidden.shape[0]
    mean_sq = jnp.mean(hidden * hidden, axis=1, keepdims=True)
    normed = (hidden * lax.rsqrt(mean_sq + EPSILON) * gain_ref[...]).astype(jnp.bfloat16)
    out_ref[:, :width] = normed
    by_lanes = (((1,), (1,)), ((), ()))
    logits = lax.dot_general(normed, router_ref[...], by_lanes, preferred_element_type=jnp.float32)
    expert = lax.broadcasted_iota(jnp.int32, (experts, rows), 0)
    routes = routes_ref[...]
    chosen = jnp.zeros(expert.shape, jnp.bool_)
    for k in range(routes.shape[0]):
        chosen = chosen | (expert == routes[k : k + 1, :])
    chosen = jnp.where(chosen, 1.0, 0.0).astype(jnp.bfloat16)
    row = lax.broadcasted_iota(jnp.int32, (rows, rows), 0)
    other = lax.broadcasted_iota(jnp.int32, (rows, rows), 1)

    def of_rows(taken):
        taken = jnp.where(taken, 1.0, 0.0).astype(jnp.bfloat16)
        return lax.dot_general(taken, chosen, by_lanes, preferred_element_type=jnp.float32)

    mine = of_rows(row == other) > 0.5
    top = jnp.max(jnp.where(mine, logits, NEG_FILL), axis=1, keepdims=True)
    raised = jnp.where(mine, jnp.exp(jnp.minimum(logits - top, 0.0)), 0.0)
    gates = raised / jnp.sum(raised, axis=1, keepdims=True)
    high = gates.astype(jnp.bfloat16).astype(jnp.float32)
    parts = [high, gates - high]
    if ranking == "block":
        parts.append(jnp.where(mine, of_rows(other < row), NOT_CHOSEN))
    elif ranking == "first":
        parts.append(jnp.where(mine, 0.0, NOT_CHOSEN))
    rest = out_ref.shape[1] - width - len(parts) * experts
    if rest:
        parts.append(jnp.zeros((rows, rest), jnp.float32))
    out_ref[:, width:] = jnp.concatenate(parts, axis=1).astype(jnp.bfloat16)


def prepare(hidden, norm_gain, router, routes, ranking=None):
    width = hidden.shape[1]
    rows = routes.shape[0]
    extra = -(-(3 if ranking else 2) * router.shape[1] // 128) * 128
    shifted = rows > hidden.shape[0]
    return pl.pallas_call(
        functools.partial(prepare_kernel, ranking),
        out_shape=jax.ShapeDtypeStruct((rows, width + extra), jnp.bfloat16),
        scratch_shapes=[pltpu.VMEM((rows, width), jnp.float32)] if shifted else [],
        compiler_params=pltpu.CompilerParams(vmem_limit_bytes=32 << 20),
        name="prepare",
    )(hidden, norm_gain.reshape(1, width), router.T, routes.T)


def expert_kernel(expert_ref, rows_ref, gate_ref, up_ref, down_ref, out_ref):
    width = gate_ref.shape[0]
    payload = rows_ref[...]
    rows = payload[:, :width]
    tail = payload[:, width:].astype(jnp.float32)
    lane = lax.broadcasted_iota(jnp.int32, tail.shape, 1)
    expert = expert_ref[0]
    experts = expert_ref[1]
    mine = (lane == expert) | (lane == expert + experts)
    weight = jnp.sum(jnp.where(mine, tail, 0.0), axis=1, keepdims=True)
    gate_act = jnp.dot(rows, gate_ref[...], preferred_element_type=jnp.float32)
    up_act = jnp.dot(rows, up_ref[...], preferred_element_type=jnp.float32)
    inner = (gate_act / (1.0 + jnp.exp(-gate_act)) * up_act).astype(jnp.bfloat16)
    result = jnp.dot(inner, down_ref[...], preferred_element_type=jnp.float32)
    out_ref[...] = (weight * result).astype(jnp.bfloat16)


def run_expert(expert, rows, gate_weights, up_weights, down_weights):
    total, padded = rows.shape
    width, hidden_units = gate_weights.shape
    tile = 256
    return pl.pallas_call(
        expert_kernel,
        grid_spec=pltpu.PrefetchScalarGridSpec(
            num_scalar_prefetch=1,
            grid=(total // tile,),
            in_specs=[
                pl.BlockSpec((tile, padded), lambda i, e: (i, 0)),
                pl.BlockSpec((width, hidden_units), lambda i, e: (0, 0), pipeline_mode=pl.Buffered(1)),
                pl.BlockSpec((width, hidden_units), lambda i, e: (0, 0), pipeline_mode=pl.Buffered(1)),
                pl.BlockSpec((hidden_units, width), lambda i, e: (0, 0), pipeline_mode=pl.Buffered(1)),
            ],
            out_specs=pl.BlockSpec((tile, width), lambda i, e: (i, 0)),
        ),
        out_shape=jax.ShapeDtypeStruct((total, width), jnp.bfloat16),
        compiler_params=pltpu.CompilerParams(vmem_limit_bytes=48 << 20),
        name="expert",
    )(expert, rows, gate_weights, up_weights, down_weights)


def plane_kernel(cap, piece_rows, block_rows, *refs):
    refs = list(refs)
    ids_ref = refs.pop(0)
    sources = [refs.pop(0) for _ in piece_rows]
    weight_refs = [refs.pop(0) for _ in range(6)]
    targets = [refs.pop(0) for _ in block_rows]
    rows, weights, downs, slots, inner, results, spread, weight_sem = refs
    width = results.shape[2]
    tokens = block_rows[0]
    pair_rows = 2 * tokens
    pair_slots = 2 * cap
    up_copies = [
        pltpu.make_async_copy(weight_refs[3 * e + i], weights.at[2 * e + i], weight_sem.at[2 * e + i])
        for e in range(2)
        for i in range(2)
    ]
    down_copies = [
        pltpu.make_async_copy(weight_refs[3 * e + 2], downs.at[e], weight_sem.at[4 + e])
        for e in range(2)
    ]
    for copy in up_copies + down_copies:
        copy.start()
    few = piece_rows[-1] - (2 * pair_rows - sum(piece_rows[:-1]))
    at = 0
    for ref, count in zip(sources, piece_rows):
        if ref is sources[-1]:
            count -= few
            decodes = ref[count:, :].astype(jnp.float32)
        if count:
            rows[pl.ds(at, count), :] = ref[:count, :]
        at += count
    is_first = lax.broadcasted_iota(jnp.int32, (few, 1), 0) == 0
    for j in range(4):
        part = pl.ds(j * tokens, few)
        kept = rows[part, :].astype(jnp.float32)
        rows[part, :] = jnp.where(is_first, decodes[j : j + 1], kept).astype(jnp.bfloat16)

    experts = ids_ref[2]
    extra = rows.shape[1] - width
    lanes = lax.broadcasted_iota(jnp.int32, (8, extra), 1)
    line = lax.broadcasted_iota(jnp.int32, (8, extra), 0)
    wanted = ((line == 0) & (lanes == ids_ref[0] + 2 * experts)) | (
        (line == 1) & (lanes == ids_ref[1] + 2 * experts)
    )
    wanted = jnp.where(wanted, 1.0, 0.0).astype(jnp.bfloat16)
    pairs = [pl.ds(p * pair_rows, pair_rows) for p in range(2)]

    def shift_of(shape, axis):
        second = lax.broadcasted_iota(jnp.int32, shape, axis) >= tokens
        return jnp.where(second, float(cap), 0.0)

    for p in range(2):
        ranks = lax.dot_general(
            wanted, rows[pairs[p], width:], (((1,), (1,)), ((), ())), preferred_element_type=jnp.float32
        )
        ranks += shift_of(ranks.shape, 1)
        slot = lax.broadcasted_iota(jnp.int32, (2 * pair_slots, pair_rows), 0).astype(jnp.float32)
        taken = (slot == ranks[0:1]) | (slot == ranks[1:2] + float(pair_slots))
        taken = jnp.where(taken, 1.0, 0.0).astype(jnp.bfloat16)
        picked = jnp.dot(taken, rows[pairs[p], :], preferred_element_type=jnp.float32)
        picked = picked.astype(jnp.bfloat16)
        for e in range(2):
            slots[e, pl.ds(p * pair_slots, pair_slots), :] = picked[e * pair_slots : (e + 1) * pair_slots]

    def make_spread(p):
        tail = rows[pairs[p], width:].astype(jnp.float32)
        lane = lax.broadcasted_iota(jnp.int32, tail.shape, 1)
        slot = lax.broadcasted_iota(jnp.int32, (pair_rows, 2 * pair_slots), 1).astype(jnp.float32)
        back = jnp.zeros(slot.shape, jnp.bool_)
        for e in range(2):
            mine = lane == ids_ref[e] + 2 * experts
            rank = jnp.sum(jnp.where(mine, tail, 0.0), axis=1, keepdims=True)
            back = back | (slot == rank + shift_of(rank.shape, 0) + float(e * pair_slots))
        spread[p] = jnp.where(back, 1.0, 0.0).astype(jnp.bfloat16)

    def weight_of(e):
        tail = slots[e, :, width:].astype(jnp.float32)
        lane = lax.broadcasted_iota(jnp.int32, tail.shape, 1)
        mine = (lane == ids_ref[e]) | (lane == ids_ref[e] + experts)
        return jnp.sum(jnp.where(mine, tail, 0.0), axis=1, keepdims=True)

    def product(e, i):
        return jnp.dot(slots[e, :, :width], weights[2 * e + i], preferred_element_type=jnp.float32)

    def activate(e, gate_act, up_act):
        act = gate_act / (1.0 + jnp.exp(-gate_act)) * up_act * weight_of(e)
        inner[e] = act.astype(jnp.bfloat16)

    def finish(e):
        result = jnp.dot(inner[e], downs[e], preferred_element_type=jnp.float32)
        result = result.astype(jnp.bfloat16)
        for p in range(2):
            results[p, pl.ds(e * pair_slots, pair_slots), :] = result[p * pair_slots : (p + 1) * pair_slots]

    up_copies[0].wait()
    gate_0 = product(0, 0)
    make_spread(0)
    up_copies[1].wait()
    up_0 = product(0, 1)
    make_spread(1)
    up_copies[2].wait()
    activate(0, gate_0, up_0)
    gate_1 = product(1, 0)
    up_copies[3].wait()
    up_1 = product(1, 1)
    down_copies[0].wait()
    finish(0)
    activate(1, gate_1, up_1)
    down_copies[1].wait()
    finish(1)
    ends = [sum(block_rows[: i + 1]) for i in range(len(block_rows))]
    for p in range(2):
        total = jnp.dot(spread[p], results[p], preferred_element_type=jnp.float32)
        total = total.astype(jnp.bfloat16)
        for ref, count, end in zip(targets, block_rows, ends):
            if p * pair_rows < end <= (p + 1) * pair_rows:
                at = end - count - p * pair_rows
                ref[...] = total[at : at + count]


def run_plane(ids, cap, few, pieces, block_rows, weights):
    width, units = weights[0].shape
    padded = pieces[0].shape[1]
    piece_rows = tuple(piece.shape[0] for piece in pieces)
    total = sum(piece_rows) - few
    kept = jnp.bfloat16
    anywhere = pl.BlockSpec(memory_space=pl.ANY)
    return pl.pallas_call(
        functools.partial(plane_kernel, cap, piece_rows, block_rows),
        in_specs=[pl.BlockSpec(memory_space=pltpu.SMEM)]
        + [pl.BlockSpec(memory_space=pltpu.VMEM)] * len(pieces)
        + [anywhere] * 6,
        out_specs=[pl.BlockSpec(memory_space=pltpu.VMEM)] * len(block_rows),
        out_shape=[jax.ShapeDtypeStruct((count, width), kept) for count in block_rows],
        scratch_shapes=[
            pltpu.VMEM((total, padded), kept),
            pltpu.VMEM((4, width, units), kept),
            pltpu.VMEM((2, units, width), kept),
            pltpu.VMEM((2, 4 * cap, padded), kept),
            pltpu.VMEM((2, 4 * cap, units), kept),
            pltpu.VMEM((2, 4 * cap, width), kept),
            pltpu.VMEM((2, total // 2, 4 * cap), kept),
            pltpu.SemaphoreType.DMA((6,)),
        ],
        compiler_params=pltpu.CompilerParams(vmem_limit_bytes=48 << 20),
        cost_estimate=pl.CostEstimate(
            flops=12 * total * width * units, bytes_accessed=24 << 20, transcendentals=total * units
        ),
        name="plane",
    )(ids, *pieces, *weights)


def merge_kernel(cut, x_ref, y_ref, passed_0_ref, passed_1_ref, x_out, y_out):
    def sum_of(one, other):
        return (one.astype(jnp.float32) + other.astype(jnp.float32)).astype(jnp.bfloat16)

    x_out[:cut, :] = sum_of(x_ref[:cut, :], passed_0_ref[...])
    x_out[cut:, :] = x_ref[cut:, :]
    y_out[:cut, :] = y_ref[:cut, :]
    y_out[cut:, :] = sum_of(y_ref[cut:, :], passed_1_ref[...])


def merge_passed(cut, to_x, to_y, passed_0, passed_1):
    return pl.pallas_call(
        functools.partial(merge_kernel, cut),
        out_shape=[jax.ShapeDtypeStruct(to_x.shape, to_x.dtype)] * 2,
        compiler_params=pltpu.CompilerParams(vmem_limit_bytes=16 << 20),
        name="merge",
    )(to_x, to_y, passed_0, passed_1)


def join_kernel(far_ref, risen_ref, own_ref, x_ref, y_ref, far_out, own_out):
    rows, width = far_ref.shape
    far = far_ref[...].astype(jnp.float32) + risen_ref[:rows, :width].astype(jnp.float32)
    far_out[...] = far.astype(jnp.bfloat16)
    total = own_ref[...].astype(jnp.float32) + x_ref[...].astype(jnp.float32) + y_ref[...].astype(jnp.float32)
    own_out[...] = total.astype(jnp.bfloat16)


def join(far, risen, own, from_x, from_y):
    return pl.pallas_call(
        join_kernel,
        out_shape=[jax.ShapeDtypeStruct(own.shape, own.dtype)] * 2,
        compiler_params=pltpu.CompilerParams(vmem_limit_bytes=16 << 20),
        name="join",
    )(far, risen, own, from_x, from_y)


def meet_kernel(far_0_ref, far_1_ref, risen_ref, x_ref, y_ref, out_0, out_1, x_out, y_out):
    x_out[...] = x_ref[...]
    y_out[...] = y_ref[...]
    cut = out_0.shape[0]
    risen = risen_ref[...].astype(jnp.float32)
    out_0[...] = (far_0_ref[...].astype(jnp.float32) + risen[:cut]).astype(jnp.bfloat16)
    out_1[...] = (far_1_ref[...].astype(jnp.float32) + risen[cut:]).astype(jnp.bfloat16)


def meet(far_0, far_1, risen, x_part, y_part):
    outputs = (far_0, far_1, x_part, y_part)
    return pl.pallas_call(
        meet_kernel,
        out_shape=[jax.ShapeDtypeStruct(output.shape, output.dtype) for output in outputs],
        compiler_params=pltpu.CompilerParams(vmem_limit_bytes=16 << 20),
        name="meet",
    )(far_0, far_1, risen, x_part, y_part)


def gather_kernel(own_ref, x_0_ref, x_1_ref, y_0_ref, y_1_ref, carried_ref, out_ref):
    cut = x_0_ref.shape[0]
    for part, x_ref, y_ref in ((slice(0, cut), x_0_ref, y_0_ref), (slice(cut, None), x_1_ref, y_1_ref)):
        total = own_ref[part, :].astype(jnp.float32) + carried_ref[part, :].astype(jnp.float32)
        total += x_ref[...].astype(jnp.float32) + y_ref[...].astype(jnp.float32)
        out_ref[part, :] = total.astype(jnp.bfloat16)


def gather_sums(own, x_0, x_1, y_0, y_1, carried):
    return pl.pallas_call(
        gather_kernel,
        out_shape=jax.ShapeDtypeStruct(own.shape, own.dtype),
        compiler_params=pltpu.CompilerParams(vmem_limit_bytes=16 << 20),
        name="gather",
    )(own, x_0, x_1, y_0, y_1, carried)


def along_x(value):
    return lax.ppermute(value, "kv", [(i, i ^ 1) for i in range(4)])


def along_y(value):
    return lax.ppermute(value, "kv", [(i, i ^ 2) for i in range(4)])


def around_z(value, hops=1):
    return lax.ppermute(value, "blk", [(i, (i + 2 * hops) % 8) for i in range(8)])


def across_chip(value):
    return lax.ppermute(value, "blk", [(i, i ^ 1) for i in range(8)])


def fence(*values):
    return lax.optimization_barrier(values)


def added(*parts):
    total = parts[0].astype(jnp.float32)
    for part in parts[1:]:
        total = total + part.astype(jnp.float32)
    return total


def permuted_plan(
    queries,
    cache_keys,
    cache_values,
    lengths,
    sinks,
    out_proj,
    decode_resid,
    prefill_hidden,
    norm_gain,
    router,
    routes,
    expert_gate,
    expert_up,
    expert_down,
):
    experts = router.shape[1]
    ids = routes[0]
    tokens = ids.shape[0]
    my_kv = lax.axis_index("kv")
    my_blk = lax.axis_index("blk")
    first_expert = my_kv * 8
    expert_ids = jnp.stack(
        [first_expert + my_blk, first_expert + (my_blk ^ 1), jnp.int32(experts)]
    ).astype(jnp.int32)
    cap = (2 * tokens * ids.shape[1] + experts - 1) // experts
    cut = tokens // 2 // 16 * 16
    few = 16

    def spread_sides(block):
        return along_x(block), along_y(block)

    def spread_corner(sides):
        return along_y(sides[0][:cut]), along_x(sides[1][cut:])

    def apply(pieces, counts):
        return run_plane(expert_ids, cap, few, pieces, counts, weights)

    def return_corner(sums):
        return along_y(sums[3]), along_x(sums[4])

    def return_sides(sums, passed=None):
        to_x, to_y = sums[1:3] if passed is None else merge_passed(cut, *sums[1:3], *passed)
        return along_x(to_x), along_y(to_y)

    prefill = prefill_hidden[0]
    block_0 = prepare(prefill, norm_gain, router, ids, "block")
    block_0, queries, cache_keys, expert_gate = fence(block_0, queries, cache_keys, expert_gate)
    block_1 = around_z(block_0)
    sides_0 = spread_sides(block_0)
    other_gate = across_chip(expert_gate[0])
    attended = attend(queries, cache_keys, cache_values, lengths, sinks)
    partial_proj = jnp.dot(attended, out_proj, preferred_element_type=jnp.float32)
    is_mine = jnp.arange(4)[:, None] == my_kv
    partial_proj += jnp.where(is_mine, decode_resid.astype(jnp.float32), 0.0)
    width = partial_proj.shape[1]
    ids_row = jnp.pad(ids[:1].astype(jnp.float32), ((0, 0), (0, width - ids.shape[1])))
    shared = jnp.concatenate([partial_proj, jnp.where(is_mine, ids_row, 0.0)], axis=0)
    shared = shared + along_x(shared)
    sides_0, block_1, other_gate = fence(sides_0, block_1, other_gate)

    corner_0 = spread_corner(sides_0)
    other_up = across_chip(expert_up[0])
    corner_0, shared, block_1, other_up, expert_down = fence(
        corner_0, shared, block_1, other_up, expert_down
    )

    shared = shared + along_y(shared)
    sides_1 = spread_sides(block_1)
    block_2 = around_z(block_1)
    other_down = across_chip(expert_down[0])
    order = [my_kv ^ j for j in range(4)]
    decoded = jnp.concatenate(
        [lax.dynamic_slice_in_dim(shared, index, 1) for index in order], axis=0
    ).astype(jnp.bfloat16)
    decode_ids = jnp.concatenate(
        [lax.dynamic_slice_in_dim(shared, 4 + index, 1) for index in order], axis=0
    )[:, : ids.shape[1]].astype(jnp.int32)
    hidden = jnp.concatenate([decoded[:1], prefill], axis=0)
    decodes_0 = prepare(
        jnp.pad(decoded, ((0, few - 4), (0, 0))),
        norm_gain,
        router,
        jnp.pad(decode_ids, ((0, few - 4), (0, 0))),
        "first",
    )
    sides_1, block_2, decodes_0, other_down = fence(sides_1, block_2, decodes_0, other_down)
    weights = (expert_gate[0], expert_up[0], expert_down[0], other_gate, other_up, other_down)
    halves = (tokens, tokens, tokens, cut, tokens - cut)

    corner_1 = spread_corner(sides_1)
    sides_2 = spread_sides(block_2)
    arrived = around_z(jnp.concatenate([block_2, decodes_0], axis=0))
    sums_0 = apply((block_0,) + sides_0 + corner_0 + (decodes_0,), halves)
    corner_1, sides_2, arrived, sums_0 = fence(corner_1, sides_2, arrived, sums_0)
    block_3, decodes_1 = arrived[:tokens], arrived[tokens:]

    sides_3 = spread_sides(block_3)
    risen = around_z(jnp.concatenate(corner_1 + (decodes_1,), axis=0))
    passed_0 = return_corner(sums_0)
    sums_1 = apply((block_1,) + sides_1 + corner_1 + (decodes_1,), (tokens,) * 4)
    sides_3, risen, passed_0, sums_0, sums_1 = fence(sides_3, risen, passed_0, sums_0, sums_1)

    far = jnp.pad(sums_1[3], ((0, 0), (0, risen.shape[1] - sums_1[3].shape[1])))
    far = around_z(jnp.concatenate([far, risen[tokens:]], axis=0))
    corner_3 = spread_corner(sides_3)
    back_1 = return_sides(sums_1)
    sums_2 = apply((block_2,) + sides_2 + (risen,), (tokens,) * 4)
    far, corner_3, back_1, sums_1, sums_2 = fence(far, corner_3, back_1, sums_1, sums_2)
    decodes_3 = far[tokens:]

    far, first = join(sums_2[3], far, sums_1[0], *back_1)
    far = around_z(far)
    back_2 = return_sides(sums_2)
    carried_1 = around_z(first, -1)
    parts = (cut, tokens - cut)
    sums_3 = apply((block_3,) + sides_3 + corner_3 + (decodes_3,), (tokens,) + parts * 3)
    far, sums_2, sums_3 = fence(far, sums_2, sums_3)

    own, x_0, x_1, y_0, y_1, far_0, far_1 = sums_3
    far_0, far_1, x_1, y_0 = meet(far_0, far_1, far, x_1, y_0)
    passed_3 = along_y(far_0), along_x(far_1)
    back_x1, back_y0 = along_x(x_1), along_y(y_0)
    passed_3, carried_1 = fence(passed_3, carried_1)
    back_x0 = along_x(added(x_0, passed_3[0]).astype(jnp.bfloat16))
    back_y1 = along_y(added(y_1, passed_3[1]).astype(jnp.bfloat16))
    carried = around_z(added(sums_2[0], *back_2).astype(jnp.bfloat16))
    carried, passed_0, sums_0 = fence(carried, passed_0, sums_0)
    back_0 = return_sides(sums_0, passed_0)
    carried = around_z(gather_sums(own, back_x0, back_x1, back_y0, back_y1, carried))
    return added(hidden, sums_0[0], carried_1, *back_0, carried).astype(jnp.bfloat16)[None]


def chunk_cuts(tokens, devices):
    step = (tokens // 2 + 15) // 16 * 16 if devices < 128 else 32
    return [(start, min(start + step, tokens)) for start in range(0, tokens, step)]


def gathered_plan(
    queries,
    cache_keys,
    cache_values,
    lengths,
    sinks,
    out_proj,
    decode_resid,
    prefill_hidden,
    norm_gain,
    router,
    routes,
    expert_gate,
    expert_up,
    expert_down,
):
    experts = router.shape[1]
    ids = routes[0]
    tokens = ids.shape[0]
    prefill = prefill_hidden[0]
    devices = lax.axis_size(AXES)
    cuts = chunk_cuts(tokens, devices)
    my_expert = lax.axis_index("kv") * lax.axis_size("blk") + lax.axis_index("blk")
    expert = jnp.stack([my_expert, jnp.int32(experts)]).astype(jnp.int32)
    weights = (expert_gate[0], expert_up[0], expert_down[0])

    attended = attend(queries, cache_keys, cache_values, lengths, sinks)
    partial_proj = jnp.dot(attended, out_proj, preferred_element_type=jnp.float32)
    projected = lax.psum_scatter(partial_proj, "kv", scatter_dimension=0, tiled=True)
    decoded = (decode_resid.astype(jnp.float32) + projected).astype(jnp.bfloat16)
    hidden = jnp.concatenate([prefill, decoded], axis=0)
    ids = jnp.concatenate([ids[1:], ids[:1]], axis=0)
    gathered = []
    for start, stop in cuts:
        source = prefill[start:stop] if stop < tokens else hidden[start:stop]
        sent = prepare(source, norm_gain, router, ids[start:stop])
        gathered.append(lax.all_gather(sent, AXES, axis=0, tiled=True))
    returned = []
    for rows in gathered:
        sums = run_expert(expert, rows, *weights)
        returned.append(lax.psum_scatter(sums, AXES, scatter_dimension=0, tiled=True))
    combined = jnp.concatenate(returned, axis=0)
    layer_sum = (hidden.astype(jnp.float32) + combined.astype(jnp.float32)).astype(jnp.bfloat16)
    layer_sum = jnp.concatenate([layer_sum[-1:], layer_sum[:-1]], axis=0)
    return layer_sum[None]


def solution(mesh):
    plan = permuted_plan if (mesh.shape["kv"], mesh.shape["blk"]) == (4, 8) else gathered_plan
    return jax.shard_map(
        plan,
        mesh=mesh,
        in_specs=(
            P("blk", "kv"),
            P("blk", None, "kv", None),
            P("blk", None, "kv", None),
            P(),
            P("kv"),
            P("kv", None),
            P(("blk", "kv"), None),
            P(("blk", "kv"), None, None),
            P(),
            P(),
            P(("blk", "kv"), None, None),
            P(("kv", "blk"), None, None),
            P(("kv", "blk"), None, None),
            P(("kv", "blk"), None, None),
        ),
        out_specs=P(("blk", "kv"), None, None),
        check_vma=False,
    )
```

```python
import functools
import math

import jax
import jax.numpy as jnp
from jax import lax
from jax.experimental import pallas as pl
from jax.experimental.pallas import tpu as pltpu
from jax.sharding import PartitionSpec as P

NEG_FILL = -1e30
EPSILON = 1e-06
NOT_CHOSEN = -256.0
AXES = ("blk", "kv")


def attend(queries, cache_keys, cache_values, lengths, sinks):
    my_block = lax.axis_index("blk")
    per_block = queries.shape[0]
    head_count = sinks.shape[0]
    head_dim = cache_keys.shape[3]
    window = cache_keys.shape[1]
    grouped_q = queries.reshape(per_block, head_count, head_dim)
    key_rows = cache_keys[:, :, 0, :]
    value_rows = cache_values[:, :, 0, :]
    my_lengths = lax.dynamic_slice_in_dim(lengths, my_block * per_block, per_block)
    scores = jnp.einsum("rgd,rjd->rgj", grouped_q, key_rows, preferred_element_type=jnp.float32) * (
        1.0 / math.sqrt(head_dim)
    )
    first_valid = window - jnp.minimum(my_lengths, window)
    is_valid = (jnp.arange(window, dtype=jnp.int32)[None, :] >= first_valid[:, None])[:, None, :]
    masked = jnp.where(is_valid, scores, NEG_FILL)
    top_limit = jnp.maximum(jnp.max(masked, axis=2), sinks[None, :])
    weights = jnp.where(is_valid, jnp.exp(masked - top_limit[..., None]), 0.0)
    denominator = jnp.sum(weights, axis=2) + jnp.exp(sinks[None, :] - top_limit)
    numerator = jnp.einsum(
        "rgj,rjd->rgd", weights.astype(jnp.bfloat16), value_rows, preferred_element_type=jnp.float32
    )
    return (
        (numerator / denominator[..., None])
        .astype(jnp.bfloat16)
        .reshape(per_block, head_count * head_dim)
    )


def prepare_kernel(ranking, hidden_ref, gain_ref, router_ref, routes_ref, out_ref, *scratch):
    experts, width = router_ref.shape
    if scratch:
        (shifted,) = scratch
        shifted[0:1, :] = jnp.zeros((1, width), jnp.float32)
        shifted[1:, :] = hidden_ref[...].astype(jnp.float32)
        hidden = shifted[...]
    else:
        hidden = hidden_ref[...].astype(jnp.float32)
    rows = hidden.shape[0]
    mean_sq = jnp.mean(hidden * hidden, axis=1, keepdims=True)
    normed = (hidden * lax.rsqrt(mean_sq + EPSILON) * gain_ref[...]).astype(jnp.bfloat16)
    out_ref[:, :width] = normed
    by_lanes = (((1,), (1,)), ((), ()))
    logits = lax.dot_general(normed, router_ref[...], by_lanes, preferred_element_type=jnp.float32)
    routes = routes_ref[...]
    if ranking == "first":
        expert = lax.broadcasted_iota(jnp.int32, logits.shape, 1)
        mine = jnp.zeros(logits.shape, jnp.bool_)
        for k in range(routes.shape[1]):
            mine = mine | (expert == routes[:, k : k + 1])
    else:
        expert = lax.broadcasted_iota(jnp.int32, (experts, rows), 0)
        chosen = jnp.zeros(expert.shape, jnp.bool_)
        for k in range(routes.shape[0]):
            chosen = chosen | (expert == routes[k : k + 1, :])
        chosen = jnp.where(chosen, 1.0, 0.0).astype(jnp.bfloat16)
        row = lax.broadcasted_iota(jnp.int32, (rows, rows), 0)
        other = lax.broadcasted_iota(jnp.int32, (rows, rows), 1)

        def of_rows(taken):
            taken = jnp.where(taken, 1.0, 0.0).astype(jnp.bfloat16)
            return lax.dot_general(taken, chosen, by_lanes, preferred_element_type=jnp.float32)

        mine = of_rows(row == other) > 0.5
    top = jnp.max(jnp.where(mine, logits, NEG_FILL), axis=1, keepdims=True)
    raised = jnp.where(mine, jnp.exp(jnp.minimum(logits - top, 0.0)), 0.0)
    gates = raised / jnp.sum(raised, axis=1, keepdims=True)
    high = gates.astype(jnp.bfloat16).astype(jnp.float32)
    parts = [high, gates - high]
    if ranking == "block":
        parts.append(jnp.where(mine, of_rows(other < row), NOT_CHOSEN))
    elif ranking == "first":
        parts.append(jnp.where(mine, 0.0, NOT_CHOSEN))
    rest = out_ref.shape[1] - width - len(parts) * experts
    if rest:
        parts.append(jnp.zeros((rows, rest), jnp.float32))
    out_ref[:, width:] = jnp.concatenate(parts, axis=1).astype(jnp.bfloat16)


def prepare(hidden, norm_gain, router, routes, ranking=None):
    width = hidden.shape[1]
    rows = routes.shape[0]
    extra = -(-(3 if ranking else 2) * router.shape[1] // 128) * 128
    shifted = rows > hidden.shape[0]
    return pl.pallas_call(
        functools.partial(prepare_kernel, ranking),
        out_shape=jax.ShapeDtypeStruct((rows, width + extra), jnp.bfloat16),
        scratch_shapes=[pltpu.VMEM((rows, width), jnp.float32)] if shifted else [],
        compiler_params=pltpu.CompilerParams(vmem_limit_bytes=32 << 20),
        name="prepare",
    )(hidden, norm_gain.reshape(1, width), router.T, routes if ranking == "first" else routes.T)


def expert_kernel(expert_ref, rows_ref, gate_ref, up_ref, down_ref, out_ref):
    width = gate_ref.shape[0]
    payload = rows_ref[...]
    rows = payload[:, :width]
    tail = payload[:, width:].astype(jnp.float32)
    lane = lax.broadcasted_iota(jnp.int32, tail.shape, 1)
    expert = expert_ref[0]
    experts = expert_ref[1]
    mine = (lane == expert) | (lane == expert + experts)
    weight = jnp.sum(jnp.where(mine, tail, 0.0), axis=1, keepdims=True)
    gate_act = jnp.dot(rows, gate_ref[...], preferred_element_type=jnp.float32)
    up_act = jnp.dot(rows, up_ref[...], preferred_element_type=jnp.float32)
    inner = (gate_act / (1.0 + jnp.exp(-gate_act)) * up_act).astype(jnp.bfloat16)
    result = jnp.dot(inner, down_ref[...], preferred_element_type=jnp.float32)
    out_ref[...] = (weight * result).astype(jnp.bfloat16)


def run_expert(expert, rows, gate_weights, up_weights, down_weights):
    total, padded = rows.shape
    width, hidden_units = gate_weights.shape
    tile = 256
    return pl.pallas_call(
        expert_kernel,
        grid_spec=pltpu.PrefetchScalarGridSpec(
            num_scalar_prefetch=1,
            grid=(total // tile,),
            in_specs=[
                pl.BlockSpec((tile, padded), lambda i, e: (i, 0)),
                pl.BlockSpec((width, hidden_units), lambda i, e: (0, 0), pipeline_mode=pl.Buffered(1)),
                pl.BlockSpec((width, hidden_units), lambda i, e: (0, 0), pipeline_mode=pl.Buffered(1)),
                pl.BlockSpec((hidden_units, width), lambda i, e: (0, 0), pipeline_mode=pl.Buffered(1)),
            ],
            out_specs=pl.BlockSpec((tile, width), lambda i, e: (i, 0)),
        ),
        out_shape=jax.ShapeDtypeStruct((total, width), jnp.bfloat16),
        compiler_params=pltpu.CompilerParams(vmem_limit_bytes=48 << 20),
        name="expert",
    )(expert, rows, gate_weights, up_weights, down_weights)


def plane_kernel(cap, piece_rows, block_rows, *refs):
    refs = list(refs)
    ids_ref = refs.pop(0)
    sources = [refs.pop(0) for _ in piece_rows]
    weight_refs = [refs.pop(0) for _ in range(6)]
    targets = [refs.pop(0) for _ in block_rows]
    rows, weights, downs, slots, inner, results, spread, weight_sem = refs
    width = results.shape[2]
    tokens = block_rows[0]
    pair_rows = 2 * tokens
    pair_slots = 2 * cap
    up_copies = [
        pltpu.make_async_copy(weight_refs[3 * e + i], weights.at[2 * e + i], weight_sem.at[2 * e + i])
        for e in range(2)
        for i in range(2)
    ]
    down_copies = [
        pltpu.make_async_copy(weight_refs[3 * e + 2], downs.at[e], weight_sem.at[4 + e])
        for e in range(2)
    ]
    for copy in up_copies + down_copies:
        copy.start()
    few = piece_rows[-1] - (2 * pair_rows - sum(piece_rows[:-1]))
    at = 0
    for ref, count in zip(sources, piece_rows):
        if ref is sources[-1]:
            count -= few
            decodes = ref[count:, :].astype(jnp.float32)
        if count:
            rows[pl.ds(at, count), :] = ref[:count, :]
        at += count
    is_first = lax.broadcasted_iota(jnp.int32, (few, 1), 0) == 0
    for j in range(4):
        part = pl.ds(j * tokens, few)
        kept = rows[part, :].astype(jnp.float32)
        rows[part, :] = jnp.where(is_first, decodes[j : j + 1], kept).astype(jnp.bfloat16)

    experts = ids_ref[2]
    extra = rows.shape[1] - width
    lanes = lax.broadcasted_iota(jnp.int32, (8, extra), 1)
    line = lax.broadcasted_iota(jnp.int32, (8, extra), 0)
    wanted = ((line == 0) & (lanes == ids_ref[0] + 2 * experts)) | (
        (line == 1) & (lanes == ids_ref[1] + 2 * experts)
    )
    wanted = jnp.where(wanted, 1.0, 0.0).astype(jnp.bfloat16)
    pairs = [pl.ds(p * pair_rows, pair_rows) for p in range(2)]

    def shift_of(shape, axis):
        second = lax.broadcasted_iota(jnp.int32, shape, axis) >= tokens
        return jnp.where(second, float(cap), 0.0)

    for p in range(2):
        ranks = lax.dot_general(
            wanted, rows[pairs[p], width:], (((1,), (1,)), ((), ())), preferred_element_type=jnp.float32
        )
        ranks += shift_of(ranks.shape, 1)
        slot = lax.broadcasted_iota(jnp.int32, (2 * pair_slots, pair_rows), 0).astype(jnp.float32)
        taken = (slot == ranks[0:1]) | (slot == ranks[1:2] + float(pair_slots))
        taken = jnp.where(taken, 1.0, 0.0).astype(jnp.bfloat16)
        picked = jnp.dot(taken, rows[pairs[p], :], preferred_element_type=jnp.float32)
        picked = picked.astype(jnp.bfloat16)
        for e in range(2):
            slots[e, pl.ds(p * pair_slots, pair_slots), :] = picked[e * pair_slots : (e + 1) * pair_slots]

    def make_spread(p):
        tail = rows[pairs[p], width:].astype(jnp.float32)
        lane = lax.broadcasted_iota(jnp.int32, tail.shape, 1)
        slot = lax.broadcasted_iota(jnp.int32, (pair_rows, 2 * pair_slots), 1).astype(jnp.float32)
        back = jnp.zeros(slot.shape, jnp.bool_)
        for e in range(2):
            mine = lane == ids_ref[e] + 2 * experts
            rank = jnp.sum(jnp.where(mine, tail, 0.0), axis=1, keepdims=True)
            back = back | (slot == rank + shift_of(rank.shape, 0) + float(e * pair_slots))
        spread[p] = jnp.where(back, 1.0, 0.0).astype(jnp.bfloat16)

    def weight_of(e):
        tail = slots[e, :, width:].astype(jnp.float32)
        lane = lax.broadcasted_iota(jnp.int32, tail.shape, 1)
        mine = (lane == ids_ref[e]) | (lane == ids_ref[e] + experts)
        return jnp.sum(jnp.where(mine, tail, 0.0), axis=1, keepdims=True)

    def product(e, i):
        return jnp.dot(slots[e, :, :width], weights[2 * e + i], preferred_element_type=jnp.float32)

    def activate(e, gate_act, up_act):
        act = gate_act / (1.0 + jnp.exp(-gate_act)) * up_act * weight_of(e)
        inner[e] = act.astype(jnp.bfloat16)

    def finish(e):
        result = jnp.dot(inner[e], downs[e], preferred_element_type=jnp.float32)
        result = result.astype(jnp.bfloat16)
        for p in range(2):
            results[p, pl.ds(e * pair_slots, pair_slots), :] = result[p * pair_slots : (p + 1) * pair_slots]

    up_copies[0].wait()
    gate_0 = product(0, 0)
    make_spread(0)
    up_copies[1].wait()
    up_0 = product(0, 1)
    make_spread(1)
    up_copies[2].wait()
    activate(0, gate_0, up_0)
    gate_1 = product(1, 0)
    up_copies[3].wait()
    up_1 = product(1, 1)
    down_copies[0].wait()
    finish(0)
    activate(1, gate_1, up_1)
    down_copies[1].wait()
    finish(1)
    ends = [sum(block_rows[: i + 1]) for i in range(len(block_rows))]
    for p in range(2):
        total = jnp.dot(spread[p], results[p], preferred_element_type=jnp.float32)
        total = total.astype(jnp.bfloat16)
        for ref, count, end in zip(targets, block_rows, ends):
            if p * pair_rows < end <= (p + 1) * pair_rows:
                at = end - count - p * pair_rows
                ref[...] = total[at : at + count]


def run_plane(ids, cap, few, pieces, block_rows, weights):
    width, units = weights[0].shape
    padded = pieces[0].shape[1]
    piece_rows = tuple(piece.shape[0] for piece in pieces)
    total = sum(piece_rows) - few
    kept = jnp.bfloat16
    anywhere = pl.BlockSpec(memory_space=pl.ANY)
    return pl.pallas_call(
        functools.partial(plane_kernel, cap, piece_rows, block_rows),
        in_specs=[pl.BlockSpec(memory_space=pltpu.SMEM)]
        + [pl.BlockSpec(memory_space=pltpu.VMEM)] * len(pieces)
        + [anywhere] * 6,
        out_specs=[pl.BlockSpec(memory_space=pltpu.VMEM)] * len(block_rows),
        out_shape=[jax.ShapeDtypeStruct((count, width), kept) for count in block_rows],
        scratch_shapes=[
            pltpu.VMEM((total, padded), kept),
            pltpu.VMEM((4, width, units), kept),
            pltpu.VMEM((2, units, width), kept),
            pltpu.VMEM((2, 4 * cap, padded), kept),
            pltpu.VMEM((2, 4 * cap, units), kept),
            pltpu.VMEM((2, 4 * cap, width), kept),
            pltpu.VMEM((2, total // 2, 4 * cap), kept),
            pltpu.SemaphoreType.DMA((6,)),
        ],
        compiler_params=pltpu.CompilerParams(vmem_limit_bytes=48 << 20),
        cost_estimate=pl.CostEstimate(
            flops=12 * total * width * units, bytes_accessed=24 << 20, transcendentals=total * units
        ),
        name="plane",
    )(ids, *pieces, *weights)


def merge_kernel(cut, x_ref, y_ref, passed_0_ref, passed_1_ref, x_out, y_out):
    def sum_of(one, other):
        return (one.astype(jnp.float32) + other.astype(jnp.float32)).astype(jnp.bfloat16)

    x_out[:cut, :] = sum_of(x_ref[:cut, :], passed_0_ref[...])
    x_out[cut:, :] = x_ref[cut:, :]
    y_out[:cut, :] = y_ref[:cut, :]
    y_out[cut:, :] = sum_of(y_ref[cut:, :], passed_1_ref[...])


def merge_passed(cut, to_x, to_y, passed_0, passed_1):
    return pl.pallas_call(
        functools.partial(merge_kernel, cut),
        out_shape=[jax.ShapeDtypeStruct(to_x.shape, to_x.dtype)] * 2,
        compiler_params=pltpu.CompilerParams(vmem_limit_bytes=16 << 20),
        name="merge",
    )(to_x, to_y, passed_0, passed_1)


def join_kernel(far_ref, risen_ref, own_ref, x_ref, y_ref, far_out, own_out):
    rows, width = far_ref.shape
    far = far_ref[...].astype(jnp.float32) + risen_ref[:rows, :width].astype(jnp.float32)
    far_out[...] = far.astype(jnp.bfloat16)
    total = own_ref[...].astype(jnp.float32) + x_ref[...].astype(jnp.float32) + y_ref[...].astype(jnp.float32)
    own_out[...] = total.astype(jnp.bfloat16)


def join(far, risen, own, from_x, from_y):
    return pl.pallas_call(
        join_kernel,
        out_shape=[jax.ShapeDtypeStruct(own.shape, own.dtype)] * 2,
        compiler_params=pltpu.CompilerParams(vmem_limit_bytes=16 << 20),
        name="join",
    )(far, risen, own, from_x, from_y)


def meet_kernel(far_0_ref, far_1_ref, risen_ref, x_ref, out_0, out_1, x_out):
    x_out[...] = x_ref[...]
    cut = out_0.shape[0]
    risen = risen_ref[...].astype(jnp.float32)
    out_0[...] = (far_0_ref[...].astype(jnp.float32) + risen[:cut]).astype(jnp.bfloat16)
    out_1[...] = (far_1_ref[...].astype(jnp.float32) + risen[cut:]).astype(jnp.bfloat16)


def meet(far_0, far_1, risen, x_part):
    outputs = (far_0, far_1, x_part)
    return pl.pallas_call(
        meet_kernel,
        out_shape=[jax.ShapeDtypeStruct(output.shape, output.dtype) for output in outputs],
        compiler_params=pltpu.CompilerParams(vmem_limit_bytes=16 << 20),
        name="meet",
    )(far_0, far_1, risen, x_part)


def join_passed_kernel(one_ref, passed_ref, other_ref, one_out, other_out):
    one_out[...] = (one_ref[...].astype(jnp.float32) + passed_ref[...].astype(jnp.float32)).astype(jnp.bfloat16)
    other_out[...] = other_ref[...]


def join_passed(one, passed, other):
    return pl.pallas_call(
        join_passed_kernel,
        out_shape=[jax.ShapeDtypeStruct(part.shape, part.dtype) for part in (one, other)],
        compiler_params=pltpu.CompilerParams(vmem_limit_bytes=16 << 20),
        name="join_passed",
    )(one, passed, other)


def along_x(value):
    return lax.ppermute(value, "kv", [(i, i ^ 1) for i in range(4)])


def along_y(value):
    return lax.ppermute(value, "kv", [(i, i ^ 2) for i in range(4)])


def around_z(value, hops=1):
    return lax.ppermute(value, "blk", [(i, (i + 2 * hops) % 8) for i in range(8)])


def across_chip(value):
    return lax.ppermute(value, "blk", [(i, i ^ 1) for i in range(8)])


def fence(*values):
    return lax.optimization_barrier(values)


def added(*parts):
    total = parts[0].astype(jnp.float32)
    for part in parts[1:]:
        total = total + part.astype(jnp.float32)
    return total


def permuted_plan(
    queries,
    cache_keys,
    cache_values,
    lengths,
    sinks,
    out_proj,
    decode_resid,
    prefill_hidden,
    norm_gain,
    router,
    routes,
    expert_gate,
    expert_up,
    expert_down,
):
    experts = router.shape[1]
    ids = routes[0]
    tokens = ids.shape[0]
    my_kv = lax.axis_index("kv")
    my_blk = lax.axis_index("blk")
    first_expert = my_kv * 8
    expert_ids = jnp.stack(
        [first_expert + my_blk, first_expert + (my_blk ^ 1), jnp.int32(experts)]
    ).astype(jnp.int32)
    cap = (2 * tokens * ids.shape[1] + experts - 1) // experts
    cut = tokens // 2 // 16 * 16
    few = 16

    def spread_sides(block):
        return along_x(block), along_y(block)

    def spread_corner(sides):
        return along_y(sides[0][:cut]), along_x(sides[1][cut:])

    def apply(pieces, counts):
        return run_plane(expert_ids, cap, few, pieces, counts, weights)

    def return_corner(sums):
        return along_y(sums[3]), along_x(sums[4])

    def return_sides(sums, passed=None):
        to_x, to_y = sums[1:3] if passed is None else merge_passed(cut, *sums[1:3], *passed)
        return along_x(to_x), along_y(to_y)

    prefill = prefill_hidden[0]
    block_0 = prepare(prefill, norm_gain, router, ids, "block")
    block_0, queries, cache_keys, expert_gate = fence(block_0, queries, cache_keys, expert_gate)
    block_1 = around_z(block_0)
    sides_0 = spread_sides(block_0)
    other_gate = across_chip(expert_gate[0])
    attended = attend(queries, cache_keys, cache_values, lengths, sinks)
    partial_proj = jnp.dot(attended, out_proj, preferred_element_type=jnp.float32)
    is_mine = jnp.arange(4)[:, None] == my_kv
    partial_proj += jnp.where(is_mine, decode_resid.astype(jnp.float32), 0.0)
    width = partial_proj.shape[1]
    ids_row = jnp.pad(ids[:1].astype(jnp.float32), ((0, 0), (0, width - ids.shape[1])))
    shared = jnp.concatenate([partial_proj, jnp.where(is_mine, ids_row, 0.0)], axis=0)
    shared = shared + along_x(shared)
    sides_0, block_1, other_gate = fence(sides_0, block_1, other_gate)

    corner_0 = spread_corner(sides_0)
    other_up = across_chip(expert_up[0])
    corner_0, shared, block_1, other_up, expert_down = fence(
        corner_0, shared, block_1, other_up, expert_down
    )

    shared = shared + along_y(shared)
    sides_1 = spread_sides(block_1)
    block_2 = around_z(block_1)
    other_down = across_chip(expert_down[0])
    order = [my_kv ^ j for j in range(4)]
    decoded = jnp.concatenate(
        [lax.dynamic_slice_in_dim(shared, index, 1) for index in order], axis=0
    ).astype(jnp.bfloat16)
    decode_ids = jnp.concatenate(
        [lax.dynamic_slice_in_dim(shared, 4 + index, 1) for index in order], axis=0
    )[:, : ids.shape[1]].astype(jnp.int32)
    hidden = jnp.concatenate([decoded[:1], prefill], axis=0)
    decodes_0 = prepare(
        jnp.pad(decoded, ((0, few - 4), (0, 0))),
        norm_gain,
        router,
        jnp.pad(decode_ids, ((0, few - 4), (0, 0))),
        "first",
    )
    sides_1, block_2, decodes_0, other_down = fence(sides_1, block_2, decodes_0, other_down)
    weights = (expert_gate[0], expert_up[0], expert_down[0], other_gate, other_up, other_down)
    halves = (tokens, tokens, tokens, cut, tokens - cut)

    corner_1 = spread_corner(sides_1)
    sides_2 = spread_sides(block_2)
    arrived = around_z(jnp.concatenate([block_2, decodes_0], axis=0))
    sums_0 = apply((block_0,) + sides_0 + corner_0 + (decodes_0,), halves)
    corner_1, sides_2, arrived, sums_0 = fence(corner_1, sides_2, arrived, sums_0)
    block_3, decodes_1 = arrived[:tokens], arrived[tokens:]

    sides_3 = spread_sides(block_3)
    risen = around_z(jnp.concatenate(corner_1 + (decodes_1,), axis=0))
    passed_0 = return_corner(sums_0)
    sums_1 = apply((block_1,) + sides_1 + corner_1 + (decodes_1,), (tokens,) * 4)
    sides_3, risen, passed_0, sums_0, sums_1 = fence(sides_3, risen, passed_0, sums_0, sums_1)

    far = jnp.pad(sums_1[3], ((0, 0), (0, risen.shape[1] - sums_1[3].shape[1])))
    far = around_z(jnp.concatenate([far, risen[tokens:]], axis=0))
    corner_3 = spread_corner(sides_3)
    back_1 = return_sides(sums_1)
    sums_2 = apply((block_2,) + sides_2 + (risen,), (tokens,) * 4)
    far, corner_3, back_1, sums_1, sums_2 = fence(far, corner_3, back_1, sums_1, sums_2)
    decodes_3 = far[tokens:]

    far, first = join(sums_2[3], far, sums_1[0], *back_1)
    far = around_z(far)
    back_2 = return_sides(sums_2)
    carried_1 = around_z(first, -1)
    parts = (cut, tokens - cut)
    sums_3 = apply((block_3,) + sides_3 + corner_3 + (decodes_3,), (tokens,) + parts * 3)
    far, sums_2, sums_3 = fence(far, sums_2, sums_3)

    own, x_0, x_1, y_0, y_1, far_0, far_1 = sums_3
    far_0, far_1, x_1 = meet(far_0, far_1, far, x_1)
    passed_3 = along_y(far_0), along_x(far_1)
    back_x1 = along_x(x_1)
    passed_3, carried_1 = fence(passed_3, carried_1)
    y_1, y_0 = join_passed(y_1, passed_3[1], y_0)
    back_y1 = along_y(y_1)
    back_x0 = along_x(added(x_0, passed_3[0]).astype(jnp.bfloat16))
    back_y0 = along_y(y_0)
    carried = around_z(added(sums_2[0], *back_2).astype(jnp.bfloat16))
    carried, passed_0, sums_0 = fence(carried, passed_0, sums_0)
    back_0 = return_sides(sums_0, passed_0)
    late = around_z(added(own[cut:], back_x1, back_y1, carried[cut:]).astype(jnp.bfloat16))
    early = around_z(added(own[:cut], back_x0, back_y0, carried[:cut]).astype(jnp.bfloat16))
    carried = jnp.concatenate([early, late], axis=0)
    return added(hidden, sums_0[0], carried_1, *back_0, carried).astype(jnp.bfloat16)[None]


def chunk_cuts(tokens, devices):
    step = (tokens // 2 + 15) // 16 * 16 if devices < 128 else 32
    return [(start, min(start + step, tokens)) for start in range(0, tokens, step)]


def gathered_plan(
    queries,
    cache_keys,
    cache_values,
    lengths,
    sinks,
    out_proj,
    decode_resid,
    prefill_hidden,
    norm_gain,
    router,
    routes,
    expert_gate,
    expert_up,
    expert_down,
):
    experts = router.shape[1]
    ids = routes[0]
    tokens = ids.shape[0]
    prefill = prefill_hidden[0]
    devices = lax.axis_size(AXES)
    cuts = chunk_cuts(tokens, devices)
    my_expert = lax.axis_index("kv") * lax.axis_size("blk") + lax.axis_index("blk")
    expert = jnp.stack([my_expert, jnp.int32(experts)]).astype(jnp.int32)
    weights = (expert_gate[0], expert_up[0], expert_down[0])

    attended = attend(queries, cache_keys, cache_values, lengths, sinks)
    partial_proj = jnp.dot(attended, out_proj, preferred_element_type=jnp.float32)
    projected = lax.psum_scatter(partial_proj, "kv", scatter_dimension=0, tiled=True)
    decoded = (decode_resid.astype(jnp.float32) + projected).astype(jnp.bfloat16)
    hidden = jnp.concatenate([prefill, decoded], axis=0)
    ids = jnp.concatenate([ids[1:], ids[:1]], axis=0)
    gathered = []
    for start, stop in cuts:
        source = prefill[start:stop] if stop < tokens else hidden[start:stop]
        sent = prepare(source, norm_gain, router, ids[start:stop])
        gathered.append(lax.all_gather(sent, AXES, axis=0, tiled=True))
    returned = []
    for rows in gathered:
        sums = run_expert(expert, rows, *weights)
        returned.append(lax.psum_scatter(sums, AXES, scatter_dimension=0, tiled=True))
    combined = jnp.concatenate(returned, axis=0)
    layer_sum = (hidden.astype(jnp.float32) + combined.astype(jnp.float32)).astype(jnp.bfloat16)
    layer_sum = jnp.concatenate([layer_sum[-1:], layer_sum[:-1]], axis=0)
    return layer_sum[None]


def solution(mesh):
    plan = permuted_plan if (mesh.shape["kv"], mesh.shape["blk"]) == (4, 8) else gathered_plan
    return jax.shard_map(
        plan,
        mesh=mesh,
        in_specs=(
            P("blk", "kv"),
            P("blk", None, "kv", None),
            P("blk", None, "kv", None),
            P(),
            P("kv"),
            P("kv", None),
            P(("blk", "kv"), None),
            P(("blk", "kv"), None, None),
            P(),
            P(),
            P(("blk", "kv"), None, None),
            P(("kv", "blk"), None, None),
            P(("kv", "blk"), None, None),
            P(("kv", "blk"), None, None),
        ),
        out_specs=P(("blk", "kv"), None, None),
        check_vma=False,
    )
```

```python
import functools
import math

import jax
import jax.numpy as jnp
from jax import lax
from jax.experimental import pallas as pl
from jax.experimental.pallas import tpu as pltpu
from jax.sharding import PartitionSpec as P

NEG_FILL = -1e30
EPSILON = 1e-06
NOT_CHOSEN = -256.0
AXES = ("blk", "kv")


def attend(queries, cache_keys, cache_values, lengths, sinks):
    my_block = lax.axis_index("blk")
    per_block = queries.shape[0]
    head_count = sinks.shape[0]
    head_dim = cache_keys.shape[3]
    window = cache_keys.shape[1]
    grouped_q = queries.reshape(per_block, head_count, head_dim)
    key_rows = cache_keys[:, :, 0, :]
    value_rows = cache_values[:, :, 0, :]
    my_lengths = lax.dynamic_slice_in_dim(lengths, my_block * per_block, per_block)
    scores = jnp.einsum("rgd,rjd->rgj", grouped_q, key_rows, preferred_element_type=jnp.float32) * (
        1.0 / math.sqrt(head_dim)
    )
    first_valid = window - jnp.minimum(my_lengths, window)
    is_valid = (jnp.arange(window, dtype=jnp.int32)[None, :] >= first_valid[:, None])[:, None, :]
    masked = jnp.where(is_valid, scores, NEG_FILL)
    top_limit = jnp.maximum(jnp.max(masked, axis=2), sinks[None, :])
    weights = jnp.where(is_valid, jnp.exp(masked - top_limit[..., None]), 0.0)
    denominator = jnp.sum(weights, axis=2) + jnp.exp(sinks[None, :] - top_limit)
    numerator = jnp.einsum(
        "rgj,rjd->rgd", weights.astype(jnp.bfloat16), value_rows, preferred_element_type=jnp.float32
    )
    return (
        (numerator / denominator[..., None])
        .astype(jnp.bfloat16)
        .reshape(per_block, head_count * head_dim)
    )


def prepare_kernel(ranking, hidden_ref, gain_ref, router_ref, routes_ref, out_ref, *scratch):
    experts, width = router_ref.shape
    if scratch:
        (shifted,) = scratch
        shifted[0:1, :] = jnp.zeros((1, width), jnp.float32)
        shifted[1:, :] = hidden_ref[...].astype(jnp.float32)
        hidden = shifted[...]
    else:
        hidden = hidden_ref[...].astype(jnp.float32)
    rows = hidden.shape[0]
    mean_sq = jnp.mean(hidden * hidden, axis=1, keepdims=True)
    normed = (hidden * lax.rsqrt(mean_sq + EPSILON) * gain_ref[...]).astype(jnp.bfloat16)
    out_ref[:, :width] = normed
    by_lanes = (((1,), (1,)), ((), ()))
    logits = lax.dot_general(normed, router_ref[...], by_lanes, preferred_element_type=jnp.float32)
    routes = routes_ref[...]
    if ranking == "first":
        expert = lax.broadcasted_iota(jnp.int32, logits.shape, 1)
        mine = jnp.zeros(logits.shape, jnp.bool_)
        for k in range(routes.shape[1]):
            mine = mine | (expert == routes[:, k : k + 1])
    else:
        expert = lax.broadcasted_iota(jnp.int32, (experts, rows), 0)
        chosen = jnp.zeros(expert.shape, jnp.bool_)
        for k in range(routes.shape[0]):
            chosen = chosen | (expert == routes[k : k + 1, :])
        chosen = jnp.where(chosen, 1.0, 0.0).astype(jnp.bfloat16)
        row = lax.broadcasted_iota(jnp.int32, (rows, rows), 0)
        other = lax.broadcasted_iota(jnp.int32, (rows, rows), 1)

        def of_rows(taken):
            taken = jnp.where(taken, 1.0, 0.0).astype(jnp.bfloat16)
            return lax.dot_general(taken, chosen, by_lanes, preferred_element_type=jnp.float32)

        mine = of_rows(row == other) > 0.5
    top = jnp.max(jnp.where(mine, logits, NEG_FILL), axis=1, keepdims=True)
    raised = jnp.where(mine, jnp.exp(jnp.minimum(logits - top, 0.0)), 0.0)
    gates = raised / jnp.sum(raised, axis=1, keepdims=True)
    high = gates.astype(jnp.bfloat16).astype(jnp.float32)
    parts = [high, gates - high]
    if ranking == "block":
        parts.append(jnp.where(mine, of_rows(other < row), NOT_CHOSEN))
    elif ranking == "first":
        parts.append(jnp.where(mine, 0.0, NOT_CHOSEN))
    rest = out_ref.shape[1] - width - len(parts) * experts
    if rest:
        parts.append(jnp.zeros((rows, rest), jnp.float32))
    out_ref[:, width:] = jnp.concatenate(parts, axis=1).astype(jnp.bfloat16)


def prepare(hidden, norm_gain, router, routes, ranking=None):
    width = hidden.shape[1]
    rows = routes.shape[0]
    extra = -(-(3 if ranking else 2) * router.shape[1] // 128) * 128
    shifted = rows > hidden.shape[0]
    return pl.pallas_call(
        functools.partial(prepare_kernel, ranking),
        out_shape=jax.ShapeDtypeStruct((rows, width + extra), jnp.bfloat16),
        scratch_shapes=[pltpu.VMEM((rows, width), jnp.float32)] if shifted else [],
        compiler_params=pltpu.CompilerParams(vmem_limit_bytes=32 << 20),
        name="prepare",
    )(hidden, norm_gain.reshape(1, width), router.T, routes if ranking == "first" else routes.T)


def expert_kernel(expert_ref, rows_ref, gate_ref, up_ref, down_ref, out_ref):
    width = gate_ref.shape[0]
    payload = rows_ref[...]
    rows = payload[:, :width]
    tail = payload[:, width:].astype(jnp.float32)
    lane = lax.broadcasted_iota(jnp.int32, tail.shape, 1)
    expert = expert_ref[0]
    experts = expert_ref[1]
    mine = (lane == expert) | (lane == expert + experts)
    weight = jnp.sum(jnp.where(mine, tail, 0.0), axis=1, keepdims=True)
    gate_act = jnp.dot(rows, gate_ref[...], preferred_element_type=jnp.float32)
    up_act = jnp.dot(rows, up_ref[...], preferred_element_type=jnp.float32)
    inner = (gate_act / (1.0 + jnp.exp(-gate_act)) * up_act).astype(jnp.bfloat16)
    result = jnp.dot(inner, down_ref[...], preferred_element_type=jnp.float32)
    out_ref[...] = (weight * result).astype(jnp.bfloat16)


def run_expert(expert, rows, gate_weights, up_weights, down_weights):
    total, padded = rows.shape
    width, hidden_units = gate_weights.shape
    tile = 256
    return pl.pallas_call(
        expert_kernel,
        grid_spec=pltpu.PrefetchScalarGridSpec(
            num_scalar_prefetch=1,
            grid=(total // tile,),
            in_specs=[
                pl.BlockSpec((tile, padded), lambda i, e: (i, 0)),
                pl.BlockSpec((width, hidden_units), lambda i, e: (0, 0), pipeline_mode=pl.Buffered(1)),
                pl.BlockSpec((width, hidden_units), lambda i, e: (0, 0), pipeline_mode=pl.Buffered(1)),
                pl.BlockSpec((hidden_units, width), lambda i, e: (0, 0), pipeline_mode=pl.Buffered(1)),
            ],
            out_specs=pl.BlockSpec((tile, width), lambda i, e: (i, 0)),
        ),
        out_shape=jax.ShapeDtypeStruct((total, width), jnp.bfloat16),
        compiler_params=pltpu.CompilerParams(vmem_limit_bytes=48 << 20),
        name="expert",
    )(expert, rows, gate_weights, up_weights, down_weights)


def plane_kernel(cap, piece_rows, block_rows, *refs):
    refs = list(refs)
    ids_ref = refs.pop(0)
    sources = [refs.pop(0) for _ in piece_rows]
    weight_refs = [refs.pop(0) for _ in range(6)]
    targets = [refs.pop(0) for _ in block_rows]
    rows, weights, downs, slots, inner, results, spread, weight_sem = refs
    width = results.shape[2]
    tokens = block_rows[0]
    pair_rows = 2 * tokens
    pair_slots = 2 * cap
    up_copies = [
        pltpu.make_async_copy(weight_refs[3 * e + i], weights.at[2 * e + i], weight_sem.at[2 * e + i])
        for e in range(2)
        for i in range(2)
    ]
    down_copies = [
        pltpu.make_async_copy(weight_refs[3 * e + 2], downs.at[e], weight_sem.at[4 + e])
        for e in range(2)
    ]
    for copy in up_copies + down_copies:
        copy.start()
    few = piece_rows[-1] - (2 * pair_rows - sum(piece_rows[:-1]))
    at = 0
    for ref, count in zip(sources, piece_rows):
        if ref is sources[-1]:
            count -= few
            decodes = ref[count:, :].astype(jnp.float32)
        if count:
            rows[pl.ds(at, count), :] = ref[:count, :]
        at += count
    is_first = lax.broadcasted_iota(jnp.int32, (few, 1), 0) == 0
    for j in range(4):
        part = pl.ds(j * tokens, few)
        kept = rows[part, :].astype(jnp.float32)
        rows[part, :] = jnp.where(is_first, decodes[j : j + 1], kept).astype(jnp.bfloat16)

    experts = ids_ref[2]
    extra = rows.shape[1] - width
    lanes = lax.broadcasted_iota(jnp.int32, (8, extra), 1)
    line = lax.broadcasted_iota(jnp.int32, (8, extra), 0)
    wanted = ((line == 0) & (lanes == ids_ref[0] + 2 * experts)) | (
        (line == 1) & (lanes == ids_ref[1] + 2 * experts)
    )
    wanted = jnp.where(wanted, 1.0, 0.0).astype(jnp.bfloat16)
    pairs = [pl.ds(p * pair_rows, pair_rows) for p in range(2)]

    def shift_of(shape, axis):
        second = lax.broadcasted_iota(jnp.int32, shape, axis) >= tokens
        return jnp.where(second, float(cap), 0.0)

    for p in range(2):
        ranks = lax.dot_general(
            wanted, rows[pairs[p], width:], (((1,), (1,)), ((), ())), preferred_element_type=jnp.float32
        )
        ranks += shift_of(ranks.shape, 1)
        slot = lax.broadcasted_iota(jnp.int32, (2 * pair_slots, pair_rows), 0).astype(jnp.float32)
        taken = (slot == ranks[0:1]) | (slot == ranks[1:2] + float(pair_slots))
        taken = jnp.where(taken, 1.0, 0.0).astype(jnp.bfloat16)
        picked = jnp.dot(taken, rows[pairs[p], :], preferred_element_type=jnp.float32)
        picked = picked.astype(jnp.bfloat16)
        for e in range(2):
            slots[e, pl.ds(p * pair_slots, pair_slots), :] = picked[e * pair_slots : (e + 1) * pair_slots]

    def make_spread(p):
        tail = rows[pairs[p], width:].astype(jnp.float32)
        lane = lax.broadcasted_iota(jnp.int32, tail.shape, 1)
        slot = lax.broadcasted_iota(jnp.int32, (pair_rows, 2 * pair_slots), 1).astype(jnp.float32)
        back = jnp.zeros(slot.shape, jnp.bool_)
        for e in range(2):
            mine = lane == ids_ref[e] + 2 * experts
            rank = jnp.sum(jnp.where(mine, tail, 0.0), axis=1, keepdims=True)
            back = back | (slot == rank + shift_of(rank.shape, 0) + float(e * pair_slots))
        spread[p] = jnp.where(back, 1.0, 0.0).astype(jnp.bfloat16)

    def weight_of(e):
        tail = slots[e, :, width:].astype(jnp.float32)
        lane = lax.broadcasted_iota(jnp.int32, tail.shape, 1)
        mine = (lane == ids_ref[e]) | (lane == ids_ref[e] + experts)
        return jnp.sum(jnp.where(mine, tail, 0.0), axis=1, keepdims=True)

    def product(e, i):
        return jnp.dot(slots[e, :, :width], weights[2 * e + i], preferred_element_type=jnp.float32)

    def activate(e, gate_act, up_act):
        act = gate_act / (1.0 + jnp.exp(-gate_act)) * up_act * weight_of(e)
        inner[e] = act.astype(jnp.bfloat16)

    def finish(e):
        result = jnp.dot(inner[e], downs[e], preferred_element_type=jnp.float32)
        result = result.astype(jnp.bfloat16)
        for p in range(2):
            results[p, pl.ds(e * pair_slots, pair_slots), :] = result[p * pair_slots : (p + 1) * pair_slots]

    up_copies[0].wait()
    gate_0 = product(0, 0)
    make_spread(0)
    up_copies[1].wait()
    up_0 = product(0, 1)
    make_spread(1)
    up_copies[2].wait()
    activate(0, gate_0, up_0)
    gate_1 = product(1, 0)
    up_copies[3].wait()
    up_1 = product(1, 1)
    down_copies[0].wait()
    finish(0)
    activate(1, gate_1, up_1)
    down_copies[1].wait()
    finish(1)
    ends = [sum(block_rows[: i + 1]) for i in range(len(block_rows))]
    for p in range(2):
        total = jnp.dot(spread[p], results[p], preferred_element_type=jnp.float32)
        total = total.astype(jnp.bfloat16)
        for ref, count, end in zip(targets, block_rows, ends):
            if p * pair_rows < end <= (p + 1) * pair_rows:
                at = end - count - p * pair_rows
                ref[...] = total[at : at + count]


def run_plane(ids, cap, few, pieces, block_rows, weights):
    width, units = weights[0].shape
    padded = pieces[0].shape[1]
    piece_rows = tuple(piece.shape[0] for piece in pieces)
    total = sum(piece_rows) - few
    kept = jnp.bfloat16
    anywhere = pl.BlockSpec(memory_space=pl.ANY)
    return pl.pallas_call(
        functools.partial(plane_kernel, cap, piece_rows, block_rows),
        in_specs=[pl.BlockSpec(memory_space=pltpu.SMEM)]
        + [pl.BlockSpec(memory_space=pltpu.VMEM)] * len(pieces)
        + [anywhere] * 6,
        out_specs=[pl.BlockSpec(memory_space=pltpu.VMEM)] * len(block_rows),
        out_shape=[jax.ShapeDtypeStruct((count, width), kept) for count in block_rows],
        scratch_shapes=[
            pltpu.VMEM((total, padded), kept),
            pltpu.VMEM((4, width, units), kept),
            pltpu.VMEM((2, units, width), kept),
            pltpu.VMEM((2, 4 * cap, padded), kept),
            pltpu.VMEM((2, 4 * cap, units), kept),
            pltpu.VMEM((2, 4 * cap, width), kept),
            pltpu.VMEM((2, total // 2, 4 * cap), kept),
            pltpu.SemaphoreType.DMA((6,)),
        ],
        compiler_params=pltpu.CompilerParams(vmem_limit_bytes=48 << 20),
        cost_estimate=pl.CostEstimate(
            flops=12 * total * width * units, bytes_accessed=24 << 20, transcendentals=total * units
        ),
        name="plane",
    )(ids, *pieces, *weights)


def merge_kernel(cut, x_ref, y_ref, passed_0_ref, passed_1_ref, x_out, y_out):
    def sum_of(one, other):
        return (one.astype(jnp.float32) + other.astype(jnp.float32)).astype(jnp.bfloat16)

    x_out[:cut, :] = sum_of(x_ref[:cut, :], passed_0_ref[...])
    x_out[cut:, :] = x_ref[cut:, :]
    y_out[:cut, :] = y_ref[:cut, :]
    y_out[cut:, :] = sum_of(y_ref[cut:, :], passed_1_ref[...])


def merge_passed(cut, to_x, to_y, passed_0, passed_1):
    return pl.pallas_call(
        functools.partial(merge_kernel, cut),
        out_shape=[jax.ShapeDtypeStruct(to_x.shape, to_x.dtype)] * 2,
        compiler_params=pltpu.CompilerParams(vmem_limit_bytes=16 << 20),
        name="merge",
    )(to_x, to_y, passed_0, passed_1)


def join_kernel(far_ref, risen_ref, own_ref, x_ref, y_ref, far_out, own_out):
    rows, width = far_ref.shape
    far = far_ref[...].astype(jnp.float32) + risen_ref[:rows, :width].astype(jnp.float32)
    far_out[...] = far.astype(jnp.bfloat16)
    total = own_ref[...].astype(jnp.float32) + x_ref[...].astype(jnp.float32) + y_ref[...].astype(jnp.float32)
    own_out[...] = total.astype(jnp.bfloat16)


def join(far, risen, own, from_x, from_y):
    return pl.pallas_call(
        join_kernel,
        out_shape=[jax.ShapeDtypeStruct(own.shape, own.dtype)] * 2,
        compiler_params=pltpu.CompilerParams(vmem_limit_bytes=16 << 20),
        name="join",
    )(far, risen, own, from_x, from_y)


def meet_kernel(far_0_ref, far_1_ref, risen_ref, x_ref, out_0, out_1, x_out):
    x_out[...] = x_ref[...]
    cut = out_0.shape[0]
    risen = risen_ref[...].astype(jnp.float32)
    out_0[...] = (far_0_ref[...].astype(jnp.float32) + risen[:cut]).astype(jnp.bfloat16)
    out_1[...] = (far_1_ref[...].astype(jnp.float32) + risen[cut:]).astype(jnp.bfloat16)


def meet(far_0, far_1, risen, x_part):
    outputs = (far_0, far_1, x_part)
    return pl.pallas_call(
        meet_kernel,
        out_shape=[jax.ShapeDtypeStruct(output.shape, output.dtype) for output in outputs],
        compiler_params=pltpu.CompilerParams(vmem_limit_bytes=16 << 20),
        name="meet",
    )(far_0, far_1, risen, x_part)


def join_passed_kernel(one_ref, passed_ref, other_ref, one_out, other_out):
    one_out[...] = (one_ref[...].astype(jnp.float32) + passed_ref[...].astype(jnp.float32)).astype(jnp.bfloat16)
    other_out[...] = other_ref[...]


def join_passed(one, passed, other):
    return pl.pallas_call(
        join_passed_kernel,
        out_shape=[jax.ShapeDtypeStruct(part.shape, part.dtype) for part in (one, other)],
        compiler_params=pltpu.CompilerParams(vmem_limit_bytes=16 << 20),
        name="join_passed",
    )(one, passed, other)


def along_x(value):
    return lax.ppermute(value, "kv", [(i, i ^ 1) for i in range(4)])


def along_y(value):
    return lax.ppermute(value, "kv", [(i, i ^ 2) for i in range(4)])


def around_z(value, hops=1):
    return lax.ppermute(value, "blk", [(i, (i + 2 * hops) % 8) for i in range(8)])


def across_chip(value):
    return lax.ppermute(value, "blk", [(i, i ^ 1) for i in range(8)])


def fence(*values):
    return lax.optimization_barrier(values)


def added(*parts):
    total = parts[0].astype(jnp.float32)
    for part in parts[1:]:
        total = total + part.astype(jnp.float32)
    return total


def permuted_plan(
    queries,
    cache_keys,
    cache_values,
    lengths,
    sinks,
    out_proj,
    decode_resid,
    prefill_hidden,
    norm_gain,
    router,
    routes,
    expert_gate,
    expert_up,
    expert_down,
):
    experts = router.shape[1]
    ids = routes[0]
    tokens = ids.shape[0]
    my_kv = lax.axis_index("kv")
    my_blk = lax.axis_index("blk")
    first_expert = my_kv * 8
    expert_ids = jnp.stack(
        [first_expert + my_blk, first_expert + (my_blk ^ 1), jnp.int32(experts)]
    ).astype(jnp.int32)
    cap = (2 * tokens * ids.shape[1] + experts - 1) // experts
    cut = tokens // 2 // 16 * 16
    few = 16

    def spread_sides(block):
        return along_x(block), along_y(block)

    def spread_corner(sides):
        return along_y(sides[0][:cut]), along_x(sides[1][cut:])

    def apply(pieces, counts):
        return run_plane(expert_ids, cap, few, pieces, counts, weights)

    def return_corner(sums):
        return along_y(sums[3]), along_x(sums[4])

    def return_sides(sums, passed=None):
        to_x, to_y = sums[1:3] if passed is None else merge_passed(cut, *sums[1:3], *passed)
        return along_x(to_x), along_y(to_y)

    prefill = prefill_hidden[0]
    block_0 = prepare(prefill, norm_gain, router, ids, "block")
    block_0, queries, cache_keys, expert_gate = fence(block_0, queries, cache_keys, expert_gate)
    block_1 = around_z(block_0)
    sides_0 = spread_sides(block_0)
    other_gate = across_chip(expert_gate[0])
    attended = attend(queries, cache_keys, cache_values, lengths, sinks)
    partial_proj = jnp.dot(attended, out_proj, preferred_element_type=jnp.float32)
    is_mine = jnp.arange(4)[:, None] == my_kv
    partial_proj += jnp.where(is_mine, decode_resid.astype(jnp.float32), 0.0)
    width = partial_proj.shape[1]
    ids_row = jnp.pad(ids[:1].astype(jnp.float32), ((0, 0), (0, width - ids.shape[1])))
    shared = jnp.concatenate([partial_proj, jnp.where(is_mine, ids_row, 0.0)], axis=0)
    shared = shared + along_x(shared)
    block_1, sides_0, other_gate = fence(block_1, sides_0, other_gate)

    corner_0 = spread_corner(sides_0)
    other_up = across_chip(expert_up[0])
    corner_0, shared, block_1, other_up, expert_down = fence(
        corner_0, shared, block_1, other_up, expert_down
    )

    shared = shared + along_y(shared)
    sides_1 = spread_sides(block_1)
    block_2 = around_z(block_1)
    other_down = across_chip(expert_down[0])
    order = [my_kv ^ j for j in range(4)]
    decoded = jnp.concatenate(
        [lax.dynamic_slice_in_dim(shared, index, 1) for index in order], axis=0
    ).astype(jnp.bfloat16)
    decode_ids = jnp.concatenate(
        [lax.dynamic_slice_in_dim(shared, 4 + index, 1) for index in order], axis=0
    )[:, : ids.shape[1]].astype(jnp.int32)
    hidden = jnp.concatenate([decoded[:1], prefill], axis=0)
    decodes_0 = prepare(
        jnp.pad(decoded, ((0, few - 4), (0, 0))),
        norm_gain,
        router,
        jnp.pad(decode_ids, ((0, few - 4), (0, 0))),
        "first",
    )
    side_x, block_2, side_y, decodes_0, other_down = fence(
        sides_1[0], block_2, sides_1[1], decodes_0, other_down
    )
    sides_1 = side_x, side_y
    weights = (expert_gate[0], expert_up[0], expert_down[0], other_gate, other_up, other_down)
    halves = (tokens, tokens, tokens, cut, tokens - cut)

    corner_1 = spread_corner(sides_1)
    sides_2 = spread_sides(block_2)
    arrived = around_z(jnp.concatenate([block_2, decodes_0], axis=0))
    sums_0 = apply((block_0,) + sides_0 + corner_0 + (decodes_0,), halves)
    corner_1, sides_2, arrived, sums_0 = fence(corner_1, sides_2, arrived, sums_0)
    block_3, decodes_1 = arrived[:tokens], arrived[tokens:]

    sides_3 = spread_sides(block_3)
    risen = around_z(jnp.concatenate(corner_1 + (decodes_1,), axis=0))
    passed_0 = return_corner(sums_0)
    sums_1 = apply((block_1,) + sides_1 + corner_1 + (decodes_1,), (tokens,) * 4)
    sides_3, risen, passed_0, sums_0, sums_1 = fence(sides_3, risen, passed_0, sums_0, sums_1)

    far = jnp.pad(sums_1[3], ((0, 0), (0, risen.shape[1] - sums_1[3].shape[1])))
    far = around_z(jnp.concatenate([far, risen[tokens:]], axis=0))
    corner_3 = spread_corner(sides_3)
    back_1 = return_sides(sums_1)
    sums_2 = apply((block_2,) + sides_2 + (risen,), (tokens,) * 4)
    far, corner_3, back_1, sums_1, sums_2 = fence(far, corner_3, back_1, sums_1, sums_2)
    decodes_3 = far[tokens:]

    far, first = join(sums_2[3], far, sums_1[0], *back_1)
    far = around_z(far)
    back_2 = return_sides(sums_2)
    carried_1 = around_z(first, -1)
    parts = (cut, tokens - cut)
    sums_3 = apply((block_3,) + sides_3 + corner_3 + (decodes_3,), (tokens,) + parts * 3)
    far, sums_2, sums_3 = fence(far, sums_2, sums_3)

    own, x_0, x_1, y_0, y_1, far_0, far_1 = sums_3
    far_0, far_1, x_1 = meet(far_0, far_1, far, x_1)
    passed_3 = along_y(far_0), along_x(far_1)
    back_x1 = along_x(x_1)
    passed_3, carried_1 = fence(passed_3, carried_1)
    y_1, y_0 = join_passed(y_1, passed_3[1], y_0)
    back_y1 = along_y(y_1)
    back_x0 = along_x(added(x_0, passed_3[0]).astype(jnp.bfloat16))
    back_y0 = along_y(y_0)
    carried = around_z(added(sums_2[0], *back_2).astype(jnp.bfloat16))
    carried, passed_0, sums_0 = fence(carried, passed_0, sums_0)
    back_0 = return_sides(sums_0, passed_0)
    late = around_z(added(own[cut:], back_x1, back_y1, carried[cut:]).astype(jnp.bfloat16))
    early = around_z(added(own[:cut], back_x0, back_y0, carried[:cut]).astype(jnp.bfloat16))
    carried = jnp.concatenate([early, late], axis=0)
    return added(hidden, sums_0[0], carried_1, *back_0, carried).astype(jnp.bfloat16)[None]


def chunk_cuts(tokens, devices):
    step = (tokens // 2 + 15) // 16 * 16 if devices < 128 else 32
    return [(start, min(start + step, tokens)) for start in range(0, tokens, step)]


def gathered_plan(
    queries,
    cache_keys,
    cache_values,
    lengths,
    sinks,
    out_proj,
    decode_resid,
    prefill_hidden,
    norm_gain,
    router,
    routes,
    expert_gate,
    expert_up,
    expert_down,
):
    experts = router.shape[1]
    ids = routes[0]
    tokens = ids.shape[0]
    prefill = prefill_hidden[0]
    devices = lax.axis_size(AXES)
    cuts = chunk_cuts(tokens, devices)
    my_expert = lax.axis_index("kv") * lax.axis_size("blk") + lax.axis_index("blk")
    expert = jnp.stack([my_expert, jnp.int32(experts)]).astype(jnp.int32)
    weights = (expert_gate[0], expert_up[0], expert_down[0])

    attended = attend(queries, cache_keys, cache_values, lengths, sinks)
    partial_proj = jnp.dot(attended, out_proj, preferred_element_type=jnp.float32)
    projected = lax.psum_scatter(partial_proj, "kv", scatter_dimension=0, tiled=True)
    decoded = (decode_resid.astype(jnp.float32) + projected).astype(jnp.bfloat16)
    hidden = jnp.concatenate([prefill, decoded], axis=0)
    ids = jnp.concatenate([ids[1:], ids[:1]], axis=0)
    gathered = []
    for start, stop in cuts:
        source = prefill[start:stop] if stop < tokens else hidden[start:stop]
        sent = prepare(source, norm_gain, router, ids[start:stop])
        gathered.append(lax.all_gather(sent, AXES, axis=0, tiled=True))
    returned = []
    for rows in gathered:
        sums = run_expert(expert, rows, *weights)
        returned.append(lax.psum_scatter(sums, AXES, scatter_dimension=0, tiled=True))
    combined = jnp.concatenate(returned, axis=0)
    layer_sum = (hidden.astype(jnp.float32) + combined.astype(jnp.float32)).astype(jnp.bfloat16)
    layer_sum = jnp.concatenate([layer_sum[-1:], layer_sum[:-1]], axis=0)
    return layer_sum[None]


def solution(mesh):
    plan = permuted_plan if (mesh.shape["kv"], mesh.shape["blk"]) == (4, 8) else gathered_plan
    return jax.shard_map(
        plan,
        mesh=mesh,
        in_specs=(
            P("blk", "kv"),
            P("blk", None, "kv", None),
            P("blk", None, "kv", None),
            P(),
            P("kv"),
            P("kv", None),
            P(("blk", "kv"), None),
            P(("blk", "kv"), None, None),
            P(),
            P(),
            P(("blk", "kv"), None, None),
            P(("kv", "blk"), None, None),
            P(("kv", "blk"), None, None),
            P(("kv", "blk"), None, None),
        ),
        out_specs=P(("blk", "kv"), None, None),
        check_vma=False,
    )
```

```python
import functools
import math

import jax
import jax.numpy as jnp
from jax import lax
from jax.experimental import pallas as pl
from jax.experimental.pallas import tpu as pltpu
from jax.sharding import PartitionSpec as P

NEG_FILL = -1e30
EPSILON = 1e-06
NOT_CHOSEN = -256.0
AXES = ("blk", "kv")


def attend(queries, cache_keys, cache_values, lengths, sinks):
    my_block = lax.axis_index("blk")
    per_block = queries.shape[0]
    head_count = sinks.shape[0]
    head_dim = cache_keys.shape[3]
    window = cache_keys.shape[1]
    grouped_q = queries.reshape(per_block, head_count, head_dim)
    key_rows = cache_keys[:, :, 0, :]
    value_rows = cache_values[:, :, 0, :]
    my_lengths = lax.dynamic_slice_in_dim(lengths, my_block * per_block, per_block)
    scores = jnp.einsum("rgd,rjd->rgj", grouped_q, key_rows, preferred_element_type=jnp.float32) * (
        1.0 / math.sqrt(head_dim)
    )
    first_valid = window - jnp.minimum(my_lengths, window)
    is_valid = (jnp.arange(window, dtype=jnp.int32)[None, :] >= first_valid[:, None])[:, None, :]
    masked = jnp.where(is_valid, scores, NEG_FILL)
    top_limit = jnp.maximum(jnp.max(masked, axis=2), sinks[None, :])
    weights = jnp.where(is_valid, jnp.exp(masked - top_limit[..., None]), 0.0)
    denominator = jnp.sum(weights, axis=2) + jnp.exp(sinks[None, :] - top_limit)
    numerator = jnp.einsum(
        "rgj,rjd->rgd", weights.astype(jnp.bfloat16), value_rows, preferred_element_type=jnp.float32
    )
    return (
        (numerator / denominator[..., None])
        .astype(jnp.bfloat16)
        .reshape(per_block, head_count * head_dim)
    )


def prepare_kernel(ranking, hidden_ref, gain_ref, router_ref, routes_ref, out_ref, *scratch):
    experts, width = router_ref.shape
    if scratch:
        (shifted,) = scratch
        shifted[0:1, :] = jnp.zeros((1, width), jnp.float32)
        shifted[1:, :] = hidden_ref[...].astype(jnp.float32)
        hidden = shifted[...]
    else:
        hidden = hidden_ref[...].astype(jnp.float32)
    rows = hidden.shape[0]
    mean_sq = jnp.mean(hidden * hidden, axis=1, keepdims=True)
    normed = (hidden * lax.rsqrt(mean_sq + EPSILON) * gain_ref[...]).astype(jnp.bfloat16)
    out_ref[:, :width] = normed
    by_lanes = (((1,), (1,)), ((), ()))
    logits = lax.dot_general(normed, router_ref[...], by_lanes, preferred_element_type=jnp.float32)
    routes = routes_ref[...]
    if ranking == "first":
        expert = lax.broadcasted_iota(jnp.int32, logits.shape, 1)
        mine = jnp.zeros(logits.shape, jnp.bool_)
        for k in range(routes.shape[1]):
            mine = mine | (expert == routes[:, k : k + 1])
    else:
        expert = lax.broadcasted_iota(jnp.int32, (experts, rows), 0)
        chosen = jnp.zeros(expert.shape, jnp.bool_)
        for k in range(routes.shape[0]):
            chosen = chosen | (expert == routes[k : k + 1, :])
        chosen = jnp.where(chosen, 1.0, 0.0).astype(jnp.bfloat16)
        row = lax.broadcasted_iota(jnp.int32, (rows, rows), 0)
        other = lax.broadcasted_iota(jnp.int32, (rows, rows), 1)

        def of_rows(taken):
            taken = jnp.where(taken, 1.0, 0.0).astype(jnp.bfloat16)
            return lax.dot_general(taken, chosen, by_lanes, preferred_element_type=jnp.float32)

        mine = of_rows(row == other) > 0.5
    top = jnp.max(jnp.where(mine, logits, NEG_FILL), axis=1, keepdims=True)
    raised = jnp.where(mine, jnp.exp(jnp.minimum(logits - top, 0.0)), 0.0)
    gates = raised / jnp.sum(raised, axis=1, keepdims=True)
    high = gates.astype(jnp.bfloat16).astype(jnp.float32)
    parts = [high, gates - high]
    if ranking == "block":
        parts.append(jnp.where(mine, of_rows(other < row), NOT_CHOSEN))
    elif ranking == "first":
        parts.append(jnp.where(mine, 0.0, NOT_CHOSEN))
    rest = out_ref.shape[1] - width - len(parts) * experts
    if rest:
        parts.append(jnp.zeros((rows, rest), jnp.float32))
    out_ref[:, width:] = jnp.concatenate(parts, axis=1).astype(jnp.bfloat16)


def prepare(hidden, norm_gain, router, routes, ranking=None):
    width = hidden.shape[1]
    rows = routes.shape[0]
    extra = -(-(3 if ranking else 2) * router.shape[1] // 128) * 128
    shifted = rows > hidden.shape[0]
    return pl.pallas_call(
        functools.partial(prepare_kernel, ranking),
        out_shape=jax.ShapeDtypeStruct((rows, width + extra), jnp.bfloat16),
        scratch_shapes=[pltpu.VMEM((rows, width), jnp.float32)] if shifted else [],
        compiler_params=pltpu.CompilerParams(vmem_limit_bytes=32 << 20),
        name="prepare",
    )(hidden, norm_gain.reshape(1, width), router.T, routes if ranking == "first" else routes.T)


def expert_kernel(expert_ref, rows_ref, gate_ref, up_ref, down_ref, out_ref):
    width = gate_ref.shape[0]
    payload = rows_ref[...]
    rows = payload[:, :width]
    tail = payload[:, width:].astype(jnp.float32)
    lane = lax.broadcasted_iota(jnp.int32, tail.shape, 1)
    expert = expert_ref[0]
    experts = expert_ref[1]
    mine = (lane == expert) | (lane == expert + experts)
    weight = jnp.sum(jnp.where(mine, tail, 0.0), axis=1, keepdims=True)
    gate_act = jnp.dot(rows, gate_ref[...], preferred_element_type=jnp.float32)
    up_act = jnp.dot(rows, up_ref[...], preferred_element_type=jnp.float32)
    inner = (gate_act / (1.0 + jnp.exp(-gate_act)) * up_act).astype(jnp.bfloat16)
    result = jnp.dot(inner, down_ref[...], preferred_element_type=jnp.float32)
    out_ref[...] = (weight * result).astype(jnp.bfloat16)


def run_expert(expert, rows, gate_weights, up_weights, down_weights):
    total, padded = rows.shape
    width, hidden_units = gate_weights.shape
    tile = 256
    return pl.pallas_call(
        expert_kernel,
        grid_spec=pltpu.PrefetchScalarGridSpec(
            num_scalar_prefetch=1,
            grid=(total // tile,),
            in_specs=[
                pl.BlockSpec((tile, padded), lambda i, e: (i, 0)),
                pl.BlockSpec((width, hidden_units), lambda i, e: (0, 0), pipeline_mode=pl.Buffered(1)),
                pl.BlockSpec((width, hidden_units), lambda i, e: (0, 0), pipeline_mode=pl.Buffered(1)),
                pl.BlockSpec((hidden_units, width), lambda i, e: (0, 0), pipeline_mode=pl.Buffered(1)),
            ],
            out_specs=pl.BlockSpec((tile, width), lambda i, e: (i, 0)),
        ),
        out_shape=jax.ShapeDtypeStruct((total, width), jnp.bfloat16),
        compiler_params=pltpu.CompilerParams(vmem_limit_bytes=48 << 20),
        name="expert",
    )(expert, rows, gate_weights, up_weights, down_weights)


def plane_kernel(cap, piece_rows, block_rows, *refs):
    refs = list(refs)
    ids_ref = refs.pop(0)
    sources = [refs.pop(0) for _ in piece_rows]
    weight_refs = [refs.pop(0) for _ in range(6)]
    targets = [refs.pop(0) for _ in block_rows]
    rows, weights, downs, slots, inner, results, spread, weight_sem = refs
    width = results.shape[2]
    tokens = block_rows[0]
    pair_rows = 2 * tokens
    pair_slots = 2 * cap
    up_copies = [
        pltpu.make_async_copy(weight_refs[3 * e + i], weights.at[2 * e + i], weight_sem.at[2 * e + i])
        for e in range(2)
        for i in range(2)
    ]
    down_copies = [
        pltpu.make_async_copy(weight_refs[3 * e + 2], downs.at[e], weight_sem.at[4 + e])
        for e in range(2)
    ]
    for copy in up_copies + down_copies:
        copy.start()
    few = piece_rows[-1] - (2 * pair_rows - sum(piece_rows[:-1]))
    at = 0
    for ref, count in zip(sources, piece_rows):
        if ref is sources[-1]:
            count -= few
            decodes = ref[count:, :].astype(jnp.float32)
        if count:
            rows[pl.ds(at, count), :] = ref[:count, :]
        at += count
    is_first = lax.broadcasted_iota(jnp.int32, (few, 1), 0) == 0
    for j in range(4):
        part = pl.ds(j * tokens, few)
        kept = rows[part, :].astype(jnp.float32)
        rows[part, :] = jnp.where(is_first, decodes[j : j + 1], kept).astype(jnp.bfloat16)

    experts = ids_ref[2]
    extra = rows.shape[1] - width
    lanes = lax.broadcasted_iota(jnp.int32, (8, extra), 1)
    line = lax.broadcasted_iota(jnp.int32, (8, extra), 0)
    wanted = ((line == 0) & (lanes == ids_ref[0] + 2 * experts)) | (
        (line == 1) & (lanes == ids_ref[1] + 2 * experts)
    )
    wanted = jnp.where(wanted, 1.0, 0.0).astype(jnp.bfloat16)
    pairs = [pl.ds(p * pair_rows, pair_rows) for p in range(2)]

    def shift_of(shape, axis):
        second = lax.broadcasted_iota(jnp.int32, shape, axis) >= tokens
        return jnp.where(second, float(cap), 0.0)

    for p in range(2):
        ranks = lax.dot_general(
            wanted, rows[pairs[p], width:], (((1,), (1,)), ((), ())), preferred_element_type=jnp.float32
        )
        ranks += shift_of(ranks.shape, 1)
        slot = lax.broadcasted_iota(jnp.int32, (2 * pair_slots, pair_rows), 0).astype(jnp.float32)
        taken = (slot == ranks[0:1]) | (slot == ranks[1:2] + float(pair_slots))
        taken = jnp.where(taken, 1.0, 0.0).astype(jnp.bfloat16)
        picked = jnp.dot(taken, rows[pairs[p], :], preferred_element_type=jnp.float32)
        picked = picked.astype(jnp.bfloat16)
        for e in range(2):
            slots[e, pl.ds(p * pair_slots, pair_slots), :] = picked[e * pair_slots : (e + 1) * pair_slots]

    def make_spread(p):
        tail = rows[pairs[p], width:].astype(jnp.float32)
        lane = lax.broadcasted_iota(jnp.int32, tail.shape, 1)
        slot = lax.broadcasted_iota(jnp.int32, (pair_rows, 2 * pair_slots), 1).astype(jnp.float32)
        back = jnp.zeros(slot.shape, jnp.bool_)
        for e in range(2):
            mine = lane == ids_ref[e] + 2 * experts
            rank = jnp.sum(jnp.where(mine, tail, 0.0), axis=1, keepdims=True)
            back = back | (slot == rank + shift_of(rank.shape, 0) + float(e * pair_slots))
        spread[p] = jnp.where(back, 1.0, 0.0).astype(jnp.bfloat16)

    def weight_of(e):
        tail = slots[e, :, width:].astype(jnp.float32)
        lane = lax.broadcasted_iota(jnp.int32, tail.shape, 1)
        mine = (lane == ids_ref[e]) | (lane == ids_ref[e] + experts)
        return jnp.sum(jnp.where(mine, tail, 0.0), axis=1, keepdims=True)

    def product(e, i):
        return jnp.dot(slots[e, :, :width], weights[2 * e + i], preferred_element_type=jnp.float32)

    def activate(e, gate_act, up_act):
        act = gate_act / (1.0 + jnp.exp(-gate_act)) * up_act * weight_of(e)
        inner[e] = act.astype(jnp.bfloat16)

    def finish(e):
        result = jnp.dot(inner[e], downs[e], preferred_element_type=jnp.float32)
        result = result.astype(jnp.bfloat16)
        for p in range(2):
            results[p, pl.ds(e * pair_slots, pair_slots), :] = result[p * pair_slots : (p + 1) * pair_slots]

    up_copies[0].wait()
    gate_0 = product(0, 0)
    make_spread(0)
    up_copies[1].wait()
    up_0 = product(0, 1)
    make_spread(1)
    up_copies[2].wait()
    activate(0, gate_0, up_0)
    gate_1 = product(1, 0)
    up_copies[3].wait()
    up_1 = product(1, 1)
    down_copies[0].wait()
    finish(0)
    activate(1, gate_1, up_1)
    down_copies[1].wait()
    finish(1)
    ends = [sum(block_rows[: i + 1]) for i in range(len(block_rows))]
    for p in range(2):
        total = jnp.dot(spread[p], results[p], preferred_element_type=jnp.float32)
        total = total.astype(jnp.bfloat16)
        for ref, count, end in zip(targets, block_rows, ends):
            if p * pair_rows < end <= (p + 1) * pair_rows:
                at = end - count - p * pair_rows
                ref[...] = total[at : at + count]


def run_plane(ids, cap, few, pieces, block_rows, weights):
    width, units = weights[0].shape
    padded = pieces[0].shape[1]
    piece_rows = tuple(piece.shape[0] for piece in pieces)
    total = sum(piece_rows) - few
    kept = jnp.bfloat16
    anywhere = pl.BlockSpec(memory_space=pl.ANY)
    return pl.pallas_call(
        functools.partial(plane_kernel, cap, piece_rows, block_rows),
        in_specs=[pl.BlockSpec(memory_space=pltpu.SMEM)]
        + [pl.BlockSpec(memory_space=pltpu.VMEM)] * len(pieces)
        + [anywhere] * 6,
        out_specs=[pl.BlockSpec(memory_space=pltpu.VMEM)] * len(block_rows),
        out_shape=[jax.ShapeDtypeStruct((count, width), kept) for count in block_rows],
        scratch_shapes=[
            pltpu.VMEM((total, padded), kept),
            pltpu.VMEM((4, width, units), kept),
            pltpu.VMEM((2, units, width), kept),
            pltpu.VMEM((2, 4 * cap, padded), kept),
            pltpu.VMEM((2, 4 * cap, units), kept),
            pltpu.VMEM((2, 4 * cap, width), kept),
            pltpu.VMEM((2, total // 2, 4 * cap), kept),
            pltpu.SemaphoreType.DMA((6,)),
        ],
        compiler_params=pltpu.CompilerParams(vmem_limit_bytes=48 << 20),
        cost_estimate=pl.CostEstimate(
            flops=12 * total * width * units, bytes_accessed=24 << 20, transcendentals=total * units
        ),
        name="plane",
    )(ids, *pieces, *weights)


def merge_kernel(cut, x_ref, y_ref, passed_0_ref, passed_1_ref, x_out, y_out):
    def sum_of(one, other):
        return (one.astype(jnp.float32) + other.astype(jnp.float32)).astype(jnp.bfloat16)

    x_out[:cut, :] = sum_of(x_ref[:cut, :], passed_0_ref[...])
    x_out[cut:, :] = x_ref[cut:, :]
    y_out[:cut, :] = y_ref[:cut, :]
    y_out[cut:, :] = sum_of(y_ref[cut:, :], passed_1_ref[...])


def merge_passed(cut, to_x, to_y, passed_0, passed_1):
    return pl.pallas_call(
        functools.partial(merge_kernel, cut),
        out_shape=[jax.ShapeDtypeStruct(to_x.shape, to_x.dtype)] * 2,
        compiler_params=pltpu.CompilerParams(vmem_limit_bytes=16 << 20),
        name="merge",
    )(to_x, to_y, passed_0, passed_1)


def join_kernel(far_ref, risen_ref, own_ref, x_ref, y_ref, far_out, own_out):
    rows, width = far_ref.shape
    far = far_ref[...].astype(jnp.float32) + risen_ref[:rows, :width].astype(jnp.float32)
    far_out[...] = far.astype(jnp.bfloat16)
    total = own_ref[...].astype(jnp.float32) + x_ref[...].astype(jnp.float32) + y_ref[...].astype(jnp.float32)
    own_out[...] = total.astype(jnp.bfloat16)


def join(far, risen, own, from_x, from_y):
    return pl.pallas_call(
        join_kernel,
        out_shape=[jax.ShapeDtypeStruct(own.shape, own.dtype)] * 2,
        compiler_params=pltpu.CompilerParams(vmem_limit_bytes=16 << 20),
        name="join",
    )(far, risen, own, from_x, from_y)


def meet_kernel(far_0_ref, far_1_ref, risen_ref, x_ref, out_0, out_1, x_out):
    x_out[...] = x_ref[...]
    cut = out_0.shape[0]
    risen = risen_ref[...].astype(jnp.float32)
    out_0[...] = (far_0_ref[...].astype(jnp.float32) + risen[:cut]).astype(jnp.bfloat16)
    out_1[...] = (far_1_ref[...].astype(jnp.float32) + risen[cut:]).astype(jnp.bfloat16)


def meet(far_0, far_1, risen, x_part):
    outputs = (far_0, far_1, x_part)
    return pl.pallas_call(
        meet_kernel,
        out_shape=[jax.ShapeDtypeStruct(output.shape, output.dtype) for output in outputs],
        compiler_params=pltpu.CompilerParams(vmem_limit_bytes=16 << 20),
        name="meet",
    )(far_0, far_1, risen, x_part)


def join_passed_kernel(one_ref, passed_ref, other_ref, one_out, other_out):
    one_out[...] = (one_ref[...].astype(jnp.float32) + passed_ref[...].astype(jnp.float32)).astype(jnp.bfloat16)
    other_out[...] = other_ref[...]


def join_passed(one, passed, other):
    return pl.pallas_call(
        join_passed_kernel,
        out_shape=[jax.ShapeDtypeStruct(part.shape, part.dtype) for part in (one, other)],
        compiler_params=pltpu.CompilerParams(vmem_limit_bytes=16 << 20),
        name="join_passed",
    )(one, passed, other)


def along_x(value):
    return lax.ppermute(value, "kv", [(i, i ^ 1) for i in range(4)])


def along_y(value):
    return lax.ppermute(value, "kv", [(i, i ^ 2) for i in range(4)])


def around_z(value, hops=1):
    return lax.ppermute(value, "blk", [(i, (i + 2 * hops) % 8) for i in range(8)])


def across_chip(value):
    return lax.ppermute(value, "blk", [(i, i ^ 1) for i in range(8)])


def fence(*values):
    return lax.optimization_barrier(values)


def added(*parts):
    total = parts[0].astype(jnp.float32)
    for part in parts[1:]:
        total = total + part.astype(jnp.float32)
    return total


def permuted_plan(
    queries,
    cache_keys,
    cache_values,
    lengths,
    sinks,
    out_proj,
    decode_resid,
    prefill_hidden,
    norm_gain,
    router,
    routes,
    expert_gate,
    expert_up,
    expert_down,
):
    experts = router.shape[1]
    ids = routes[0]
    tokens = ids.shape[0]
    my_kv = lax.axis_index("kv")
    my_blk = lax.axis_index("blk")
    first_expert = my_kv * 8
    expert_ids = jnp.stack(
        [first_expert + my_blk, first_expert + (my_blk ^ 1), jnp.int32(experts)]
    ).astype(jnp.int32)
    cap = (2 * tokens * ids.shape[1] + experts - 1) // experts
    cut = tokens // 2 // 16 * 16
    few = 16

    def spread_sides(block):
        return along_x(block), along_y(block)

    def spread_corner(sides):
        return along_y(sides[0][:cut]), along_x(sides[1][cut:])

    def apply(pieces, counts):
        return run_plane(expert_ids, cap, few, pieces, counts, weights)

    def return_corner(sums):
        return along_y(sums[3]), along_x(sums[4])

    def return_sides(sums, passed=None):
        to_x, to_y = sums[1:3] if passed is None else merge_passed(cut, *sums[1:3], *passed)
        return along_x(to_x), along_y(to_y)

    prefill = prefill_hidden[0]
    block_0 = prepare(prefill, norm_gain, router, ids, "block")
    block_0, queries, cache_keys, expert_gate = fence(block_0, queries, cache_keys, expert_gate)
    block_1 = around_z(block_0)
    sides_0 = spread_sides(block_0)
    other_gate = across_chip(expert_gate[0])
    attended = attend(queries, cache_keys, cache_values, lengths, sinks)
    partial_proj = jnp.dot(attended, out_proj, preferred_element_type=jnp.float32)
    is_mine = jnp.arange(4)[:, None] == my_kv
    partial_proj += jnp.where(is_mine, decode_resid.astype(jnp.float32), 0.0)
    width = partial_proj.shape[1]
    ids_row = jnp.pad(ids[:1].astype(jnp.float32), ((0, 0), (0, width - ids.shape[1])))
    shared = jnp.concatenate([partial_proj, jnp.where(is_mine, ids_row, 0.0)], axis=0)
    shared = shared + along_x(shared)
    sides_0, block_1, other_gate = fence(sides_0, block_1, other_gate)

    corner_0 = spread_corner(sides_0)
    other_up = across_chip(expert_up[0])
    corner_0, shared, block_1, other_up, expert_down = fence(
        corner_0, shared, block_1, other_up, expert_down
    )

    shared = shared + along_y(shared)
    sides_1 = spread_sides(block_1)
    block_2 = around_z(block_1)
    other_down = across_chip(expert_down[0])
    order = [my_kv ^ j for j in range(4)]
    decoded = jnp.concatenate(
        [lax.dynamic_slice_in_dim(shared, index, 1) for index in order], axis=0
    ).astype(jnp.bfloat16)
    decode_ids = jnp.concatenate(
        [lax.dynamic_slice_in_dim(shared, 4 + index, 1) for index in order], axis=0
    )[:, : ids.shape[1]].astype(jnp.int32)
    hidden = jnp.concatenate([decoded[:1], prefill], axis=0)
    decodes_0 = prepare(
        jnp.pad(decoded, ((0, few - 4), (0, 0))),
        norm_gain,
        router,
        jnp.pad(decode_ids, ((0, few - 4), (0, 0))),
        "first",
    )
    sides_1, block_2, decodes_0, other_down = fence(sides_1, block_2, decodes_0, other_down)
    weights = (expert_gate[0], expert_up[0], expert_down[0], other_gate, other_up, other_down)
    halves = (tokens, tokens, tokens, cut, tokens - cut)

    corner_1 = spread_corner(sides_1)
    sides_2 = spread_sides(block_2)
    arrived = around_z(jnp.concatenate([block_2, decodes_0], axis=0))
    sums_0 = apply((block_0,) + sides_0 + corner_0 + (decodes_0,), halves)
    corner_1, sides_2, arrived, sums_0 = fence(corner_1, sides_2, arrived, sums_0)
    block_3, decodes_1 = arrived[:tokens], arrived[tokens:]

    sides_3 = spread_sides(block_3)
    risen = around_z(jnp.concatenate(corner_1 + (decodes_1,), axis=0))
    passed_0 = return_corner(sums_0)
    sums_1 = apply((block_1,) + sides_1 + corner_1 + (decodes_1,), (tokens,) * 4)
    sides_3, risen, passed_0, sums_0, sums_1 = fence(sides_3, risen, passed_0, sums_0, sums_1)

    far = jnp.pad(sums_1[3], ((0, 0), (0, risen.shape[1] - sums_1[3].shape[1])))
    far = around_z(jnp.concatenate([far, risen[tokens:]], axis=0))
    corner_3 = spread_corner(sides_3)
    back_1 = return_sides(sums_1)
    sums_2 = apply((block_2,) + sides_2 + (risen,), (tokens,) * 4)
    back_y, far, back_x, corner_3, sums_1, sums_2 = fence(
        back_1[1], far, back_1[0], corner_3, sums_1, sums_2
    )
    back_1 = back_x, back_y
    decodes_3 = far[tokens:]

    far, first = join(sums_2[3], far, sums_1[0], *back_1)
    far = around_z(far)
    back_2 = return_sides(sums_2)
    carried_1 = around_z(first, -1)
    parts = (cut, tokens - cut)
    sums_3 = apply((block_3,) + sides_3 + corner_3 + (decodes_3,), (tokens,) + parts * 3)
    far, sums_2, sums_3 = fence(far, sums_2, sums_3)

    own, x_0, x_1, y_0, y_1, far_0, far_1 = sums_3
    far_0, far_1, x_1 = meet(far_0, far_1, far, x_1)
    passed_3 = along_y(far_0), along_x(far_1)
    back_x1 = along_x(x_1)
    passed_3, carried_1 = fence(passed_3, carried_1)
    y_1, y_0 = join_passed(y_1, passed_3[1], y_0)
    back_y1 = along_y(y_1)
    back_x0 = along_x(added(x_0, passed_3[0]).astype(jnp.bfloat16))
    back_y0 = along_y(y_0)
    carried = around_z(added(sums_2[0], *back_2).astype(jnp.bfloat16))
    carried, passed_0, sums_0 = fence(carried, passed_0, sums_0)
    back_0 = return_sides(sums_0, passed_0)
    late = around_z(added(own[cut:], back_x1, back_y1, carried[cut:]).astype(jnp.bfloat16))
    early = around_z(added(own[:cut], back_x0, back_y0, carried[:cut]).astype(jnp.bfloat16))
    carried = jnp.concatenate([early, late], axis=0)
    return added(hidden, sums_0[0], carried_1, *back_0, carried).astype(jnp.bfloat16)[None]


def chunk_cuts(tokens, devices):
    step = (tokens // 2 + 15) // 16 * 16 if devices < 128 else 32
    return [(start, min(start + step, tokens)) for start in range(0, tokens, step)]


def gathered_plan(
    queries,
    cache_keys,
    cache_values,
    lengths,
    sinks,
    out_proj,
    decode_resid,
    prefill_hidden,
    norm_gain,
    router,
    routes,
    expert_gate,
    expert_up,
    expert_down,
):
    experts = router.shape[1]
    ids = routes[0]
    tokens = ids.shape[0]
    prefill = prefill_hidden[0]
    devices = lax.axis_size(AXES)
    cuts = chunk_cuts(tokens, devices)
    my_expert = lax.axis_index("kv") * lax.axis_size("blk") + lax.axis_index("blk")
    expert = jnp.stack([my_expert, jnp.int32(experts)]).astype(jnp.int32)
    weights = (expert_gate[0], expert_up[0], expert_down[0])

    attended = attend(queries, cache_keys, cache_values, lengths, sinks)
    partial_proj = jnp.dot(attended, out_proj, preferred_element_type=jnp.float32)
    projected = lax.psum_scatter(partial_proj, "kv", scatter_dimension=0, tiled=True)
    decoded = (decode_resid.astype(jnp.float32) + projected).astype(jnp.bfloat16)
    hidden = jnp.concatenate([prefill, decoded], axis=0)
    ids = jnp.concatenate([ids[1:], ids[:1]], axis=0)
    gathered = []
    for start, stop in cuts:
        source = prefill[start:stop] if stop < tokens else hidden[start:stop]
        sent = prepare(source, norm_gain, router, ids[start:stop])
        gathered.append(lax.all_gather(sent, AXES, axis=0, tiled=True))
    returned = []
    for rows in gathered:
        sums = run_expert(expert, rows, *weights)
        returned.append(lax.psum_scatter(sums, AXES, scatter_dimension=0, tiled=True))
    combined = jnp.concatenate(returned, axis=0)
    layer_sum = (hidden.astype(jnp.float32) + combined.astype(jnp.float32)).astype(jnp.bfloat16)
    layer_sum = jnp.concatenate([layer_sum[-1:], layer_sum[:-1]], axis=0)
    return layer_sum[None]


def solution(mesh):
    plan = permuted_plan if (mesh.shape["kv"], mesh.shape["blk"]) == (4, 8) else gathered_plan
    return jax.shard_map(
        plan,
        mesh=mesh,
        in_specs=(
            P("blk", "kv"),
            P("blk", None, "kv", None),
            P("blk", None, "kv", None),
            P(),
            P("kv"),
            P("kv", None),
            P(("blk", "kv"), None),
            P(("blk", "kv"), None, None),
            P(),
            P(),
            P(("blk", "kv"), None, None),
            P(("kv", "blk"), None, None),
            P(("kv", "blk"), None, None),
            P(("kv", "blk"), None, None),
        ),
        out_specs=P(("blk", "kv"), None, None),
        check_vma=False,
    )
```
